32 devices in a mesh: dp: 8 (over z, x), mp: 4 (over y, core).
Axes of the slice: x: 2, y: 2, z: 4, core: 2. Of those that a mesh axis runs over, the one named last changes fastest.
Arguments:
- block_input: bfloat16 [12544, 1280], P('dp'), may hold values from -6 to 6
- window_place: int32 [64], P('dp'), may hold values from 0 to 24, as said below
- slot_live: int32 [64], P('dp'), may hold values from 0 to 1, as said below
- norm_one_gain: float32 [1280], replicated, may hold values from 0.25 to 1.75
- norm_one_shift: float32 [1280], replicated, may hold values from -1 to 1
- qkv_weight: bfloat16 [3, 1280, 1280], P(None, 'dp', 'mp'), may hold values from -0.15625 to 0.15625
- qv_bias: float32 [2, 1280], replicated, may hold values from -1.5 to 1.5
- proj_weight: bfloat16 [1280, 1280], P('mp', 'dp'), may hold values from -1.25 to 1.25
- proj_bias: float32 [1280], replicated, may hold values from -1 to 1
- norm_two_gain: float32 [1280], replicated, may hold values from 0.25 to 1.75
- norm_two_shift: float32 [1280], replicated, may hold values from -1 to 1
- up_weight: bfloat16 [1280, 5120], P('dp', 'mp'), may hold values from -0.15625 to 0.15625
- up_bias: float32 [5120], replicated, may hold values from -1.5 to 1.5
- down_weight: bfloat16 [5120, 1280], P('mp', 'dp'), may hold values from -0.078125 to 0.078125
- down_bias: float32 [1280], replicated, may hold values from -1 to 1
- rel_height: float32 [27, 80], replicated, may hold values from -0.9 to 0.9
- rel_width: float32 [27, 80], replicated, may hold values from -0.9 to 0.9
- cotangent: bfloat16 [12544, 1280], P('dp'), may hold values from -6 to 6
Outputs:
- block_output: bfloat16 [12544, 1280], P('dp')
- input_grad: float32 [12544, 1280], P('dp')
- norm_one_gain_grad: float32 [1280], replicated
- norm_one_shift_grad: float32 [1280], replicated
- qkv_grad: float32 [3, 1280, 1280], P(None, 'dp', 'mp')
- qv_bias_grad: float32 [2, 1280], replicated
- proj_grad: float32 [1280, 1280], P('mp', 'dp')
- proj_bias_grad: float32 [1280], replicated
- norm_two_gain_grad: float32 [1280], replicated
- norm_two_shift_grad: float32 [1280], replicated
- up_grad: float32 [1280, 5120], P('dp', 'mp')
- up_bias_grad: float32 [5120], replicated
- down_grad: float32 [5120, 1280], P('mp', 'dp')
- down_bias_grad: float32 [1280], replicated
- rel_height_grad: float32 [27, 80], replicated
- rel_width_grad: float32 [27, 80], replicated
The draws below stay inside these ranges and needn't reach their ends.
Inputs may be any that keep to these rules, and one draw needn't show every extreme that they name: `window_place`: the first 4 slots of each device belong to the first micro-batch, the next 4 to the second. Over all devices, the live slots of the first micro-batch hold the windows of 1 image, those of the second micro-batch the windows of 1 image, each image's 5 * 5 places once each; a padding slot's place is arbitrary. `slot_live`: exactly 25 of the first micro-batch's slots and 25 of the second's are live, spread over the devices in any way.
All inputs are finite; a program needn't handle non-finite values.
Results may differ from the reference program's by a relative error of at most 0.017.
Values may be sent and summed in bfloat16 or wider, within the bound.
No kernel may reach another device: no remote copies, remote signals or barrier semaphores. Data moves between devices by JAX's collectives and lax.ppermute only.
A program may use at most 256 MiB of HBM per device.

```python
import jax
import jax.numpy as jnp
from jax import lax

D = 1280
HEADS = 16
HD = 80
FF = 5120
WIN = 14
SIDE = 64
GRID = 5
WTOK = 196
RELN = 27
IMG_A = 1
IMG_B = 1
SLOT_A = 4
SLOT_B = 4
SLOTS = 8
TOKENS = 12544
N_DP = 8


def slot_table(key):
    places = GRID * GRID
    place_parts = []
    live_parts = []
    for section, slots, images in ((0, SLOT_A, IMG_A), (1, SLOT_B, IMG_B)):
        order = jax.random.permutation(jax.random.fold_in(key, 101 + section), N_DP * slots).astype(jnp.int32)
        place_parts.append((order % places).reshape(N_DP, slots))
        live_parts.append(jnp.where(order < images * places, 1, 0).astype(jnp.int32).reshape(N_DP, slots))
    return (jnp.concatenate(place_parts, axis=1).reshape(-1), jnp.concatenate(live_parts, axis=1).reshape(-1))


def draw_window_place(key, part):
    return slot_table(key)[0]


def draw_slot_live(key, part):
    return slot_table(key)[1]


def block_scale(key, shape, split, smallest, high):
    def one(dim, parts):
        draws = jax.random.uniform(jax.random.fold_in(jax.random.fold_in(key, 6), dim), (parts,), jnp.float32, smallest / len(split), high / len(split))
        return jnp.repeat(jnp.exp(draws), shape[dim] // parts).reshape((-1,) + (1,) * (len(shape) - dim - 1))

    level = one(*split[0])
    for cut in split[1:]:
        level = level * one(*cut)
    return level


def gaussian(rng, dims, width, most, shards=(), kind=jnp.bfloat16):
    level = block_scale(rng, dims, shards, -0.22, 0.18) if shards else 1.0
    array = jax.random.normal(rng, dims, jnp.float32) * width * level
    return jnp.minimum(jnp.maximum(array, -most), most).astype(kind)


def setup_inputs(seed: int = 0) -> dict:
    streams_of = jax.random.split(jax.random.key(seed), 19)
    return {
        "block_input": gaussian(streams_of[0], (TOKENS, D), 1.0, 6.0, ((0, 8),)),
        "window_place": draw_window_place(jax.random.fold_in(streams_of[18], 71), 0),
        "slot_live": draw_slot_live(jax.random.fold_in(streams_of[18], 71), 0),
        "norm_one_gain": jnp.clip(1.0 + 0.15 * jax.random.normal(streams_of[3], (D,), jnp.float32), 0.25, 1.75),
        "norm_one_shift": gaussian(streams_of[4], (D,), 0.2, 1.0, (), jnp.float32),
        "qkv_weight": gaussian(streams_of[5], (3, D, D), D ** -0.5, 0.15625, ((1, 8), (2, 4))),
        "qv_bias": gaussian(streams_of[6], (2, D), 0.3, 1.5, (), jnp.float32),
        "proj_weight": gaussian(streams_of[7], (D, D), (D // 48) ** -0.5, 1.25, ((0, 4), (1, 8))),
        "proj_bias": gaussian(streams_of[8], (D,), 0.2, 1.0, (), jnp.float32),
        "norm_two_gain": jnp.clip(1.0 + 0.15 * jax.random.normal(streams_of[9], (D,), jnp.float32), 0.25, 1.75),
        "norm_two_shift": gaussian(streams_of[10], (D,), 0.2, 1.0, (), jnp.float32),
        "up_weight": gaussian(streams_of[11], (D, FF), D ** -0.5, 0.15625, ((0, 8), (1, 4))),
        "up_bias": gaussian(streams_of[12], (FF,), 0.3, 1.5, (), jnp.float32),
        "down_weight": gaussian(streams_of[13], (FF, D), FF ** -0.5, 0.078125, ((0, 4), (1, 8))),
        "down_bias": gaussian(streams_of[14], (D,), 0.2, 1.0, (), jnp.float32),
        "rel_height": gaussian(streams_of[15], (RELN, HD), 0.15, 0.9, (), jnp.float32),
        "rel_width": gaussian(streams_of[16], (RELN, HD), 0.15, 0.9, (), jnp.float32),
        "cotangent": gaussian(streams_of[17], (TOKENS, D), 1.0, 6.0, ((0, 8),)),
    }


@jax.custom_vjp
def low(v):
    return lax.optimization_barrier(v.astype(jnp.bfloat16)).astype(jnp.float32)

@jax.custom_vjp
def low_back(v):
    return v

def low_keep(v):
    return (low(v), None)

def low_pass(kept, grad):
    return (grad,)

def back_keep(v):
    return (v, None)

def back_low(kept, grad):
    return (low(grad),)
low.defvjp(low_keep, low_pass)
low_back.defvjp(back_keep, back_low)
epsilon = 1e-06
highest = lax.Precision.HIGHEST

def layer_norm(values, gain, shift):
    center = lax.optimization_barrier(jnp.mean(values, axis=-1, keepdims=True))
    centred = values - center
    spread = lax.optimization_barrier(jnp.mean(centred * centred, axis=-1, keepdims=True))
    return centred * lax.rsqrt(spread + epsilon) * gain + shift

def token_valid(window_place, slot_live):
    position = jnp.arange(WTOK, dtype=jnp.int32)
    inner_row = position // WIN
    inner_col = position % WIN
    grid_row = (window_place // GRID)[:, None]
    grid_col = (window_place % GRID)[:, None]
    inside = (grid_row * WIN + inner_row[None, :] < SIDE) & (grid_col * WIN + inner_col[None, :] < SIDE) & (slot_live[:, None] == 1)
    return jnp.where(inside, 1.0, 0.0).astype(jnp.float32)

def offset_table():
    first = jnp.arange(WIN, dtype=jnp.int32)
    target = first[:, None] - first[None, :] + WIN - 1
    return jnp.where(target[:, :, None] == jnp.arange(RELN, dtype=jnp.int32)[None, None, :], 1.0, 0.0).astype(jnp.float32)

def window_block(params, rows, valid):
    gain_one, shift_one, qkv_weight, qv_bias, proj_weight, proj_bias, gain_two, shift_two, up_weight, up_bias, down_weight, down_bias, rel_height, rel_width = params
    windows = rows.shape[0] // WTOK
    normed = low(layer_norm(rows, gain_one, shift_one) * valid[:, None])
    queries = low(low_back(jnp.dot(normed, qkv_weight[0], precision=highest, preferred_element_type=jnp.float32) + qv_bias[0]))
    keys = low(low_back(jnp.dot(normed, qkv_weight[1], precision=highest, preferred_element_type=jnp.float32)))
    values = low(low_back(jnp.dot(normed, qkv_weight[2], precision=highest, preferred_element_type=jnp.float32) + qv_bias[1]))
    query_heads = queries.reshape(windows, WTOK, HEADS, HD)
    key_heads = keys.reshape(windows, WTOK, HEADS, HD)
    value_heads = values.reshape(windows, WTOK, HEADS, HD)
    query_grid = queries.reshape(windows, WIN, WIN, HEADS, HD)
    table = offset_table()
    table_height = jnp.einsum('abr,rc->abc', table, rel_height, precision=highest)
    table_width = jnp.einsum('abr,rc->abc', table, rel_width, precision=highest)
    scores = HD ** (-0.5) * jnp.einsum('gqhc,gkhc->ghqk', query_heads, key_heads, precision=highest)
    bias_height = jnp.einsum('gxyhc,xkc->ghxyk', query_grid, table_height, precision=highest)
    bias_width = jnp.einsum('gxyhc,ykc->ghxyk', query_grid, table_width, precision=highest)
    scores = scores.reshape(windows, HEADS, WIN, WIN, WIN, WIN) + bias_height[:, :, :, :, :, None] + bias_width[:, :, :, :, None, :]
    scores = low_back(scores.reshape(windows, HEADS, WTOK, WTOK))
    shares = low(jax.nn.softmax(scores, axis=-1))
    mixed = jnp.einsum('ghqk,gkhc->gqhc', shares, value_heads, precision=highest).reshape(windows * WTOK, D)
    mixed = low(low_back(mixed))
    branch = low_back(jnp.dot(mixed, proj_weight, precision=highest, preferred_element_type=jnp.float32) + proj_bias)
    after = rows + branch
    normed_two = low(layer_norm(after, gain_two, shift_two))
    hidden = low_back(jnp.dot(normed_two, up_weight, precision=highest, preferred_element_type=jnp.float32) + up_bias)
    active = low(jax.nn.gelu(hidden, approximate=False))
    branch_two = low_back(jnp.dot(active, down_weight, precision=highest, preferred_element_type=jnp.float32) + down_bias)
    return valid[:, None] * (after + branch_two)

def reference(block_input, window_place, slot_live, norm_one_gain, norm_one_shift, qkv_weight, qv_bias, proj_weight, proj_bias, norm_two_gain, norm_two_shift, up_weight, up_bias, down_weight, down_bias, rel_height, rel_width, cotangent):
    valid = token_valid(window_place, slot_live).reshape(N_DP, SLOTS * WTOK)
    params = (norm_one_gain.astype(jnp.float32), norm_one_shift.astype(jnp.float32), qkv_weight.astype(jnp.float32), qv_bias.astype(jnp.float32), proj_weight.astype(jnp.float32), proj_bias.astype(jnp.float32), norm_two_gain.astype(jnp.float32), norm_two_shift.astype(jnp.float32), up_weight.astype(jnp.float32), up_bias.astype(jnp.float32), down_weight.astype(jnp.float32), down_bias.astype(jnp.float32), rel_height.astype(jnp.float32), rel_width.astype(jnp.float32))

    def forward(rows, weights):
        grouped = rows.reshape(N_DP, SLOTS * WTOK, D)

        def one_group(pair):
            return window_block(weights, pair[0], pair[1])
        results = lax.map(jax.checkpoint(one_group), (grouped, valid))
        return results.reshape(N_DP * SLOTS * WTOK, D)
    output, pullback = jax.vjp(forward, block_input.astype(jnp.float32), params)
    input_grad, grads = pullback(cotangent.astype(jnp.float32))
    return (output.astype(jnp.bfloat16), input_grad, grads[0], grads[1], grads[2], grads[3], grads[4], grads[5], grads[6], grads[7], grads[8], grads[9], grads[10], grads[11], grads[12], grads[13])
```

```python
from functools import partial

import jax
import jax.numpy as jnp
import numpy as np
from jax import lax
from jax.experimental import pallas as pl
from jax.experimental.pallas import tpu as pltpu
from jax.sharding import PartitionSpec as P

HD = 80
WIN = 14
SIDE = 64
GRID = 5
WTOK = 196
RELN = 27
ROWS = 208
SCALE = HD ** (-0.5)
EPS = 1e-06
F32 = jnp.float32
BF16 = jnp.bfloat16
ANY = pl.BlockSpec(memory_space=pl.ANY)
highest = lax.Precision.HIGHEST


def dot(left, right):
    return lax.dot_general(left, right, (((1,), (0,)), ((), ())), preferred_element_type=F32)


def dot_nt(left, right):
    return lax.dot_general(left, right, (((1,), (1,)), ((), ())), preferred_element_type=F32)


def dot_tn(left, right):
    return lax.dot_general(left, right, (((0,), (0,)), ((), ())), preferred_element_type=F32)


def whole(array):
    zeros = (0,) * len(array.shape)
    return pl.BlockSpec(array.shape, lambda *_: zeros)


def params(megabytes):
    return pltpu.CompilerParams(vmem_limit_bytes=megabytes * 2**20)


def struct(shape, dtype):
    return jax.ShapeDtypeStruct(shape, dtype)


def assemble(offsets, pieces, target, sems):
    copies = []
    for index, piece in enumerate(pieces):
        count = piece.shape[0]
        start = pl.multiple_of(offsets[index], 16)
        copies.append(
            pltpu.make_async_copy(piece, target.at[pl.ds(start, count)], sems.at[index])
        )
    for copy in copies:
        copy.start()
    for copy in copies:
        copy.wait()


def norm_parts(values):
    center = jnp.mean(values, axis=-1, keepdims=True)
    centred = values - center
    spread = jnp.mean(centred * centred, axis=-1, keepdims=True)
    rstd = lax.rsqrt(spread + EPS)
    return centred * rstd, rstd


def norm_one_kernel(x_ref, valid_ref, gain_ref, shift_ref, out_ref):
    xhat, _ = norm_parts(x_ref[...].astype(F32))
    out_ref[...] = ((xhat * gain_ref[...] + shift_ref[...]) * valid_ref[...]).astype(BF16)


def norm_one(x, valid, gain, shift):
    rows, width = x.shape
    return pl.pallas_call(
        norm_one_kernel,
        grid=(rows // ROWS,),
        in_specs=[
            pl.BlockSpec((ROWS, width), lambda i: (i, 0)),
            pl.BlockSpec((ROWS, 1), lambda i: (i, 0)),
            whole(gain),
            whole(shift),
        ],
        out_specs=pl.BlockSpec((ROWS, width), lambda i: (i, 0)),
        out_shape=struct(x.shape, BF16),
        name="norm_one",
    )(x, valid, gain, shift)


def total(refs, rows):
    value = refs[0][:rows].astype(F32)
    for ref in refs[1:]:
        value = value + ref[:rows].astype(F32)
    return value


def norm_two_kernel(count, *refs):
    parts, (x_ref, bias_ref, gain_ref, shift_ref, after_ref, normed_ref) = (
        refs[:count],
        refs[count:],
    )
    rows = x_ref.shape[0]
    after = x_ref[...].astype(F32) + total(parts, rows) + bias_ref[...]
    xhat, _ = norm_parts(after)
    after_ref[...] = after
    normed_ref[...] = (xhat * gain_ref[...] + shift_ref[...]).astype(BF16)


def norm_two(parts, x, bias, gain, shift):
    return pl.pallas_call(
        partial(norm_two_kernel, len(parts)),
        out_shape=(struct(x.shape, F32), struct(x.shape, BF16)),
        compiler_params=params(32),
        name="norm_two",
    )(*parts, x, bias, gain, shift)


def finish_kernel(count, *refs):
    parts, (after_ref, valid_ref, bias_ref, out_ref) = refs[:count], refs[count:]
    rows = after_ref.shape[0]
    branch = total(parts, rows) + bias_ref[...]
    out_ref[...] = (valid_ref[...] * (after_ref[...] + branch)).astype(BF16)


def finish(parts, after, valid, bias):
    return pl.pallas_call(
        partial(finish_kernel, len(parts)),
        out_shape=struct(after.shape, BF16),
        compiler_params=params(32),
        name="finish",
    )(*parts, after, valid, bias)


def norm_back(upstream, xhat, rstd, gain):
    weighted = upstream * gain
    inner = jnp.mean(weighted * xhat, axis=-1, keepdims=True)
    level = jnp.mean(weighted, axis=-1, keepdims=True)
    return rstd * (weighted - level - xhat * inner)


def norm_two_back_kernel(count, *refs):
    parts = refs[:count]
    after_ref, top_ref, gain_ref, grad_ref, branch_ref, sums_ref = refs[count:]
    rows = after_ref.shape[0]
    upstream = total(parts, rows)
    xhat, rstd = norm_parts(after_ref[...])
    top = top_ref[...].astype(F32)
    grad = top + norm_back(upstream, xhat, rstd, gain_ref[...])
    branch = grad.astype(BF16)
    grad_ref[...] = grad
    branch_ref[...] = branch
    sums_ref[0:1] = jnp.sum(upstream * xhat, axis=0, keepdims=True)
    sums_ref[1:2] = jnp.sum(upstream, axis=0, keepdims=True)
    sums_ref[2:3] = jnp.sum(branch.astype(F32), axis=0, keepdims=True)
    sums_ref[3:4] = jnp.sum(top, axis=0, keepdims=True)


def norm_two_back(parts, after, top, gain):
    return pl.pallas_call(
        partial(norm_two_back_kernel, len(parts)),
        out_shape=(
            struct(after.shape, F32),
            struct(after.shape, BF16),
            struct((4, after.shape[1]), F32),
        ),
        compiler_params=params(40),
        name="norm_two_back",
    )(*parts, after, top, gain)


def norm_one_back_kernel(count, *refs):
    parts = refs[:count]
    x_ref, valid_ref, grad_ref, gain_ref, out_ref, sums_ref = refs[count:]
    rows = x_ref.shape[0]
    upstream = total(parts, rows) * valid_ref[...]
    xhat, rstd = norm_parts(x_ref[...].astype(F32))
    out_ref[...] = (grad_ref[...] + norm_back(upstream, xhat, rstd, gain_ref[...])).astype(BF16)
    sums_ref[0:1] = jnp.sum(upstream * xhat, axis=0, keepdims=True)
    sums_ref[1:2] = jnp.sum(upstream, axis=0, keepdims=True)


def norm_one_back(parts, x, valid, grad, gain):
    return pl.pallas_call(
        partial(norm_one_back_kernel, len(parts)),
        out_shape=(struct(x.shape, BF16), struct((2, x.shape[1]), F32)),
        compiler_params=params(40),
        name="norm_one_back",
    )(*parts, x, valid, grad, gain)


def qkv_kernel(count, cols, offsets, *refs):
    pieces = refs[:count]
    x_ref, bias_ref, q_ref, k_ref, v_ref, w_ref, buffer, sems = refs[count:]
    wide = q_ref.shape[1]

    @pl.when(pl.program_id(0) == 0)
    def _():
        assemble(offsets, pieces, buffer, sems)
        for slot in range(4):
            base = slot * wide
            w_ref[:, base : base + cols] = buffer[:, slot * cols : (slot + 1) * cols]
            if wide > cols:
                w_ref[:, base + cols : base + wide] = jnp.zeros(
                    (w_ref.shape[0], wide - cols), BF16
                )

    x = x_ref[...]
    for slot, ref in enumerate((q_ref, k_ref, v_ref)):
        span = slice(slot * wide, (slot + 1) * wide)
        ref[...] = (dot(x, w_ref[:, span]) + bias_ref[:, span]).astype(BF16)


def project(offsets, pieces, x, bias, cols, wide):
    rows, width = x.shape
    step = 2 * ROWS
    block = pl.BlockSpec((step, wide), lambda i, *_: (i, 0))
    return pl.pallas_call(
        partial(qkv_kernel, len(pieces), cols),
        grid_spec=pltpu.PrefetchScalarGridSpec(
            num_scalar_prefetch=1,
            grid=(rows // step,),
            in_specs=[ANY] * len(pieces)
            + [pl.BlockSpec((step, width), lambda i, *_: (i, 0)), whole(bias)],
            out_specs=[block, block, block, pl.BlockSpec((width, 4 * wide), lambda i, *_: (0, 0))],
            scratch_shapes=[
                pltpu.VMEM((width, 4 * cols), BF16),
                pltpu.SemaphoreType.DMA((len(pieces),)),
            ],
        ),
        out_shape=[struct((rows, wide), BF16)] * 3 + [struct((width, 4 * wide), BF16)],
        compiler_params=params(48),
        name="qkv",
    )(offsets, *pieces, x, bias)


def head_spans(heads, wide):
    spans = []
    for head in range(heads):
        first, last = head * HD, head * HD + HD
        low = first // 128 * 128
        high = min((last + 127) // 128 * 128, wide)
        spans.append((low, high, first, last))
    return spans


def lane_mask(span):
    low, high, first, last = span
    lane = lax.broadcasted_iota(jnp.int32, (1, high - low), 1) + low
    return jnp.where((lane >= first) & (lane < last), 1.0, 0.0).astype(BF16)


def shift_counts():
    token = lax.broadcasted_iota(jnp.int32, (ROWS, 128), 0)
    row = (token * 9363) >> 17
    col = token - row * WIN
    return jnp.maximum(WIN - 1 - row, 0), WIN - 1 - col


def shift_lanes(values, counts, back):
    for step in (1, 2, 4, 8):
        moved = pltpu.roll(values, step if back else 128 - step, 1)
        values = jnp.where((counts & step) != 0, moved, values)
    return values


def lane_kind():
    lane = lax.broadcasted_iota(jnp.int32, (ROWS, 128), 1) & 31
    return lane < WIN, (lane >= 16) & (lane < 16 + WIN), lane == 31


def split_two(values):
    high = values.astype(BF16)
    return high, (values - high.astype(F32)).astype(BF16)


def bias_operand(q, rel_high, rel_low, counts):
    table = dot(q, rel_high) + dot(q, rel_low)
    by_row = shift_lanes(table[:, :128], counts[0], False)
    by_col = shift_lanes(table[:, 128:], counts[1], False)
    is_row, is_col, is_last = lane_kind()
    packed = jnp.where(
        is_row, by_row, jnp.where(is_col, by_col, jnp.where(is_last, 1.0, 0.0))
    )
    high, low = split_two(packed)
    return jnp.concatenate([high, low], axis=1)


def add_lanes(parts, values, span):
    low, high = span[0], span[1]
    for index in range(low // 128, high // 128):
        piece = values[:, index * 128 - low : index * 128 - low + 128]
        parts[index] = piece if parts[index] is None else parts[index] + piece


def attend_kernel(heads, split, q_ref, k_ref, v_ref, rh_ref, rl_ref, mark_ref, w_ref, *outs):
    mixed_ref, log_ref = outs[:2]
    q, k, v = q_ref[...], k_ref[...], v_ref[...]
    wide = q.shape[1]
    bias = bias_operand(q, rh_ref[...], rl_ref[...], shift_counts())
    lane = lax.broadcasted_iota(jnp.int32, (ROWS, 128), 1)
    logs = jnp.zeros((ROWS, 128), F32)
    parts = [None] * (wide // 128)
    for head, span in enumerate(head_spans(heads, wide)):
        mask = lane_mask(span)
        cut = slice(span[0], span[1])
        scores = SCALE * dot_nt(q[:, cut], k[:, cut] * mask) + dot_nt(bias, mark_ref[head])
        top = jnp.max(scores, axis=-1, keepdims=True)
        shifted = jnp.exp(scores - top)
        norm = jnp.sum(shifted, axis=-1, keepdims=True)
        shares = (shifted * (1.0 / norm)).astype(BF16)
        logs = jnp.where(lane == head, top + jnp.log(norm), logs)
        add_lanes(parts, dot(shares, v[:, cut] * mask), span)
    mixed = jnp.concatenate(parts, axis=1).astype(BF16)
    mixed_ref[...] = mixed
    log_ref[...] = logs
    branch = dot_nt(mixed, w_ref[...]).astype(BF16)
    if split:
        keep_ref, send_ref = outs[2:]
        step = pl.program_id(0)

        @pl.when(step < split)
        def _():
            send_ref[...] = branch

        @pl.when(step >= split)
        def _():
            keep_ref[...] = branch
    else:
        outs[2][...] = branch


def split_specs(windows, split, width):
    rows = ROWS * (windows - split)
    if not split:
        return [pl.BlockSpec((ROWS, width), lambda i: (i, 0))], [struct((rows, width), BF16)]
    return (
        [
            pl.BlockSpec((ROWS, width), lambda i: (jnp.maximum(i - split, 0), 0)),
            pl.BlockSpec((ROWS, width), lambda i: (jnp.minimum(i, split - 1), 0)),
        ],
        [struct((rows, width), BF16), struct((ROWS * split, width), BF16)],
    )


def attend(heads, part, windows, split, q, k, v, rel_high, rel_low, marks, weights):
    wide = q.shape[1]
    width = weights.shape[0]

    def place(i):
        return (i + split) % windows if split else i

    block = pl.BlockSpec((ROWS, wide), lambda i: (part * windows + place(i), 0))
    specs, shapes = split_specs(windows, split, width)
    return pl.pallas_call(
        partial(attend_kernel, heads, split),
        grid=(windows,),
        in_specs=[
            block,
            block,
            block,
            whole(rel_high),
            whole(rel_low),
            whole(marks),
            pl.BlockSpec((width, wide), lambda i: (0, 3)),
        ],
        out_specs=[
            pl.BlockSpec((ROWS, wide), lambda i: (place(i), 0)),
            pl.BlockSpec((ROWS, 128), lambda i: (place(i), 0)),
        ]
        + specs,
        out_shape=[
            struct((windows * ROWS, wide), BF16),
            struct((windows * ROWS, 128), F32),
        ]
        + shapes,
        compiler_params=params(40),
        name="attend",
    )(q, k, v, rel_high, rel_low, marks, weights)


def attend_back_kernel(heads, windows, split, count, *refs):
    pieces = refs[:count]
    q_ref, k_ref, v_ref, log_ref, rh_ref, rl_ref, mark_ref, w_ref = refs[count : count + 8]
    grads_ref, branch_ref, rel_ref, sum_ref = refs[count + 8 : count + 12]
    outs = refs[count + 12 :]
    step = pl.program_id(0)

    @pl.when(step == 0)
    def _():
        start = 0
        for piece in pieces:
            branch_ref[start : start + piece.shape[0]] = piece[...]
            start += piece.shape[0]
        rel_ref[...] = jnp.zeros(rel_ref.shape, F32)
        sum_ref[...] = jnp.zeros(sum_ref.shape, F32)

    place = lax.rem(step + split, windows) if split else step
    q, k, v = q_ref[...], k_ref[...], v_ref[...]
    wide = q.shape[1]
    top = branch_ref[pl.ds(pl.multiple_of(place * ROWS, 16), ROWS), :]
    grad_mixed = dot(top, w_ref[:, 3 * wide :]).astype(BF16)
    rel_high, rel_low = rh_ref[...], rl_ref[...]
    counts = shift_counts()
    bias = bias_operand(q, rel_high, rel_low, counts)
    grad_q, grad_k, grad_v = ([None] * (wide // 128) for _ in range(3))
    grad_bias = None
    for head, span in enumerate(head_spans(heads, wide)):
        mask = lane_mask(span)
        cut = slice(span[0], span[1])
        key = k[:, cut] * mask
        query = q[:, cut]
        upper = grad_mixed[:, cut]
        mark = mark_ref[head]
        scores = SCALE * dot_nt(query, key) + dot_nt(bias, mark)
        shares = jnp.exp(scores - log_ref[:, head : head + 1])
        grad_shares = dot_nt(upper, v[:, cut] * mask)
        inner = jnp.sum(shares * grad_shares, axis=-1, keepdims=True)
        grad_scores = (shares * (grad_shares - inner)).astype(BF16)
        add_lanes(grad_v, dot_tn(shares.astype(BF16), upper * mask), span)
        add_lanes(grad_q, dot(grad_scores, key), span)
        add_lanes(grad_k, dot_tn(grad_scores, query * mask), span)
        part = dot(grad_scores, mark[:, :128])
        grad_bias = part if grad_bias is None else grad_bias + part
    is_row, is_col, _ = lane_kind()
    by_row = shift_lanes(jnp.where(is_row, grad_bias, 0.0), counts[0], True)
    by_col = shift_lanes(jnp.where(is_col, grad_bias, 0.0), counts[1], True)
    high, low = split_two(jnp.concatenate([by_row, by_col], axis=1))
    extra = dot_nt(high, rel_high) + dot_nt(low, rel_high) + dot_nt(high, rel_low)
    extra = extra + dot_nt(low, rel_low)
    rel_ref[...] += dot_tn(high, q) + dot_tn(low, q)
    grad_q = (SCALE * jnp.concatenate(grad_q, axis=1) + extra).astype(BF16)
    grad_k = (SCALE * jnp.concatenate(grad_k, axis=1)).astype(BF16)
    grad_v = jnp.concatenate(grad_v, axis=1).astype(BF16)
    partial_sum = None
    for slot, grad in enumerate((grad_q, grad_k, grad_v)):
        cut = slice(slot * wide, (slot + 1) * wide)
        grads_ref[:, cut] = grad
        sum_ref[:, cut] += jnp.sum(grad.astype(F32), axis=0, keepdims=True)
        term = dot_nt(grad, w_ref[:, cut])
        partial_sum = term if partial_sum is None else partial_sum + term
    result = partial_sum.astype(BF16)
    if split:
        keep_ref, send_ref = outs

        @pl.when(step < split)
        def _():
            send_ref[...] = result

        @pl.when(step >= split)
        def _():
            keep_ref[...] = result
    else:
        outs[0][...] = result


def attend_back(
    heads, part, windows, split, pieces, q, k, v, logs, rel_high, rel_low, marks, weights
):
    wide = q.shape[1]
    width = weights.shape[0]

    def place(i):
        return (i + split) % windows if split else i

    block = pl.BlockSpec((ROWS, wide), lambda i: (part * windows + place(i), 0))
    specs, shapes = split_specs(windows, split, width)
    rows = windows * ROWS
    branch = struct((rows, width), BF16)
    rel = struct((256, wide), F32)
    sums = struct((1, 3 * wide), F32)
    return pl.pallas_call(
        partial(attend_back_kernel, heads, windows, split, len(pieces)),
        grid=(windows,),
        in_specs=[whole(piece) for piece in pieces]
        + [
            block,
            block,
            block,
            pl.BlockSpec((ROWS, 128), lambda i: (place(i), 0)),
            whole(rel_high),
            whole(rel_low),
            whole(marks),
            whole(weights),
        ],
        out_specs=[
            pl.BlockSpec((ROWS, 3 * wide), lambda i: (place(i), 0)),
            whole(branch),
            whole(rel),
            whole(sums),
        ]
        + specs,
        out_shape=[struct((rows, 3 * wide), BF16), branch, rel, sums] + shapes,
        compiler_params=params(56),
        name="attend_back",
    )(*pieces, q, k, v, logs, rel_high, rel_low, marks, weights)


def mlp_kernel(count, weights, chunk, offsets, *refs):
    pieces = refs[:count]
    up_pieces = refs[count : count + weights]
    down_pieces = refs[count + weights : count + 2 * weights]
    refs = refs[count + 2 * weights :]
    top_ref, bias_ref, active_ref, hidden_ref, normed_ref, sum_ref = refs[:6]
    back_ref, out_ref, up, down, sems = refs[6:]
    step = pl.program_id(0)
    block = top_ref.shape[0]

    @pl.when(step == 0)
    def _():
        start = 0
        for piece in pieces:
            normed_ref[start : start + piece.shape[0]] = piece[...]
            start += piece.shape[0]
        sum_ref[...] = jnp.zeros(sum_ref.shape, F32)
        assemble(offsets, up_pieces, up, sems.at[0])
        assemble(offsets, down_pieces, down, sems.at[1])

    normed = normed_ref[pl.ds(pl.multiple_of(step * block, 16), block), :]
    top = top_ref[...]
    units = up.shape[1]
    width = up.shape[0]

    def first(index, carry):
        cut = pl.ds(pl.multiple_of(index * chunk, 128), chunk)
        hidden = dot(normed, up[:, cut]) + bias_ref[:, cut]
        half = 0.5 * (1.0 + lax.erf(hidden * (0.5**0.5)))
        slope = half + hidden * jnp.exp(-0.5 * hidden * hidden) * float((2.0 * np.pi) ** -0.5)
        active_ref[:, cut] = (hidden * half).astype(BF16)
        grad = (dot(top, down[:, cut]) * slope).astype(BF16)
        hidden_ref[:, cut] = grad
        sum_ref[:, cut] += jnp.sum(grad.astype(F32), axis=0, keepdims=True)
        return carry

    lax.fori_loop(0, units // chunk, first, 0)
    grad_hidden = hidden_ref[...]
    active = active_ref[...]

    def second(index, carry):
        cut = pl.ds(pl.multiple_of(index * 256, 128), 256)
        back_ref[:, cut] = dot_nt(grad_hidden, up[cut, :]).astype(BF16)
        out_ref[:, cut] = dot_nt(active, down[cut, :]).astype(BF16)
        return carry

    lax.fori_loop(0, width // 256, second, 0)


def mlp(offsets, pieces, up_pieces, down_pieces, top, part, bias):
    rows = sum(piece.shape[0] for piece in pieces)
    width = pieces[0].shape[1]
    units = up_pieces[0].shape[1]
    block = 2 * ROWS
    blocks = rows // block
    chunk = 256 if units % 256 == 0 else 128
    normed = struct((rows, width), BF16)
    sums = struct((1, units), F32)
    wide = pl.BlockSpec((block, units), lambda i, *_: (i, 0))
    narrow = pl.BlockSpec((block, width), lambda i, *_: (i, 0))
    return pl.pallas_call(
        partial(mlp_kernel, len(pieces), len(up_pieces), chunk),
        grid_spec=pltpu.PrefetchScalarGridSpec(
            num_scalar_prefetch=1,
            grid=(blocks,),
            in_specs=[whole(piece) for piece in pieces]
            + [ANY] * (2 * len(up_pieces))
            + [pl.BlockSpec((block, width), lambda i, *_: (part * blocks + i, 0)), whole(bias)],
            out_specs=[wide, wide, whole(normed), whole(sums), narrow, narrow],
            scratch_shapes=[
                pltpu.VMEM((width, units), BF16),
                pltpu.VMEM((width, units), BF16),
                pltpu.SemaphoreType.DMA((2, len(up_pieces))),
            ],
        ),
        out_shape=[struct((rows, units), BF16)] * 2
        + [normed, sums]
        + [struct((rows, width), BF16)] * 2,
        compiler_params=params(56),
        name="mlp",
    )(offsets, *pieces, *up_pieces, *down_pieces, top, bias)


def weight_grad_kernel(groups, cols, chunk, starts, *refs):
    count = sum(2 * len(group) for group in groups)
    operands = refs[:count]
    outs = refs[count:-2]
    result, sems = refs[-2:]
    width = result.shape[0]

    def loop(index, carry):
        rows = pl.ds(pl.multiple_of(index * chunk, 128), chunk)
        at = 0
        for slot, group in enumerate(groups):
            for member, (low, high) in enumerate(group):
                left, right = operands[at], operands[at + 1]
                at += 2
                term = dot_tn(left[:, rows], right[:, low:high])
                value = term if member == 0 else value + term
            result[rows, slot * cols : (slot + 1) * cols] = value[:, :cols].astype(BF16)
        return carry

    lax.fori_loop(0, width // chunk, loop, 0)
    copies = []
    for out in outs:
        for index in range(out.shape[0]):
            size = out.shape[1]
            start = pl.multiple_of(starts[len(copies)], 16)
            copies.append(
                pltpu.make_async_copy(
                    result.at[pl.ds(start, size)], out.at[index], sems.at[len(copies)]
                )
            )
    for copy in copies:
        copy.start()
    for copy in copies:
        copy.wait()


def weight_grad(starts, groups, cols, shapes):
    operands = []
    for group in groups:
        for left, right, _, _ in group:
            operands += [left, right]
    spans = [[(low, high) for _, _, low, high in group] for group in groups]
    width = operands[0].shape[1]
    count = sum(shape[0] for shape in shapes)
    return pl.pallas_call(
        partial(weight_grad_kernel, spans, cols, 256),
        grid_spec=pltpu.PrefetchScalarGridSpec(
            num_scalar_prefetch=1,
            grid=(1,),
            in_specs=[whole(operand) for operand in operands],
            out_specs=[ANY] * len(shapes),
            scratch_shapes=[
                pltpu.VMEM((width, cols * len(groups)), BF16),
                pltpu.SemaphoreType.DMA((count,)),
            ],
        ),
        out_shape=[struct(shape, BF16) for shape in shapes],
        compiler_params=params(56),
        name="weight_grad",
    )(starts, *operands)


def place_kernel(count, order, *refs):
    pieces, out_ref, buffer = refs[:count], refs[count], refs[count + 1]
    for me in range(4):

        @pl.when(order[0] == me)
        def _(me=me):
            for index in range(count):
                step = (0, 2, 1, 3)[index % 4]
                start = (index // 4 * 4 + (me ^ step)) * WTOK
                buffer[start : start + WTOK] = pieces[index][:WTOK].astype(F32)

    out_ref[...] = buffer[...].astype(out_ref.dtype)


def place_windows(order, pieces, dtype):
    width = pieces[0].shape[1]
    shape = (len(pieces) * WTOK, width)
    return pl.pallas_call(
        partial(place_kernel, len(pieces)),
        grid_spec=pltpu.PrefetchScalarGridSpec(
            num_scalar_prefetch=1,
            grid=(1,),
            in_specs=[whole(piece) for piece in pieces],
            out_specs=pl.BlockSpec(shape, lambda *_: (0, 0)),
            scratch_shapes=[pltpu.VMEM(shape, F32)],
        ),
        out_shape=struct(shape, dtype),
        compiler_params=params(56),
        name="place_windows",
    )(order, *pieces)


def token_valid(window_place, slot_live):
    position = jnp.arange(WTOK, dtype=jnp.int32)
    inner_row = position // WIN
    inner_col = position % WIN
    grid_row = (window_place // GRID)[:, None]
    grid_col = (window_place % GRID)[:, None]
    inside = (
        (grid_row * WIN + inner_row[None, :] < SIDE)
        & (grid_col * WIN + inner_col[None, :] < SIDE)
        & (slot_live[:, None] == 1)
    )
    return jnp.where(inside, 1.0, 0.0).astype(F32)


def key_marks(heads):
    marks = np.zeros((heads, ROWS, 256), np.float32)
    for head in range(heads):
        for token in range(WTOK):
            for half in (0, 128):
                marks[head, token, half + head * 32 + token // WIN] = 1.0
                marks[head, token, half + head * 32 + 16 + token % WIN] = 1.0
        marks[head, WTOK:, head * 32 + 31] = -1e30
    return marks.astype(BF16)


def rel_operand(rel_height, rel_width, heads, wide):
    lanes = jnp.zeros((wide, 256), F32)
    high = rel_height[::-1].T
    flat = rel_width[::-1].T
    for head in range(heads):
        rows = slice(head * HD, head * HD + HD)
        lanes = lanes.at[rows, head * 32 : head * 32 + RELN].set(high)
        first = head * 32 + 16
        fit = min(RELN, 128 - first)
        lanes = lanes.at[rows, 128 + first : 128 + first + fit].set(flat[:, :fit])
        if fit < RELN:
            lanes = lanes.at[rows, 128 : 128 + RELN - fit].set(flat[:, fit:])
    return split_two(lanes)


def rel_result(sums, heads):
    high = jnp.zeros((RELN, HD), F32)
    flat = jnp.zeros((RELN, HD), F32)
    for head in range(heads):
        cols = sums[:, head * HD : head * HD + HD]
        high = high + cols[head * 32 : head * 32 + RELN]
        rolled = jnp.concatenate([cols[128:], cols[128:]], axis=0)
        flat = flat + rolled[head * 32 + 16 : head * 32 + 16 + RELN]
    return high[::-1], flat[::-1]


def add_all(values):
    out = values[0]
    for value in values[1:]:
        out = out + value
    return out


def body(
    block_input,
    window_place,
    slot_live,
    norm_one_gain,
    norm_one_shift,
    qkv_weight,
    qv_bias,
    proj_weight,
    proj_bias,
    norm_two_gain,
    norm_two_shift,
    up_weight,
    up_bias,
    down_weight,
    down_bias,
    rel_height,
    rel_width,
    cotangent,
):
    data_parts = lax.axis_size("dp")
    model_parts = lax.axis_size("mp")
    data_index = lax.axis_index("dp")
    model_index = lax.axis_index("mp")
    width = block_input.shape[1]
    share = qkv_weight.shape[1]
    cols = qkv_weight.shape[2]
    heads = cols // HD
    wide = (cols + 127) // 128 * 128
    units = up_weight.shape[1]
    slots = window_place.shape[0]
    rings = data_parts == 8 and model_parts == 4 and slots % 4 == 0
    padded = (slots + model_parts - 1) // model_parts * model_parts
    halves = padded // 4 if rings else 1
    windows = padded // halves
    split = 2 if rings else 0
    part_rows = windows * ROWS
    own_rows = part_rows // model_parts

    if rings:
        depth, side = data_index // 2, data_index % 2
        y_bit, core_bit = model_index // 2, model_index % 2
        over_x = partial(lax.ppermute, axis_name="dp", perm=[(d, d ^ 1) for d in range(8)])
        over_z = partial(lax.ppermute, axis_name="dp", perm=[(d, (d + 2) % 8) for d in range(8)])
        over_y = partial(lax.ppermute, axis_name="mp", perm=[(m, m ^ 2) for m in range(4)])
        over_core = partial(lax.ppermute, axis_name="mp", perm=[(m, m ^ 1) for m in range(4)])

    def gather(piece):
        if not rings:
            return [lax.all_gather(piece, "dp", axis=0, tiled=True)]
        line = [piece]
        for _ in range(3):
            line.append(over_z(line[-1]))
        return [item for held in line for item in (held, over_x(held))]

    if rings:
        offsets = []
        starts = []
        for back in range(4):
            behind = (depth - back) % 4
            offsets += [share * (2 * behind + side), share * (2 * behind + 1 - side)]
        for other in (0, 1):
            for ahead in range(4):
                target = 2 * ((depth + ahead) % 4) + (1 - side if other == 0 else side)
                starts.append(share * target)
        offsets = jnp.stack(offsets).astype(jnp.int32)
        starts = jnp.stack(starts).astype(jnp.int32)
        grad_shapes = [(4, share), (4, share)]
    else:
        offsets = jnp.zeros((1,), jnp.int32)
        starts = jnp.zeros((1,), jnp.int32)
        grad_shapes = [(1, width)]

    def scatter(parts):
        if not rings:
            return lax.psum_scatter(
                parts[0][0], "dp", scatter_dimension=0, tiled=True
            ).astype(F32)
        send, keep = parts
        came = over_x(send)
        sums = [keep[k].astype(F32) + came[k].astype(F32) for k in range(4)]
        moving = over_z(sums[3].astype(BF16))
        moving = over_z((sums[2] + moving.astype(F32)).astype(BF16))
        moving = over_z((sums[1] + moving.astype(F32)).astype(BF16))
        return sums[0] + moving.astype(F32)

    def rows_scatter(parts):
        if not rings:
            return [lax.psum_scatter(parts[0], "mp", scatter_dimension=0, tiled=True)]
        keep, send = parts
        came = over_core(send)
        passed = (keep[ROWS:].astype(F32) + came[ROWS:].astype(F32)).astype(BF16)
        return [keep, came, over_y(passed)]

    def rows_gather(own):
        if not rings:
            return [lax.all_gather(own, "mp", axis=0, tiled=True)]
        across = over_y(own)
        return [own, across, over_core(own), over_core(across)]

    def sum_all(vector):
        if not rings:
            return lax.psum(vector, ("dp", "mp"))
        for step in (1, 2):
            vector = vector + lax.ppermute(
                vector, "mp", [(m, m ^ step) for m in range(4)]
            )
        for step in (1, 2, 4):
            vector = vector + lax.ppermute(
                vector, "dp", [(d, d ^ step) for d in range(8)]
            )
        return vector

    def to_local(array):
        array = array.reshape((slots, WTOK) + array.shape[1:])
        tail = [(0, 0)] * (array.ndim - 2)
        if rings:
            shape = array.shape
            array = array.reshape((halves, 2, 2) + shape[1:])
            array = jnp.where(y_bit == 1, jnp.flip(array, 1), array)
            array = jnp.where(core_bit == 1, jnp.flip(array, 2), array)
            array = jnp.swapaxes(array, 1, 2).reshape(shape)
        array = jnp.pad(array, [(0, padded - slots), (0, ROWS - WTOK)] + tail)
        return array.reshape((padded * ROWS,) + array.shape[2:])

    def own_slice(array, part):
        if rings:
            return array[part * part_rows : part * part_rows + own_rows]
        return lax.dynamic_slice_in_dim(array, model_index * own_rows, own_rows, 0)

    def to_global(pieces, dtype):
        if rings:
            return place_windows(model_index.astype(jnp.int32).reshape(1), pieces, dtype)
        whole_rows = pieces[0].reshape(padded, ROWS, width)
        return whole_rows[:slots, :WTOK].reshape(slots * WTOK, width).astype(dtype)

    first_piece = jnp.concatenate([qkv_weight[0], qkv_weight[1], qkv_weight[2], proj_weight.T], 1)
    first_weights = gather(first_piece)
    down_pieces = gather(down_weight.T)
    up_pieces = gather(up_weight)

    row = lambda v: v.reshape(1, -1)
    gain_one, shift_one = row(norm_one_gain), row(norm_one_shift)
    gain_two, shift_two = row(norm_two_gain), row(norm_two_shift)
    bias_local = lax.dynamic_slice_in_dim(qv_bias, model_index * cols, cols, 1)
    bias_local = jnp.pad(bias_local, [(0, 0), (0, wide - cols)])
    bias_qkv = row(jnp.stack([bias_local[0], jnp.zeros_like(bias_local[0]), bias_local[1]]))
    up_local = row(lax.dynamic_slice_in_dim(up_bias, model_index * units, units, 0))
    rel_high, rel_low = rel_operand(rel_height, rel_width, heads, wide)
    marks = jnp.asarray(key_marks(heads))

    valid = to_local(token_valid(window_place, slot_live).reshape(slots * WTOK, 1))
    rows_in = to_local(block_input)
    grad_top = (to_local(cotangent) * valid.astype(BF16)).astype(BF16)
    normed = norm_one(rows_in, valid, gain_one, shift_one)

    q, k, v, weights = project(offsets, first_weights, normed, bias_qkv, cols, wide)
    attended = [
        attend(heads, part, windows, split, q, k, v, rel_high, rel_low, marks, weights)
        for part in range(halves)
    ]
    afters, normed_twos = [], []
    for part in range(halves):
        parts = rows_scatter(attended[part][2:])
        after, normed_two = norm_two(
            parts, own_slice(rows_in, part), row(proj_bias), gain_two, shift_two
        )
        afters.append(after)
        normed_twos.append(rows_gather(normed_two))

    mlps = [
        mlp(offsets, normed_twos[part], up_pieces, down_pieces, grad_top, part, up_local)
        for part in range(halves)
    ]

    def split_rows(array):
        return [array[: 2 * ROWS], array[2 * ROWS :]] if rings else [array]

    grad_afters, branches, sums_two = [], [], []
    for part in range(halves):
        parts = rows_scatter(split_rows(mlps[part][4]))
        grad_after, branch, sums = norm_two_back(
            parts, afters[part], own_slice(grad_top, part), gain_two
        )
        grad_afters.append(grad_after)
        branches.append(rows_gather(branch))
        sums_two.append(sums)
    out_pieces = []
    for part in range(halves):
        parts = rows_scatter(split_rows(mlps[part][5]))
        own = finish(parts, afters[part], own_slice(valid, part), row(down_bias))
        out_pieces += rows_gather(own)
    block_output = to_global(out_pieces, BF16)

    top_parts = [
        grad_top[part * part_rows : (part + 1) * part_rows] for part in range(halves)
    ]
    normed_parts = [
        normed[part * part_rows : (part + 1) * part_rows] for part in range(halves)
    ]
    shapes = [shape + (units,) for shape in grad_shapes]
    down_grad = scatter(
        weight_grad(
            starts, [[(top_parts[i], mlps[i][0], 0, units) for i in range(halves)]], units, shapes
        )
    )
    up_grad = scatter(
        weight_grad(
            starts, [[(mlps[i][2], mlps[i][1], 0, units) for i in range(halves)]], units, shapes
        )
    )

    backs = [
        attend_back(
            heads,
            part,
            windows,
            split,
            branches[part],
            q,
            k,
            v,
            attended[part][1],
            rel_high,
            rel_low,
            marks,
            weights,
        )
        for part in range(halves)
    ]
    in_pieces, sums_one = [], []
    for part in range(halves):
        parts = rows_scatter(backs[part][4:])
        own, sums = norm_one_back(
            parts, own_slice(rows_in, part), own_slice(valid, part), grad_afters[part], gain_one
        )
        sums_one.append(sums)
        in_pieces += rows_gather(own)
    input_grad = to_global(in_pieces, F32)
    groups = [
        [
            (normed_parts[i], backs[i][0], slot * wide, (slot + 1) * wide)
            for i in range(halves)
        ]
        for slot in range(3)
    ]
    groups.append([(backs[i][1], attended[i][0], 0, wide) for i in range(halves)])
    first_grad = scatter(
        weight_grad(starts, groups, cols, [shape + (4 * cols,) for shape in grad_shapes])
    )

    two = add_all(sums_two)
    one = add_all(sums_one)
    qv_sums = add_all([item[3] for item in backs]).reshape(3, wide)[0::2, :cols]
    rel_sums = rel_result(add_all([item[2] for item in backs]), heads)
    up_sums = add_all([item[3] for item in mlps]).reshape(units)
    qv_full = lax.dynamic_update_slice_in_dim(
        jnp.zeros((2, width), F32), qv_sums, model_index * cols, 1
    )
    up_full = lax.dynamic_update_slice_in_dim(
        jnp.zeros(up_bias.shape, F32), up_sums, model_index * units, 0
    )

    def sum_bundle(arrays):
        sizes = [array.size for array in arrays]
        flat = jnp.concatenate([array.reshape(-1) for array in arrays])
        count = (flat.size + 1023) // 1024 * 1024
        flat = jnp.pad(flat, (0, count - flat.size)).reshape(-1, 128)
        flat = sum_all(flat).reshape(-1)
        outs, at = [], 0
        for array, size in zip(arrays, sizes):
            outs.append(flat[at : at + size].reshape(array.shape))
            at += size
        return outs

    two_sums, up_bias_grad = sum_bundle([two, up_full])
    one_sums, qv_bias_grad, height_grad, width_grad = sum_bundle(
        [one, qv_full, rel_sums[0], rel_sums[1]]
    )
    qkv_grad = jnp.stack([first_grad[:, slot * cols : (slot + 1) * cols] for slot in range(3)])
    proj_grad = first_grad[:, 3 * cols :].T
    return (
        block_output,
        input_grad,
        one_sums[0],
        one_sums[1],
        qkv_grad,
        qv_bias_grad,
        proj_grad,
        two_sums[2],
        two_sums[0],
        two_sums[1],
        up_grad,
        up_bias_grad,
        down_grad.T,
        two_sums[3],
        height_grad,
        width_grad,
    )


def solution(mesh):
    in_specs = (
        P("dp", None),
        P("dp"),
        P("dp"),
        P(),
        P(),
        P(None, "dp", "mp"),
        P(),
        P("mp", "dp"),
        P(),
        P(),
        P(),
        P("dp", "mp"),
        P(),
        P("mp", "dp"),
        P(),
        P(),
        P(),
        P("dp", None),
    )
    out_specs = (
        P("dp", None),
        P("dp", None),
        P(),
        P(),
        P(None, "dp", "mp"),
        P(),
        P("mp", "dp"),
        P(),
        P(),
        P(),
        P("dp", "mp"),
        P(),
        P("mp", "dp"),
        P(),
        P(),
        P(),
    )
    return jax.shard_map(body, mesh=mesh, in_specs=in_specs, out_specs=out_specs, check_vma=False)
```

```python
from functools import partial

import jax
import jax.numpy as jnp
import numpy as np
from jax import lax
from jax.experimental import pallas as pl
from jax.experimental.pallas import tpu as pltpu
from jax.sharding import PartitionSpec as P

HD = 80
WIN = 14
SIDE = 64
GRID = 5
WTOK = 196
RELN = 27
ROWS = 208
SCALE = HD ** (-0.5)
EPS = 1e-06
F32 = jnp.float32
BF16 = jnp.bfloat16
ANY = pl.BlockSpec(memory_space=pltpu.HBM)
highest = lax.Precision.HIGHEST


def dot(left, right):
    return lax.dot_general(left, right, (((1,), (0,)), ((), ())), preferred_element_type=F32)


def dot_nt(left, right):
    return lax.dot_general(left, right, (((1,), (1,)), ((), ())), preferred_element_type=F32)


def dot_tn(left, right):
    return lax.dot_general(left, right, (((0,), (0,)), ((), ())), preferred_element_type=F32)


def whole(array):
    zeros = (0,) * len(array.shape)
    return pl.BlockSpec(array.shape, lambda *_: zeros)


def params(megabytes):
    return pltpu.CompilerParams(vmem_limit_bytes=megabytes * 2**20)


def struct(shape, dtype):
    return jax.ShapeDtypeStruct(shape, dtype)


def assemble(offsets, pieces, target, sems):
    copies = []
    for index, piece in enumerate(pieces):
        count = piece.shape[0]
        start = pl.multiple_of(offsets[index], 16)
        copies.append(
            pltpu.make_async_copy(piece, target.at[pl.ds(start, count)], sems.at[index])
        )
    for copy in copies:
        copy.start()
    for copy in copies:
        copy.wait()


def norm_parts(values):
    center = jnp.mean(values, axis=-1, keepdims=True)
    centred = values - center
    spread = jnp.mean(centred * centred, axis=-1, keepdims=True)
    rstd = lax.rsqrt(spread + EPS)
    return centred * rstd, rstd


def prepare_kernel(order, places, lives, x_ref, top_ref, gain_ref, shift_ref, *outs):
    rows_ref, normed_ref, grad_ref, valid_ref = outs
    slot = order[pl.program_id(0)]
    token = lax.broadcasted_iota(jnp.int32, (WTOK, 1), 0)
    row = (token * 9363) >> 17
    col = token - row * WIN
    spot = places[slot]
    high = spot // GRID * WIN
    wide = spot % GRID * WIN
    inside = (high + row < SIDE) & (wide + col < SIDE) & (lives[slot] == 1)
    valid = jnp.where(inside, 1.0, 0.0).astype(F32)
    x = x_ref[0]
    xhat, _ = norm_parts(x.astype(F32))
    normed = (xhat * gain_ref[...] + shift_ref[...]) * valid
    empty = jnp.zeros((ROWS - WTOK, x.shape[1]), F32)
    normed_ref[...] = jnp.concatenate([normed, empty], axis=0).astype(BF16)
    grad = top_ref[0].astype(F32) * valid
    grad_ref[...] = jnp.concatenate([grad, empty], axis=0).astype(BF16)
    rows_ref[...] = jnp.concatenate([x.astype(F32), empty], axis=0).astype(BF16)
    valid_ref[...] = jnp.concatenate([valid, empty[:, :1]], axis=0)


def prepare(order, places, lives, x, top, gain, shift):
    count = order.shape[0]
    width = x.shape[2]
    window = pl.BlockSpec((1, WTOK, width), lambda i, order, *_: (order[i], 0, 0))
    block = pl.BlockSpec((ROWS, width), lambda i, *_: (i, 0))
    return pl.pallas_call(
        prepare_kernel,
        grid_spec=pltpu.PrefetchScalarGridSpec(
            num_scalar_prefetch=3,
            grid=(count,),
            in_specs=[window, window, whole(gain), whole(shift)],
            out_specs=[block] * 3 + [pl.BlockSpec((ROWS, 1), lambda i, *_: (i, 0))],
        ),
        out_shape=[struct((count * ROWS, width), BF16)] * 3 + [struct((count * ROWS, 1), F32)],
        compiler_params=params(60),
        name="prepare",
    )(order, places, lives, x, top, gain, shift)


def top_rows(shape):
    return pl.BlockSpec(shape, lambda i: (0, 0))


def row_block(shape, at):
    return pl.BlockSpec(shape, lambda i: (at, 0))


def total(refs, rows):
    value = refs[0][:rows].astype(F32)
    for ref in refs[1:]:
        value = value + ref[:rows].astype(F32)
    return value


def norm_two_kernel(count, *refs):
    parts, (x_ref, bias_ref, gain_ref, shift_ref, after_ref, normed_ref) = (
        refs[:count],
        refs[count:],
    )
    rows = x_ref.shape[0]
    after = x_ref[...].astype(F32) + total(parts, rows) + bias_ref[...]
    xhat, _ = norm_parts(after)
    after_ref[...] = after
    normed_ref[...] = (xhat * gain_ref[...] + shift_ref[...]).astype(BF16)


def norm_two(parts, x, at, bias, gain, shift):
    shape = (parts[-1].shape[0], x.shape[1])
    return pl.pallas_call(
        partial(norm_two_kernel, len(parts)),
        grid=(1,),
        in_specs=[top_rows(shape)] * len(parts)
        + [row_block(shape, at), whole(bias), whole(gain), whole(shift)],
        out_specs=[top_rows(shape)] * 2,
        out_shape=[struct(shape, F32), struct(shape, BF16)],
        compiler_params=params(60),
        name="norm_two",
    )(*parts, x, bias, gain, shift)


def finish_kernel(count, *refs):
    parts, (after_ref, valid_ref, bias_ref, out_ref) = refs[:count], refs[count:]
    rows = after_ref.shape[0]
    branch = total(parts, rows) + bias_ref[...]
    out_ref[...] = (valid_ref[...] * (after_ref[...] + branch)).astype(BF16)


def finish(parts, after, valid, at, bias):
    return pl.pallas_call(
        partial(finish_kernel, len(parts)),
        grid=(1,),
        in_specs=[top_rows(after.shape)] * (len(parts) + 1)
        + [row_block((after.shape[0], 1), at), whole(bias)],
        out_specs=top_rows(after.shape),
        out_shape=struct(after.shape, BF16),
        compiler_params=params(60),
        name="finish",
    )(*parts, after, valid, bias)


def norm_back(upstream, xhat, rstd, gain):
    weighted = upstream * gain
    inner = jnp.mean(weighted * xhat, axis=-1, keepdims=True)
    level = jnp.mean(weighted, axis=-1, keepdims=True)
    return rstd * (weighted - level - xhat * inner)


def norm_two_back_kernel(count, *refs):
    parts = refs[:count]
    after_ref, top_ref, gain_ref, grad_ref, branch_ref, sums_ref = refs[count:]
    rows = after_ref.shape[0]
    upstream = total(parts, rows)
    xhat, rstd = norm_parts(after_ref[...])
    top = top_ref[...].astype(F32)
    grad = top + norm_back(upstream, xhat, rstd, gain_ref[...])
    branch = grad.astype(BF16)
    grad_ref[...] = grad
    branch_ref[...] = branch
    sums_ref[0:1] = jnp.sum(upstream * xhat, axis=0, keepdims=True)
    sums_ref[1:2] = jnp.sum(upstream, axis=0, keepdims=True)
    sums_ref[2:3] = jnp.sum(branch.astype(F32), axis=0, keepdims=True)
    sums_ref[3:4] = jnp.sum(top, axis=0, keepdims=True)


def norm_two_back(parts, after, top, at, gain):
    sums = struct((4, after.shape[1]), F32)
    return pl.pallas_call(
        partial(norm_two_back_kernel, len(parts)),
        grid=(1,),
        in_specs=[top_rows(after.shape)] * (len(parts) + 1)
        + [row_block(after.shape, at), whole(gain)],
        out_specs=[top_rows(after.shape)] * 2 + [whole(sums)],
        out_shape=[struct(after.shape, F32), struct(after.shape, BF16), sums],
        compiler_params=params(60),
        name="norm_two_back",
    )(*parts, after, top, gain)


def norm_one_back_kernel(count, *refs):
    parts = refs[:count]
    x_ref, valid_ref, grad_ref, gain_ref, out_ref, sums_ref = refs[count:]
    rows = x_ref.shape[0]
    upstream = total(parts, rows) * valid_ref[...]
    xhat, rstd = norm_parts(x_ref[...].astype(F32))
    out_ref[...] = (grad_ref[...] + norm_back(upstream, xhat, rstd, gain_ref[...])).astype(BF16)
    sums_ref[0:1] = jnp.sum(upstream * xhat, axis=0, keepdims=True)
    sums_ref[1:2] = jnp.sum(upstream, axis=0, keepdims=True)


def norm_one_back(parts, x, valid, at, grad, gain):
    shape = grad.shape
    sums = struct((2, shape[1]), F32)
    return pl.pallas_call(
        partial(norm_one_back_kernel, len(parts)),
        grid=(1,),
        in_specs=[top_rows(shape)] * len(parts)
        + [row_block(shape, at), row_block((shape[0], 1), at), top_rows(shape), whole(gain)],
        out_specs=[top_rows(shape), whole(sums)],
        out_shape=[struct(shape, BF16), sums],
        compiler_params=params(60),
        name="norm_one_back",
    )(*parts, x, valid, grad, gain)


def qkv_kernel(count, cols, offsets, *refs):
    pieces = refs[:count]
    x_ref, bias_ref, q_ref, k_ref, v_ref, w_ref, buffer, sems = refs[count:]
    wide = q_ref.shape[1]

    @pl.when(pl.program_id(0) == 0)
    def _():
        assemble(offsets, pieces, buffer, sems)
        for slot in range(4):
            base = slot * wide
            w_ref[:, base : base + cols] = buffer[:, slot * cols : (slot + 1) * cols]
            if wide > cols:
                w_ref[:, base + cols : base + wide] = jnp.zeros(
                    (w_ref.shape[0], wide - cols), BF16
                )

    x = x_ref[...]
    for slot, ref in enumerate((q_ref, k_ref, v_ref)):
        span = slice(slot * wide, (slot + 1) * wide)
        ref[...] = (dot(x, w_ref[:, span]) + bias_ref[:, span]).astype(BF16)


def project(offsets, pieces, x, bias, cols, wide):
    rows, width = x.shape
    step = 2 * ROWS
    block = pl.BlockSpec((step, wide), lambda i, *_: (i, 0))
    return pl.pallas_call(
        partial(qkv_kernel, len(pieces), cols),
        grid_spec=pltpu.PrefetchScalarGridSpec(
            num_scalar_prefetch=1,
            grid=(rows // step,),
            in_specs=[ANY] * len(pieces)
            + [pl.BlockSpec((step, width), lambda i, *_: (i, 0)), whole(bias)],
            out_specs=[block, block, block, pl.BlockSpec((width, 4 * wide), lambda i, *_: (0, 0))],
            scratch_shapes=[
                pltpu.VMEM((width, 4 * cols), BF16),
                pltpu.SemaphoreType.DMA((len(pieces),)),
            ],
        ),
        out_shape=[struct((rows, wide), BF16)] * 3 + [struct((width, 4 * wide), BF16)],
        compiler_params=params(60),
        name="qkv",
    )(offsets, *pieces, x, bias)


def head_spans(heads, wide):
    spans = []
    for head in range(heads):
        first, last = head * HD, head * HD + HD
        low = first // 128 * 128
        high = min((last + 127) // 128 * 128, wide)
        spans.append((low, high, first, last))
    return spans


def lane_mask(span):
    low, high, first, last = span
    lane = lax.broadcasted_iota(jnp.int32, (1, high - low), 1) + low
    return jnp.where((lane >= first) & (lane < last), 1.0, 0.0).astype(BF16)


def shift_counts():
    token = lax.broadcasted_iota(jnp.int32, (ROWS, 128), 0)
    row = (token * 9363) >> 17
    col = token - row * WIN
    return jnp.maximum(WIN - 1 - row, 0), WIN - 1 - col


def shift_lanes(values, counts, back):
    for step in (1, 2, 4, 8):
        moved = pltpu.roll(values, step if back else 128 - step, 1)
        values = jnp.where((counts & step) != 0, moved, values)
    return values


def lane_kind():
    lane = lax.broadcasted_iota(jnp.int32, (ROWS, 128), 1) & 31
    return lane < WIN, (lane >= 16) & (lane < 16 + WIN), lane == 31


def split_two(values):
    high = values.astype(BF16)
    return high, (values - high.astype(F32)).astype(BF16)


def bias_operand(q, rel_high, rel_low, counts):
    table = (dot(q, rel_high) + dot(q, rel_low)) * (1.0 / SCALE)
    by_row = shift_lanes(table[:, :128], counts[0], False)
    by_col = shift_lanes(table[:, 128:], counts[1], False)
    is_row, is_col, is_last = lane_kind()
    packed = jnp.where(
        is_row, by_row, jnp.where(is_col, by_col, jnp.where(is_last, 1.0, 0.0))
    )
    high, low = split_two(packed)
    return jnp.concatenate([high, low], axis=1)


def add_lanes(parts, values, span):
    low, high = span[0], span[1]
    for index in range(low // 128, high // 128):
        piece = values[:, index * 128 - low : index * 128 - low + 128]
        parts[index] = piece if parts[index] is None else parts[index] + piece


def attend_kernel(heads, split, q_ref, k_ref, v_ref, rh_ref, rl_ref, mark_ref, w_ref, *outs):
    mixed_ref, shares_ref = outs[:2]
    q, k, v = q_ref[...], k_ref[...], v_ref[...]
    wide = q.shape[1]
    bias = bias_operand(q, rh_ref[...], rl_ref[...], shift_counts())
    parts = [None] * (wide // 128)
    for head, span in enumerate(head_spans(heads, wide)):
        mask = lane_mask(span)
        cut = slice(span[0], span[1])
        scores = dot_nt(
            jnp.concatenate([q[:, cut], bias], axis=1),
            jnp.concatenate([k[:, cut] * mask, mark_ref[head]], axis=1),
        )
        top = jnp.max(scores, axis=-1, keepdims=True)
        shifted = jnp.exp(SCALE * (scores - top))
        norm = jnp.sum(shifted, axis=-1, keepdims=True)
        shares = (shifted * (1.0 / norm)).astype(BF16)
        shares_ref[:, head * 256 : head * 256 + ROWS] = shares
        add_lanes(parts, dot(shares, v[:, cut] * mask), span)
    mixed = jnp.concatenate(parts, axis=1).astype(BF16)
    cols = heads * HD
    mixed_ref[...] = mixed[:, :cols]
    branch = dot_nt(mixed, w_ref[...]).astype(BF16)
    if split:
        keep_ref, send_ref = outs[2:]
        step = pl.program_id(0)

        @pl.when(step < split)
        def _():
            send_ref[...] = branch

        @pl.when(step >= split)
        def _():
            keep_ref[...] = branch
    else:
        outs[2][...] = branch


def split_specs(windows, split, width):
    rows = ROWS * (windows - split)
    if not split:
        return [pl.BlockSpec((ROWS, width), lambda i: (i, 0))], [struct((rows, width), BF16)]
    return (
        [
            pl.BlockSpec((ROWS, width), lambda i: (jnp.maximum(i - split, 0), 0)),
            pl.BlockSpec((ROWS, width), lambda i: (jnp.minimum(i, split - 1), 0)),
        ],
        [struct((rows, width), BF16), struct((ROWS * split, width), BF16)],
    )


def attend(heads, part, windows, split, q, k, v, rel_high, rel_low, marks, weights):
    wide = q.shape[1]
    width = weights.shape[0]

    def place(i):
        return (i + split) % windows if split else i

    block = pl.BlockSpec((ROWS, wide), lambda i: (part * windows + place(i), 0))
    specs, shapes = split_specs(windows, split, width)
    return pl.pallas_call(
        partial(attend_kernel, heads, split),
        grid=(windows,),
        in_specs=[
            block,
            block,
            block,
            whole(rel_high),
            whole(rel_low),
            whole(marks),
            pl.BlockSpec((width, wide), lambda i: (0, 3)),
        ],
        out_specs=[
            pl.BlockSpec((ROWS, heads * HD), lambda i: (place(i), 0)),
            pl.BlockSpec((ROWS, heads * 256), lambda i: (place(i), 0)),
        ]
        + specs,
        out_shape=[
            struct((windows * ROWS, heads * HD), BF16),
            struct((windows * ROWS, heads * 256), BF16),
        ]
        + shapes,
        compiler_params=params(60),
        name="attend",
    )(q, k, v, rel_high, rel_low, marks, weights)


def attend_back_kernel(heads, windows, split, count, *refs):
    pieces = refs[:count]
    q_ref, k_ref, v_ref, shares_ref, rh_ref, mark_ref, w_ref = refs[count : count + 7]
    grads_ref, branch_ref, rel_ref, sum_ref = refs[count + 7 : count + 11]
    outs = refs[count + 11 :]
    step = pl.program_id(0)

    @pl.when(step == 0)
    def _():
        start = 0
        for piece in pieces:
            branch_ref[start : start + piece.shape[0]] = piece[...]
            start += piece.shape[0]
        rel_ref[...] = jnp.zeros(rel_ref.shape, F32)
        sum_ref[...] = jnp.zeros(sum_ref.shape, F32)

    place = lax.rem(step + split, windows) if split else step
    q, k, v = q_ref[...], k_ref[...], v_ref[...]
    wide = q.shape[1]
    top = branch_ref[pl.ds(pl.multiple_of(place * ROWS, 16), ROWS), :]
    grad_mixed = dot(top, w_ref[:, 3 * wide :]).astype(BF16)
    grad_q, grad_k, grad_v = ([None] * (wide // 128) for _ in range(3))
    grad_bias = None
    for head, span in enumerate(head_spans(heads, wide)):
        mask = lane_mask(span)
        cut = slice(span[0], span[1])
        size = span[1] - span[0]
        upper = grad_mixed[:, cut]
        rounded = shares_ref[:, head * 256 : head * 256 + ROWS]
        shares = rounded.astype(F32)
        weighted = shares * dot_nt(upper, v[:, cut] * mask)
        inner = jnp.sum(weighted, axis=-1, keepdims=True)
        grad_scores = (weighted - shares * inner).astype(BF16)
        add_lanes(grad_v, dot_tn(rounded, upper * mask), span)
        both = dot(
            grad_scores,
            jnp.concatenate([k[:, cut] * mask, mark_ref[head][:, :128]], axis=1),
        )
        add_lanes(grad_q, both[:, :size], span)
        part = both[:, size:]
        grad_bias = part if grad_bias is None else grad_bias + part
        add_lanes(grad_k, dot_tn(grad_scores, q[:, cut] * mask), span)
    counts = shift_counts()
    is_row, is_col, _ = lane_kind()
    by_row = shift_lanes(jnp.where(is_row, grad_bias, 0.0), counts[0], True)
    by_col = shift_lanes(jnp.where(is_col, grad_bias, 0.0), counts[1], True)
    packed = jnp.concatenate([by_row, by_col], axis=1).astype(BF16)
    extra = dot_nt(packed, rh_ref[...])
    rel_ref[...] += dot_tn(packed, q)
    grad_q = (SCALE * jnp.concatenate(grad_q, axis=1) + extra).astype(BF16)
    grad_k = (SCALE * jnp.concatenate(grad_k, axis=1)).astype(BF16)
    grad_v = jnp.concatenate(grad_v, axis=1).astype(BF16)
    cols = heads * HD
    for slot, grad in enumerate((grad_q, grad_k, grad_v)):
        cut = slice(slot * wide, (slot + 1) * wide)
        grads_ref[:, slot * cols : (slot + 1) * cols] = grad[:, :cols]
        sum_ref[:, cut] += jnp.sum(grad.astype(F32), axis=0, keepdims=True)
    partial_sum = dot_nt(
        jnp.concatenate([grad_q, grad_k, grad_v], axis=1), w_ref[:, : 3 * wide]
    )
    result = partial_sum.astype(BF16)
    if split:
        keep_ref, send_ref = outs

        @pl.when(step < split)
        def _():
            send_ref[...] = result

        @pl.when(step >= split)
        def _():
            keep_ref[...] = result
    else:
        outs[0][...] = result


def attend_back(
    heads, part, windows, split, pieces, q, k, v, shares, rel_high, marks, weights
):
    wide = q.shape[1]
    width = weights.shape[0]

    def place(i):
        return (i + split) % windows if split else i

    block = pl.BlockSpec((ROWS, wide), lambda i: (part * windows + place(i), 0))
    specs, shapes = split_specs(windows, split, width)
    rows = windows * ROWS
    branch = struct((rows, width), BF16)
    rel = struct((256, wide), F32)
    sums = struct((1, 3 * wide), F32)
    return pl.pallas_call(
        partial(attend_back_kernel, heads, windows, split, len(pieces)),
        grid=(windows,),
        in_specs=[whole(piece) for piece in pieces]
        + [
            block,
            block,
            block,
            pl.BlockSpec((ROWS, heads * 256), lambda i: (place(i), 0)),
            whole(rel_high),
            whole(marks),
            whole(weights),
        ],
        out_specs=[
            pl.BlockSpec((ROWS, 3 * heads * HD), lambda i: (place(i), 0)),
            whole(branch),
            whole(rel),
            whole(sums),
        ]
        + specs,
        out_shape=[struct((rows, 3 * heads * HD), BF16), branch, rel, sums] + shapes,
        compiler_params=params(60),
        name="attend_back",
    )(*pieces, q, k, v, shares, rel_high, marks, weights)


def mlp_kernel(count, weights, split, offsets, order, *refs):
    pieces = refs[:count]
    weight_pieces = refs[count : count + weights]
    refs = refs[count + weights :]
    top_ref, bias_ref, active_ref, hidden_ref, normed_ref, sum_ref, out_ref = refs[:7]
    backs = refs[7:-3]
    up, down, sems = refs[-3:]
    step = pl.program_id(0)
    block = top_ref.shape[0]
    units = up.shape[1]
    copies = []
    for half, target in enumerate((down, up)):
        copies.append([])
        for index, piece in enumerate(weight_pieces):
            rows = piece.shape[0]
            start = pl.multiple_of(offsets[index], 16)
            copies[half].append(
                pltpu.make_async_copy(
                    piece.at[:, half * units : (half + 1) * units],
                    target.at[pl.ds(start, rows)],
                    sems.at[half, index],
                )
            )

    @pl.when(step == 0)
    def _():
        for copy in copies[1] + copies[0]:
            copy.start()
        start = 0
        for piece in pieces:
            normed_ref[start : start + piece.shape[0]] = piece[...]
            start += piece.shape[0]
        sum_ref[...] = jnp.zeros(sum_ref.shape, F32)
        for copy in copies[1]:
            copy.wait()

    place = 1 - step if split else step
    normed = normed_ref[pl.ds(pl.multiple_of(place * block, 16), block), :]
    hidden = dot(normed, up[...]) + bias_ref[...]

    @pl.when(step == 0)
    def _():
        for copy in copies[0]:
            copy.wait()

    half = 0.5 * (1.0 + lax.erf(hidden * (0.5**0.5)))
    slope = half + hidden * jnp.exp(-0.5 * hidden * hidden) * float((2.0 * np.pi) ** -0.5)
    active = (hidden * half).astype(BF16)
    active_ref[...] = active
    grad = (dot(top_ref[...], down[...]) * slope).astype(BF16)
    hidden_ref[...] = grad
    sum_ref[...] += jnp.sum(grad.astype(F32), axis=0, keepdims=True)
    back = dot_nt(grad, up[...]).astype(BF16)
    if split:

        @pl.when(step == 0)
        def _():
            backs[1][...] = back

        @pl.when(step == 1)
        def _():
            backs[0][...] = back
    else:
        backs[0][...] = back
    result = dot_nt(active, down[...]).astype(BF16)
    for index in range(block // ROWS):
        target = order[place * (block // ROWS) + index]
        out_ref[pl.ds(pl.multiple_of(target * ROWS, 16), ROWS), :] = result[
            index * ROWS : (index + 1) * ROWS
        ]


def mlp(offsets, order, pieces, weight_pieces, top, part, bias, split):
    rows = sum(piece.shape[0] for piece in pieces)
    width = pieces[0].shape[1]
    units = weight_pieces[0].shape[1] // 2
    block = 2 * ROWS
    blocks = rows // block
    normed = struct((rows, width), BF16)
    sums = struct((1, units), F32)

    def place(i):
        return 1 - i if split else i

    wide = pl.BlockSpec((block, units), lambda i, *_: (place(i), 0))
    back = struct((block, width), BF16)
    if split:
        back_specs, back_shapes = [whole(back)] * 2, [back] * 2
    else:
        back_specs = [pl.BlockSpec((block, width), lambda i, *_: (i, 0))]
        back_shapes = [normed]
    return pl.pallas_call(
        partial(mlp_kernel, len(pieces), len(weight_pieces), split),
        grid_spec=pltpu.PrefetchScalarGridSpec(
            num_scalar_prefetch=2,
            grid=(blocks,),
            in_specs=[whole(piece) for piece in pieces]
            + [ANY] * len(weight_pieces)
            + [
                pl.BlockSpec((block, width), lambda i, *_: (part * blocks + place(i), 0)),
                whole(bias),
            ],
            out_specs=[wide, wide, whole(normed), whole(sums), whole(normed)] + back_specs,
            scratch_shapes=[
                pltpu.VMEM((width, units), BF16),
                pltpu.VMEM((width, units), BF16),
                pltpu.SemaphoreType.DMA((2, len(weight_pieces))),
            ],
        ),
        out_shape=[struct((rows, units), BF16)] * 2 + [normed, sums, normed] + back_shapes,
        compiler_params=params(60),
        name="mlp",
    )(offsets, order, *pieces, *weight_pieces, top, bias)


def weight_grad_kernel(sizes, share, targets, *refs):
    count = 2 * sum(sizes)
    operands = refs[:count]
    send_ref, keep_ref, result, sems = refs[count:]
    step = pl.program_id(0)
    steps = pl.num_programs(0)
    chunk = operands[0].shape[1]
    pieces = chunk // share
    base = pl.multiple_of(step * chunk, 16)
    at, first = 0, 0
    for size in sizes:
        value = None
        for _ in range(size):
            left, right = operands[at], operands[at + 1]
            at += 2
            term = dot_tn(left[...], right[...])
            value = term if value is None else value + term
        span = value.shape[1]
        result[pl.ds(base, chunk), first : first + span] = value.astype(BF16)
        first += span

    def copy(index, out, slot):
        return pltpu.make_async_copy(
            result.at[pl.ds(pl.multiple_of(index * share, 16), share)], out.at[slot], sems.at[index]
        )

    for piece in range(pieces):
        index = step * pieces + piece
        slot = targets[index]

        @pl.when(slot < 4)
        def _():
            copy(index, send_ref, slot).start()

        @pl.when(slot >= 4)
        def _():
            copy(index, keep_ref, slot - 4).start()

    @pl.when(step == steps - 1)
    def _():
        for index in range(8):
            copy(index, send_ref, 0).wait()


def plain_grad_kernel(sizes, *refs):
    count = 2 * sum(sizes)
    operands, out_ref = refs[:count], refs[count]
    at, first = 0, 0
    for size in sizes:
        value = None
        for _ in range(size):
            left, right = operands[at], operands[at + 1]
            at += 2
            term = dot_tn(left[...], right[...])
            value = term if value is None else value + term
        span = value.shape[1]
        out_ref[:, first : first + span] = value.astype(BF16)
        first += span


def weight_grad(targets, groups, share):
    operands, specs = [], []
    chunk = 640 if targets is not None else 256
    total_cols = 0
    for group in groups:
        for left, at, rows, right in group:
            operands += [left, right]
            specs.append(pl.BlockSpec((rows, chunk), lambda i, *_, at=at: (at, i)))
            specs.append(whole(right))
        total_cols += group[0][3].shape[1]
    width = operands[0].shape[1]
    sizes = [len(group) for group in groups]
    if targets is None:
        return [
            pl.pallas_call(
                partial(plain_grad_kernel, sizes),
                grid=(width // chunk,),
                in_specs=specs,
                out_specs=pl.BlockSpec((chunk, total_cols), lambda i: (i, 0)),
                out_shape=struct((width, total_cols), BF16),
                compiler_params=params(60),
                name="weight_grad",
            )(*operands)
        ]
    return pl.pallas_call(
        partial(weight_grad_kernel, sizes, share),
        grid_spec=pltpu.PrefetchScalarGridSpec(
            num_scalar_prefetch=1,
            grid=(width // chunk,),
            in_specs=specs,
            out_specs=[ANY] * 2,
            scratch_shapes=[
                pltpu.VMEM((width, total_cols), BF16),
                pltpu.SemaphoreType.DMA((8,)),
            ],
        ),
        out_shape=[struct((4, share, total_cols), BF16)] * 2,
        compiler_params=params(60),
        name="weight_grad",
    )(targets, *operands)


def place_kernel(part, order, *refs):
    pieces, out_ref, buffer, sem = refs[:4], refs[-3], refs[-2], refs[-1]
    rows = buffer.shape[0]
    for me in range(4):

        @pl.when(order[0] == me)
        def _(me=me):
            for index, step in enumerate((0, 2, 1, 3)):
                start = (me ^ step) * WTOK
                buffer[start : start + WTOK] = pieces[index][:WTOK].astype(F32)

    copy = pltpu.make_async_copy(buffer, out_ref.at[pl.ds(part * rows, rows)], sem)
    copy.start()
    copy.wait()


def place_windows(part, order, pieces, rows, held):
    width = pieces[0].shape[1]
    operands = list(pieces) + ([] if held is None else [held])
    return pl.pallas_call(
        partial(place_kernel, part),
        grid_spec=pltpu.PrefetchScalarGridSpec(
            num_scalar_prefetch=1,
            grid=(1,),
            in_specs=[whole(piece) for piece in pieces] + [ANY] * (len(operands) - 4),
            out_specs=ANY,
            scratch_shapes=[pltpu.VMEM((4 * WTOK, width), F32), pltpu.SemaphoreType.DMA(())],
        ),
        out_shape=struct((rows, width), F32),
        input_output_aliases={} if held is None else {5: 0},
        compiler_params=params(60),
        name="place_windows",
    )(order, *operands)


def key_marks(heads):
    marks = np.zeros((heads, ROWS, 256), np.float32)
    for head in range(heads):
        for token in range(WTOK):
            for half in (0, 128):
                marks[head, token, half + head * 32 + token // WIN] = 1.0
                marks[head, token, half + head * 32 + 16 + token % WIN] = 1.0
        marks[head, WTOK:, head * 32 + 31] = -1e30
    return marks.astype(BF16)


def rel_operand(rel_height, rel_width, heads, wide):
    high = rel_height[::-1].T
    flat = rel_width[::-1].T
    lanes = jnp.zeros((wide, 256), F32)

    def spread(block, row, lane):
        below = wide - row - HD
        return jnp.pad(block, ((row, below), (lane, 256 - lane - block.shape[1])))

    for head in range(heads):
        first = head * 32 + 16
        fit = min(RELN, 128 - first)
        lanes = lanes + spread(high, head * HD, head * 32)
        lanes = lanes + spread(flat[:, :fit], head * HD, 128 + first)
        if fit < RELN:
            lanes = lanes + spread(flat[:, fit:], head * HD, 128)
    return split_two(lanes)


def rel_result(sums, heads):
    high = jnp.zeros((RELN, HD), F32)
    flat = jnp.zeros((RELN, HD), F32)
    for head in range(heads):
        cols = sums[:, head * HD : head * HD + HD]
        high = high + cols[head * 32 : head * 32 + RELN]
        rolled = jnp.concatenate([cols[128:], cols[128:]], axis=0)
        flat = flat + rolled[head * 32 + 16 : head * 32 + 16 + RELN]
    return high[::-1], flat[::-1]


def add_all(values):
    out = values[0]
    for value in values[1:]:
        out = out + value
    return out


def body(
    block_input,
    window_place,
    slot_live,
    norm_one_gain,
    norm_one_shift,
    qkv_weight,
    qv_bias,
    proj_weight,
    proj_bias,
    norm_two_gain,
    norm_two_shift,
    up_weight,
    up_bias,
    down_weight,
    down_bias,
    rel_height,
    rel_width,
    cotangent,
):
    data_parts = lax.axis_size("dp")
    model_parts = lax.axis_size("mp")
    data_index = lax.axis_index("dp")
    model_index = lax.axis_index("mp")
    width = block_input.shape[1]
    share = qkv_weight.shape[1]
    cols = qkv_weight.shape[2]
    heads = cols // HD
    wide = (cols + 127) // 128 * 128
    units = up_weight.shape[1]
    slots = window_place.shape[0]
    rings = data_parts == 8 and model_parts == 4 and slots % 4 == 0
    padded = (slots + model_parts - 1) // model_parts * model_parts
    halves = padded // 4 if rings else 1
    windows = padded // halves
    split = 2 if rings else 0
    part_rows = windows * ROWS
    own_rows = part_rows // model_parts

    if rings:
        depth, side = data_index // 2, data_index % 2
        y_bit, core_bit = model_index // 2, model_index % 2
        over_x = partial(lax.ppermute, axis_name="dp", perm=[(d, d ^ 1) for d in range(8)])
        over_z = partial(lax.ppermute, axis_name="dp", perm=[(d, (d + 2) % 8) for d in range(8)])
        over_y = partial(lax.ppermute, axis_name="mp", perm=[(m, m ^ 2) for m in range(4)])
        over_core = partial(lax.ppermute, axis_name="mp", perm=[(m, m ^ 1) for m in range(4)])

    def gather(piece):
        if not rings:
            return [lax.all_gather(piece, "dp", axis=0, tiled=True)]
        line = [piece]
        for _ in range(3):
            line.append(over_z(line[-1]))
        return [item for held in line for item in (held, over_x(held))]

    if rings:
        offsets = []
        for back in range(4):
            behind = (depth - back) % 4
            offsets += [share * (2 * behind + side), share * (2 * behind + 1 - side)]
        offsets = jnp.stack(offsets).astype(jnp.int32)
    else:
        offsets = jnp.zeros((1,), jnp.int32)

    def scatter(parts):
        if not rings:
            return lax.psum_scatter(
                parts[0], "dp", scatter_dimension=0, tiled=True
            ).astype(F32)
        send, keep = parts
        came = over_x(send)
        sums = [keep[k].astype(F32) + came[k].astype(F32) for k in range(4)]
        moving = over_z(sums[3].astype(BF16))
        moving = over_z((sums[2] + moving.astype(F32)).astype(BF16))
        moving = over_z((sums[1] + moving.astype(F32)).astype(BF16))
        return sums[0] + moving.astype(F32)

    def rows_scatter(parts):
        if not rings:
            return [lax.psum_scatter(parts[0], "mp", scatter_dimension=0, tiled=True)]
        keep, send = parts
        came = over_core(send)
        passed = (keep[ROWS:].astype(F32) + came[ROWS:].astype(F32)).astype(BF16)
        return [keep, came, over_y(passed)]

    def rows_gather(own):
        if not rings:
            return [lax.all_gather(own, "mp", axis=0, tiled=True)]
        across = over_y(own)
        return [own, across, over_core(own), over_core(across)]

    def sum_all(vector):
        if not rings:
            return lax.psum(vector, ("dp", "mp"))
        for step in (1, 2):
            vector = vector + lax.ppermute(
                vector, "mp", [(m, m ^ step) for m in range(4)]
            )
        for step in (1, 2, 4):
            vector = vector + lax.ppermute(
                vector, "dp", [(d, d ^ step) for d in range(8)]
            )
        return vector

    def own_slice(array):
        rows = array.shape[0] // model_parts
        return lax.dynamic_slice_in_dim(array, model_index * rows, rows, 0)

    first_piece = jnp.concatenate([qkv_weight[0], qkv_weight[1], qkv_weight[2], proj_weight.T], 1)
    first_weights = gather(first_piece)
    other_weights = gather(jnp.concatenate([down_weight.T, up_weight], 1))

    row = lambda v: v.reshape(1, -1)
    gain_one, shift_one = row(norm_one_gain), row(norm_one_shift)
    gain_two, shift_two = row(norm_two_gain), row(norm_two_shift)
    bias_local = lax.dynamic_slice_in_dim(qv_bias, model_index * cols, cols, 1)
    bias_local = jnp.pad(bias_local, [(0, 0), (0, wide - cols)])
    bias_qkv = row(jnp.stack([bias_local[0], jnp.zeros_like(bias_local[0]), bias_local[1]]))
    up_local = row(lax.dynamic_slice_in_dim(up_bias, model_index * units, units, 0))
    rel_high, rel_low = rel_operand(rel_height, rel_width, heads, wide)
    marks = jnp.asarray(key_marks(heads))

    steps = (0, 2, 1, 3)
    if rings:
        local = [model_index ^ step for step in steps]
        places = [4 * part + spot for part in range(halves) for spot in local]
    else:
        local = [jnp.int32(spot) for spot in range(windows)]
        places = local
    local = jnp.stack(local).astype(jnp.int32)
    places = jnp.stack(places).astype(jnp.int32)
    if rings:
        targets = []
        for d in range(8):
            ahead = (d // 2 - depth) % 4
            targets.append(ahead + jnp.where(d % 2 == side, 4, 0))
        targets = jnp.stack(targets).astype(jnp.int32)
    else:
        targets = None

    def by_window(array):
        array = array.reshape((slots, WTOK) + array.shape[1:])
        return jnp.pad(array, [(0, padded - slots)] + [(0, 0)] * (array.ndim - 1))

    rows_in, normed, grad_top, valid = prepare(
        places,
        jnp.pad(window_place, (0, padded - slots)),
        jnp.pad(slot_live, (0, padded - slots)),
        by_window(block_input),
        by_window(cotangent),
        gain_one,
        shift_one,
    )
    if rings:
        own_in, own_top, own_valid = rows_in, grad_top, valid
        at = [4 * part for part in range(halves)]
    else:
        own_in, own_top, own_valid = own_slice(rows_in), own_slice(grad_top), own_slice(valid)
        at = [0]

    q, k, v, weights = project(offsets, first_weights, normed, bias_qkv, cols, wide)
    attended = [
        attend(heads, part, windows, split, q, k, v, rel_high, rel_low, marks, weights)
        for part in range(halves)
    ]
    afters, normed_twos = [], []
    for part in range(halves):
        parts = rows_scatter(attended[part][2:])
        after, normed_two = norm_two(
            parts, own_in, at[part], row(proj_bias), gain_two, shift_two
        )
        afters.append(after)
        normed_twos.append(rows_gather(normed_two))

    mlps = [
        mlp(
            offsets,
            local,
            normed_twos[part],
            other_weights,
            grad_top,
            part,
            up_local,
            bool(split),
        )
        for part in range(halves)
    ]
    grad_afters, branches, sums_two = [], [], []
    for part in range(halves):
        parts = rows_scatter(mlps[part][5:])
        grad_after, branch, sums = norm_two_back(
            parts, afters[part], own_top, at[part], gain_two
        )
        grad_afters.append(grad_after)
        branches.append(rows_gather(branch))
        sums_two.append(sums)
    out_pieces = []
    for part in range(halves):
        result = lax.psum_scatter(mlps[part][4], "mp", scatter_dimension=0, tiled=True)
        own = finish([result], afters[part], own_valid, at[part], row(down_bias))
        out_pieces.append(own)
    full = lax.all_gather(jnp.concatenate(out_pieces, 0), "mp", axis=0, tiled=True)
    if rings:
        full = full.reshape(4, halves, ROWS, width).swapaxes(0, 1)
    full = full.reshape(padded, ROWS, width)
    block_output = full[:slots, :WTOK].reshape(slots * WTOK, width)

    blocks = [(part, part_rows) for part in range(halves)]
    down_grad = scatter(
        weight_grad(
            targets, [[(grad_top, *blocks[i], mlps[i][0]) for i in range(halves)]], share
        )
    )
    up_grad = scatter(
        weight_grad(
            targets, [[(mlps[i][2], 0, part_rows, mlps[i][1]) for i in range(halves)]], share
        )
    )

    backs = [
        attend_back(
            heads,
            part,
            windows,
            split,
            branches[part],
            q,
            k,
            v,
            attended[part][1],
            rel_high,
            marks,
            weights,
        )
        for part in range(halves)
    ]
    sums_one = []
    input_grad = None
    for part in range(halves):
        parts = rows_scatter(backs[part][4:])
        own, sums = norm_one_back(
            parts, own_in, own_valid, at[part], grad_afters[part], gain_one
        )
        sums_one.append(sums)
        gathered = rows_gather(own)
        if rings:
            input_grad = place_windows(part, local, gathered, slots * WTOK, input_grad)
        else:
            full = gathered[0].reshape(padded, ROWS, width)[:slots, :WTOK]
            input_grad = full.reshape(slots * WTOK, width).astype(F32)
    groups = [
        [(normed, *blocks[i], backs[i][0]) for i in range(halves)],
        [(backs[i][1], 0, part_rows, attended[i][0]) for i in range(halves)],
    ]
    first_grad = scatter(weight_grad(targets, groups, share))

    two = add_all(sums_two)
    one = add_all(sums_one)
    qv_sums = add_all([item[3] for item in backs]).reshape(3, wide)[0::2, :cols]
    rel_sums = rel_result(add_all([item[2] for item in backs]), heads)
    up_sums = add_all([item[3] for item in mlps]).reshape(units)
    qv_full = lax.dynamic_update_slice_in_dim(
        jnp.zeros((2, width), F32), qv_sums, model_index * cols, 1
    )
    up_full = lax.dynamic_update_slice_in_dim(
        jnp.zeros(up_bias.shape, F32), up_sums, model_index * units, 0
    )

    def sum_bundle(arrays):
        sizes = [array.size for array in arrays]
        flat = jnp.concatenate([array.reshape(-1) for array in arrays])
        count = (flat.size + 1023) // 1024 * 1024
        flat = jnp.pad(flat, (0, count - flat.size)).reshape(-1, 128)
        flat = sum_all(flat).reshape(-1)
        outs, at = [], 0
        for array, size in zip(arrays, sizes):
            outs.append(flat[at : at + size].reshape(array.shape))
            at += size
        return outs

    two_sums, up_bias_grad, one_sums, qv_bias_grad, height_grad, width_grad = sum_bundle(
        [two, up_full, one, qv_full, rel_sums[0], rel_sums[1]]
    )
    qkv_grad = jnp.stack([first_grad[:, slot * cols : (slot + 1) * cols] for slot in range(3)])
    proj_grad = first_grad[:, 3 * cols :].T
    return (
        block_output,
        input_grad,
        one_sums[0],
        one_sums[1],
        qkv_grad,
        qv_bias_grad,
        proj_grad,
        two_sums[2],
        two_sums[0],
        two_sums[1],
        up_grad,
        up_bias_grad,
        down_grad.T,
        two_sums[3],
        height_grad,
        width_grad,
    )


def solution(mesh):
    in_specs = (
        P("dp", None),
        P("dp"),
        P("dp"),
        P(),
        P(),
        P(None, "dp", "mp"),
        P(),
        P("mp", "dp"),
        P(),
        P(),
        P(),
        P("dp", "mp"),
        P(),
        P("mp", "dp"),
        P(),
        P(),
        P(),
        P("dp", None),
    )
    out_specs = (
        P("dp", None),
        P("dp", None),
        P(),
        P(),
        P(None, "dp", "mp"),
        P(),
        P("mp", "dp"),
        P(),
        P(),
        P(),
        P("dp", "mp"),
        P(),
        P("mp", "dp"),
        P(),
        P(),
        P(),
    )
    return jax.shard_map(body, mesh=mesh, in_specs=in_specs, out_specs=out_specs, check_vma=False)
```

```python
from functools import partial

import jax
import jax.numpy as jnp
import numpy as np
from jax import lax
from jax.experimental import pallas as pl
from jax.experimental.pallas import tpu as pltpu
from jax.sharding import PartitionSpec as P

HD = 80
WIN = 14
SIDE = 64
GRID = 5
WTOK = 196
RELN = 27
ROWS = 208
SCALE = HD ** (-0.5)
EPS = 1e-06
F32 = jnp.float32
BF16 = jnp.bfloat16
ANY = pl.BlockSpec(memory_space=pltpu.HBM)
highest = lax.Precision.HIGHEST


def dot(left, right):
    return lax.dot_general(left, right, (((1,), (0,)), ((), ())), preferred_element_type=F32)


def dot_nt(left, right):
    return lax.dot_general(left, right, (((1,), (1,)), ((), ())), preferred_element_type=F32)


def dot_tn(left, right):
    return lax.dot_general(left, right, (((0,), (0,)), ((), ())), preferred_element_type=F32)


def whole(array):
    zeros = (0,) * len(array.shape)
    return pl.BlockSpec(array.shape, lambda *_: zeros)


def params(megabytes):
    return pltpu.CompilerParams(vmem_limit_bytes=megabytes * 2**20)


def cost(micros):
    return pl.CostEstimate(
        flops=int(micros * 0.05e9), bytes_accessed=int(micros * 1.0e4), transcendentals=0
    )


def struct(shape, dtype):
    return jax.ShapeDtypeStruct(shape, dtype)


def assemble(offsets, pieces, target, sems):
    copies = []
    for index, piece in enumerate(pieces):
        count = piece.shape[0]
        start = pl.multiple_of(offsets[index], 16)
        copies.append(
            pltpu.make_async_copy(piece, target.at[pl.ds(start, count)], sems.at[index])
        )
    for copy in copies:
        copy.start()
    for copy in copies:
        copy.wait()


def norm_parts(values):
    center = jnp.mean(values, axis=-1, keepdims=True)
    centred = values - center
    spread = jnp.mean(centred * centred, axis=-1, keepdims=True)
    rstd = lax.rsqrt(spread + EPS)
    return centred * rstd, rstd


def token_valid(spot, live):
    token = lax.broadcasted_iota(jnp.int32, (WTOK, 1), 0)
    row = (token * 9363) >> 17
    col = token - row * WIN
    high = spot // GRID * WIN
    wide = spot % GRID * WIN
    inside = (high + row < SIDE) & (wide + col < SIDE) & (live == 1)
    return jnp.where(inside, 1.0, 0.0).astype(F32)


def pad_rows(values):
    empty = jnp.zeros((ROWS - WTOK, values.shape[1]), F32)
    return jnp.concatenate([values, empty], axis=0)


def prepare_kernel(order, places, lives, x_ref, gain_ref, shift_ref, *outs):
    rows_ref, normed_ref, valid_ref = outs
    slot = order[pl.program_id(0)]
    valid = token_valid(places[slot], lives[slot])
    x = x_ref[0].astype(F32)
    xhat, _ = norm_parts(x)
    normed_ref[...] = pad_rows((xhat * gain_ref[...] + shift_ref[...]) * valid).astype(BF16)
    rows_ref[...] = pad_rows(x).astype(BF16)
    valid_ref[...] = pad_rows(valid)


def prepare(order, places, lives, x, gain, shift):
    count = order.shape[0]
    width = x.shape[2]
    window = pl.BlockSpec((1, WTOK, width), lambda i, order, *_: (order[i], 0, 0))
    block = pl.BlockSpec((ROWS, width), lambda i, *_: (i, 0))
    return pl.pallas_call(
        prepare_kernel,
        grid_spec=pltpu.PrefetchScalarGridSpec(
            num_scalar_prefetch=3,
            grid=(count,),
            in_specs=[window, whole(gain), whole(shift)],
            out_specs=[block] * 2 + [pl.BlockSpec((ROWS, 1), lambda i, *_: (i, 0))],
        ),
        out_shape=[struct((count * ROWS, width), BF16)] * 2 + [struct((count * ROWS, 1), F32)],
        compiler_params=params(60),
        cost_estimate=cost(9),
        name="prepare",
    )(order, places, lives, x, gain, shift)


def mask_kernel(order, places, lives, top_ref, grad_ref):
    slot = order[pl.program_id(0)]
    valid = token_valid(places[slot], lives[slot])
    grad_ref[...] = pad_rows(top_ref[0].astype(F32) * valid).astype(BF16)


def mask_rows(order, places, lives, top):
    count = order.shape[0]
    width = top.shape[2]
    return pl.pallas_call(
        mask_kernel,
        grid_spec=pltpu.PrefetchScalarGridSpec(
            num_scalar_prefetch=3,
            grid=(count,),
            in_specs=[pl.BlockSpec((1, WTOK, width), lambda i, order, *_: (order[i], 0, 0))],
            out_specs=pl.BlockSpec((ROWS, width), lambda i, *_: (i, 0)),
        ),
        out_shape=struct((count * ROWS, width), BF16),
        compiler_params=params(60),
        cost_estimate=cost(6),
        name="mask_rows",
    )(order, places, lives, top)


def top_rows(shape):
    return pl.BlockSpec(shape, lambda i: (0, 0))


def row_block(shape, at):
    return pl.BlockSpec(shape, lambda i: (at, 0))


def total(refs, rows):
    value = refs[0][:rows].astype(F32)
    for ref in refs[1:]:
        value = value + ref[:rows].astype(F32)
    return value


def norm_two_kernel(count, *refs):
    parts, (x_ref, bias_ref, gain_ref, shift_ref, after_ref, normed_ref) = (
        refs[:count],
        refs[count:],
    )
    rows = x_ref.shape[0]
    after = x_ref[...].astype(F32) + total(parts, rows) + bias_ref[...]
    xhat, _ = norm_parts(after)
    after_ref[...] = after
    normed_ref[...] = (xhat * gain_ref[...] + shift_ref[...]).astype(BF16)


def norm_two(parts, x, at, bias, gain, shift):
    shape = (parts[-1].shape[0], x.shape[1])
    return pl.pallas_call(
        partial(norm_two_kernel, len(parts)),
        grid=(1,),
        in_specs=[top_rows(shape)] * len(parts)
        + [row_block(shape, at), whole(bias), whole(gain), whole(shift)],
        out_specs=[top_rows(shape)] * 2,
        out_shape=[struct(shape, F32), struct(shape, BF16)],
        compiler_params=params(60),
        cost_estimate=cost(3),
        name="norm_two",
    )(*parts, x, bias, gain, shift)


def finish_kernel(count, *refs):
    parts, (after_ref, valid_ref, bias_ref, out_ref) = refs[:count], refs[count:]
    rows = after_ref.shape[0]
    branch = total(parts, rows) + bias_ref[...]
    out_ref[...] = (valid_ref[...] * (after_ref[...] + branch)).astype(BF16)


def finish(parts, after, valid, at, bias):
    return pl.pallas_call(
        partial(finish_kernel, len(parts)),
        grid=(1,),
        in_specs=[top_rows(after.shape)] * (len(parts) + 1)
        + [row_block((after.shape[0], 1), at), whole(bias)],
        out_specs=top_rows(after.shape),
        out_shape=struct(after.shape, BF16),
        compiler_params=params(60),
        cost_estimate=cost(2.5),
        name="finish",
    )(*parts, after, valid, bias)


def norm_back(upstream, xhat, rstd, gain):
    weighted = upstream * gain
    inner = jnp.mean(weighted * xhat, axis=-1, keepdims=True)
    level = jnp.mean(weighted, axis=-1, keepdims=True)
    return rstd * (weighted - level - xhat * inner)


def norm_two_back_kernel(count, *refs):
    parts = refs[:count]
    after_ref, top_ref, gain_ref, grad_ref, branch_ref, sums_ref = refs[count:]
    rows = after_ref.shape[0]
    upstream = total(parts, rows)
    xhat, rstd = norm_parts(after_ref[...])
    top = top_ref[...].astype(F32)
    grad = top + norm_back(upstream, xhat, rstd, gain_ref[...])
    branch = grad.astype(BF16)
    grad_ref[...] = grad
    branch_ref[...] = branch
    sums_ref[0:1] = jnp.sum(upstream * xhat, axis=0, keepdims=True)
    sums_ref[1:2] = jnp.sum(upstream, axis=0, keepdims=True)
    sums_ref[2:3] = jnp.sum(branch.astype(F32), axis=0, keepdims=True)
    sums_ref[3:4] = jnp.sum(top, axis=0, keepdims=True)


def norm_two_back(parts, after, top, at, gain):
    sums = struct((4, after.shape[1]), F32)
    return pl.pallas_call(
        partial(norm_two_back_kernel, len(parts)),
        grid=(1,),
        in_specs=[top_rows(after.shape)] * (len(parts) + 1)
        + [row_block(after.shape, at), whole(gain)],
        out_specs=[top_rows(after.shape)] * 2 + [whole(sums)],
        out_shape=[struct(after.shape, F32), struct(after.shape, BF16), sums],
        compiler_params=params(60),
        cost_estimate=cost(4),
        name="norm_two_back",
    )(*parts, after, top, gain)


def norm_one_back_kernel(count, *refs):
    parts = refs[:count]
    x_ref, valid_ref, grad_ref, gain_ref, out_ref, sums_ref = refs[count:]
    rows = x_ref.shape[0]
    upstream = total(parts, rows) * valid_ref[...]
    xhat, rstd = norm_parts(x_ref[...].astype(F32))
    out_ref[...] = (grad_ref[...] + norm_back(upstream, xhat, rstd, gain_ref[...])).astype(BF16)
    sums_ref[0:1] = jnp.sum(upstream * xhat, axis=0, keepdims=True)
    sums_ref[1:2] = jnp.sum(upstream, axis=0, keepdims=True)


def norm_one_back(parts, x, valid, at, grad, gain):
    shape = grad.shape
    sums = struct((2, shape[1]), F32)
    return pl.pallas_call(
        partial(norm_one_back_kernel, len(parts)),
        grid=(1,),
        in_specs=[top_rows(shape)] * len(parts)
        + [row_block(shape, at), row_block((shape[0], 1), at), top_rows(shape), whole(gain)],
        out_specs=[top_rows(shape), whole(sums)],
        out_shape=[struct(shape, BF16), sums],
        compiler_params=params(60),
        cost_estimate=cost(3.5),
        name="norm_one_back",
    )(*parts, x, valid, grad, gain)


def qkv_kernel(count, cols, offsets, *refs):
    pieces = refs[:count]
    x_ref, bias_ref, q_ref, k_ref, v_ref, w_ref, buffer, sems = refs[count:]
    wide = q_ref.shape[1]

    @pl.when(pl.program_id(0) == 0)
    def _():
        assemble(offsets, pieces, buffer, sems)
        for slot in range(4):
            base = slot * wide
            w_ref[:, base : base + cols] = buffer[:, slot * cols : (slot + 1) * cols]
            if wide > cols:
                w_ref[:, base + cols : base + wide] = jnp.zeros(
                    (w_ref.shape[0], wide - cols), BF16
                )

    x = x_ref[...]
    for slot, ref in enumerate((q_ref, k_ref, v_ref)):
        span = slice(slot * wide, (slot + 1) * wide)
        ref[...] = (dot(x, w_ref[:, span]) + bias_ref[:, span]).astype(BF16)


def project(offsets, pieces, x, bias, cols, wide):
    rows, width = x.shape
    step = 2 * ROWS
    block = pl.BlockSpec((step, wide), lambda i, *_: (i, 0))
    return pl.pallas_call(
        partial(qkv_kernel, len(pieces), cols),
        grid_spec=pltpu.PrefetchScalarGridSpec(
            num_scalar_prefetch=1,
            grid=(rows // step,),
            in_specs=[ANY] * len(pieces)
            + [pl.BlockSpec((step, width), lambda i, *_: (i, 0)), whole(bias)],
            out_specs=[block, block, block, pl.BlockSpec((width, 4 * wide), lambda i, *_: (0, 0))],
            scratch_shapes=[
                pltpu.VMEM((width, 4 * cols), BF16),
                pltpu.SemaphoreType.DMA((len(pieces),)),
            ],
        ),
        out_shape=[struct((rows, wide), BF16)] * 3 + [struct((width, 4 * wide), BF16)],
        compiler_params=params(60),
        cost_estimate=cost(14),
        name="qkv",
    )(offsets, *pieces, x, bias)


def head_spans(heads, wide):
    spans = []
    for head in range(heads):
        first, last = head * HD, head * HD + HD
        low = first // 128 * 128
        high = min((last + 127) // 128 * 128, wide)
        spans.append((low, high, first, last))
    return spans


def lane_mask(span):
    low, high, first, last = span
    lane = lax.broadcasted_iota(jnp.int32, (1, high - low), 1) + low
    return jnp.where((lane >= first) & (lane < last), 1.0, 0.0).astype(BF16)


def shift_counts():
    token = lax.broadcasted_iota(jnp.int32, (ROWS, 128), 0)
    row = (token * 9363) >> 17
    col = token - row * WIN
    return jnp.maximum(WIN - 1 - row, 0), WIN - 1 - col


def shift_lanes(values, counts, back):
    for step in (1, 2, 4, 8):
        moved = pltpu.roll(values, step if back else 128 - step, 1)
        values = jnp.where((counts & step) != 0, moved, values)
    return values


def lane_kind():
    lane = lax.broadcasted_iota(jnp.int32, (ROWS, 128), 1) & 31
    return lane < WIN, (lane >= 16) & (lane < 16 + WIN), lane == 31


def split_two(values):
    high = values.astype(BF16)
    return high, (values - high.astype(F32)).astype(BF16)


def bias_operand(q, rel_high, rel_low, counts):
    table = (dot(q, rel_high) + dot(q, rel_low)) * (1.0 / SCALE)
    by_row = shift_lanes(table[:, :128], counts[0], False)
    by_col = shift_lanes(table[:, 128:], counts[1], False)
    is_row, is_col, is_last = lane_kind()
    packed = jnp.where(
        is_row, by_row, jnp.where(is_col, by_col, jnp.where(is_last, 1.0, 0.0))
    )
    high, low = split_two(packed)
    return jnp.concatenate([high, low], axis=1)


def add_lanes(parts, values, span):
    low, high = span[0], span[1]
    for index in range(low // 128, high // 128):
        piece = values[:, index * 128 - low : index * 128 - low + 128]
        parts[index] = piece if parts[index] is None else parts[index] + piece


def attend_kernel(heads, split, q_ref, k_ref, v_ref, rh_ref, rl_ref, mark_ref, w_ref, *outs):
    mixed_ref, shares_ref = outs[:2]
    q, k, v = q_ref[...], k_ref[...], v_ref[...]
    wide = q.shape[1]
    bias = bias_operand(q, rh_ref[...], rl_ref[...], shift_counts())
    parts = [None] * (wide // 128)
    for head, span in enumerate(head_spans(heads, wide)):
        mask = lane_mask(span)
        cut = slice(span[0], span[1])
        scores = dot_nt(
            jnp.concatenate([q[:, cut], bias], axis=1),
            jnp.concatenate([k[:, cut] * mask, mark_ref[head]], axis=1),
        )
        top = jnp.max(scores, axis=-1, keepdims=True)
        shifted = jnp.exp(SCALE * (scores - top))
        norm = jnp.sum(shifted, axis=-1, keepdims=True)
        shares = (shifted * (1.0 / norm)).astype(BF16)
        shares_ref[:, head * 256 : head * 256 + ROWS] = shares
        add_lanes(parts, dot(shares, v[:, cut] * mask), span)
    mixed = jnp.concatenate(parts, axis=1).astype(BF16)
    cols = heads * HD
    mixed_ref[...] = mixed[:, :cols]
    branch = dot_nt(mixed, w_ref[...]).astype(BF16)
    if split:
        keep_ref, send_ref = outs[2:]
        step = pl.program_id(0)

        @pl.when(step < split)
        def _():
            send_ref[...] = branch

        @pl.when(step >= split)
        def _():
            keep_ref[...] = branch
    else:
        outs[2][...] = branch


def split_specs(windows, split, width):
    rows = ROWS * (windows - split)
    if not split:
        return [pl.BlockSpec((ROWS, width), lambda i: (i, 0))], [struct((rows, width), BF16)]
    return (
        [
            pl.BlockSpec((ROWS, width), lambda i: (jnp.maximum(i - split, 0), 0)),
            pl.BlockSpec((ROWS, width), lambda i: (jnp.minimum(i, split - 1), 0)),
        ],
        [struct((rows, width), BF16), struct((ROWS * split, width), BF16)],
    )


def attend(heads, part, windows, split, q, k, v, rel_high, rel_low, marks, weights):
    wide = q.shape[1]
    width = weights.shape[0]

    def place(i):
        return (i + split) % windows if split else i

    block = pl.BlockSpec((ROWS, wide), lambda i: (part * windows + place(i), 0))
    specs, shapes = split_specs(windows, split, width)
    return pl.pallas_call(
        partial(attend_kernel, heads, split),
        grid=(windows,),
        in_specs=[
            block,
            block,
            block,
            whole(rel_high),
            whole(rel_low),
            whole(marks),
            pl.BlockSpec((width, wide), lambda i: (0, 3)),
        ],
        out_specs=[
            pl.BlockSpec((ROWS, heads * HD), lambda i: (place(i), 0)),
            pl.BlockSpec((ROWS, heads * 256), lambda i: (place(i), 0)),
        ]
        + specs,
        out_shape=[
            struct((windows * ROWS, heads * HD), BF16),
            struct((windows * ROWS, heads * 256), BF16),
        ]
        + shapes,
        compiler_params=params(60),
        cost_estimate=cost(13.5),
        name="attend",
    )(q, k, v, rel_high, rel_low, marks, weights)


def attend_back_kernel(heads, windows, split, count, *refs):
    pieces = refs[:count]
    q_ref, k_ref, v_ref, shares_ref, rh_ref, mark_ref, w_ref = refs[count : count + 7]
    grads_ref, branch_ref, rel_ref, sum_ref = refs[count + 7 : count + 11]
    outs = refs[count + 11 :]
    step = pl.program_id(0)

    @pl.when(step == 0)
    def _():
        start = 0
        for piece in pieces:
            branch_ref[start : start + piece.shape[0]] = piece[...]
            start += piece.shape[0]
        rel_ref[...] = jnp.zeros(rel_ref.shape, F32)
        sum_ref[...] = jnp.zeros(sum_ref.shape, F32)

    place = lax.rem(step + split, windows) if split else step
    q, k, v = q_ref[...], k_ref[...], v_ref[...]
    wide = q.shape[1]
    top = branch_ref[pl.ds(pl.multiple_of(place * ROWS, 16), ROWS), :]
    grad_mixed = dot(top, w_ref[:, 3 * wide :]).astype(BF16)
    grad_q, grad_k, grad_v = ([None] * (wide // 128) for _ in range(3))
    grad_bias = None
    for head, span in enumerate(head_spans(heads, wide)):
        mask = lane_mask(span)
        cut = slice(span[0], span[1])
        size = span[1] - span[0]
        upper = grad_mixed[:, cut]
        rounded = shares_ref[:, head * 256 : head * 256 + ROWS]
        shares = rounded.astype(F32)
        weighted = shares * dot_nt(upper, v[:, cut] * mask)
        inner = jnp.sum(weighted, axis=-1, keepdims=True)
        grad_scores = (weighted - shares * inner).astype(BF16)
        add_lanes(grad_v, dot_tn(rounded, upper * mask), span)
        both = dot(
            grad_scores,
            jnp.concatenate([k[:, cut] * mask, mark_ref[head][:, :128]], axis=1),
        )
        add_lanes(grad_q, both[:, :size], span)
        part = both[:, size:]
        grad_bias = part if grad_bias is None else grad_bias + part
        add_lanes(grad_k, dot_tn(grad_scores, q[:, cut] * mask), span)
    counts = shift_counts()
    is_row, is_col, _ = lane_kind()
    by_row = shift_lanes(jnp.where(is_row, grad_bias, 0.0), counts[0], True)
    by_col = shift_lanes(jnp.where(is_col, grad_bias, 0.0), counts[1], True)
    packed = jnp.concatenate([by_row, by_col], axis=1).astype(BF16)
    extra = dot_nt(packed, rh_ref[...])
    rel_ref[...] += dot_tn(packed, q)
    grad_q = (SCALE * jnp.concatenate(grad_q, axis=1) + extra).astype(BF16)
    grad_k = (SCALE * jnp.concatenate(grad_k, axis=1)).astype(BF16)
    grad_v = jnp.concatenate(grad_v, axis=1).astype(BF16)
    cols = heads * HD
    for slot, grad in enumerate((grad_q, grad_k, grad_v)):
        cut = slice(slot * wide, (slot + 1) * wide)
        grads_ref[:, slot * cols : (slot + 1) * cols] = grad[:, :cols]
        sum_ref[:, cut] += jnp.sum(grad.astype(F32), axis=0, keepdims=True)
    partial_sum = dot_nt(
        jnp.concatenate([grad_q, grad_k, grad_v], axis=1), w_ref[:, : 3 * wide]
    )
    result = partial_sum.astype(BF16)
    if split:
        keep_ref, send_ref = outs

        @pl.when(step < split)
        def _():
            send_ref[...] = result

        @pl.when(step >= split)
        def _():
            keep_ref[...] = result
    else:
        outs[0][...] = result


def attend_back(
    heads, part, windows, split, pieces, q, k, v, shares, rel_high, marks, weights
):
    wide = q.shape[1]
    width = weights.shape[0]

    def place(i):
        return (i + split) % windows if split else i

    block = pl.BlockSpec((ROWS, wide), lambda i: (part * windows + place(i), 0))
    specs, shapes = split_specs(windows, split, width)
    rows = windows * ROWS
    branch = struct((rows, width), BF16)
    rel = struct((256, wide), F32)
    sums = struct((1, 3 * wide), F32)
    return pl.pallas_call(
        partial(attend_back_kernel, heads, windows, split, len(pieces)),
        grid=(windows,),
        in_specs=[whole(piece) for piece in pieces]
        + [
            block,
            block,
            block,
            pl.BlockSpec((ROWS, heads * 256), lambda i: (place(i), 0)),
            whole(rel_high),
            whole(marks),
            whole(weights),
        ],
        out_specs=[
            pl.BlockSpec((ROWS, 3 * heads * HD), lambda i: (place(i), 0)),
            whole(branch),
            whole(rel),
            whole(sums),
        ]
        + specs,
        out_shape=[struct((rows, 3 * heads * HD), BF16), branch, rel, sums] + shapes,
        compiler_params=params(60),
        cost_estimate=cost(18.5),
        name="attend_back",
    )(*pieces, q, k, v, shares, rel_high, marks, weights)


def mlp_kernel(count, weights, split, offsets, *refs):
    pieces = refs[:count]
    weight_pieces = refs[count : count + weights]
    refs = refs[count + weights :]
    top_ref, bias_ref, after_ref, down_bias_ref = refs[:4]
    active_ref, hidden_ref, normed_ref, sum_ref = refs[4:8]
    backs, outs = (refs[8:10], refs[10:12]) if split else (refs[8:9], refs[9:10])
    up, down, sems = refs[-3:]
    step = pl.program_id(0)
    block = top_ref.shape[0]
    units = up.shape[1]
    copies = []
    for half, target in enumerate((down, up)):
        copies.append([])
        for index, piece in enumerate(weight_pieces):
            rows = piece.shape[0]
            start = pl.multiple_of(offsets[index], 16)
            copies[half].append(
                pltpu.make_async_copy(
                    piece.at[:, half * units : (half + 1) * units],
                    target.at[pl.ds(start, rows)],
                    sems.at[half, index],
                )
            )

    @pl.when(step == 0)
    def _():
        for copy in copies[1] + copies[0]:
            copy.start()
        start = 0
        for piece in pieces:
            normed_ref[start : start + piece.shape[0]] = piece[...]
            start += piece.shape[0]
        sum_ref[...] = jnp.zeros(sum_ref.shape, F32)
        for copy in copies[1]:
            copy.wait()

    place = 1 - step if split else step
    normed = normed_ref[pl.ds(pl.multiple_of(place * block, 16), block), :]
    hidden = dot(normed, up[...]) + bias_ref[...]

    @pl.when(step == 0)
    def _():
        for copy in copies[0]:
            copy.wait()

    half = 0.5 * (1.0 + lax.erf(hidden * (0.5**0.5)))
    slope = half + hidden * jnp.exp(-0.5 * hidden * hidden) * float((2.0 * np.pi) ** -0.5)
    active = (hidden * half).astype(BF16)
    active_ref[...] = active
    grad = (dot(top_ref[...], down[...]) * slope).astype(BF16)
    hidden_ref[...] = grad
    sum_ref[...] += jnp.sum(grad.astype(F32), axis=0, keepdims=True)
    back = dot_nt(grad, up[...]).astype(BF16)
    result = dot_nt(active, down[...])
    if split:

        @pl.when(step == 0)
        def _():
            backs[1][...] = back
            outs[1][...] = result.astype(BF16)

        @pl.when(step == 1)
        def _():
            backs[0][...] = back
            own = result[:ROWS] + after_ref[...] + down_bias_ref[...]
            outs[0][:ROWS] = own.astype(BF16)
            outs[0][ROWS:] = result[ROWS:].astype(BF16)
    else:
        backs[0][...] = back
        outs[0][...] = result.astype(BF16)


def mlp(offsets, pieces, weight_pieces, top, part, bias, after, down_bias, split):
    rows = sum(piece.shape[0] for piece in pieces)
    width = pieces[0].shape[1]
    units = weight_pieces[0].shape[1] // 2
    block = 2 * ROWS
    blocks = rows // block
    normed = struct((rows, width), BF16)
    sums = struct((1, units), F32)

    def place(i):
        return 1 - i if split else i

    wide = pl.BlockSpec((block, units), lambda i, *_: (place(i), 0))
    back = struct((block, width), BF16)
    if split:
        back_specs, back_shapes = [whole(back)] * 2, [back] * 2
    else:
        back_specs = [pl.BlockSpec((block, width), lambda i, *_: (i, 0))]
        back_shapes = [normed]
    return pl.pallas_call(
        partial(mlp_kernel, len(pieces), len(weight_pieces), split),
        grid_spec=pltpu.PrefetchScalarGridSpec(
            num_scalar_prefetch=1,
            grid=(blocks,),
            in_specs=[whole(piece) for piece in pieces]
            + [ANY] * len(weight_pieces)
            + [
                pl.BlockSpec((block, width), lambda i, *_: (part * blocks + place(i), 0)),
                whole(bias),
                whole(after),
                whole(down_bias),
            ],
            out_specs=[wide, wide, whole(normed), whole(sums)] + back_specs * 2,
            scratch_shapes=[
                pltpu.VMEM((width, units), BF16),
                pltpu.VMEM((width, units), BF16),
                pltpu.SemaphoreType.DMA((2, len(weight_pieces))),
            ],
        ),
        out_shape=[struct((rows, units), BF16)] * 2 + [normed, sums] + back_shapes * 2,
        compiler_params=params(60),
        cost_estimate=cost(21),
        name="mlp",
    )(offsets, *pieces, *weight_pieces, top, bias, after, down_bias)


def weight_grad_kernel(sizes, share, targets, *refs):
    count = 2 * sum(sizes)
    operands = refs[:count]
    outs, (result, sems) = refs[count:-2], refs[-2:]
    pair_ref = outs[-1] if len(outs) != 2 else None
    send_ref, keep_ref = outs[:2] if len(outs) > 1 else (None, None)
    lead = send_ref.shape[2] if len(outs) > 1 else 0
    step = pl.program_id(0)
    steps = pl.num_programs(0)
    chunk = operands[0].shape[1]
    pieces = chunk // share
    base = pl.multiple_of(step * chunk, 16)
    at, first = 0, 0
    for size in sizes:
        value = None
        for _ in range(size):
            left, right = operands[at], operands[at + 1]
            at += 2
            term = dot_tn(left[...], right[...])
            value = term if value is None else value + term
        span = value.shape[1]
        result[pl.ds(base, chunk), first : first + span] = value.astype(BF16)
        first += span

    def copy(index, out, slot):
        return pltpu.make_async_copy(
            result.at[pl.ds(pl.multiple_of(index * share, 16), share), pl.ds(0, lead)],
            out.at[slot],
            sems.at[0, index],
        )

    def pair_copy(index, slot):
        return pltpu.make_async_copy(
            result.at[
                pl.ds(pl.multiple_of(index * share, 16), share),
                pl.ds(lead, result.shape[1] - lead),
            ],
            pair_ref.at[lax.rem(slot, 4), 1 - slot // 4],
            sems.at[1, index],
        )

    for piece in range(pieces):
        index = step * pieces + piece
        slot = targets[index]

        if lead:

            @pl.when(slot < 4)
            def _():
                copy(index, send_ref, slot).start()

            @pl.when(slot >= 4)
            def _():
                copy(index, keep_ref, slot - 4).start()

        if pair_ref is not None:
            pair_copy(index, slot).start()

    @pl.when(step == steps - 1)
    def _():
        for index in range(8):
            if lead:
                copy(index, send_ref, 0).wait()
            if pair_ref is not None:
                pair_copy(index, 0).wait()


def plain_grad_kernel(sizes, *refs):
    count = 2 * sum(sizes)
    operands, out_ref = refs[:count], refs[count]
    at, first = 0, 0
    for size in sizes:
        value = None
        for _ in range(size):
            left, right = operands[at], operands[at + 1]
            at += 2
            term = dot_tn(left[...], right[...])
            value = term if value is None else value + term
        span = value.shape[1]
        out_ref[:, first : first + span] = value.astype(BF16)
        first += span


def weight_grad(targets, groups, share, lead=None):
    operands, specs = [], []
    chunk = 640 if targets is not None else 256
    total_cols = 0
    for group in groups:
        for left, at, rows, right in group:
            operands += [left, right]
            specs.append(pl.BlockSpec((rows, chunk), lambda i, *_, at=at: (at, i)))
            specs.append(whole(right))
        total_cols += group[0][3].shape[1]
    width = operands[0].shape[1]
    sizes = [len(group) for group in groups]
    if targets is None:
        return [
            pl.pallas_call(
                partial(plain_grad_kernel, sizes),
                grid=(width // chunk,),
                in_specs=specs,
                out_specs=pl.BlockSpec((chunk, total_cols), lambda i: (i, 0)),
                out_shape=struct((width, total_cols), BF16),
                compiler_params=params(60),
                cost_estimate=cost(13),
        name="weight_grad",
            )(*operands)
        ]
    lead = total_cols if lead is None else lead
    shapes = [struct((4, share, lead), BF16)] * 2 if lead else []
    if lead < total_cols:
        shapes.append(struct((4, 2, share, total_cols - lead), BF16))
    return pl.pallas_call(
        partial(weight_grad_kernel, sizes, share),
        grid_spec=pltpu.PrefetchScalarGridSpec(
            num_scalar_prefetch=1,
            grid=(width // chunk,),
            in_specs=specs,
            out_specs=[ANY] * len(shapes),
            scratch_shapes=[
                pltpu.VMEM((width, total_cols), BF16),
                pltpu.SemaphoreType.DMA((2, 8)),
            ],
        ),
        out_shape=shapes,
        compiler_params=params(60),
        cost_estimate=cost(13),
        name="weight_grad",
    )(targets, *operands)


def place_kernel(part, order, *refs):
    pieces, out_ref, buffer, sem = refs[:4], refs[-3], refs[-2], refs[-1]
    rows = buffer.shape[0]
    for me in range(4):

        @pl.when(order[0] == me)
        def _(me=me):
            for index, step in enumerate((0, 2, 1, 3)):
                start = (me ^ step) * WTOK
                buffer[start : start + WTOK] = pieces[index][:WTOK].astype(F32)

    copy = pltpu.make_async_copy(buffer, out_ref.at[pl.ds(part * rows, rows)], sem)
    copy.start()
    copy.wait()


def place_windows(part, order, pieces, rows, held):
    width = pieces[0].shape[1]
    operands = list(pieces) + ([] if held is None else [held])
    return pl.pallas_call(
        partial(place_kernel, part),
        grid_spec=pltpu.PrefetchScalarGridSpec(
            num_scalar_prefetch=1,
            grid=(1,),
            in_specs=[whole(piece) for piece in pieces] + [ANY] * (len(operands) - 4),
            out_specs=ANY,
            scratch_shapes=[pltpu.VMEM((4 * WTOK, width), F32), pltpu.SemaphoreType.DMA(())],
        ),
        out_shape=struct((rows, width), F32),
        input_output_aliases={} if held is None else {5: 0},
        compiler_params=params(60),
        cost_estimate=cost(4.5),
        name="place_windows",
    )(order, *operands)


def output_kernel(part, order, places, lives, *refs):
    pieces, out_ref, buffer, rounded, sem = refs[:4], refs[-4], refs[-3], refs[-2], refs[-1]
    rows = buffer.shape[0]
    for me in range(4):

        @pl.when(order[0] == me)
        def _(me=me):
            for index, step in enumerate((0, 2, 1, 3)):
                slot = me ^ step
                valid = token_valid(places[4 * part + slot], lives[4 * part + slot])
                value = pieces[index][:WTOK].astype(F32) * valid
                buffer[slot * WTOK : (slot + 1) * WTOK] = value

    rounded[...] = buffer[...].astype(BF16)
    copy = pltpu.make_async_copy(rounded, out_ref.at[pl.ds(part * rows, rows)], sem)
    copy.start()
    copy.wait()


def write_output(part, order, places, lives, pieces, rows, held):
    width = pieces[0].shape[1]
    operands = list(pieces) + ([] if held is None else [held])
    shape = (4 * WTOK, width)
    return pl.pallas_call(
        partial(output_kernel, part),
        grid_spec=pltpu.PrefetchScalarGridSpec(
            num_scalar_prefetch=3,
            grid=(1,),
            in_specs=[whole(piece) for piece in pieces] + [ANY] * (len(operands) - 4),
            out_specs=ANY,
            scratch_shapes=[
                pltpu.VMEM(shape, F32),
                pltpu.VMEM(shape, BF16),
                pltpu.SemaphoreType.DMA(()),
            ],
        ),
        out_shape=struct((rows, width), BF16),
        input_output_aliases={} if held is None else {7: 0},
        compiler_params=params(60),
        cost_estimate=cost(5),
        name="write_output",
    )(order, places, lives, *operands)


def key_marks(heads):
    marks = np.zeros((heads, ROWS, 256), np.float32)
    for head in range(heads):
        for token in range(WTOK):
            for half in (0, 128):
                marks[head, token, half + head * 32 + token // WIN] = 1.0
                marks[head, token, half + head * 32 + 16 + token % WIN] = 1.0
        marks[head, WTOK:, head * 32 + 31] = -1e30
    return marks.astype(BF16)


def rel_operand(rel_height, rel_width, heads, wide):
    high = rel_height[::-1].T
    flat = rel_width[::-1].T
    lanes = jnp.zeros((wide, 256), F32)

    def spread(block, row, lane):
        below = wide - row - HD
        return jnp.pad(block, ((row, below), (lane, 256 - lane - block.shape[1])))

    for head in range(heads):
        first = head * 32 + 16
        fit = min(RELN, 128 - first)
        lanes = lanes + spread(high, head * HD, head * 32)
        lanes = lanes + spread(flat[:, :fit], head * HD, 128 + first)
        if fit < RELN:
            lanes = lanes + spread(flat[:, fit:], head * HD, 128)
    return split_two(lanes)


def rel_result(sums, heads):
    high = jnp.zeros((RELN, HD), F32)
    flat = jnp.zeros((RELN, HD), F32)
    for head in range(heads):
        cols = sums[:, head * HD : head * HD + HD]
        high = high + cols[head * 32 : head * 32 + RELN]
        rolled = jnp.concatenate([cols[128:], cols[128:]], axis=0)
        flat = flat + rolled[head * 32 + 16 : head * 32 + 16 + RELN]
    return high[::-1], flat[::-1]


def add_all(values):
    out = values[0]
    for value in values[1:]:
        out = out + value
    return out


def tie(value, *others):
    return lax.optimization_barrier((value,) + others)[0]


def sync(*values):
    return lax.optimization_barrier(values)


def body(
    block_input,
    window_place,
    slot_live,
    norm_one_gain,
    norm_one_shift,
    qkv_weight,
    qv_bias,
    proj_weight,
    proj_bias,
    norm_two_gain,
    norm_two_shift,
    up_weight,
    up_bias,
    down_weight,
    down_bias,
    rel_height,
    rel_width,
    cotangent,
):
    data_parts = lax.axis_size("dp")
    model_parts = lax.axis_size("mp")
    data_index = lax.axis_index("dp")
    model_index = lax.axis_index("mp")
    width = block_input.shape[1]
    share = qkv_weight.shape[1]
    cols = qkv_weight.shape[2]
    heads = cols // HD
    wide = (cols + 127) // 128 * 128
    units = up_weight.shape[1]
    slots = window_place.shape[0]
    rings = data_parts == 8 and model_parts == 4 and slots == 8
    padded = (slots + model_parts - 1) // model_parts * model_parts
    halves = padded // 4 if rings else 1
    windows = padded // halves
    split = 2 if rings else 0
    part_rows = windows * ROWS
    own_rows = part_rows // model_parts

    if rings:
        depth, side = data_index // 2, data_index % 2
        y_bit, core_bit = model_index // 2, model_index % 2
        over_x = partial(lax.ppermute, axis_name="dp", perm=[(d, d ^ 1) for d in range(8)])
        over_z = partial(lax.ppermute, axis_name="dp", perm=[(d, (d + 2) % 8) for d in range(8)])
        over_y = partial(lax.ppermute, axis_name="mp", perm=[(m, m ^ 2) for m in range(4)])
        over_core = partial(lax.ppermute, axis_name="mp", perm=[(m, m ^ 1) for m in range(4)])

    def gather(piece):
        return [lax.all_gather(piece, "dp", axis=0, tiled=True)]

    if rings:
        offsets = []
        for back in range(4):
            behind = (depth - back) % 4
            offsets += [share * (2 * behind + side), share * (2 * behind + 1 - side)]
        offsets = jnp.stack(offsets).astype(jnp.int32)
    else:
        offsets = jnp.zeros((1,), jnp.int32)

    def scatter(parts):
        return lax.psum_scatter(parts[0], "dp", scatter_dimension=0, tiled=True).astype(F32)

    def joined(*values):
        total_value = values[0].astype(F32)
        for value in values[1:]:
            total_value = total_value + value.astype(F32)
        return total_value.astype(BF16)

    def rows_scatter(parts):
        return [lax.psum_scatter(parts[0], "mp", scatter_dimension=0, tiled=True)]

    def rows_gather(own):
        return [lax.all_gather(own, "mp", axis=0, tiled=True)]

    def sum_all(vector):
        if not rings:
            return lax.psum(vector, ("dp", "mp"))
        for step in (1, 2):
            vector = vector + lax.ppermute(
                vector, "mp", [(m, m ^ step) for m in range(4)]
            )
        for step in (2, 4, 1):
            vector = vector + lax.ppermute(
                vector, "dp", [(d, d ^ step) for d in range(8)]
            )
        return vector

    def own_slice(array):
        rows = array.shape[0] // model_parts
        return lax.dynamic_slice_in_dim(array, model_index * rows, rows, 0)

    first_piece = jnp.concatenate([qkv_weight[0], qkv_weight[1], qkv_weight[2], proj_weight.T], 1)
    other_piece = jnp.concatenate([down_weight.T, up_weight], 1)

    row = lambda v: v.reshape(1, -1)
    gain_one, shift_one = row(norm_one_gain), row(norm_one_shift)
    gain_two, shift_two = row(norm_two_gain), row(norm_two_shift)
    bias_local = lax.dynamic_slice_in_dim(qv_bias, model_index * cols, cols, 1)
    bias_local = jnp.pad(bias_local, [(0, 0), (0, wide - cols)])
    bias_qkv = row(jnp.stack([bias_local[0], jnp.zeros_like(bias_local[0]), bias_local[1]]))
    up_local = row(lax.dynamic_slice_in_dim(up_bias, model_index * units, units, 0))
    rel_high, rel_low = rel_operand(rel_height, rel_width, heads, wide)
    marks = jnp.asarray(key_marks(heads))

    steps = (0, 2, 1, 3)
    if rings:
        local = [model_index ^ step for step in steps]
        places = [4 * part + spot for part in range(halves) for spot in local]
    else:
        local = [jnp.int32(spot) for spot in range(windows)]
        places = local
    local = jnp.stack(local).astype(jnp.int32)
    places = jnp.stack(places).astype(jnp.int32)
    if rings:
        targets = []
        for d in range(8):
            ahead = (d // 2 - depth) % 4
            targets.append(ahead + jnp.where(d % 2 == side, 4, 0))
        targets = jnp.stack(targets).astype(jnp.int32)
    else:
        targets = None

    def by_window(array):
        array = array.reshape((slots, WTOK) + array.shape[1:])
        return jnp.pad(array, [(0, padded - slots)] + [(0, 0)] * (array.ndim - 1))

    places_all = jnp.pad(window_place, (0, padded - slots))
    lives_all = jnp.pad(slot_live, (0, padded - slots))
    blocks = [(part, part_rows) for part in range(halves)]

    def start(x):
        return prepare(places, places_all, lives_all, x, gain_one, shift_one)

    def masked(top):
        return mask_rows(places, places_all, lives_all, top)

    def attention(part, q, k, v, weights):
        return attend(heads, part, windows, split, q, k, v, rel_high, rel_low, marks, weights)

    def attention_back(part, pieces, q, k, v, shares, weights):
        return attend_back(
            heads, part, windows, split, pieces, q, k, v, shares, rel_high, marks, weights
        )

    def down_groups(mlps):
        return [[(grad_top, *blocks[i], mlps[i][0]) for i in range(halves)]]

    def up_groups(mlps):
        return [[(mlps[i][2], 0, part_rows, mlps[i][1]) for i in range(halves)]]

    def first_groups(backs, attended):
        return [
            [(normed, *blocks[i], backs[i][0]) for i in range(halves)],
            [(backs[i][1], 0, part_rows, attended[i][0]) for i in range(halves)],
        ]

    x_windows, top_windows = by_window(block_input), by_window(cotangent)
    if not rings:
        first_weights, other_weights = gather(first_piece), gather(other_piece)
        rows_in, normed, valid = start(x_windows)
        grad_top = masked(top_windows)
        own_in, own_top, own_valid = own_slice(rows_in), own_slice(grad_top), own_slice(valid)
        q, k, v, weights = project(offsets, first_weights, normed, bias_qkv, cols, wide)
        attended = [attention(0, q, k, v, weights)]
        after, normed_two = norm_two(
            rows_scatter(attended[0][2:]), own_in, 0, row(proj_bias), gain_two, shift_two
        )
        none = jnp.zeros((1, 128), F32)
        mlps = [
            mlp(
                offsets,
                rows_gather(normed_two),
                other_weights,
                grad_top,
                0,
                up_local,
                none,
                none,
                False,
            )
        ]
        grad_after, branch, sums = norm_two_back(
            rows_scatter(mlps[0][4:5]), after, own_top, 0, gain_two
        )
        sums_two = [sums]
        result = mlps[0][5]
        own = finish(rows_scatter([result]), after, own_valid, 0, row(down_bias))

        def unpad(array):
            array = array.reshape(padded, ROWS, width)[:slots, :WTOK]
            return array.reshape(slots * WTOK, width)

        block_output = unpad(rows_gather(own)[0])
        down_grad = scatter(weight_grad(None, down_groups(mlps), share))
        up_grad = scatter(weight_grad(None, up_groups(mlps), share))
        backs = [attention_back(0, rows_gather(branch), q, k, v, attended[0][1], weights)]
        own, sums = norm_one_back(
            rows_scatter(backs[0][4:]), own_in, own_valid, 0, grad_after, gain_one
        )
        sums_one = [sums]
        input_grad = unpad(rows_gather(own)[0]).astype(F32)
        first_grad = scatter(weight_grad(None, first_groups(backs, attended), share))
    else:
        def second_norm(part, keep, came, crossed):
            return norm_two(
                [keep, came, crossed], rows_in, 4 * part, row(proj_bias), gain_two, shift_two
            )

        def second_back(part, after, keep, came, crossed):
            return norm_two_back([keep, came, crossed], after, grad_top, 4 * part, gain_two)

        def first_back(part, grad_after, keep, came, crossed):
            return norm_one_back(
                [keep, came, crossed], rows_in, valid, 4 * part, grad_after, gain_one
            )

        def spread(own, across):
            return [own, across, over_core(own), over_core(across)]

        def to_core(keep, send):
            came = over_core(send)
            return came, joined(keep[ROWS:], came[ROWS:])

        bias_row = row(down_bias)

        z1, x0 = over_z(first_piece), over_x(first_piece)
        z1, x0, x_windows, top_windows, other_piece, rel_high, rel_low = sync(
            z1, x0, x_windows, top_windows, other_piece, rel_high, rel_low
        )
        z2, x1 = over_z(z1), over_x(z1)
        rows_in, normed, valid = start(x_windows)
        z2, x1, normed, top_windows = sync(z2, x1, normed, top_windows)
        z3, x2 = over_z(z2), over_x(z2)
        grad_top = masked(top_windows)
        z3, x2, normed, grad_top, other_piece = sync(z3, x2, normed, grad_top, other_piece)
        x3 = over_x(z3)
        oz1 = over_z(other_piece)
        x3, normed, other_late = sync(x3, normed, other_piece)
        ox0 = over_x(other_late)
        first_weights = [first_piece, x0, z1, x1, z2, x2, z3, x3]
        q, k, v, weights = project(offsets, first_weights, normed, bias_qkv, cols, wide)
        oz1, ox0, q = sync(oz1, ox0, q)

        oz2, ox1 = over_z(oz1), over_x(oz1)
        a0 = attention(0, q, k, v, weights)
        oz2, ox1, a0 = sync(oz2, ox1, a0)
        oz3, ox2 = over_z(oz2), over_x(oz2)
        came0, passed0 = to_core(a0[2], a0[3])
        crossed0 = over_y(passed0)
        a1 = attention(1, tie(q, passed0), k, v, weights)
        oz3, ox2, crossed0, a1 = sync(oz3, ox2, crossed0, a1)
        ox3 = over_x(oz3)
        after0, own0 = second_norm(0, a0[2], came0, crossed0)
        across0 = over_y(own0)
        came1, passed1 = to_core(a1[2], a1[3])
        crossed1 = over_y(tie(passed1, own0))
        attended = [a0, a1]
        ox3, across0, crossed1 = sync(ox3, across0, crossed1)
        other_weights = [other_piece, ox0, oz1, ox1, oz2, ox2, oz3, ox3]
        after1, own1 = second_norm(1, a1[2], came1, crossed1)
        across1 = over_y(own1)
        pieces0 = spread(own0, across0)
        pieces0[0] = tie(pieces0[0], own1)

        m0 = mlp(offsets, pieces0, other_weights, grad_top, 0, up_local, after0, bias_row, True)
        across1, m0 = sync(across1, m0)
        pieces1 = spread(own1, across1)
        came0, passed0 = to_core(m0[4], m0[5])
        crossed0 = over_y(passed0)
        pieces1[0] = tie(pieces1[0], passed0)
        m1 = mlp(offsets, pieces1, other_weights, grad_top, 1, up_local, after1, bias_row, True)
        crossed0, m1 = sync(crossed0, m1)
        mlps = [m0, m1]
        grad_after0, branch0, sums0 = second_back(0, after0, m0[4], came0, crossed0)
        came1, passed1 = to_core(m1[4], m1[5])
        across0 = over_y(branch0)
        crossed1 = over_y(tie(passed1, branch0))
        left = tie(m0, branch0, passed1)
        (down_pairs,) = weight_grad(targets, down_groups([left, m1]), share, 0)
        down_pairs = sync(down_pairs)[0]
        down_held = over_z(down_pairs[3])
        up_send, up_keep = weight_grad(
            targets, up_groups([tie(m0, down_pairs), m1]), share
        )
        across0, crossed1, down_held, up_send, up_keep = sync(
            across0, crossed1, down_held, up_send, up_keep
        )

        grad_after1, branch1, sums1 = second_back(1, after1, m1[4], came1, crossed1)
        sums_two = [sums0, sums1]
        across1 = over_y(branch1)
        branches0 = spread(branch0, across0)
        out_came0, out_passed0 = to_core(m0[6], tie(m0[7], branch1))
        out_crossed0 = over_y(out_passed0)
        down_held = over_z(joined(down_pairs[2], down_held))
        up_came_high = over_x(up_send[2:])
        branches0[0] = tie(branches0[0], branch1, out_passed0)
        b0 = attention_back(0, branches0, q, k, v, a0[1], weights)
        across1, out_crossed0, down_held, up_came_high, b0 = sync(
            across1, out_crossed0, down_held, up_came_high, b0
        )
        branches1 = spread(branch1, across1)
        came0, passed0 = to_core(b0[4], b0[5])
        crossed0 = over_y(passed0)
        out_came1, out_passed1 = to_core(m1[6], tie(m1[7], passed0))
        out_crossed1 = over_y(out_passed1)
        down_held = over_z(joined(down_pairs[1], down_held))
        up_came_low = over_x(up_send[:2])
        branches1[0] = tie(branches1[0], out_passed1)
        b1 = attention_back(1, branches1, q, k, v, a1[1], weights)
        crossed0, out_crossed1, down_held, up_came_low, b1 = sync(
            crossed0, out_crossed1, down_held, up_came_low, b1
        )
        backs = [b0, b1]
        own0, one0 = first_back(0, grad_after0, b0[4], came0, crossed0)
        in_across0 = over_y(own0)
        came1, passed1 = to_core(b1[4], b1[5])
        crossed1 = over_y(tie(passed1, own0))
        down_last = joined(down_pairs[0], down_held)
        down_other = over_x(down_last[1])
        up_held = over_z(joined(up_keep[3], up_came_high[1]))
        left = tie(b0, own0, passed1, down_last)
        first_send, first_keep, first_pairs = weight_grad(
            targets, first_groups([left, b1], attended), share, 3 * cols // 128 * 128
        )
        in_across0, crossed1, down_other, up_held, first_send, first_keep, first_pairs = sync(
            in_across0, crossed1, down_other, up_held, first_send, first_keep, first_pairs
        )

        first_came = over_x(first_send)
        pair_held = over_z(first_pairs[3])
        own1, one1 = first_back(1, grad_after1, b1[4], came1, crossed1)
        sums_one = [one0, one1]
        in_across1 = over_y(own1)
        in_pieces0 = spread(own0, in_across0)
        up_held = over_z(joined(up_keep[2], up_came_high[0], up_held))
        pair_held = over_z(joined(first_pairs[2], pair_held))
        out_own0 = joined(m0[6][:ROWS], out_came0[:ROWS], out_crossed0)
        out_own1 = joined(m1[6][:ROWS], out_came1[:ROWS], out_crossed1)
        out_across0, out_across1 = over_y(tie(out_own0, own1)), over_y(tie(out_own1, own1))
        input_grad = place_windows(0, local, in_pieces0, slots * WTOK, None)
        in_across1, up_held, pair_held, first_came, input_grad = sync(
            in_across1, up_held, pair_held, first_came, input_grad
        )
        first_held = over_z(joined(first_keep[3], first_came[3]))
        pair_held = over_z(joined(first_pairs[1], pair_held))
        up_held = over_z(joined(up_keep[1], up_came_low[1], up_held))
        in_pieces1 = spread(own1, in_across1)
        input_grad = place_windows(1, local, in_pieces1, slots * WTOK, input_grad)
        first_held, pair_held, up_held, input_grad, out_across0, out_across1 = sync(
            first_held, pair_held, up_held, input_grad, out_across0, out_across1
        )
        first_held = over_z(joined(first_keep[2], first_came[2], first_held))
        pair_last = joined(first_pairs[0], pair_held)
        pair_other = over_x(pair_last[1])
        out_pieces0 = spread(out_own0, out_across0)
        block_output = write_output(
            0, local, places_all, lives_all, out_pieces0, slots * WTOK, None
        )
        first_held, pair_other, block_output = sync(first_held, pair_other, block_output)
        first_held = over_z(joined(first_keep[1], first_came[1], first_held))
        out_pieces1 = spread(out_own1, out_across1)
        block_output = write_output(
            1, local, places_all, lives_all, out_pieces1, slots * WTOK, block_output
        )

        def last(*values):
            out = values[0].astype(F32)
            for value in values[1:]:
                out = out + value.astype(F32)
            return out

        down_grad = last(down_pairs[0, 0], down_held[0], down_other)
        up_grad = last(up_keep[0], up_came_low[0], up_held)
        first_grad = jnp.concatenate(
            [
                last(first_keep[0], first_came[0], first_held),
                last(first_pairs[0, 0], pair_held[0], pair_other),
            ],
            axis=1,
        )

    two = add_all(sums_two)
    one = add_all(sums_one)
    qv_sums = add_all([item[3] for item in backs]).reshape(3, wide)[0::2, :cols]
    rel_sums = rel_result(add_all([item[2] for item in backs]), heads)
    up_sums = add_all([item[3] for item in mlps]).reshape(units)
    qv_full = lax.dynamic_update_slice_in_dim(
        jnp.zeros((2, width), F32), qv_sums, model_index * cols, 1
    )
    up_full = lax.dynamic_update_slice_in_dim(
        jnp.zeros(up_bias.shape, F32), up_sums, model_index * units, 0
    )

    def sum_bundle(arrays):
        sizes = [array.size for array in arrays]
        flat = jnp.concatenate([array.reshape(-1) for array in arrays])
        count = (flat.size + 1023) // 1024 * 1024
        flat = jnp.pad(flat, (0, count - flat.size)).reshape(-1, 128)
        flat = sum_all(flat).reshape(-1)
        outs, at = [], 0
        for array, size in zip(arrays, sizes):
            outs.append(flat[at : at + size].reshape(array.shape))
            at += size
        return outs

    two_sums, up_bias_grad, one_sums, qv_bias_grad, height_grad, width_grad = sum_bundle(
        [two, up_full, one, qv_full, rel_sums[0], rel_sums[1]]
    )
    qkv_grad = jnp.stack([first_grad[:, slot * cols : (slot + 1) * cols] for slot in range(3)])
    proj_grad = first_grad[:, 3 * cols :].T
    return (
        block_output,
        input_grad,
        one_sums[0],
        one_sums[1],
        qkv_grad,
        qv_bias_grad,
        proj_grad,
        two_sums[2],
        two_sums[0],
        two_sums[1],
        up_grad,
        up_bias_grad,
        down_grad.T,
        two_sums[3],
        height_grad,
        width_grad,
    )


def solution(mesh):
    in_specs = (
        P("dp", None),
        P("dp"),
        P("dp"),
        P(),
        P(),
        P(None, "dp", "mp"),
        P(),
        P("mp", "dp"),
        P(),
        P(),
        P(),
        P("dp", "mp"),
        P(),
        P("mp", "dp"),
        P(),
        P(),
        P(),
        P("dp", None),
    )
    out_specs = (
        P("dp", None),
        P("dp", None),
        P(),
        P(),
        P(None, "dp", "mp"),
        P(),
        P("mp", "dp"),
        P(),
        P(),
        P(),
        P("dp", "mp"),
        P(),
        P("mp", "dp"),
        P(),
        P(),
        P(),
    )
    return jax.shard_map(body, mesh=mesh, in_specs=in_specs, out_specs=out_specs, check_vma=False)
```

```python
from functools import partial

import jax
import jax.numpy as jnp
import numpy as np
from jax import lax
from jax.experimental import pallas as pl
from jax.experimental.pallas import tpu as pltpu
from jax.sharding import PartitionSpec as P

HD = 80
WIN = 14
SIDE = 64
GRID = 5
WTOK = 196
RELN = 27
ROWS = 208
SCALE = HD ** (-0.5)
EPS = 1e-06
F32 = jnp.float32
BF16 = jnp.bfloat16
ANY = pl.BlockSpec(memory_space=pl.ANY)
highest = lax.Precision.HIGHEST


def dot(left, right):
    return lax.dot_general(left, right, (((1,), (0,)), ((), ())), preferred_element_type=F32)


def dot_nt(left, right):
    return lax.dot_general(left, right, (((1,), (1,)), ((), ())), preferred_element_type=F32)


def dot_tn(left, right):
    return lax.dot_general(left, right, (((0,), (0,)), ((), ())), preferred_element_type=F32)


def whole(array):
    zeros = (0,) * len(array.shape)
    return pl.BlockSpec(array.shape, lambda *_: zeros)


def params(megabytes):
    return pltpu.CompilerParams(vmem_limit_bytes=megabytes * 2**20)


def cost(micros):
    return pl.CostEstimate(
        flops=int(micros * 0.05e9), bytes_accessed=int(micros * 1.0e4), transcendentals=0
    )


def struct(shape, dtype):
    return jax.ShapeDtypeStruct(shape, dtype)


def assemble(offsets, pieces, target, sems):
    copies = []
    for index, piece in enumerate(pieces):
        count = piece.shape[0]
        start = pl.multiple_of(offsets[index], 16)
        copies.append(
            pltpu.make_async_copy(piece, target.at[pl.ds(start, count)], sems.at[index])
        )
    for copy in copies:
        copy.start()
    for copy in copies:
        copy.wait()


def norm_parts(values):
    center = jnp.mean(values, axis=-1, keepdims=True)
    centred = values - center
    spread = jnp.mean(centred * centred, axis=-1, keepdims=True)
    rstd = lax.rsqrt(spread + EPS)
    return centred * rstd, rstd


def token_valid(spot, live):
    token = lax.broadcasted_iota(jnp.int32, (WTOK, 1), 0)
    row = (token * 9363) >> 17
    col = token - row * WIN
    high = spot // GRID * WIN
    wide = spot % GRID * WIN
    inside = (high + row < SIDE) & (wide + col < SIDE) & (live == 1)
    return jnp.where(inside, 1.0, 0.0).astype(F32)


def pad_rows(values):
    empty = jnp.zeros((ROWS - WTOK, values.shape[1]), F32)
    return jnp.concatenate([values, empty], axis=0)


def prepare_kernel(every, order, places, lives, x_ref, gain_ref, shift_ref, *outs):
    rows_ref, own_ref, normed_ref, valid_ref = outs
    step = pl.program_id(0)
    slot = order[step]
    valid = token_valid(places[slot], lives[slot])
    x = x_ref[0].astype(F32)
    xhat, _ = norm_parts(x)
    normed_ref[...] = pad_rows((xhat * gain_ref[...] + shift_ref[...]) * valid).astype(BF16)
    valid_ref[...] = pad_rows(valid)

    @pl.when(lax.rem(step, every) == 0)
    def _():
        rows_ref[...] = pad_rows(x).astype(BF16)
        own_ref[...] = pad_rows(valid)


def prepare(order, places, lives, x, gain, shift, every):
    count = order.shape[0]
    width = x.shape[2]
    window = pl.BlockSpec((1, WTOK, width), lambda i, order, *_: (order[i], 0, 0))
    block = pl.BlockSpec((ROWS, width), lambda i, *_: (i, 0))
    return pl.pallas_call(
        partial(prepare_kernel, every),
        grid_spec=pltpu.PrefetchScalarGridSpec(
            num_scalar_prefetch=3,
            grid=(count,),
            in_specs=[window, whole(gain), whole(shift)],
            out_specs=[
                pl.BlockSpec((ROWS, width), lambda i, *_: (i // every, 0)),
                pl.BlockSpec((ROWS, 1), lambda i, *_: (i // every, 0)),
                block,
                pl.BlockSpec((ROWS, 1), lambda i, *_: (i, 0)),
            ],
        ),
        out_shape=[
            struct((count // every * ROWS, width), BF16),
            struct((count // every * ROWS, 1), F32),
            struct((count * ROWS, width), BF16),
            struct((count * ROWS, 1), F32),
        ],
        compiler_params=params(12),
        cost_estimate=cost(9),
        name="prepare",
    )(order, places, lives, x, gain, shift)


def mask_kernel(order, places, lives, top_ref, grad_ref):
    slot = order[pl.program_id(0)]
    valid = token_valid(places[slot], lives[slot])
    grad_ref[...] = pad_rows(top_ref[0].astype(F32) * valid).astype(BF16)


def mask_rows(order, places, lives, top):
    count = order.shape[0]
    width = top.shape[2]
    return pl.pallas_call(
        mask_kernel,
        grid_spec=pltpu.PrefetchScalarGridSpec(
            num_scalar_prefetch=3,
            grid=(count,),
            in_specs=[pl.BlockSpec((1, WTOK, width), lambda i, order, *_: (order[i], 0, 0))],
            out_specs=pl.BlockSpec((ROWS, width), lambda i, *_: (i, 0)),
        ),
        out_shape=struct((count * ROWS, width), BF16),
        compiler_params=params(12),
        cost_estimate=cost(6),
        name="mask_rows",
    )(order, places, lives, top)


def top_rows(shape):
    return pl.BlockSpec(shape, lambda i: (0, 0))


def row_block(shape, at):
    return pl.BlockSpec(shape, lambda i: (at, 0))


def total(refs, rows):
    value = refs[0][:rows].astype(F32)
    for ref in refs[1:]:
        value = value + ref[:rows].astype(F32)
    return value


def norm_two_kernel(count, *refs):
    parts, (x_ref, bias_ref, gain_ref, shift_ref, after_ref, normed_ref) = (
        refs[:count],
        refs[count:],
    )
    rows = x_ref.shape[0]
    after = x_ref[...].astype(F32) + total(parts, rows) + bias_ref[...]
    xhat, _ = norm_parts(after)
    after_ref[...] = after
    normed_ref[...] = (xhat * gain_ref[...] + shift_ref[...]).astype(BF16)


def norm_two(parts, x, at, bias, gain, shift):
    shape = (parts[-1].shape[0], x.shape[1])
    return pl.pallas_call(
        partial(norm_two_kernel, len(parts)),
        grid=(1,),
        in_specs=[top_rows(shape)] * len(parts)
        + [row_block(shape, at), whole(bias), whole(gain), whole(shift)],
        out_specs=[top_rows(shape)] * 2,
        out_shape=[struct(shape, F32), struct(shape, BF16)],
        compiler_params=params(14),
        cost_estimate=cost(3),
        name="norm_two",
    )(*parts, x, bias, gain, shift)


def finish_kernel(count, *refs):
    parts, (after_ref, valid_ref, bias_ref, out_ref) = refs[:count], refs[count:]
    rows = after_ref.shape[0]
    branch = total(parts, rows) + bias_ref[...]
    out_ref[...] = (valid_ref[...] * (after_ref[...] + branch)).astype(BF16)


def finish(parts, after, valid, at, bias):
    return pl.pallas_call(
        partial(finish_kernel, len(parts)),
        grid=(1,),
        in_specs=[top_rows(after.shape)] * (len(parts) + 1)
        + [row_block((after.shape[0], 1), at), whole(bias)],
        out_specs=top_rows(after.shape),
        out_shape=struct(after.shape, BF16),
        compiler_params=params(14),
        cost_estimate=cost(2.5),
        name="finish",
    )(*parts, after, valid, bias)


def norm_back(upstream, xhat, rstd, gain):
    weighted = upstream * gain
    inner = jnp.mean(weighted * xhat, axis=-1, keepdims=True)
    level = jnp.mean(weighted, axis=-1, keepdims=True)
    return rstd * (weighted - level - xhat * inner)


def norm_two_back_kernel(count, *refs):
    parts = refs[:count]
    after_ref, top_ref, gain_ref, grad_ref, branch_ref, sums_ref = refs[count:]
    rows = after_ref.shape[0]
    upstream = total(parts, rows)
    xhat, rstd = norm_parts(after_ref[...])
    top = top_ref[...].astype(F32)
    grad = top + norm_back(upstream, xhat, rstd, gain_ref[...])
    branch = grad.astype(BF16)
    grad_ref[...] = grad
    branch_ref[...] = branch
    sums_ref[0:1] = jnp.sum(upstream * xhat, axis=0, keepdims=True)
    sums_ref[1:2] = jnp.sum(upstream, axis=0, keepdims=True)
    sums_ref[2:3] = jnp.sum(branch.astype(F32), axis=0, keepdims=True)
    sums_ref[3:4] = jnp.sum(top, axis=0, keepdims=True)


def norm_two_back(parts, after, top, at, gain):
    sums = struct((4, after.shape[1]), F32)
    return pl.pallas_call(
        partial(norm_two_back_kernel, len(parts)),
        grid=(1,),
        in_specs=[top_rows(after.shape)] * (len(parts) + 1)
        + [row_block(after.shape, at), whole(gain)],
        out_specs=[top_rows(after.shape)] * 2 + [whole(sums)],
        out_shape=[struct(after.shape, F32), struct(after.shape, BF16), sums],
        compiler_params=params(14),
        cost_estimate=cost(4),
        name="norm_two_back",
    )(*parts, after, top, gain)


def norm_one_back_kernel(counts, *refs):
    x_ref, valid_ref, gain_ref, out_ref = refs[-4:]
    at = 0
    for part, count in enumerate(counts):
        parts, grad_ref = refs[at : at + count], refs[at + count]
        at += count + 1
        rows = slice(part * ROWS, part * ROWS + ROWS)
        upstream = total(parts, ROWS) * valid_ref[rows]
        xhat, rstd = norm_parts(x_ref[rows].astype(F32))
        grad = grad_ref[...] + norm_back(upstream, xhat, rstd, gain_ref[...])
        out_ref[rows] = grad.astype(BF16)


def norm_one_back(windows, x, valid, gain):
    shape = (ROWS, x.shape[1])
    operands, specs = [], []
    for parts, grad in windows:
        operands += [part[0] for part in parts] + [grad]
        specs += [
            pl.BlockSpec(shape, lambda i, at=at: (at, 0)) for at in (part[1] for part in parts)
        ]
        specs.append(whole(grad))
    return pl.pallas_call(
        partial(norm_one_back_kernel, [len(parts) for parts, _ in windows]),
        grid=(1,),
        in_specs=specs + [whole(x), whole(valid), whole(gain)],
        out_specs=whole(x),
        out_shape=struct(x.shape, BF16),
        compiler_params=params(20),
        cost_estimate=cost(3.5 * len(windows)),
        name="norm_one_back",
    )(*operands, x, valid, gain)


def qkv_kernel(count, cols, offsets, *refs):
    pieces = refs[:count]
    x_ref, bias_ref, q_ref, k_ref, v_ref, w_ref, sems = refs[count:]
    wide = q_ref.shape[1]

    @pl.when(pl.program_id(0) == 0)
    def _():
        assemble(offsets, pieces, w_ref, sems)

    result = (dot(x_ref[...], w_ref[:, wide:]) + bias_ref[...]).astype(BF16)
    for slot, ref in enumerate((q_ref, k_ref, v_ref)):
        ref[:, :cols] = result[:, slot * cols : (slot + 1) * cols]
        if wide > cols:
            ref[:, cols:] = jnp.zeros((ref.shape[0], wide - cols), BF16)


def project(offsets, pieces, x, bias, cols, wide):
    rows, width = x.shape
    step = 2 * ROWS
    block = pl.BlockSpec((step, wide), lambda i, *_: (i, 0))
    total_cols = wide + 3 * cols
    return pl.pallas_call(
        partial(qkv_kernel, len(pieces), cols),
        grid_spec=pltpu.PrefetchScalarGridSpec(
            num_scalar_prefetch=1,
            grid=(rows // step,),
            in_specs=[ANY] * len(pieces)
            + [pl.BlockSpec((step, width), lambda i, *_: (i, 0)), whole(bias)],
            out_specs=[block, block, block, pl.BlockSpec((width, total_cols), lambda i, *_: (0, 0))],
            scratch_shapes=[pltpu.SemaphoreType.DMA((len(pieces),))],
        ),
        out_shape=[struct((rows, wide), BF16)] * 3 + [struct((width, total_cols), BF16)],
        compiler_params=params(28),
        cost_estimate=cost(14),
        name="qkv",
    )(offsets, *pieces, x, bias)


def head_spans(heads, wide):
    spans = []
    for head in range(heads):
        first, last = head * HD, head * HD + HD
        low = first // 128 * 128
        high = min((last + 127) // 128 * 128, wide)
        spans.append((low, high, first, last))
    return spans


def lane_mask(span):
    low, high, first, last = span
    lane = lax.broadcasted_iota(jnp.int32, (1, high - low), 1) + low
    return jnp.where((lane >= first) & (lane < last), 1.0, 0.0).astype(BF16)


def shift_counts():
    token = lax.broadcasted_iota(jnp.int32, (ROWS, 128), 0)
    row = (token * 9363) >> 17
    col = token - row * WIN
    return jnp.maximum(WIN - 1 - row, 0), WIN - 1 - col


def shift_lanes(values, counts, back):
    for step in (1, 2, 4, 8):
        moved = pltpu.roll(values, step if back else 128 - step, 1)
        values = jnp.where((counts & step) != 0, moved, values)
    return values


def lane_kind():
    lane = lax.broadcasted_iota(jnp.int32, (ROWS, 128), 1) & 31
    return lane < WIN, (lane >= 16) & (lane < 16 + WIN), lane == 31


def split_two(values):
    high = values.astype(BF16)
    return high, (values - high.astype(F32)).astype(BF16)


def bias_operand(q, rel_high, rel_low, counts):
    table = (dot(q, rel_high) + dot(q, rel_low)) * (1.0 / SCALE)
    by_row = shift_lanes(table[:, :128], counts[0], False)
    by_col = shift_lanes(table[:, 128:], counts[1], False)
    is_row, is_col, is_last = lane_kind()
    packed = jnp.where(
        is_row, by_row, jnp.where(is_col, by_col, jnp.where(is_last, 1.0, 0.0))
    )
    high, low = split_two(packed)
    return jnp.concatenate([high, low], axis=1)


def add_lanes(parts, values, span):
    low, high = span[0], span[1]
    for index in range(low // 128, high // 128):
        piece = values[:, index * 128 - low : index * 128 - low + 128]
        parts[index] = piece if parts[index] is None else parts[index] + piece


def attend_kernel(heads, split, q_ref, k_ref, v_ref, rh_ref, rl_ref, mark_ref, w_ref, *outs):
    mixed_ref, shares_ref = outs[:2]
    q, k, v = q_ref[...], k_ref[...], v_ref[...]
    wide = q.shape[1]
    bias = bias_operand(q, rh_ref[...], rl_ref[...], shift_counts())
    parts = [None] * (wide // 128)
    for head, span in enumerate(head_spans(heads, wide)):
        mask = lane_mask(span)
        cut = slice(span[0], span[1])
        scores = dot_nt(
            jnp.concatenate([q[:, cut], bias], axis=1),
            jnp.concatenate([k[:, cut] * mask, mark_ref[head]], axis=1),
        )
        top = jnp.max(scores, axis=-1, keepdims=True)
        shifted = jnp.exp(SCALE * (scores - top))
        norm = jnp.sum(shifted, axis=-1, keepdims=True)
        shares = (shifted * (1.0 / norm)).astype(BF16)
        shares_ref[:, head * 256 : head * 256 + ROWS] = shares
        add_lanes(parts, dot(shares, v[:, cut] * mask), span)
    mixed = jnp.concatenate(parts, axis=1).astype(BF16)
    cols = heads * HD
    mixed_ref[...] = mixed[:, :cols]
    branch = dot_nt(mixed, w_ref[...]).astype(BF16)
    if split:
        keep_ref, send_ref = outs[2:]
        step = pl.program_id(0)

        @pl.when(step < split)
        def _():
            send_ref[...] = branch

        @pl.when(step >= split)
        def _():
            keep_ref[...] = branch
    else:
        outs[2][...] = branch


def split_specs(windows, split, width):
    rows = ROWS * (windows - split)
    if not split:
        return [pl.BlockSpec((ROWS, width), lambda i: (i, 0))], [struct((rows, width), BF16)]
    return (
        [
            pl.BlockSpec((ROWS, width), lambda i: (jnp.maximum(i - split, 0), 0)),
            pl.BlockSpec((ROWS, width), lambda i: (jnp.minimum(i, split - 1), 0)),
        ],
        [struct((rows, width), BF16), struct((ROWS * split, width), BF16)],
    )


def attend(heads, part, windows, split, q, k, v, rel_high, rel_low, marks, weights):
    wide = q.shape[1]
    width = weights.shape[0]

    def place(i):
        return (i + split) % windows if split else i

    block = pl.BlockSpec((ROWS, wide), lambda i: (part * windows + place(i), 0))
    specs, shapes = split_specs(windows, split, width)
    return pl.pallas_call(
        partial(attend_kernel, heads, split),
        grid=(windows,),
        in_specs=[
            block,
            block,
            block,
            whole(rel_high),
            whole(rel_low),
            whole(marks),
            pl.BlockSpec((width, wide), lambda i: (0, 0)),
        ],
        out_specs=[
            pl.BlockSpec((ROWS, heads * HD), lambda i: (place(i), 0)),
            pl.BlockSpec((ROWS, heads * 256), lambda i: (place(i), 0)),
        ]
        + specs,
        out_shape=[
            struct((windows * ROWS, heads * HD), BF16),
            struct((windows * ROWS, heads * 256), BF16),
        ]
        + shapes,
        compiler_params=params(16),
        cost_estimate=cost(13.5),
        name="attend",
    )(q, k, v, rel_high, rel_low, marks, weights)


def attend_back_kernel(heads, windows, split, count, *refs):
    pieces = refs[:count]
    q_ref, k_ref, v_ref, shares_ref, rh_ref, mark_ref, w_ref = refs[count : count + 7]
    normed_ref, valid_ref = refs[count + 7 : count + 9]
    grads_ref, branch_ref, rel_ref, sum_ref, norm_ref = refs[count + 9 : count + 14]
    outs = refs[count + 14 :]
    step = pl.program_id(0)

    @pl.when(step == 0)
    def _():
        start = 0
        for piece in pieces:
            branch_ref[start : start + piece.shape[0]] = piece[...]
            start += piece.shape[0]
        rel_ref[...] = jnp.zeros(rel_ref.shape, F32)
        sum_ref[...] = jnp.zeros(sum_ref.shape, F32)
        norm_ref[...] = jnp.zeros(norm_ref.shape, F32)

    place = lax.rem(step + split, windows) if split else step
    q, k, v = q_ref[...], k_ref[...], v_ref[...]
    wide = q.shape[1]
    top = branch_ref[pl.ds(pl.multiple_of(place * ROWS, 16), ROWS), :]
    grad_mixed = dot(top, w_ref[:, :wide]).astype(BF16)
    grad_q, grad_k, grad_v = ([None] * (wide // 128) for _ in range(3))
    grad_bias = None
    for head, span in enumerate(head_spans(heads, wide)):
        mask = lane_mask(span)
        cut = slice(span[0], span[1])
        size = span[1] - span[0]
        upper = grad_mixed[:, cut]
        rounded = shares_ref[:, head * 256 : head * 256 + ROWS]
        shares = rounded.astype(F32)
        weighted = shares * dot_nt(upper, v[:, cut] * mask)
        inner = jnp.sum(weighted, axis=-1, keepdims=True)
        grad_scores = (weighted - shares * inner).astype(BF16)
        add_lanes(grad_v, dot_tn(rounded, upper * mask), span)
        both = dot(
            grad_scores,
            jnp.concatenate([k[:, cut] * mask, mark_ref[head][:, :128]], axis=1),
        )
        add_lanes(grad_q, both[:, :size], span)
        part = both[:, size:]
        grad_bias = part if grad_bias is None else grad_bias + part
        add_lanes(grad_k, dot_tn(grad_scores, q[:, cut] * mask), span)
    counts = shift_counts()
    is_row, is_col, _ = lane_kind()
    by_row = shift_lanes(jnp.where(is_row, grad_bias, 0.0), counts[0], True)
    by_col = shift_lanes(jnp.where(is_col, grad_bias, 0.0), counts[1], True)
    packed = jnp.concatenate([by_row, by_col], axis=1).astype(BF16)
    extra = dot_nt(packed, rh_ref[...])
    rel_ref[...] += dot_tn(packed, q)
    grad_q = (SCALE * jnp.concatenate(grad_q, axis=1) + extra).astype(BF16)
    grad_k = (SCALE * jnp.concatenate(grad_k, axis=1)).astype(BF16)
    grad_v = jnp.concatenate(grad_v, axis=1).astype(BF16)
    cols = heads * HD
    for slot, grad in enumerate((grad_q, grad_k, grad_v)):
        grads_ref[:, slot * cols : (slot + 1) * cols] = grad[:, :cols]
    packed_grads = grads_ref[...]
    sum_ref[...] += jnp.sum(packed_grads.astype(F32), axis=0, keepdims=True)
    partial_sum = dot_nt(packed_grads, w_ref[:, wide:])
    norm_ref[0:1] += jnp.sum(partial_sum * normed_ref[...].astype(F32), axis=0, keepdims=True)
    norm_ref[1:2] += jnp.sum(partial_sum * valid_ref[...], axis=0, keepdims=True)
    result = partial_sum.astype(BF16)
    if split:
        keep_ref, send_ref = outs

        @pl.when(step < split)
        def _():
            send_ref[...] = result

        @pl.when(step >= split)
        def _():
            keep_ref[...] = result
    else:
        outs[0][...] = result


def attend_back(
    heads, part, windows, split, pieces, q, k, v, shares, rel_high, marks, weights, normed, valid
):
    wide = q.shape[1]
    width = weights.shape[0]

    def place(i):
        return (i + split) % windows if split else i

    block = pl.BlockSpec((ROWS, wide), lambda i: (part * windows + place(i), 0))
    specs, shapes = split_specs(windows, split, width)
    rows = windows * ROWS
    branch = struct((rows, width), BF16)
    rel = struct((256, wide), F32)
    sums = struct((1, 3 * heads * HD), F32)
    norms = struct((2, width), F32)
    return pl.pallas_call(
        partial(attend_back_kernel, heads, windows, split, len(pieces)),
        grid=(windows,),
        in_specs=[whole(piece) for piece in pieces]
        + [
            block,
            block,
            block,
            pl.BlockSpec((ROWS, heads * 256), lambda i: (place(i), 0)),
            whole(rel_high),
            whole(marks),
            whole(weights),
            pl.BlockSpec((ROWS, width), lambda i: (part * windows + place(i), 0)),
            pl.BlockSpec((ROWS, 1), lambda i: (part * windows + place(i), 0)),
        ],
        out_specs=[
            pl.BlockSpec((ROWS, 3 * heads * HD), lambda i: (place(i), 0)),
            whole(branch),
            whole(rel),
            whole(sums),
            whole(norms),
        ]
        + specs,
        out_shape=[struct((rows, 3 * heads * HD), BF16), branch, rel, sums, norms] + shapes,
        compiler_params=params(28),
        cost_estimate=cost(18.5),
        name="attend_back",
    )(*pieces, q, k, v, shares, rel_high, marks, weights, normed, valid)


def mlp_kernel(count, weights, split, offsets, *refs):
    pieces = refs[:count]
    weight_pieces = refs[count : count + weights]
    refs = refs[count + weights :]
    after_any, top_ref, bias_ref, down_bias_ref = refs[:4]
    active_ref, hidden_ref, normed_any, sum_ref = refs[4:8]
    outs = refs[8 : 12 if split else 10]
    up, down, normed_ref, after_ref, send_ref, out_send_ref, sems, row_sems = refs[len(outs) + 8 :]
    step = pl.program_id(0)
    steps = pl.num_programs(0)
    block = top_ref.shape[0]
    units = up.shape[1]
    copies = []
    for half, target in enumerate((down, up)):
        copies.append([])
        for index, piece in enumerate(weight_pieces):
            rows = piece.shape[0]
            start = pl.multiple_of(offsets[index], 16)
            copies[half].append(
                pltpu.make_async_copy(
                    piece.at[:, half * units : (half + 1) * units],
                    target.at[pl.ds(start, rows)],
                    sems.at[half, index],
                )
            )
    row_copies, start = [], 0
    for index, piece in enumerate(pieces):
        rows = piece.shape[0]
        row_copies.append(
            pltpu.make_async_copy(
                piece, normed_ref.at[pl.ds(start, rows)], row_sems.at[index]
            )
        )
        start += rows
    normed_out = pltpu.make_async_copy(normed_ref, normed_any, row_sems.at[count])
    after_in = pltpu.make_async_copy(after_any, after_ref, row_sems.at[count + 1])
    if split:
        send_out = pltpu.make_async_copy(send_ref, outs[1], row_sems.at[count + 2])
        out_send_out = pltpu.make_async_copy(out_send_ref, outs[3], row_sems.at[count + 3])

    @pl.when(step == 0)
    def _():
        for copy in row_copies + copies[1] + copies[0]:
            copy.start()
        after_in.start()
        sum_ref[...] = jnp.zeros(sum_ref.shape, F32)
        for copy in row_copies + copies[1]:
            copy.wait()
        normed_out.start()

    place = 1 - step if split else step
    normed = normed_ref[pl.ds(pl.multiple_of(place * block, 16), block), :]
    hidden = dot(normed, up[...]) + bias_ref[...]

    @pl.when(step == 0)
    def _():
        for copy in copies[0]:
            copy.wait()

    half = 0.5 * (1.0 + lax.erf(hidden * (0.5**0.5)))
    slope = half + hidden * jnp.exp(-0.5 * hidden * hidden) * float((2.0 * np.pi) ** -0.5)
    active = (hidden * half).astype(BF16)
    active_ref[...] = active
    grad = (dot(top_ref[...], down[...]) * slope).astype(BF16)
    hidden_ref[...] = grad
    sum_ref[...] += jnp.sum(grad.astype(F32), axis=0, keepdims=True)
    back = dot_nt(grad, up[...]).astype(BF16)
    result = dot_nt(active, down[...])
    if split:

        @pl.when(step == 0)
        def _():
            send_ref[...] = back
            out_send_ref[...] = result.astype(BF16)
            send_out.start()
            out_send_out.start()
            after_in.wait()

        @pl.when(step == 1)
        def _():
            outs[0][...] = back
            own = result[:ROWS] + after_ref[...] + down_bias_ref[...]
            outs[2][:ROWS] = own.astype(BF16)
            outs[2][ROWS:] = result[ROWS:].astype(BF16)
            send_out.wait()
            out_send_out.wait()
    else:
        outs[0][...] = back
        outs[1][...] = result.astype(BF16)

        @pl.when(step == 0)
        def _():
            after_in.wait()

    @pl.when(step == steps - 1)
    def _():
        normed_out.wait()


def mlp(offsets, pieces, weight_pieces, top, part, bias, after, down_bias, split):
    rows = sum(piece.shape[0] for piece in pieces)
    width = pieces[0].shape[1]
    units = weight_pieces[0].shape[1] // 2
    block = 2 * ROWS
    blocks = rows // block
    normed = struct((rows, width), BF16)
    sums = struct((1, units), F32)

    def place(i):
        return 1 - i if split else i

    wide = pl.BlockSpec((block, units), lambda i, *_: (place(i), 0))
    back = struct((block, width), BF16)
    if split:
        back_specs, back_shapes = [whole(back), ANY] * 2, [back] * 4
    else:
        back_specs = [pl.BlockSpec((block, width), lambda i, *_: (i, 0))] * 2
        back_shapes = [normed] * 2
    return pl.pallas_call(
        partial(mlp_kernel, len(pieces), len(weight_pieces), split),
        grid_spec=pltpu.PrefetchScalarGridSpec(
            num_scalar_prefetch=1,
            grid=(blocks,),
            in_specs=[ANY] * (len(pieces) + len(weight_pieces) + 1)
            + [
                pl.BlockSpec((block, width), lambda i, *_: (part * blocks + place(i), 0)),
                whole(bias),
                whole(down_bias),
            ],
            out_specs=[wide, wide, ANY, whole(sums)] + back_specs,
            scratch_shapes=[
                pltpu.VMEM((width, units), BF16),
                pltpu.VMEM((width, units), BF16),
                pltpu.VMEM((rows, width), BF16),
                pltpu.VMEM(after.shape, F32),
                pltpu.VMEM((block, width), BF16),
                pltpu.VMEM((block, width), BF16),
                pltpu.SemaphoreType.DMA((2, len(weight_pieces))),
                pltpu.SemaphoreType.DMA((len(pieces) + 4,)),
            ],
        ),
        out_shape=[struct((rows, units), BF16)] * 2 + [normed, sums] + back_shapes,
        compiler_params=params(48),
        cost_estimate=cost(21),
        name="mlp",
    )(offsets, *pieces, *weight_pieces, after, top, bias, down_bias)


def weight_grad_kernel(sizes, share, targets, *refs):
    count = 2 * sum(sizes)
    operands = refs[:count]
    outs, (result, sems) = refs[count:-2], refs[-2:]
    high_ref, low_ref, keep_ref = outs[:3] if len(outs) > 1 else (None,) * 3
    pair_ref = outs[-1] if len(outs) != 3 else None
    lead = 0 if keep_ref is None else keep_ref.shape[2]
    step = pl.program_id(0)
    steps = pl.num_programs(0)
    chunk = operands[0].shape[1]
    pieces = chunk // share
    base = pl.multiple_of(step * chunk, 16)
    at, first = 0, 0
    for size in sizes:
        value = None
        for _ in range(size):
            left, right = operands[at], operands[at + 1]
            at += 2
            term = dot_tn(left[...], right[...])
            value = term if value is None else value + term
        span = value.shape[1]
        result[pl.ds(base, chunk), first : first + span] = value.astype(BF16)
        first += span

    def copy(index, out, slot):
        return pltpu.make_async_copy(
            result.at[pl.ds(pl.multiple_of(index * share, 16), share), pl.ds(0, lead)],
            out.at[slot],
            sems.at[0, index],
        )

    def pair_copy(index, slot):
        return pltpu.make_async_copy(
            result.at[
                pl.ds(pl.multiple_of(index * share, 16), share),
                pl.ds(lead, result.shape[1] - lead),
            ],
            pair_ref.at[lax.rem(slot, 4), 1 - slot // 4],
            sems.at[1, index],
        )

    for piece in range(pieces):
        index = step * pieces + piece
        slot = targets[index]

        if lead:

            @pl.when(slot < 2)
            def _():
                copy(index, low_ref, slot).start()

            @pl.when((slot >= 2) & (slot < 4))
            def _():
                copy(index, high_ref, slot - 2).start()

            @pl.when(slot >= 4)
            def _():
                copy(index, keep_ref, slot - 4).start()

        if pair_ref is not None:
            pair_copy(index, slot).start()

    @pl.when(step == steps - 1)
    def _():
        for index in range(8):
            if lead:
                copy(index, keep_ref, 0).wait()
            if pair_ref is not None:
                pair_copy(index, 0).wait()


def plain_grad_kernel(sizes, *refs):
    count = 2 * sum(sizes)
    operands, out_ref = refs[:count], refs[count]
    at, first = 0, 0
    for size in sizes:
        value = None
        for _ in range(size):
            left, right = operands[at], operands[at + 1]
            at += 2
            term = dot_tn(left[...], right[...])
            value = term if value is None else value + term
        span = value.shape[1]
        out_ref[:, first : first + span] = value.astype(BF16)
        first += span


def weight_grad(targets, groups, share, lead=None):
    operands, specs = [], []
    chunk = 640 if targets is not None else 256
    total_cols = 0
    for group in groups:
        for left, at, rows, right in group:
            operands += [left, right]
            specs.append(pl.BlockSpec((rows, chunk), lambda i, *_, at=at: (at, i)))
            specs.append(whole(right))
        total_cols += group[0][3].shape[1]
    width = operands[0].shape[1]
    sizes = [len(group) for group in groups]
    if targets is None:
        return [
            pl.pallas_call(
                partial(plain_grad_kernel, sizes),
                grid=(width // chunk,),
                in_specs=specs,
                out_specs=pl.BlockSpec((chunk, total_cols), lambda i: (i, 0)),
                out_shape=struct((width, total_cols), BF16),
                compiler_params=params(36),
                cost_estimate=cost(13),
        name="weight_grad",
            )(*operands)
        ]
    lead = total_cols if lead is None else lead
    shapes = [struct((count, share, lead), BF16) for count in (2, 2, 4)] if lead else []
    if lead < total_cols:
        shapes.append(struct((4, 2, share, total_cols - lead), BF16))
    return pl.pallas_call(
        partial(weight_grad_kernel, sizes, share),
        grid_spec=pltpu.PrefetchScalarGridSpec(
            num_scalar_prefetch=1,
            grid=(width // chunk,),
            in_specs=specs,
            out_specs=[ANY] * len(shapes),
            scratch_shapes=[
                pltpu.VMEM((width, total_cols), BF16),
                pltpu.SemaphoreType.DMA((2, 8)),
            ],
        ),
        out_shape=shapes,
        compiler_params=params(36),
        cost_estimate=cost(13),
        name="weight_grad",
    )(targets, *operands)


def combine_kernel(layout, *refs):
    outs = refs[len(refs) - len(layout) :]
    at = 0
    for cells, out in zip(layout, outs):
        for row, lane, rows, lanes, terms in cells:
            value = None
            for lead, first in terms:
                term = refs[at][(0,) * lead + (slice(None), slice(first, first + lanes))]
                at += 1
                value = term.astype(F32) if value is None else value + term.astype(F32)
            out[row : row + rows, lane : lane + lanes] = value.astype(BF16)


def combine(*outs):
    operands, specs, layout = [], [], []
    for _, cells in outs:
        layout.append([])
        for row, lane, rows, lanes, terms in cells:
            places = []
            for array, index, first in terms:
                lead = array.ndim - 2
                block = (1,) * lead + (rows, array.shape[-1])
                place = tuple(index) + (0,) * (array.ndim - len(index))
                operands.append(array)
                specs.append(pl.BlockSpec(block, lambda i, place=place: place))
                places.append((lead, first))
            layout[-1].append((row, lane, rows, lanes, places))
    shapes = [struct(shape, BF16) for shape, _ in outs]
    return pl.pallas_call(
        partial(combine_kernel, layout),
        grid=(1,),
        in_specs=specs,
        out_specs=[whole(shape) for shape in shapes],
        out_shape=shapes,
        compiler_params=params(16),
        cost_estimate=cost(2),
        name="combine",
    )(*operands)


def place_kernel(order, *refs):
    pieces, out_ref = refs[:4], refs[4]
    for me in range(4):

        @pl.when(order[0] == me)
        def _(me=me):
            for part in range(pieces[0].shape[0] // ROWS):
                for index, step in enumerate((0, 2, 1, 3)):
                    start = (4 * part + (me ^ step)) * WTOK
                    value = pieces[index][part * ROWS : part * ROWS + WTOK]
                    out_ref[start : start + WTOK] = value.astype(F32)


def place_windows(order, pieces):
    height, width = pieces[0].shape
    rows = height // ROWS * 4 * WTOK
    lanes = width // 2
    return pl.pallas_call(
        place_kernel,
        grid_spec=pltpu.PrefetchScalarGridSpec(
            num_scalar_prefetch=1,
            grid=(2,),
            in_specs=[pl.BlockSpec((height, lanes), lambda i, *_: (0, i))] * 4,
            out_specs=pl.BlockSpec((rows, lanes), lambda i, *_: (0, i)),
        ),
        out_shape=struct((rows, width), F32),
        compiler_params=params(32),
        cost_estimate=cost(7),
        name="place_windows",
    )(order, *pieces)


def output_kernel(order, places, lives, *refs):
    pieces, out_ref, buffer = refs[:4], refs[4], refs[5]
    for me in range(4):

        @pl.when(order[0] == me)
        def _(me=me):
            for part in range(pieces[0].shape[0] // ROWS):
                for index, step in enumerate((0, 2, 1, 3)):
                    slot = 4 * part + (me ^ step)
                    value = pieces[index][part * ROWS : part * ROWS + WTOK].astype(F32)
                    value = value * token_valid(places[slot], lives[slot])
                    buffer[slot * WTOK : (slot + 1) * WTOK] = value

    out_ref[...] = buffer[...].astype(BF16)


def write_output(order, places, lives, pieces):
    height, width = pieces[0].shape
    rows = height // ROWS * 4 * WTOK
    lanes = width // 2
    return pl.pallas_call(
        output_kernel,
        grid_spec=pltpu.PrefetchScalarGridSpec(
            num_scalar_prefetch=3,
            grid=(2,),
            in_specs=[pl.BlockSpec((height, lanes), lambda i, *_: (0, i))] * 4,
            out_specs=pl.BlockSpec((rows, lanes), lambda i, *_: (0, i)),
            scratch_shapes=[pltpu.VMEM((rows, lanes), F32)],
        ),
        out_shape=struct((rows, width), BF16),
        compiler_params=params(32),
        cost_estimate=cost(7),
        name="write_output",
    )(order, places, lives, *pieces)


def key_marks(heads):
    marks = np.zeros((heads, ROWS, 256), np.float32)
    for head in range(heads):
        for token in range(WTOK):
            for half in (0, 128):
                marks[head, token, half + head * 32 + token // WIN] = 1.0
                marks[head, token, half + head * 32 + 16 + token % WIN] = 1.0
        marks[head, WTOK:, head * 32 + 31] = -1e30
    return marks.astype(BF16)


def rel_operand(rel_height, rel_width, heads, wide):
    high = rel_height[::-1].T
    flat = rel_width[::-1].T
    lanes = jnp.zeros((wide, 256), F32)

    def spread(block, row, lane):
        below = wide - row - HD
        return jnp.pad(block, ((row, below), (lane, 256 - lane - block.shape[1])))

    for head in range(heads):
        first = head * 32 + 16
        fit = min(RELN, 128 - first)
        lanes = lanes + spread(high, head * HD, head * 32)
        lanes = lanes + spread(flat[:, :fit], head * HD, 128 + first)
        if fit < RELN:
            lanes = lanes + spread(flat[:, fit:], head * HD, 128)
    return split_two(lanes)


def rel_result(sums, heads):
    high = jnp.zeros((RELN, HD), F32)
    flat = jnp.zeros((RELN, HD), F32)
    for head in range(heads):
        cols = sums[:, head * HD : head * HD + HD]
        high = high + cols[head * 32 : head * 32 + RELN]
        rolled = jnp.concatenate([cols[128:], cols[128:]], axis=0)
        flat = flat + rolled[head * 32 + 16 : head * 32 + 16 + RELN]
    return high[::-1], flat[::-1]


def add_all(values):
    out = values[0]
    for value in values[1:]:
        out = out + value
    return out


def tie(value, *others):
    return lax.optimization_barrier((value,) + others)[0]


def sync(*values):
    return lax.optimization_barrier(values)


def body(
    block_input,
    window_place,
    slot_live,
    norm_one_gain,
    norm_one_shift,
    qkv_weight,
    qv_bias,
    proj_weight,
    proj_bias,
    norm_two_gain,
    norm_two_shift,
    up_weight,
    up_bias,
    down_weight,
    down_bias,
    rel_height,
    rel_width,
    cotangent,
):
    data_parts = lax.axis_size("dp")
    model_parts = lax.axis_size("mp")
    data_index = lax.axis_index("dp")
    model_index = lax.axis_index("mp")
    width = block_input.shape[1]
    share = qkv_weight.shape[1]
    cols = qkv_weight.shape[2]
    heads = cols // HD
    wide = (cols + 127) // 128 * 128
    units = up_weight.shape[1]
    slots = window_place.shape[0]
    rings = data_parts == 8 and model_parts == 4 and slots == 8
    padded = (slots + model_parts - 1) // model_parts * model_parts
    halves = padded // 4 if rings else 1
    windows = padded // halves
    split = 2 if rings else 0
    part_rows = windows * ROWS
    own_rows = part_rows // model_parts

    if rings:
        depth, side = data_index // 2, data_index % 2
        y_bit, core_bit = model_index // 2, model_index % 2
        over_x = partial(lax.ppermute, axis_name="dp", perm=[(d, d ^ 1) for d in range(8)])
        over_z = partial(lax.ppermute, axis_name="dp", perm=[(d, (d + 2) % 8) for d in range(8)])
        over_y = partial(lax.ppermute, axis_name="mp", perm=[(m, m ^ 2) for m in range(4)])
        over_core = partial(lax.ppermute, axis_name="mp", perm=[(m, m ^ 1) for m in range(4)])

    def gather(piece):
        return [lax.all_gather(piece, "dp", axis=0, tiled=True)]

    if rings:
        offsets = []
        for back in range(4):
            behind = (depth - back) % 4
            offsets += [share * (2 * behind + side), share * (2 * behind + 1 - side)]
        offsets = jnp.stack(offsets).astype(jnp.int32)
    else:
        offsets = jnp.zeros((1,), jnp.int32)

    def scatter(parts):
        return lax.psum_scatter(parts[0], "dp", scatter_dimension=0, tiled=True).astype(F32)

    def rows_scatter(parts):
        return [lax.psum_scatter(parts[0], "mp", scatter_dimension=0, tiled=True)]

    def rows_gather(own):
        return [lax.all_gather(own, "mp", axis=0, tiled=True)]

    def own_slice(array):
        rows = array.shape[0] // model_parts
        return lax.dynamic_slice_in_dim(array, model_index * rows, rows, 0)

    first_piece = jnp.concatenate(
        [
            jnp.pad(proj_weight.T, ((0, 0), (0, wide - cols))),
            qkv_weight[0],
            qkv_weight[1],
            qkv_weight[2],
        ],
        axis=1,
    )
    other_piece = jnp.concatenate([down_weight.T, up_weight], 1)

    row = lambda v: v.reshape(1, -1)
    gain_one, shift_one = row(norm_one_gain), row(norm_one_shift)
    gain_two, shift_two = row(norm_two_gain), row(norm_two_shift)
    bias_local = lax.dynamic_slice_in_dim(qv_bias, model_index * cols, cols, 1)
    bias_qkv = row(jnp.stack([bias_local[0], jnp.zeros_like(bias_local[0]), bias_local[1]]))
    up_local = row(lax.dynamic_slice_in_dim(up_bias, model_index * units, units, 0))
    rel_high, rel_low = rel_operand(rel_height, rel_width, heads, wide)
    marks = jnp.asarray(key_marks(heads))

    steps = (0, 2, 1, 3)
    if rings:
        local = [model_index ^ step for step in steps]
        places = [4 * part + spot for part in range(halves) for spot in local]
    else:
        local = [jnp.int32(spot) for spot in range(windows)]
        places = local
    local = jnp.stack(local).astype(jnp.int32)
    places = jnp.stack(places).astype(jnp.int32)
    if rings:
        targets = []
        for d in range(8):
            ahead = (d // 2 - depth) % 4
            targets.append(ahead + jnp.where(d % 2 == side, 4, 0))
        targets = jnp.stack(targets).astype(jnp.int32)
    else:
        targets = None

    def by_window(array):
        array = array.reshape((slots, WTOK) + array.shape[1:])
        return jnp.pad(array, [(0, padded - slots)] + [(0, 0)] * (array.ndim - 1))

    places_all = jnp.pad(window_place, (0, padded - slots))
    lives_all = jnp.pad(slot_live, (0, padded - slots))
    blocks = [(part, part_rows) for part in range(halves)]

    def start(x):
        every = 4 if rings else 1
        return prepare(places, places_all, lives_all, x, gain_one, shift_one, every)

    def masked(top):
        return mask_rows(places, places_all, lives_all, top)

    def attention(part, q, k, v, weights):
        return attend(heads, part, windows, split, q, k, v, rel_high, rel_low, marks, weights)

    def attention_back(part, pieces, q, k, v, shares, weights):
        return attend_back(
            heads,
            part,
            windows,
            split,
            pieces,
            q,
            k,
            v,
            shares,
            rel_high,
            marks,
            weights,
            normed,
            valid,
        )

    def down_groups(mlps):
        return [[(grad_top, *blocks[i], mlps[i][0]) for i in range(halves)]]

    def up_groups(mlps):
        return [[(mlps[i][2], 0, part_rows, mlps[i][1]) for i in range(halves)]]

    def first_groups(backs, attended):
        return [
            [(normed, *blocks[i], backs[i][0]) for i in range(halves)],
            [(backs[i][1], 0, part_rows, attended[i][0]) for i in range(halves)],
        ]

    def bundle(sums_two, backs, mlps):
        qv_sums = add_all([item[3] for item in backs]).reshape(3, cols)[0::2]
        rel_sums = rel_result(add_all([item[2] for item in backs]), heads)
        up_sums = add_all([item[3] for item in mlps]).reshape(units)
        qv_full = lax.dynamic_update_slice_in_dim(
            jnp.zeros((2, width), F32), qv_sums, model_index * cols, 1
        )
        up_full = lax.dynamic_update_slice_in_dim(
            jnp.zeros(up_bias.shape, F32), up_sums, model_index * units, 0
        )
        norms = add_all([item[4] for item in backs])
        arrays = [norms, add_all(sums_two), up_full, qv_full, *rel_sums]
        flat = jnp.concatenate([array.reshape(-1) for array in arrays])
        count = (flat.size + 1023) // 1024 * 1024
        return jnp.pad(flat, (0, count - flat.size)).reshape(-1, 128)

    x_windows = by_window(block_input)
    if not rings:
        first_weights, other_weights = gather(first_piece), gather(other_piece)
        rows_in, own_valid, normed, valid = start(x_windows)
        grad_top = masked(by_window(cotangent))
        own_in, own_top, own_valid = own_slice(rows_in), own_slice(grad_top), own_slice(own_valid)
        q, k, v, weights = project(offsets, first_weights, normed, bias_qkv, cols, wide)
        attended = [attention(0, q, k, v, weights)]
        after, normed_two = norm_two(
            rows_scatter(attended[0][2:]), own_in, 0, row(proj_bias), gain_two, shift_two
        )
        none = jnp.zeros((8, 128), F32)
        mlps = [
            mlp(
                offsets,
                rows_gather(normed_two),
                other_weights,
                grad_top,
                0,
                up_local,
                none,
                row(down_bias),
                False,
            )
        ]
        grad_after, branch, sums = norm_two_back(
            rows_scatter(mlps[0][4:5]), after, own_top, 0, gain_two
        )
        sums_two = [sums]
        result = mlps[0][5]
        own = finish(rows_scatter([result]), after, own_valid, 0, row(down_bias))

        def unpad(array):
            array = array.reshape(padded, ROWS, width)[:slots, :WTOK]
            return array.reshape(slots * WTOK, width)

        block_output = unpad(rows_gather(own)[0])
        down_grad = scatter(weight_grad(None, down_groups(mlps), share))
        up_grad = scatter(weight_grad(None, up_groups(mlps), share))
        backs = [attention_back(0, rows_gather(branch), q, k, v, attended[0][1], weights)]
        parts = [(part, 0) for part in rows_scatter(backs[0][5:])]
        own = norm_one_back([(parts, grad_after)], own_in, own_valid, gain_one)
        input_grad = unpad(rows_gather(own)[0]).astype(F32)
        first_grad = scatter(weight_grad(None, first_groups(backs, attended), share))
        vector = lax.psum(bundle(sums_two, backs, mlps), ("dp", "mp"))
    else:
        def second_norm(part, keep, came, crossed):
            return norm_two(
                [keep, came, crossed], rows_in, part, bias_proj, gain_two, shift_two
            )

        def second_back(part, after, keep, came, crossed):
            return norm_two_back([keep, came, crossed], after, grad_top, 4 * part, gain_two)

        def spread(own, across):
            return [own, across, over_core(own), over_core(across)]

        rows = (ROWS, width)

        def second(keep, came, at=0):
            return (at, 0, *rows, [(keep, (1,), 0), (came, (1,), 0)])

        z1, x0 = over_z(first_piece), over_x(first_piece)
        z1, x0, x_windows, other_piece, rel_high, rel_low, cotangent = sync(
            z1, x0, x_windows, other_piece, rel_high, rel_low, cotangent
        )
        z2, x1 = over_z(z1), over_x(z1)
        rows_in, own_valid, normed, valid = start(x_windows)
        z2, x1, normed, cotangent, gain_two, shift_two, bias_proj, bias_down = sync(
            z2, x1, normed, cotangent, gain_two, shift_two, row(proj_bias), row(down_bias)
        )
        z3, x2 = over_z(z2), over_x(z2)
        z3, x2, normed, top_windows, other_piece = sync(
            z3, x2, normed, by_window(cotangent), other_piece
        )
        x3 = over_x(z3)
        oz1 = over_z(other_piece)
        grad_top = masked(top_windows)
        x3, normed, grad_top, other_late, gain_two, shift_two, bias_proj, bias_down = sync(
            x3, normed, grad_top, other_piece, gain_two, shift_two, bias_proj, bias_down
        )
        ox0 = over_x(other_late)
        first_weights = [first_piece, x0, z1, x1, z2, x2, z3, x3]
        q, k, v, weights = project(offsets, first_weights, normed, bias_qkv, cols, wide)
        oz1, ox0, q = sync(oz1, ox0, q)

        oz2, ox1 = over_z(oz1), over_x(oz1)
        a0 = attention(0, q, k, v, weights)
        oz2, ox1, a0 = sync(oz2, ox1, a0)
        oz3, ox2 = over_z(oz2), over_x(oz2)
        came0 = over_core(a0[3])
        (passed0,) = combine((rows, [second(a0[2], came0)]))
        crossed0 = over_y(passed0)
        a1 = attention(1, tie(q, passed0), k, v, weights)
        oz3, ox2, crossed0, a1 = sync(oz3, ox2, crossed0, a1)
        ox3 = over_x(oz3)
        came1 = over_core(a1[3])
        (passed1,) = combine((rows, [second(a1[2], came1)]))
        crossed1 = over_y(passed1)
        after0, own0 = second_norm(0, tie(a0[2], passed1), came0, crossed0)
        across0 = over_y(own0)
        attended = [a0, a1]
        after1, own1 = second_norm(1, tie(a1[2], own0), came1, crossed1)
        ox3, across0, own1 = sync(ox3, across0, own1)
        other_weights = [other_piece, ox0, oz1, ox1, oz2, ox2, oz3, ox3]
        across1 = over_y(own1)
        pieces0 = spread(own0, across0)

        m0 = mlp(offsets, pieces0, other_weights, grad_top, 0, up_local, after0, bias_down, True)
        across1, m0 = sync(across1, m0)
        pieces1 = spread(own1, across1)
        came0, out_came0 = over_core(m0[5]), over_core(m0[7])
        (passed0,) = combine((rows, [second(m0[4], came0)]))
        crossed0 = over_y(passed0)
        pieces1[0] = tie(pieces1[0], passed0)
        m1 = mlp(offsets, pieces1, other_weights, grad_top, 1, up_local, after1, bias_down, True)
        crossed0, out_came0, m1 = sync(crossed0, out_came0, m1)
        mlps = [m0, m1]
        came1, out_came1 = over_core(m1[5]), over_core(m1[7])
        grad_after0, branch0, sums0 = second_back(0, after0, m0[4], came0, crossed0)
        across0 = over_y(branch0)
        passed1, out_passed = combine(
            (rows, [second(tie(m1[4], branch0), came1)]),
            (
                (2 * ROWS, width),
                [second(m0[6], out_came0), second(m1[6], out_came1, ROWS)],
            ),
        )
        left = tie(m0, passed1)
        (down_pairs,) = weight_grad(targets, down_groups([left, m1]), share, 0)
        across0, passed1, down_pairs = sync(across0, passed1, down_pairs)
        crossed1 = over_y(passed1)
        branches0 = spread(branch0, across0)
        left = tie(m0, down_pairs)
        up_high, up_low, up_keep = weight_grad(targets, up_groups([left, m1]), share)
        crossed1, branches0, up_high, up_low, up_keep = sync(
            crossed1, branches0, up_high, up_low, up_keep
        )

        up_came_high = over_x(up_high)
        down_held = over_z(down_pairs[3])
        grad_after1, branch1, sums1 = second_back(1, after1, m1[4], came1, crossed1)
        sums_two = [sums0, sums1]
        across1 = over_y(branch1)
        branches0[0] = tie(branches0[0], branch1)
        b0 = attention_back(0, branches0, q, k, v, a0[1], weights)
        across1, up_came_high, down_held, b0, out_passed = sync(
            across1, up_came_high, down_held, b0, out_passed
        )
        out_crossed = over_y(out_passed)
        branches1 = spread(branch1, across1)
        came0 = over_core(b0[6])
        up_came_low = over_x(up_low)

        def down_cells(k, held, lane):
            return [
                (0, half * units, share, units, [(down_pairs, (k, half), 0), (held, at, first)])
                for half, (at, first) in enumerate(lane)
            ]

        passed0, held = combine(
            (rows, [second(b0[5], came0)]),
            (
                (share, 3 * units),
                down_cells(2, down_held, [((0,), 0), ((1,), 0)])
                + [
                    (
                        0,
                        2 * units,
                        share,
                        units,
                        [(up_keep, (3,), 0), (up_came_high, (1,), 0)],
                    )
                ],
            ),
        )
        crossed0 = over_y(passed0)
        held = over_z(held)
        branches1[0] = tie(branches1[0], passed0)
        b1 = attention_back(1, branches1, q, k, v, a1[1], weights)
        crossed0, held, up_came_low, out_crossed, b1 = sync(
            crossed0, held, up_came_low, out_crossed, b1
        )
        backs = [b0, b1]
        came1 = over_core(b1[6])
        vector = bundle(sums_two, backs, mlps)
        vector_came = lax.ppermute(vector, "mp", [(m, m ^ 1) for m in range(4)])
        came1, vector_came, vector = sync(came1, vector_came, vector)
        vector = vector + vector_came
        vector_came = lax.ppermute(vector, "mp", [(m, m ^ 2) for m in range(4)])
        passed1, out_own, down_held, up_held = combine(
            (rows, [second(tie(b1[5], vector), came1)]),
            (
                (2 * ROWS, width),
                [
                    (
                        part * ROWS,
                        0,
                        *rows,
                        [(keep, (0,), 0), (came, (0,), 0), (out_crossed, (part,), 0)],
                    )
                    for part, (keep, came) in enumerate(((m0[6], out_came0), (m1[6], out_came1)))
                ],
            ),
            (
                (share, 2 * units),
                down_cells(1, held, [((0,), 0), ((0,), units)]),
            ),
            (
                (share, units),
                [
                    (
                        0,
                        0,
                        share,
                        units,
                        [(up_keep, (2,), 0), (up_came_high, (0,), 0), (held, (0,), 2 * units)],
                    )
                ],
            ),
        )
        crossed1 = over_y(passed1)
        down_held = over_z(down_held)
        left = tie(b0, passed1)
        lead = 3 * cols // 128 * 128
        rest = 4 * cols - lead
        firsts = weight_grad(targets, first_groups([left, b1], attended), share, lead)
        crossed1, down_held, up_held, vector, vector_came, firsts = sync(
            crossed1, down_held, up_held, vector, vector_came, firsts
        )
        first_high, first_low, first_keep, first_pairs = firsts
        vector = vector + vector_came

        def pair_cells(k, lane, held=None, first=0):
            cells = []
            for half in range(2):
                terms = [(first_pairs, (k, half), 0)]
                if held is not None:
                    terms.append((held, (0,), first + half * rest))
                cells.append((0, lane + half * rest, share, rest, terms))
            return cells

        first_came_high = over_x(first_high)
        (held_sum,) = combine(
            (
                (share, 2 * rest + units),
                pair_cells(3, 0) + [(0, 2 * rest, share, units, [(up_held, (0,), 0)])],
            )
        )
        held = over_z(held_sum)
        vector_came = lax.ppermute(vector, "dp", [(d, d ^ 2) for d in range(8)])
        own = norm_one_back(
            [
                ([(b0[5], 0), (came0, 0), (tie(crossed0, held_sum), 0)], grad_after0),
                ([(b1[5], 0), (came1, 0), (crossed1, 0)], grad_after1),
            ],
            rows_in,
            own_valid,
            gain_one,
        )
        in_across = over_y(own)
        first_came_high, held, vector_came, own = sync(first_came_high, held, vector_came, own)
        vector = vector + vector_came
        first_came_low = over_x(first_low)
        held, down_other = combine(
            (
                (share, lead + 2 * rest + units),
                [(0, 0, share, lead, [(first_keep, (3,), 0), (first_came_high, (1,), 0)])]
                + pair_cells(2, lead, held, 0)
                + [
                    (
                        0,
                        lead + 2 * rest,
                        share,
                        units,
                        [(up_keep, (1,), 0), (up_came_low, (1,), 0), (held, (0,), 2 * rest)],
                    )
                ],
            ),
            (
                (share, units),
                [(0, 0, share, units, [(down_pairs, (0, 1), 0), (down_held, (0,), units)])],
            ),
        )
        held = over_z(held)
        down_other = over_x(down_other)
        vector_came = lax.ppermute(vector, "dp", [(d, d ^ 4) for d in range(8)])
        first_came_low, held, vector_came, down_other, in_across, out_own = sync(
            first_came_low, held, vector_came, down_other, in_across, out_own
        )
        vector = vector + vector_came
        up_last = held[:, lead + 2 * rest :]
        (held,) = combine(
            (
                (share, lead + 2 * rest),
                [
                    (
                        0,
                        0,
                        share,
                        lead,
                        [(first_keep, (2,), 0), (first_came_high, (0,), 0), (held, (0,), 0)],
                    )
                ]
                + pair_cells(1, lead, held, lead),
            ),
        )
        held = over_z(held)
        vector_came = lax.ppermute(vector, "dp", [(d, d ^ 1) for d in range(8)])
        out_across = over_y(out_own)
        in_pieces = spread(own, in_across)
        input_grad = place_windows(local, in_pieces)
        held, vector_came, input_grad = sync(held, vector_came, input_grad)
        out_pieces = spread(out_own, out_across)
        block_output = write_output(local, places_all, lives_all, out_pieces)
        vector = vector + vector_came
        first_held, pair_other = combine(
            (
                (share, lead),
                [
                    (
                        0,
                        0,
                        share,
                        lead,
                        [(first_keep, (1,), 0), (first_came_low, (1,), 0), (held, (0,), 0)],
                    )
                ],
            ),
            (
                (share, rest),
                [(0, 0, share, rest, [(first_pairs, (0, 1), 0), (held, (0,), lead + rest)])],
            ),
        )
        pair_other = over_x(pair_other)
        first_held = over_z(first_held)

        def last(*values):
            out = values[0].astype(F32)
            for value in values[1:]:
                out = out + value.astype(F32)
            return out

        down_grad = last(down_pairs[0, 0], down_held[:, :units], down_other)
        up_grad = last(up_keep[0], up_came_low[0], up_last)
        first_grad = jnp.concatenate(
            [
                last(first_keep[0], first_came_low[0], first_held),
                last(first_pairs[0, 0], held[:, lead : lead + rest], pair_other),
            ],
            axis=1,
        )

    shapes = [(2, width), (4, width), (up_bias.size,), (2, width), (RELN, HD), (RELN, HD)]
    outs, at = [], 0
    flat = vector.reshape(-1)
    for shape in shapes:
        size = int(np.prod(shape))
        outs.append(flat[at : at + size].reshape(shape))
        at += size
    one_sums, two_sums, up_bias_grad, qv_bias_grad, height_grad, width_grad = outs
    shift_one_grad = one_sums[1]
    gain_one_grad = (one_sums[0] - norm_one_shift * shift_one_grad) / norm_one_gain
    qkv_grad = jnp.stack([first_grad[:, slot * cols : (slot + 1) * cols] for slot in range(3)])
    proj_grad = first_grad[:, 3 * cols :].T
    return (
        block_output,
        input_grad,
        gain_one_grad,
        shift_one_grad,
        qkv_grad,
        qv_bias_grad,
        proj_grad,
        two_sums[2],
        two_sums[0],
        two_sums[1],
        up_grad,
        up_bias_grad,
        down_grad.T,
        two_sums[3],
        height_grad,
        width_grad,
    )


def solution(mesh):
    in_specs = (
        P("dp", None),
        P("dp"),
        P("dp"),
        P(),
        P(),
        P(None, "dp", "mp"),
        P(),
        P("mp", "dp"),
        P(),
        P(),
        P(),
        P("dp", "mp"),
        P(),
        P("mp", "dp"),
        P(),
        P(),
        P(),
        P("dp", None),
    )
    out_specs = (
        P("dp", None),
        P("dp", None),
        P(),
        P(),
        P(None, "dp", "mp"),
        P(),
        P("mp", "dp"),
        P(),
        P(),
        P(),
        P("dp", "mp"),
        P(),
        P("mp", "dp"),
        P(),
        P(),
        P(),
    )
    return jax.shard_map(body, mesh=mesh, in_specs=in_specs, out_specs=out_specs, check_vma=False)
```

```python
from functools import partial

import jax
import jax.numpy as jnp
import numpy as np
from jax import lax
from jax.experimental import pallas as pl
from jax.experimental.pallas import tpu as pltpu
from jax.sharding import PartitionSpec as P

HD = 80
WIN = 14
SIDE = 64
GRID = 5
WTOK = 196
RELN = 27
ROWS = 208
SCALE = HD ** (-0.5)
EPS = 1e-06
F32 = jnp.float32
BF16 = jnp.bfloat16
ANY = pl.BlockSpec(memory_space=pl.ANY)
highest = lax.Precision.HIGHEST


def dot(left, right):
    return lax.dot_general(left, right, (((1,), (0,)), ((), ())), preferred_element_type=F32)


def dot_nt(left, right):
    return lax.dot_general(left, right, (((1,), (1,)), ((), ())), preferred_element_type=F32)


def dot_tn(left, right):
    return lax.dot_general(left, right, (((0,), (0,)), ((), ())), preferred_element_type=F32)


def whole(array):
    zeros = (0,) * len(array.shape)
    return pl.BlockSpec(array.shape, lambda *_: zeros)


def params(megabytes):
    return pltpu.CompilerParams(vmem_limit_bytes=megabytes * 2**20)


def cost(micros):
    return pl.CostEstimate(
        flops=int(micros * 0.05e9), bytes_accessed=int(micros * 1.0e4), transcendentals=0
    )


def struct(shape, dtype):
    return jax.ShapeDtypeStruct(shape, dtype)


def assemble(offsets, pieces, target, sems):
    copies = []
    for index, piece in enumerate(pieces):
        count = piece.shape[0]
        start = pl.multiple_of(offsets[index], 16)
        copies.append(
            pltpu.make_async_copy(piece, target.at[pl.ds(start, count)], sems.at[index])
        )
    for copy in copies:
        copy.start()
    for copy in copies:
        copy.wait()


def norm_parts(values):
    center = jnp.mean(values, axis=-1, keepdims=True)
    centred = values - center
    spread = jnp.mean(centred * centred, axis=-1, keepdims=True)
    rstd = lax.rsqrt(spread + EPS)
    return centred * rstd, rstd


def token_valid(spot, live):
    token = lax.broadcasted_iota(jnp.int32, (WTOK, 1), 0)
    row = (token * 9363) >> 17
    col = token - row * WIN
    high = spot // GRID * WIN
    wide = spot % GRID * WIN
    inside = (high + row < SIDE) & (wide + col < SIDE) & (live == 1)
    return jnp.where(inside, 1.0, 0.0).astype(F32)


def pad_rows(values):
    empty = jnp.zeros((ROWS - WTOK, values.shape[1]), F32)
    return jnp.concatenate([values, empty], axis=0)


def prepare_kernel(every, order, places, lives, x_ref, gain_ref, shift_ref, *outs):
    rows_ref, own_ref, normed_ref, valid_ref = outs
    step = pl.program_id(0)
    slot = order[step]
    valid = token_valid(places[slot], lives[slot])
    x = x_ref[0].astype(F32)
    xhat, _ = norm_parts(x)
    normed_ref[...] = pad_rows((xhat * gain_ref[...] + shift_ref[...]) * valid).astype(BF16)
    valid_ref[...] = pad_rows(valid)

    @pl.when(lax.rem(step, every) == 0)
    def _():
        rows_ref[...] = pad_rows(x).astype(BF16)
        own_ref[...] = pad_rows(valid)


def prepare(order, places, lives, x, gain, shift, every):
    count = order.shape[0]
    width = x.shape[2]
    window = pl.BlockSpec((1, WTOK, width), lambda i, order, *_: (order[i], 0, 0))
    block = pl.BlockSpec((ROWS, width), lambda i, *_: (i, 0))
    return pl.pallas_call(
        partial(prepare_kernel, every),
        grid_spec=pltpu.PrefetchScalarGridSpec(
            num_scalar_prefetch=3,
            grid=(count,),
            in_specs=[window, whole(gain), whole(shift)],
            out_specs=[
                pl.BlockSpec((ROWS, width), lambda i, *_: (i // every, 0)),
                pl.BlockSpec((ROWS, 1), lambda i, *_: (i // every, 0)),
                block,
                pl.BlockSpec((ROWS, 1), lambda i, *_: (i, 0)),
            ],
        ),
        out_shape=[
            struct((count // every * ROWS, width), BF16),
            struct((count // every * ROWS, 1), F32),
            struct((count * ROWS, width), BF16),
            struct((count * ROWS, 1), F32),
        ],
        compiler_params=params(63),
        cost_estimate=cost(9),
        name="prepare",
    )(order, places, lives, x, gain, shift)


def mask_kernel(order, places, lives, top_ref, grad_ref):
    slot = order[pl.program_id(0)]
    valid = token_valid(places[slot], lives[slot])
    grad_ref[...] = pad_rows(top_ref[0].astype(F32) * valid).astype(BF16)


def mask_rows(order, places, lives, top):
    count = order.shape[0]
    width = top.shape[2]
    return pl.pallas_call(
        mask_kernel,
        grid_spec=pltpu.PrefetchScalarGridSpec(
            num_scalar_prefetch=3,
            grid=(count,),
            in_specs=[pl.BlockSpec((1, WTOK, width), lambda i, order, *_: (order[i], 0, 0))],
            out_specs=pl.BlockSpec((ROWS, width), lambda i, *_: (i, 0)),
        ),
        out_shape=struct((count * ROWS, width), BF16),
        compiler_params=params(63),
        cost_estimate=cost(6),
        name="mask_rows",
    )(order, places, lives, top)


def top_rows(shape):
    return pl.BlockSpec(shape, lambda i: (0, 0))


def row_block(shape, at):
    return pl.BlockSpec(shape, lambda i: (at, 0))


def total(refs, rows):
    value = refs[0][:rows].astype(F32)
    for ref in refs[1:]:
        value = value + ref[:rows].astype(F32)
    return value


def norm_two_kernel(count, *refs):
    parts, (x_ref, bias_ref, gain_ref, shift_ref, after_ref, normed_ref) = (
        refs[:count],
        refs[count:],
    )
    rows = x_ref.shape[0]
    after = x_ref[...].astype(F32) + total(parts, rows) + bias_ref[...]
    xhat, _ = norm_parts(after)
    after_ref[...] = after
    normed_ref[...] = (xhat * gain_ref[...] + shift_ref[...]).astype(BF16)


def norm_two(parts, x, at, bias, gain, shift):
    shape = (parts[-1].shape[0], x.shape[1])
    return pl.pallas_call(
        partial(norm_two_kernel, len(parts)),
        grid=(1,),
        in_specs=[top_rows(shape)] * len(parts)
        + [row_block(shape, at), whole(bias), whole(gain), whole(shift)],
        out_specs=[top_rows(shape)] * 2,
        out_shape=[struct(shape, F32), struct(shape, BF16)],
        compiler_params=params(14),
        cost_estimate=cost(3),
        name="norm_two",
    )(*parts, x, bias, gain, shift)


def finish_kernel(count, *refs):
    parts, (after_ref, valid_ref, bias_ref, out_ref) = refs[:count], refs[count:]
    rows = after_ref.shape[0]
    branch = total(parts, rows) + bias_ref[...]
    out_ref[...] = (valid_ref[...] * (after_ref[...] + branch)).astype(BF16)


def finish(parts, after, valid, at, bias):
    return pl.pallas_call(
        partial(finish_kernel, len(parts)),
        grid=(1,),
        in_specs=[top_rows(after.shape)] * (len(parts) + 1)
        + [row_block((after.shape[0], 1), at), whole(bias)],
        out_specs=top_rows(after.shape),
        out_shape=struct(after.shape, BF16),
        compiler_params=params(14),
        cost_estimate=cost(2.5),
        name="finish",
    )(*parts, after, valid, bias)


def norm_back(upstream, xhat, rstd, gain):
    weighted = upstream * gain
    inner = jnp.mean(weighted * xhat, axis=-1, keepdims=True)
    level = jnp.mean(weighted, axis=-1, keepdims=True)
    return rstd * (weighted - level - xhat * inner)


def norm_two_back_kernel(count, *refs):
    parts = refs[:count]
    after_ref, top_ref, gain_ref, grad_ref, branch_ref, sums_ref = refs[count:]
    rows = after_ref.shape[0]
    upstream = total(parts, rows)
    xhat, rstd = norm_parts(after_ref[...])
    top = top_ref[...].astype(F32)
    grad = top + norm_back(upstream, xhat, rstd, gain_ref[...])
    branch = grad.astype(BF16)
    grad_ref[...] = grad
    branch_ref[...] = branch
    sums_ref[0:1] = jnp.sum(upstream * xhat, axis=0, keepdims=True)
    sums_ref[1:2] = jnp.sum(upstream, axis=0, keepdims=True)
    sums_ref[2:3] = jnp.sum(branch.astype(F32), axis=0, keepdims=True)
    sums_ref[3:4] = jnp.sum(top, axis=0, keepdims=True)


def norm_two_back(parts, after, top, at, gain):
    sums = struct((4, after.shape[1]), F32)
    return pl.pallas_call(
        partial(norm_two_back_kernel, len(parts)),
        grid=(1,),
        in_specs=[top_rows(after.shape)] * (len(parts) + 1)
        + [row_block(after.shape, at), whole(gain)],
        out_specs=[top_rows(after.shape)] * 2 + [whole(sums)],
        out_shape=[struct(after.shape, F32), struct(after.shape, BF16), sums],
        compiler_params=params(14),
        cost_estimate=cost(4),
        name="norm_two_back",
    )(*parts, after, top, gain)


def norm_one_back_kernel(counts, *refs):
    x_ref, valid_ref, gain_ref, out_ref = refs[-4:]
    at = 0
    for part, count in enumerate(counts):
        parts, grad_ref = refs[at : at + count], refs[at + count]
        at += count + 1
        rows = slice(part * ROWS, part * ROWS + ROWS)
        upstream = total(parts, ROWS) * valid_ref[rows]
        xhat, rstd = norm_parts(x_ref[rows].astype(F32))
        grad = grad_ref[...] + norm_back(upstream, xhat, rstd, gain_ref[...])
        out_ref[rows] = grad.astype(BF16)


def norm_one_back(windows, x, valid, gain):
    shape = (ROWS, x.shape[1])
    operands, specs = [], []
    for parts, grad in windows:
        operands += [part[0] for part in parts] + [grad]
        specs += [
            pl.BlockSpec(shape, lambda i, at=at: (at, 0)) for at in (part[1] for part in parts)
        ]
        specs.append(whole(grad))
    return pl.pallas_call(
        partial(norm_one_back_kernel, [len(parts) for parts, _ in windows]),
        grid=(1,),
        in_specs=specs + [whole(x), whole(valid), whole(gain)],
        out_specs=whole(x),
        out_shape=struct(x.shape, BF16),
        compiler_params=params(20),
        cost_estimate=cost(3.5 * len(windows)),
        name="norm_one_back",
    )(*operands, x, valid, gain)


def qkv_kernel(count, cols, offsets, *refs):
    pieces = refs[:count]
    x_ref, bias_ref, q_ref, k_ref, v_ref, w_ref, sems = refs[count:]
    wide = q_ref.shape[1]

    @pl.when(pl.program_id(0) == 0)
    def _():
        assemble(offsets, pieces, w_ref, sems)

    result = (dot(x_ref[...], w_ref[:, wide:]) + bias_ref[...]).astype(BF16)
    for slot, ref in enumerate((q_ref, k_ref, v_ref)):
        ref[:, :cols] = result[:, slot * cols : (slot + 1) * cols]
        if wide > cols:
            ref[:, cols:] = jnp.zeros((ref.shape[0], wide - cols), BF16)


def project(offsets, pieces, x, bias, cols, wide):
    rows, width = x.shape
    step = 2 * ROWS
    block = pl.BlockSpec((step, wide), lambda i, *_: (i, 0))
    total_cols = wide + 3 * cols
    return pl.pallas_call(
        partial(qkv_kernel, len(pieces), cols),
        grid_spec=pltpu.PrefetchScalarGridSpec(
            num_scalar_prefetch=1,
            grid=(rows // step,),
            in_specs=[ANY] * len(pieces)
            + [pl.BlockSpec((step, width), lambda i, *_: (i, 0)), whole(bias)],
            out_specs=[block, block, block, pl.BlockSpec((width, total_cols), lambda i, *_: (0, 0))],
            scratch_shapes=[pltpu.SemaphoreType.DMA((len(pieces),))],
        ),
        out_shape=[struct((rows, wide), BF16)] * 3 + [struct((width, total_cols), BF16)],
        compiler_params=params(28),
        cost_estimate=cost(14),
        name="qkv",
    )(offsets, *pieces, x, bias)


def head_spans(heads, wide):
    spans = []
    for head in range(heads):
        first, last = head * HD, head * HD + HD
        low = first // 128 * 128
        high = min((last + 127) // 128 * 128, wide)
        spans.append((low, high, first, last))
    return spans


def lane_mask(span):
    low, high, first, last = span
    lane = lax.broadcasted_iota(jnp.int32, (1, high - low), 1) + low
    return jnp.where((lane >= first) & (lane < last), 1.0, 0.0).astype(BF16)


def shift_counts():
    token = lax.broadcasted_iota(jnp.int32, (ROWS, 128), 0)
    row = (token * 9363) >> 17
    col = token - row * WIN
    return jnp.maximum(WIN - 1 - row, 0), WIN - 1 - col


def shift_lanes(values, counts, back):
    for step in (1, 2, 4, 8):
        moved = pltpu.roll(values, step if back else 128 - step, 1)
        values = jnp.where((counts & step) != 0, moved, values)
    return values


def lane_kind():
    lane = lax.broadcasted_iota(jnp.int32, (ROWS, 128), 1) & 31
    return lane < WIN, (lane >= 16) & (lane < 16 + WIN), lane == 31


def split_two(values):
    high = values.astype(BF16)
    return high, (values - high.astype(F32)).astype(BF16)


def bias_operand(q, rel_high, rel_low, counts):
    table = (dot(q, rel_high) + dot(q, rel_low)) * (1.0 / SCALE)
    by_row = shift_lanes(table[:, :128], counts[0], False)
    by_col = shift_lanes(table[:, 128:], counts[1], False)
    is_row, is_col, is_last = lane_kind()
    packed = jnp.where(
        is_row, by_row, jnp.where(is_col, by_col, jnp.where(is_last, 1.0, 0.0))
    )
    high, low = split_two(packed)
    return jnp.concatenate([high, low], axis=1)


def add_lanes(parts, values, span):
    low, high = span[0], span[1]
    for index in range(low // 128, high // 128):
        piece = values[:, index * 128 - low : index * 128 - low + 128]
        parts[index] = piece if parts[index] is None else parts[index] + piece


def attend_kernel(heads, split, q_ref, k_ref, v_ref, rh_ref, rl_ref, mark_ref, w_ref, *outs):
    mixed_ref, shares_ref = outs[:2]
    q, k, v = q_ref[...], k_ref[...], v_ref[...]
    wide = q.shape[1]
    bias = bias_operand(q, rh_ref[...], rl_ref[...], shift_counts())
    parts = [None] * (wide // 128)
    for head, span in enumerate(head_spans(heads, wide)):
        mask = lane_mask(span)
        cut = slice(span[0], span[1])
        scores = dot_nt(
            jnp.concatenate([q[:, cut], bias], axis=1),
            jnp.concatenate([k[:, cut] * mask, mark_ref[head]], axis=1),
        )
        top = jnp.max(scores, axis=-1, keepdims=True)
        shifted = jnp.exp(SCALE * (scores - top))
        norm = jnp.sum(shifted, axis=-1, keepdims=True)
        shares = (shifted * (1.0 / norm)).astype(BF16)
        shares_ref[:, head * 256 : head * 256 + ROWS] = shares
        add_lanes(parts, dot(shares, v[:, cut] * mask), span)
    mixed = jnp.concatenate(parts, axis=1).astype(BF16)
    cols = heads * HD
    mixed_ref[...] = mixed[:, :cols]
    branch = dot_nt(mixed, w_ref[...]).astype(BF16)
    if split:
        keep_ref, send_ref = outs[2:]
        step = pl.program_id(0)

        @pl.when(step < split)
        def _():
            send_ref[...] = branch

        @pl.when(step >= split)
        def _():
            keep_ref[...] = branch
    else:
        outs[2][...] = branch


def split_specs(windows, split, width):
    rows = ROWS * (windows - split)
    if not split:
        return [pl.BlockSpec((ROWS, width), lambda i: (i, 0))], [struct((rows, width), BF16)]
    return (
        [
            pl.BlockSpec((ROWS, width), lambda i: (jnp.maximum(i - split, 0), 0)),
            pl.BlockSpec((ROWS, width), lambda i: (jnp.minimum(i, split - 1), 0)),
        ],
        [struct((rows, width), BF16), struct((ROWS * split, width), BF16)],
    )


def attend(heads, part, windows, split, q, k, v, rel_high, rel_low, marks, weights):
    wide = q.shape[1]
    width = weights.shape[0]

    def place(i):
        return (i + split) % windows if split else i

    block = pl.BlockSpec((ROWS, wide), lambda i: (part * windows + place(i), 0))
    specs, shapes = split_specs(windows, split, width)
    return pl.pallas_call(
        partial(attend_kernel, heads, split),
        grid=(windows,),
        in_specs=[
            block,
            block,
            block,
            whole(rel_high),
            whole(rel_low),
            whole(marks),
            pl.BlockSpec((width, wide), lambda i: (0, 0)),
        ],
        out_specs=[
            pl.BlockSpec((ROWS, heads * HD), lambda i: (place(i), 0)),
            pl.BlockSpec((ROWS, heads * 256), lambda i: (place(i), 0)),
        ]
        + specs,
        out_shape=[
            struct((windows * ROWS, heads * HD), BF16),
            struct((windows * ROWS, heads * 256), BF16),
        ]
        + shapes,
        compiler_params=params(16),
        cost_estimate=cost(13.5),
        name="attend",
    )(q, k, v, rel_high, rel_low, marks, weights)


def attend_back_kernel(heads, windows, split, count, *refs):
    pieces = refs[:count]
    q_ref, k_ref, v_ref, shares_ref, rh_ref, mark_ref, w_ref = refs[count : count + 7]
    normed_ref, valid_ref = refs[count + 7 : count + 9]
    grads_ref, branch_ref, rel_ref, sum_ref, norm_ref = refs[count + 9 : count + 14]
    outs = refs[count + 14 :]
    step = pl.program_id(0)

    @pl.when(step == 0)
    def _():
        start = 0
        for piece in pieces:
            branch_ref[start : start + piece.shape[0]] = piece[...]
            start += piece.shape[0]
        rel_ref[...] = jnp.zeros(rel_ref.shape, F32)
        sum_ref[...] = jnp.zeros(sum_ref.shape, F32)
        norm_ref[...] = jnp.zeros(norm_ref.shape, F32)

    place = lax.rem(step + split, windows) if split else step
    q, k, v = q_ref[...], k_ref[...], v_ref[...]
    wide = q.shape[1]
    top = branch_ref[pl.ds(pl.multiple_of(place * ROWS, 16), ROWS), :]
    grad_mixed = dot(top, w_ref[:, :wide]).astype(BF16)
    grad_q, grad_k, grad_v = ([None] * (wide // 128) for _ in range(3))
    grad_bias = None
    for head, span in enumerate(head_spans(heads, wide)):
        mask = lane_mask(span)
        cut = slice(span[0], span[1])
        size = span[1] - span[0]
        upper = grad_mixed[:, cut]
        rounded = shares_ref[:, head * 256 : head * 256 + ROWS]
        shares = rounded.astype(F32)
        weighted = shares * dot_nt(upper, v[:, cut] * mask)
        inner = jnp.sum(weighted, axis=-1, keepdims=True)
        grad_scores = (weighted - shares * inner).astype(BF16)
        add_lanes(grad_v, dot_tn(rounded, upper * mask), span)
        both = dot(
            grad_scores,
            jnp.concatenate([k[:, cut] * mask, mark_ref[head][:, :128]], axis=1),
        )
        add_lanes(grad_q, both[:, :size], span)
        part = both[:, size:]
        grad_bias = part if grad_bias is None else grad_bias + part
        add_lanes(grad_k, dot_tn(grad_scores, q[:, cut] * mask), span)
    counts = shift_counts()
    is_row, is_col, _ = lane_kind()
    by_row = shift_lanes(jnp.where(is_row, grad_bias, 0.0), counts[0], True)
    by_col = shift_lanes(jnp.where(is_col, grad_bias, 0.0), counts[1], True)
    packed = jnp.concatenate([by_row, by_col], axis=1).astype(BF16)
    extra = dot_nt(packed, rh_ref[...])
    rel_ref[...] += dot_tn(packed, q)
    grad_q = (SCALE * jnp.concatenate(grad_q, axis=1) + extra).astype(BF16)
    grad_k = (SCALE * jnp.concatenate(grad_k, axis=1)).astype(BF16)
    grad_v = jnp.concatenate(grad_v, axis=1).astype(BF16)
    cols = heads * HD
    for slot, grad in enumerate((grad_q, grad_k, grad_v)):
        grads_ref[:, slot * cols : (slot + 1) * cols] = grad[:, :cols]
    packed_grads = grads_ref[...]
    sum_ref[...] += jnp.sum(packed_grads.astype(F32), axis=0, keepdims=True)
    partial_sum = dot_nt(packed_grads, w_ref[:, wide:])
    norm_ref[0:1] += jnp.sum(partial_sum * normed_ref[...].astype(F32), axis=0, keepdims=True)
    norm_ref[1:2] += jnp.sum(partial_sum * valid_ref[...], axis=0, keepdims=True)
    result = partial_sum.astype(BF16)
    if split:
        keep_ref, send_ref = outs

        @pl.when(step < split)
        def _():
            send_ref[...] = result

        @pl.when(step >= split)
        def _():
            keep_ref[...] = result
    else:
        outs[0][...] = result


def attend_back(
    heads, part, windows, split, pieces, q, k, v, shares, rel_high, marks, weights, normed, valid
):
    wide = q.shape[1]
    width = weights.shape[0]

    def place(i):
        return (i + split) % windows if split else i

    block = pl.BlockSpec((ROWS, wide), lambda i: (part * windows + place(i), 0))
    specs, shapes = split_specs(windows, split, width)
    rows = windows * ROWS
    branch = struct((rows, width), BF16)
    rel = struct((256, wide), F32)
    sums = struct((1, 3 * heads * HD), F32)
    norms = struct((2, width), F32)
    return pl.pallas_call(
        partial(attend_back_kernel, heads, windows, split, len(pieces)),
        grid=(windows,),
        in_specs=[whole(piece) for piece in pieces]
        + [
            block,
            block,
            block,
            pl.BlockSpec((ROWS, heads * 256), lambda i: (place(i), 0)),
            whole(rel_high),
            whole(marks),
            whole(weights),
            pl.BlockSpec((ROWS, width), lambda i: (part * windows + place(i), 0)),
            pl.BlockSpec((ROWS, 1), lambda i: (part * windows + place(i), 0)),
        ],
        out_specs=[
            pl.BlockSpec((ROWS, 3 * heads * HD), lambda i: (place(i), 0)),
            whole(branch),
            whole(rel),
            whole(sums),
            whole(norms),
        ]
        + specs,
        out_shape=[struct((rows, 3 * heads * HD), BF16), branch, rel, sums, norms] + shapes,
        compiler_params=params(28),
        cost_estimate=cost(18.5),
        name="attend_back",
    )(*pieces, q, k, v, shares, rel_high, marks, weights, normed, valid)


def mlp_kernel(count, weights, split, offsets, *refs):
    pieces = refs[:count]
    weight_pieces = refs[count : count + weights]
    refs = refs[count + weights :]
    after_any, top_ref, bias_ref, down_bias_ref = refs[:4]
    active_ref, hidden_ref, normed_any, sum_ref = refs[4:8]
    outs = refs[8 : 12 if split else 10]
    up, down, normed_ref, after_ref, send_ref, out_send_ref, sems, row_sems = refs[len(outs) + 8 :]
    step = pl.program_id(0)
    steps = pl.num_programs(0)
    block = top_ref.shape[0]
    units = up.shape[1]
    copies = []
    for half, target in enumerate((down, up)):
        copies.append([])
        for index, piece in enumerate(weight_pieces):
            rows = piece.shape[0]
            start = pl.multiple_of(offsets[index], 16)
            copies[half].append(
                pltpu.make_async_copy(
                    piece.at[:, half * units : (half + 1) * units],
                    target.at[pl.ds(start, rows)],
                    sems.at[half, index],
                )
            )
    row_copies, start = [], 0
    for index, piece in enumerate(pieces):
        rows = piece.shape[0]
        row_copies.append(
            pltpu.make_async_copy(
                piece, normed_ref.at[pl.ds(start, rows)], row_sems.at[index]
            )
        )
        start += rows
    normed_out = pltpu.make_async_copy(normed_ref, normed_any, row_sems.at[count])
    after_in = pltpu.make_async_copy(after_any, after_ref, row_sems.at[count + 1])
    if split:
        send_out = pltpu.make_async_copy(send_ref, outs[1], row_sems.at[count + 2])
        out_send_out = pltpu.make_async_copy(out_send_ref, outs[3], row_sems.at[count + 3])

    @pl.when(step == 0)
    def _():
        for copy in row_copies + copies[1] + copies[0]:
            copy.start()
        after_in.start()
        sum_ref[...] = jnp.zeros(sum_ref.shape, F32)
        for copy in row_copies + copies[1]:
            copy.wait()
        normed_out.start()

    place = 1 - step if split else step
    normed = normed_ref[pl.ds(pl.multiple_of(place * block, 16), block), :]
    hidden = dot(normed, up[...]) + bias_ref[...]

    @pl.when(step == 0)
    def _():
        for copy in copies[0]:
            copy.wait()

    half = 0.5 * (1.0 + lax.erf(hidden * (0.5**0.5)))
    slope = half + hidden * jnp.exp(-0.5 * hidden * hidden) * float((2.0 * np.pi) ** -0.5)
    active = (hidden * half).astype(BF16)
    active_ref[...] = active
    grad = (dot(top_ref[...], down[...]) * slope).astype(BF16)
    hidden_ref[...] = grad
    sum_ref[...] += jnp.sum(grad.astype(F32), axis=0, keepdims=True)
    back = dot_nt(grad, up[...]).astype(BF16)
    result = dot_nt(active, down[...])
    if split:

        @pl.when(step == 0)
        def _():
            send_ref[...] = back
            out_send_ref[...] = result.astype(BF16)
            send_out.start()
            out_send_out.start()
            after_in.wait()

        @pl.when(step == 1)
        def _():
            outs[0][...] = back
            own = result[:ROWS] + after_ref[...] + down_bias_ref[...]
            outs[2][:ROWS] = own.astype(BF16)
            outs[2][ROWS:] = result[ROWS:].astype(BF16)
            send_out.wait()
            out_send_out.wait()
    else:
        outs[0][...] = back
        outs[1][...] = result.astype(BF16)

        @pl.when(step == 0)
        def _():
            after_in.wait()

    @pl.when(step == steps - 1)
    def _():
        normed_out.wait()


def mlp(offsets, pieces, weight_pieces, top, part, bias, after, down_bias, split):
    rows = sum(piece.shape[0] for piece in pieces)
    width = pieces[0].shape[1]
    units = weight_pieces[0].shape[1] // 2
    block = 2 * ROWS
    blocks = rows // block
    normed = struct((rows, width), BF16)
    sums = struct((1, units), F32)

    def place(i):
        return 1 - i if split else i

    wide = pl.BlockSpec((block, units), lambda i, *_: (place(i), 0))
    back = struct((block, width), BF16)
    if split:
        back_specs, back_shapes = [whole(back), ANY] * 2, [back] * 4
    else:
        back_specs = [pl.BlockSpec((block, width), lambda i, *_: (i, 0))] * 2
        back_shapes = [normed] * 2
    return pl.pallas_call(
        partial(mlp_kernel, len(pieces), len(weight_pieces), split),
        grid_spec=pltpu.PrefetchScalarGridSpec(
            num_scalar_prefetch=1,
            grid=(blocks,),
            in_specs=[ANY] * (len(pieces) + len(weight_pieces) + 1)
            + [
                pl.BlockSpec((block, width), lambda i, *_: (part * blocks + place(i), 0)),
                whole(bias),
                whole(down_bias),
            ],
            out_specs=[wide, wide, ANY, whole(sums)] + back_specs,
            scratch_shapes=[
                pltpu.VMEM((width, units), BF16),
                pltpu.VMEM((width, units), BF16),
                pltpu.VMEM((rows, width), BF16),
                pltpu.VMEM(after.shape, F32),
                pltpu.VMEM((block, width), BF16),
                pltpu.VMEM((block, width), BF16),
                pltpu.SemaphoreType.DMA((2, len(weight_pieces))),
                pltpu.SemaphoreType.DMA((len(pieces) + 4,)),
            ],
        ),
        out_shape=[struct((rows, units), BF16)] * 2 + [normed, sums] + back_shapes,
        compiler_params=params(48),
        cost_estimate=cost(21),
        name="mlp",
    )(offsets, *pieces, *weight_pieces, after, top, bias, down_bias)


SEND_PARTS = {2: ((2, 3), (0, 1)), 3: ((3,), (1, 2), (0,))}


def weight_grad_kernel(sizes, share, sends, targets, *refs):
    count = 2 * sum(sizes)
    operands = refs[:count]
    outs, (result, sems) = refs[count:-2], refs[-2:]
    keep_ref = outs[sends] if sends else None
    pair_ref = None if sends else outs[0]
    lead = keep_ref.shape[2] if sends else 0
    step = pl.program_id(0)
    steps = pl.num_programs(0)
    chunk = operands[0].shape[1]
    pieces = chunk // share
    base = pl.multiple_of(step * chunk, 16)
    at, first = 0, 0
    for size in sizes:
        value = None
        for _ in range(size):
            left, right = operands[at], operands[at + 1]
            at += 2
            term = dot_tn(left[...], right[...])
            value = term if value is None else value + term
        span = value.shape[1]
        result[pl.ds(base, chunk), first : first + span] = value.astype(BF16)
        first += span

    def copy(index, out, slot):
        return pltpu.make_async_copy(
            result.at[pl.ds(pl.multiple_of(index * share, 16), share), pl.ds(0, lead)],
            out.at[slot],
            sems.at[0, index],
        )

    def pair_copy(index, slot):
        return pltpu.make_async_copy(
            result.at[
                pl.ds(pl.multiple_of(index * share, 16), share),
                pl.ds(lead, result.shape[1] - lead),
            ],
            pair_ref.at[lax.rem(slot, 4), 1 - slot // 4],
            sems.at[1, index],
        )

    for piece in range(pieces):
        index = step * pieces + piece
        slot = targets[index]

        if lead:

            for out, slots in zip(outs, SEND_PARTS[sends]):

                @pl.when((slot >= slots[0]) & (slot <= slots[-1]))
                def _(out=out, slots=slots):
                    copy(index, out, slot - slots[0]).start()

            @pl.when(slot >= 4)
            def _():
                copy(index, keep_ref, slot - 4).start()

        if pair_ref is not None:
            pair_copy(index, slot).start()

    @pl.when(step == steps - 1)
    def _():
        for index in range(8):
            if lead:
                copy(index, keep_ref, 0).wait()
            if pair_ref is not None:
                pair_copy(index, 0).wait()


def plain_grad_kernel(sizes, *refs):
    count = 2 * sum(sizes)
    operands, out_ref = refs[:count], refs[count]
    at, first = 0, 0
    for size in sizes:
        value = None
        for _ in range(size):
            left, right = operands[at], operands[at + 1]
            at += 2
            term = dot_tn(left[...], right[...])
            value = term if value is None else value + term
        span = value.shape[1]
        out_ref[:, first : first + span] = value.astype(BF16)
        first += span


def weight_grad(targets, groups, share, sends=0):
    operands, specs = [], []
    chunk = 640 if targets is not None else 256
    total_cols = 0
    for group in groups:
        for left, at, rows, right in group:
            operands += [left, right]
            specs.append(pl.BlockSpec((rows, chunk), lambda i, *_, at=at: (at, i)))
            specs.append(whole(right))
        total_cols += group[0][3].shape[1]
    width = operands[0].shape[1]
    sizes = [len(group) for group in groups]
    if targets is None:
        return [
            pl.pallas_call(
                partial(plain_grad_kernel, sizes),
                grid=(width // chunk,),
                in_specs=specs,
                out_specs=pl.BlockSpec((chunk, total_cols), lambda i: (i, 0)),
                out_shape=struct((width, total_cols), BF16),
                compiler_params=params(36),
                cost_estimate=cost(13),
        name="weight_grad",
            )(*operands)
        ]
    if sends:
        counts = [len(slots) for slots in SEND_PARTS[sends]] + [4]
        shapes = [struct((count, share, total_cols), BF16) for count in counts]
    else:
        shapes = [struct((4, 2, share, total_cols), BF16)]
    return pl.pallas_call(
        partial(weight_grad_kernel, sizes, share, sends),
        grid_spec=pltpu.PrefetchScalarGridSpec(
            num_scalar_prefetch=1,
            grid=(width // chunk,),
            in_specs=specs,
            out_specs=[ANY] * len(shapes),
            scratch_shapes=[
                pltpu.VMEM((width, total_cols), BF16),
                pltpu.SemaphoreType.DMA((2, 8)),
            ],
        ),
        out_shape=shapes,
        compiler_params=params(36),
        cost_estimate=cost(13),
        name="weight_grad",
    )(targets, *operands)


def combine_kernel(layout, *refs):
    outs = refs[len(refs) - len(layout) :]
    at = 0
    for cells, out in zip(layout, outs):
        for row, lane, rows, lanes, terms in cells:
            value = None
            for lead, first in terms:
                term = refs[at][(0,) * lead + (slice(None), slice(first, first + lanes))]
                at += 1
                value = term.astype(F32) if value is None else value + term.astype(F32)
            out[row : row + rows, lane : lane + lanes] = value.astype(BF16)


def combine(*outs):
    operands, specs, layout = [], [], []
    for _, cells in outs:
        layout.append([])
        for row, lane, rows, lanes, terms in cells:
            places = []
            for array, index, first in terms:
                lead = array.ndim - 2
                block = (1,) * lead + (rows, array.shape[-1])
                place = tuple(index) + (0,) * (array.ndim - len(index))
                operands.append(array)
                specs.append(pl.BlockSpec(block, lambda i, place=place: place))
                places.append((lead, first))
            layout[-1].append((row, lane, rows, lanes, places))
    shapes = [struct(shape, BF16) for shape, _ in outs]
    return pl.pallas_call(
        partial(combine_kernel, layout),
        grid=(1,),
        in_specs=specs,
        out_specs=[whole(shape) for shape in shapes],
        out_shape=shapes,
        compiler_params=params(16),
        cost_estimate=cost(2),
        name="combine",
    )(*operands)


def place_kernel(order, *refs):
    pieces, out_ref = refs[:4], refs[4]
    for me in range(4):

        @pl.when(order[0] == me)
        def _(me=me):
            for part in range(pieces[0].shape[0] // ROWS):
                for index, step in enumerate((0, 2, 1, 3)):
                    start = (4 * part + (me ^ step)) * WTOK
                    value = pieces[index][part * ROWS : part * ROWS + WTOK]
                    out_ref[start : start + WTOK] = value.astype(F32)


def place_windows(order, pieces):
    height, width = pieces[0].shape
    rows = height // ROWS * 4 * WTOK
    lanes = width // 2
    return pl.pallas_call(
        place_kernel,
        grid_spec=pltpu.PrefetchScalarGridSpec(
            num_scalar_prefetch=1,
            grid=(2,),
            in_specs=[pl.BlockSpec((height, lanes), lambda i, *_: (0, i))] * 4,
            out_specs=pl.BlockSpec((rows, lanes), lambda i, *_: (0, i)),
        ),
        out_shape=struct((rows, width), F32),
        compiler_params=params(32),
        cost_estimate=cost(7),
        name="place_windows",
    )(order, *pieces)


def output_kernel(order, places, lives, *refs):
    pieces, out_ref, buffer = refs[:4], refs[4], refs[5]
    for me in range(4):

        @pl.when(order[0] == me)
        def _(me=me):
            for part in range(pieces[0].shape[0] // ROWS):
                for index, step in enumerate((0, 2, 1, 3)):
                    slot = 4 * part + (me ^ step)
                    value = pieces[index][part * ROWS : part * ROWS + WTOK].astype(F32)
                    value = value * token_valid(places[slot], lives[slot])
                    buffer[slot * WTOK : (slot + 1) * WTOK] = value

    out_ref[...] = buffer[...].astype(BF16)


def write_output(order, places, lives, pieces):
    height, width = pieces[0].shape
    rows = height // ROWS * 4 * WTOK
    lanes = width // 2
    return pl.pallas_call(
        output_kernel,
        grid_spec=pltpu.PrefetchScalarGridSpec(
            num_scalar_prefetch=3,
            grid=(2,),
            in_specs=[pl.BlockSpec((height, lanes), lambda i, *_: (0, i))] * 4,
            out_specs=pl.BlockSpec((rows, lanes), lambda i, *_: (0, i)),
            scratch_shapes=[pltpu.VMEM((rows, lanes), F32)],
        ),
        out_shape=struct((rows, width), BF16),
        compiler_params=params(32),
        cost_estimate=cost(7),
        name="write_output",
    )(order, places, lives, *pieces)


def key_marks(heads):
    marks = np.zeros((heads, ROWS, 256), np.float32)
    for head in range(heads):
        for token in range(WTOK):
            for half in (0, 128):
                marks[head, token, half + head * 32 + token // WIN] = 1.0
                marks[head, token, half + head * 32 + 16 + token % WIN] = 1.0
        marks[head, WTOK:, head * 32 + 31] = -1e30
    return marks.astype(BF16)


def rel_operand(rel_height, rel_width, heads, wide):
    high = rel_height[::-1].T
    flat = rel_width[::-1].T
    lanes = jnp.zeros((wide, 256), F32)

    def spread(block, row, lane):
        below = wide - row - HD
        return jnp.pad(block, ((row, below), (lane, 256 - lane - block.shape[1])))

    for head in range(heads):
        first = head * 32 + 16
        fit = min(RELN, 128 - first)
        lanes = lanes + spread(high, head * HD, head * 32)
        lanes = lanes + spread(flat[:, :fit], head * HD, 128 + first)
        if fit < RELN:
            lanes = lanes + spread(flat[:, fit:], head * HD, 128)
    return split_two(lanes)


def rel_result(sums, heads):
    high = jnp.zeros((RELN, HD), F32)
    flat = jnp.zeros((RELN, HD), F32)
    for head in range(heads):
        cols = sums[:, head * HD : head * HD + HD]
        high = high + cols[head * 32 : head * 32 + RELN]
        rolled = jnp.concatenate([cols[128:], cols[128:]], axis=0)
        flat = flat + rolled[head * 32 + 16 : head * 32 + 16 + RELN]
    return high[::-1], flat[::-1]


def add_all(values):
    out = values[0]
    for value in values[1:]:
        out = out + value
    return out


def tie(value, *others):
    return lax.optimization_barrier((value,) + others)[0]


def sync(*values):
    return lax.optimization_barrier(values)


def body(
    block_input,
    window_place,
    slot_live,
    norm_one_gain,
    norm_one_shift,
    qkv_weight,
    qv_bias,
    proj_weight,
    proj_bias,
    norm_two_gain,
    norm_two_shift,
    up_weight,
    up_bias,
    down_weight,
    down_bias,
    rel_height,
    rel_width,
    cotangent,
):
    data_parts = lax.axis_size("dp")
    model_parts = lax.axis_size("mp")
    data_index = lax.axis_index("dp")
    model_index = lax.axis_index("mp")
    width = block_input.shape[1]
    share = qkv_weight.shape[1]
    cols = qkv_weight.shape[2]
    heads = cols // HD
    wide = (cols + 127) // 128 * 128
    units = up_weight.shape[1]
    slots = window_place.shape[0]
    rings = data_parts == 8 and model_parts == 4 and slots == 8
    padded = (slots + model_parts - 1) // model_parts * model_parts
    halves = padded // 4 if rings else 1
    windows = padded // halves
    split = 2 if rings else 0
    part_rows = windows * ROWS
    own_rows = part_rows // model_parts

    if rings:
        depth, side = data_index // 2, data_index % 2
        y_bit, core_bit = model_index // 2, model_index % 2
        over_x = partial(lax.ppermute, axis_name="dp", perm=[(d, d ^ 1) for d in range(8)])
        over_z = partial(lax.ppermute, axis_name="dp", perm=[(d, (d + 2) % 8) for d in range(8)])
        over_y = partial(lax.ppermute, axis_name="mp", perm=[(m, m ^ 2) for m in range(4)])
        over_core = partial(lax.ppermute, axis_name="mp", perm=[(m, m ^ 1) for m in range(4)])

    def gather(piece):
        return [lax.all_gather(piece, "dp", axis=0, tiled=True)]

    if rings:
        offsets = []
        for back in range(4):
            behind = (depth - back) % 4
            offsets += [share * (2 * behind + side), share * (2 * behind + 1 - side)]
        offsets = jnp.stack(offsets).astype(jnp.int32)
    else:
        offsets = jnp.zeros((1,), jnp.int32)

    def scatter(parts):
        return lax.psum_scatter(parts[0], "dp", scatter_dimension=0, tiled=True).astype(F32)

    def rows_scatter(parts):
        return [lax.psum_scatter(parts[0], "mp", scatter_dimension=0, tiled=True)]

    def rows_gather(own):
        return [lax.all_gather(own, "mp", axis=0, tiled=True)]

    def own_slice(array):
        rows = array.shape[0] // model_parts
        return lax.dynamic_slice_in_dim(array, model_index * rows, rows, 0)

    first_piece = jnp.concatenate(
        [
            jnp.pad(proj_weight.T, ((0, 0), (0, wide - cols))),
            qkv_weight[0],
            qkv_weight[1],
            qkv_weight[2],
        ],
        axis=1,
    )
    other_piece = jnp.concatenate([down_weight.T, up_weight], 1)

    row = lambda v: v.reshape(1, -1)
    gain_one, shift_one = row(norm_one_gain), row(norm_one_shift)
    gain_two, shift_two = row(norm_two_gain), row(norm_two_shift)
    bias_local = lax.dynamic_slice_in_dim(qv_bias, model_index * cols, cols, 1)
    bias_qkv = row(jnp.stack([bias_local[0], jnp.zeros_like(bias_local[0]), bias_local[1]]))
    up_local = row(lax.dynamic_slice_in_dim(up_bias, model_index * units, units, 0))
    rel_high, rel_low = rel_operand(rel_height, rel_width, heads, wide)
    marks = jnp.asarray(key_marks(heads))

    steps = (0, 2, 1, 3)
    if rings:
        local = [model_index ^ step for step in steps]
        places = [4 * part + spot for part in range(halves) for spot in local]
    else:
        local = [jnp.int32(spot) for spot in range(windows)]
        places = local
    local = jnp.stack(local).astype(jnp.int32)
    places = jnp.stack(places).astype(jnp.int32)
    if rings:
        targets = []
        for d in range(8):
            ahead = (d // 2 - depth) % 4
            targets.append(ahead + jnp.where(d % 2 == side, 4, 0))
        targets = jnp.stack(targets).astype(jnp.int32)
    else:
        targets = None

    def by_window(array):
        array = array.reshape((slots, WTOK) + array.shape[1:])
        return jnp.pad(array, [(0, padded - slots)] + [(0, 0)] * (array.ndim - 1))

    places_all = jnp.pad(window_place, (0, padded - slots))
    lives_all = jnp.pad(slot_live, (0, padded - slots))
    blocks = [(part, part_rows) for part in range(halves)]

    def start(x):
        every = 4 if rings else 1
        return prepare(places, places_all, lives_all, x, gain_one, shift_one, every)

    def masked(top):
        return mask_rows(places, places_all, lives_all, top)

    def attention(part, q, k, v, weights):
        return attend(heads, part, windows, split, q, k, v, rel_high, rel_low, marks, weights)

    def attention_back(part, pieces, q, k, v, shares, weights):
        return attend_back(
            heads,
            part,
            windows,
            split,
            pieces,
            q,
            k,
            v,
            shares,
            rel_high,
            marks,
            weights,
            normed,
            valid,
        )

    def down_groups(mlps):
        return [[(grad_top, *blocks[i], mlps[i][0]) for i in range(halves)]]

    def up_groups(mlps):
        return [[(mlps[i][2], 0, part_rows, mlps[i][1]) for i in range(halves)]]

    def first_groups(backs, attended):
        return [
            [(normed, *blocks[i], backs[i][0]) for i in range(halves)],
            [(backs[i][1], 0, part_rows, attended[i][0]) for i in range(halves)],
        ]

    def bundle(sums_two, backs, mlps):
        qv_sums = add_all([item[3] for item in backs]).reshape(3, cols)[0::2]
        rel_sums = rel_result(add_all([item[2] for item in backs]), heads)
        up_sums = add_all([item[3] for item in mlps]).reshape(units)
        qv_full = lax.dynamic_update_slice_in_dim(
            jnp.zeros((2, width), F32), qv_sums, model_index * cols, 1
        )
        up_full = lax.dynamic_update_slice_in_dim(
            jnp.zeros(up_bias.shape, F32), up_sums, model_index * units, 0
        )
        norms = add_all([item[4] for item in backs])
        arrays = [norms, add_all(sums_two), up_full, qv_full, *rel_sums]
        flat = jnp.concatenate([array.reshape(-1) for array in arrays])
        count = (flat.size + 1023) // 1024 * 1024
        return jnp.pad(flat, (0, count - flat.size)).reshape(-1, 128)

    x_windows = by_window(block_input)
    if not rings:
        first_weights, other_weights = gather(first_piece), gather(other_piece)
        rows_in, own_valid, normed, valid = start(x_windows)
        grad_top = masked(by_window(cotangent))
        own_in, own_top, own_valid = own_slice(rows_in), own_slice(grad_top), own_slice(own_valid)
        q, k, v, weights = project(offsets, first_weights, normed, bias_qkv, cols, wide)
        attended = [attention(0, q, k, v, weights)]
        after, normed_two = norm_two(
            rows_scatter(attended[0][2:]), own_in, 0, row(proj_bias), gain_two, shift_two
        )
        none = jnp.zeros((8, 128), F32)
        mlps = [
            mlp(
                offsets,
                rows_gather(normed_two),
                other_weights,
                grad_top,
                0,
                up_local,
                none,
                row(down_bias),
                False,
            )
        ]
        grad_after, branch, sums = norm_two_back(
            rows_scatter(mlps[0][4:5]), after, own_top, 0, gain_two
        )
        sums_two = [sums]
        result = mlps[0][5]
        own = finish(rows_scatter([result]), after, own_valid, 0, row(down_bias))

        def unpad(array):
            array = array.reshape(padded, ROWS, width)[:slots, :WTOK]
            return array.reshape(slots * WTOK, width)

        block_output = unpad(rows_gather(own)[0])
        down_grad = scatter(weight_grad(None, down_groups(mlps), share))
        up_grad = scatter(weight_grad(None, up_groups(mlps), share))
        backs = [attention_back(0, rows_gather(branch), q, k, v, attended[0][1], weights)]
        parts = [(part, 0) for part in rows_scatter(backs[0][5:])]
        own = norm_one_back([(parts, grad_after)], own_in, own_valid, gain_one)
        input_grad = unpad(rows_gather(own)[0]).astype(F32)
        first_grad = scatter(weight_grad(None, first_groups(backs, attended), share))
        vector = lax.psum(bundle(sums_two, backs, mlps), ("dp", "mp"))
    else:
        def second_norm(part, keep, came, crossed):
            return norm_two(
                [keep, came, crossed], rows_in, part, bias_proj, gain_two, shift_two
            )

        def second_back(part, after, keep, came, crossed):
            return norm_two_back([keep, came, crossed], after, grad_top, 4 * part, gain_two)

        def spread(own, across):
            return [own, across, over_core(own), over_core(across)]

        rows = (ROWS, width)

        def second(keep, came, at=0):
            return (at, 0, *rows, [(keep, (1,), 0), (came, (1,), 0)])

        z1, x0 = over_z(first_piece), over_x(first_piece)
        z1, x0, x_windows, other_piece, rel_high, rel_low, cotangent = sync(
            z1, x0, x_windows, other_piece, rel_high, rel_low, cotangent
        )
        z2, x1 = over_z(z1), over_x(z1)
        rows_in, own_valid, normed, valid = start(x_windows)
        z2, x1, normed, cotangent, gain_two, shift_two, bias_proj, bias_down = sync(
            z2, x1, normed, cotangent, gain_two, shift_two, row(proj_bias), row(down_bias)
        )
        z3, x2 = over_z(z2), over_x(z2)
        z3, x2, normed, top_windows, other_piece = sync(
            z3, x2, normed, by_window(cotangent), other_piece
        )
        x3 = over_x(z3)
        oz1 = over_z(other_piece)
        grad_top = masked(top_windows)
        x3, normed, grad_top, other_late, gain_two, shift_two, bias_proj, bias_down = sync(
            x3, normed, grad_top, other_piece, gain_two, shift_two, bias_proj, bias_down
        )
        ox0 = over_x(other_late)
        first_weights = [first_piece, x0, z1, x1, z2, x2, z3, x3]
        q, k, v, weights = project(offsets, first_weights, normed, bias_qkv, cols, wide)
        oz1, ox0, q = sync(oz1, ox0, q)

        oz2, ox1 = over_z(oz1), over_x(oz1)
        a0 = attention(0, q, k, v, weights)
        oz2, ox1, a0 = sync(oz2, ox1, a0)
        oz3, ox2 = over_z(oz2), over_x(oz2)
        came0 = over_core(a0[3])
        (passed0,) = combine((rows, [second(a0[2], came0)]))
        crossed0 = over_y(passed0)
        a1 = attention(1, tie(q, passed0), k, v, weights)
        oz3, ox2, crossed0, a1 = sync(oz3, ox2, crossed0, a1)
        ox3 = over_x(oz3)
        came1 = over_core(a1[3])
        (passed1,) = combine((rows, [second(a1[2], came1)]))
        crossed1 = over_y(passed1)
        after0, own0 = second_norm(0, tie(a0[2], passed1), came0, crossed0)
        across0 = over_y(own0)
        attended = [a0, a1]
        after1, own1 = second_norm(1, tie(a1[2], own0), came1, crossed1)
        ox3, across0, own1 = sync(ox3, across0, own1)
        other_weights = [other_piece, ox0, oz1, ox1, oz2, ox2, oz3, ox3]
        across1 = over_y(own1)
        pieces0 = spread(own0, across0)

        m0 = mlp(offsets, pieces0, other_weights, grad_top, 0, up_local, after0, bias_down, True)
        across1, m0 = sync(across1, m0)
        pieces1 = spread(own1, across1)
        came0, out_came0 = over_core(m0[5]), over_core(m0[7])
        (passed0,) = combine((rows, [second(m0[4], came0)]))
        crossed0 = over_y(passed0)
        pieces1[0] = tie(pieces1[0], passed0)
        m1 = mlp(offsets, pieces1, other_weights, grad_top, 1, up_local, after1, bias_down, True)
        crossed0, out_came0, m1 = sync(crossed0, out_came0, m1)
        mlps = [m0, m1]
        came1, out_came1 = over_core(m1[5]), over_core(m1[7])
        grad_after0, branch0, sums0 = second_back(0, after0, m0[4], came0, crossed0)
        across0 = over_y(branch0)
        passed1, out_passed0, out_passed1 = combine(
            (rows, [second(tie(m1[4], branch0), came1)]),
            (rows, [second(m0[6], out_came0)]),
            (rows, [second(m1[6], out_came1)]),
        )
        left = tie(m0, passed1)
        (down_pairs,) = weight_grad(targets, down_groups([left, m1]), share)
        across0, passed1, down_pairs = sync(across0, passed1, down_pairs)
        crossed1 = over_y(passed1)
        branches0 = spread(branch0, across0)
        left = tie(m0, down_pairs)
        up_high, up_low, up_keep = weight_grad(targets, up_groups([left, m1]), share, 2)
        down_held = over_z(down_pairs[3])
        crossed1, branches0, up_high, up_low, up_keep = sync(
            crossed1, branches0, up_high, up_low, up_keep
        )

        up_came_high = over_x(up_high)

        def down_cells(k, held, lane):
            return [
                (0, half * units, share, units, [(down_pairs, (k, half), 0), (held, at, first)])
                for half, (at, first) in enumerate(lane)
            ]

        grad_after1, branch1, sums1 = second_back(1, after1, m1[4], came1, crossed1)
        sums_two = [sums0, sums1]
        across1 = over_y(branch1)
        (down_held,) = combine(
            (
                (share, 2 * units),
                down_cells(2, tie(down_held, branch1), [((0,), 0), ((1,), 0)]),
            )
        )
        branches0[0] = tie(branches0[0], down_held)
        down_held = over_z(down_held)
        b0 = attention_back(0, branches0, q, k, v, a0[1], weights)
        across1, up_came_high, down_held, b0 = sync(across1, up_came_high, down_held, b0)
        branches1 = spread(branch1, across1)
        came0 = over_core(b0[6])
        up_came_low = over_x(up_low)

        passed0, held = combine(
            (rows, [second(b0[5], came0)]),
            ((share, 2 * units), down_cells(1, down_held, [((0,), 0), ((0,), units)])),
        )
        crossed0 = over_y(passed0)
        held = over_z(held)
        branches1[0] = tie(branches1[0], passed0)
        out_crossed0 = over_y(tie(out_passed0, passed0))
        b1 = attention_back(1, branches1, q, k, v, a1[1], weights)
        crossed0, held, up_came_low, out_crossed0, b1 = sync(
            crossed0, held, up_came_low, out_crossed0, b1
        )
        backs = [b0, b1]
        came1 = over_core(b1[6])
        vector = bundle(sums_two, backs, mlps)
        vector_came = lax.ppermute(vector, "mp", [(m, m ^ 1) for m in range(4)])
        came1, vector_came, vector = sync(came1, vector_came, vector)
        vector = vector + vector_came
        vector_came = lax.ppermute(vector, "mp", [(m, m ^ 2) for m in range(4)])
        vector_came, vector, held = sync(vector_came, vector, held)
        vector = vector + vector_came
        vector_came = lax.ppermute(vector, "dp", [(d, d ^ 2) for d in range(8)])
        down_held = held
        passed1, down_other, up_held = combine(
            (rows, [second(b1[5], came1)]),
            (
                (share, units),
                [(0, 0, share, units, [(down_pairs, (0, 1), 0), (down_held, (0,), units)])],
            ),
            (
                (share, units),
                [(0, 0, share, units, [(up_keep, (3,), 0), (up_came_high, (1,), 0)])],
            ),
        )
        crossed1 = over_y(passed1)
        up_held, down_other = over_z(up_held), over_x(down_other)
        left = tie(b0, passed1)
        out_crossed1 = over_y(tie(out_passed1, passed1))
        firsts = weight_grad(targets, first_groups([left, b1], attended), share, 3)
        crossed1, down_other, up_held, vector, vector_came, firsts = sync(
            crossed1, down_other, up_held, vector, vector_came, firsts
        )
        first_three, first_two, first_last, first_keep = firsts
        vector = vector + vector_came

        came_three = over_x(first_three)
        (up_sum,) = combine(
            (
                (share, units),
                [
                    (
                        0,
                        0,
                        share,
                        units,
                        [(up_keep, (2,), 0), (up_came_high, (0,), 0), (up_held, (0,), 0)],
                    )
                ],
            )
        )
        held = over_z(up_sum)
        own = norm_one_back(
            [
                ([(b0[5], 0), (came0, 0), (tie(crossed0, up_sum), 0)], grad_after0),
                ([(b1[5], 0), (came1, 0), (crossed1, 0)], grad_after1),
            ],
            rows_in,
            own_valid,
            gain_one,
        )
        in_across = over_y(own)
        (out_own,) = combine(
            (
                (2 * ROWS, width),
                [
                    (
                        part * ROWS,
                        0,
                        *rows,
                        [(keep, (0,), 0), (came, (0,), 0), (crossed, (0,), 0)],
                    )
                    for part, (keep, came, crossed) in enumerate(
                        (
                            (m0[6], out_came0, tie(out_crossed0, own)),
                            (m1[6], out_came1, out_crossed1),
                        )
                    )
                ],
            ),
        )
        came_three, held, own, out_own, vector = sync(came_three, held, own, out_own, vector)
        came_two = over_x(first_two)
        (held,) = combine(
            (
                (share, 2 * units),
                [
                    (0, 0, share, units, [(first_keep, (3,), 0), (came_three, (0,), 0)]),
                    (
                        0,
                        units,
                        share,
                        units,
                        [(up_keep, (1,), 0), (up_came_low, (1,), 0), (held, (0,), 0)],
                    ),
                ],
            ),
        )
        held = over_z(held)
        vector_came = lax.ppermute(vector, "dp", [(d, d ^ 4) for d in range(8)])
        out_across = over_y(tie(out_own, own))
        came_two, held, vector_came, in_across = sync(came_two, held, vector_came, in_across)
        vector = vector + vector_came
        up_last = held[:, units:]

        def first_cell(k, held):
            return (
                0,
                0,
                share,
                4 * cols,
                [(first_keep, (k,), 0), (came_two, (k - 1,), 0), (held, (0,), 0)],
            )

        (held,) = combine(((share, 4 * cols), [first_cell(2, held)]))
        held = over_z(held)
        vector_came = lax.ppermute(vector, "dp", [(d, d ^ 1) for d in range(8)])
        in_pieces = spread(own, in_across)
        input_grad = place_windows(local, in_pieces)
        held, vector_came, input_grad = sync(held, vector_came, input_grad)
        vector = vector + vector_came
        came_last = over_x(tie(first_last, held))
        (held,) = combine(((share, 4 * cols), [first_cell(1, held)]))
        vector = tie(vector, held)
        held = over_z(held)
        came_last, out_own, out_across = sync(came_last, out_own, out_across)
        out_pieces = spread(out_own, out_across)
        block_output = write_output(local, places_all, lives_all, out_pieces)

        def last(*values):
            out = values[0].astype(F32)
            for value in values[1:]:
                out = out + value.astype(F32)
            return out

        down_grad = last(down_pairs[0, 0], down_held[:, :units], down_other)
        up_grad = last(up_keep[0], up_came_low[0], up_last)
        first_grad = last(first_keep[0], came_last[0], held)

    shapes = [(2, width), (4, width), (up_bias.size,), (2, width), (RELN, HD), (RELN, HD)]
    outs, at = [], 0
    flat = vector.reshape(-1)
    for shape in shapes:
        size = int(np.prod(shape))
        outs.append(flat[at : at + size].reshape(shape))
        at += size
    one_sums, two_sums, up_bias_grad, qv_bias_grad, height_grad, width_grad = outs
    shift_one_grad = one_sums[1]
    gain_one_grad = (one_sums[0] - norm_one_shift * shift_one_grad) / norm_one_gain
    qkv_grad = jnp.stack([first_grad[:, slot * cols : (slot + 1) * cols] for slot in range(3)])
    proj_grad = first_grad[:, 3 * cols :].T
    return (
        block_output,
        input_grad,
        gain_one_grad,
        shift_one_grad,
        qkv_grad,
        qv_bias_grad,
        proj_grad,
        two_sums[2],
        two_sums[0],
        two_sums[1],
        up_grad,
        up_bias_grad,
        down_grad.T,
        two_sums[3],
        height_grad,
        width_grad,
    )


def solution(mesh):
    in_specs = (
        P("dp", None),
        P("dp"),
        P("dp"),
        P(),
        P(),
        P(None, "dp", "mp"),
        P(),
        P("mp", "dp"),
        P(),
        P(),
        P(),
        P("dp", "mp"),
        P(),
        P("mp", "dp"),
        P(),
        P(),
        P(),
        P("dp", None),
    )
    out_specs = (
        P("dp", None),
        P("dp", None),
        P(),
        P(),
        P(None, "dp", "mp"),
        P(),
        P("mp", "dp"),
        P(),
        P(),
        P(),
        P("dp", "mp"),
        P(),
        P("mp", "dp"),
        P(),
        P(),
        P(),
    )
    return jax.shard_map(body, mesh=mesh, in_specs=in_specs, out_specs=out_specs, check_vma=False)
```

```python
from functools import partial

import jax
import jax.numpy as jnp
import numpy as np
from jax import lax
from jax.experimental import pallas as pl
from jax.experimental.pallas import tpu as pltpu
from jax.sharding import PartitionSpec as P

HD = 80
WIN = 14
SIDE = 64
GRID = 5
WTOK = 196
RELN = 27
ROWS = 208
SCALE = HD ** (-0.5)
EPS = 1e-06
F32 = jnp.float32
BF16 = jnp.bfloat16
ANY = pl.BlockSpec(memory_space=pl.ANY)
highest = lax.Precision.HIGHEST


def dot(left, right):
    return lax.dot_general(left, right, (((1,), (0,)), ((), ())), preferred_element_type=F32)


def dot_nt(left, right):
    return lax.dot_general(left, right, (((1,), (1,)), ((), ())), preferred_element_type=F32)


def dot_tn(left, right):
    return lax.dot_general(left, right, (((0,), (0,)), ((), ())), preferred_element_type=F32)


def whole(array):
    zeros = (0,) * len(array.shape)
    return pl.BlockSpec(array.shape, lambda *_: zeros)


def params(megabytes):
    return pltpu.CompilerParams(vmem_limit_bytes=megabytes * 2**20)


def cost(micros):
    return pl.CostEstimate(
        flops=int(micros * 0.05e9), bytes_accessed=int(micros * 1.0e4), transcendentals=0
    )


def struct(shape, dtype):
    return jax.ShapeDtypeStruct(shape, dtype)


def assemble(offsets, pieces, target, sems):
    copies = []
    for index, piece in enumerate(pieces):
        count = piece.shape[0]
        start = pl.multiple_of(offsets[index], 16)
        copies.append(
            pltpu.make_async_copy(piece, target.at[pl.ds(start, count)], sems.at[index])
        )
    for copy in copies:
        copy.start()
    for copy in copies:
        copy.wait()


def norm_parts(values):
    center = jnp.mean(values, axis=-1, keepdims=True)
    centred = values - center
    spread = jnp.mean(centred * centred, axis=-1, keepdims=True)
    rstd = lax.rsqrt(spread + EPS)
    return centred * rstd, rstd


def token_valid(spot, live):
    token = lax.broadcasted_iota(jnp.int32, (WTOK, 1), 0)
    row = (token * 9363) >> 17
    col = token - row * WIN
    high = spot // GRID * WIN
    wide = spot % GRID * WIN
    inside = (high + row < SIDE) & (wide + col < SIDE) & (live == 1)
    return jnp.where(inside, 1.0, 0.0).astype(F32)


def pad_rows(values):
    empty = jnp.zeros((ROWS - WTOK, values.shape[1]), F32)
    return jnp.concatenate([values, empty], axis=0)


def prepare_kernel(every, order, places, lives, x_ref, gain_ref, shift_ref, *outs):
    rows_ref, own_ref, normed_ref, valid_ref = outs
    step = pl.program_id(0)
    slot = order[step]
    valid = token_valid(places[slot], lives[slot])
    x = x_ref[0].astype(F32)
    xhat, _ = norm_parts(x)
    normed_ref[...] = pad_rows((xhat * gain_ref[...] + shift_ref[...]) * valid).astype(BF16)
    valid_ref[...] = pad_rows(valid)

    @pl.when(lax.rem(step, every) == 0)
    def _():
        rows_ref[...] = pad_rows(x).astype(BF16)
        own_ref[...] = pad_rows(valid)


def prepare(order, places, lives, x, gain, shift, every):
    count = order.shape[0]
    width = x.shape[2]
    window = pl.BlockSpec((1, WTOK, width), lambda i, order, *_: (order[i], 0, 0))
    block = pl.BlockSpec((ROWS, width), lambda i, *_: (i, 0))
    return pl.pallas_call(
        partial(prepare_kernel, every),
        grid_spec=pltpu.PrefetchScalarGridSpec(
            num_scalar_prefetch=3,
            grid=(count,),
            in_specs=[window, whole(gain), whole(shift)],
            out_specs=[
                pl.BlockSpec((ROWS, width), lambda i, *_: (i // every, 0)),
                pl.BlockSpec((ROWS, 1), lambda i, *_: (i // every, 0)),
                block,
                pl.BlockSpec((ROWS, 1), lambda i, *_: (i, 0)),
            ],
        ),
        out_shape=[
            struct((count // every * ROWS, width), BF16),
            struct((count // every * ROWS, 1), F32),
            struct((count * ROWS, width), BF16),
            struct((count * ROWS, 1), F32),
        ],
        compiler_params=params(63),
        cost_estimate=cost(9),
        name="prepare",
    )(order, places, lives, x, gain, shift)


def mask_kernel(order, places, lives, top_ref, grad_ref):
    slot = order[pl.program_id(0)]
    valid = token_valid(places[slot], lives[slot])
    grad_ref[...] = pad_rows(top_ref[0].astype(F32) * valid).astype(BF16)


def mask_rows(order, places, lives, top):
    count = order.shape[0]
    width = top.shape[2]
    return pl.pallas_call(
        mask_kernel,
        grid_spec=pltpu.PrefetchScalarGridSpec(
            num_scalar_prefetch=3,
            grid=(count,),
            in_specs=[pl.BlockSpec((1, WTOK, width), lambda i, order, *_: (order[i], 0, 0))],
            out_specs=pl.BlockSpec((ROWS, width), lambda i, *_: (i, 0)),
        ),
        out_shape=struct((count * ROWS, width), BF16),
        compiler_params=params(63),
        cost_estimate=cost(6),
        name="mask_rows",
    )(order, places, lives, top)


def top_rows(shape):
    return pl.BlockSpec(shape, lambda i: (0, 0))


def row_block(shape, at):
    return pl.BlockSpec(shape, lambda i: (at, 0))


def total(refs, rows):
    value = refs[0][:rows].astype(F32)
    for ref in refs[1:]:
        value = value + ref[:rows].astype(F32)
    return value


def norm_two_kernel(count, *refs):
    parts, (x_ref, bias_ref, gain_ref, shift_ref, after_ref, normed_ref) = (
        refs[:count],
        refs[count:],
    )
    rows = x_ref.shape[0]
    after = x_ref[...].astype(F32) + total(parts, rows) + bias_ref[...]
    xhat, _ = norm_parts(after)
    after_ref[...] = after
    normed_ref[...] = (xhat * gain_ref[...] + shift_ref[...]).astype(BF16)


def norm_two(parts, x, at, bias, gain, shift):
    shape = (parts[-1].shape[0], x.shape[1])
    return pl.pallas_call(
        partial(norm_two_kernel, len(parts)),
        grid=(1,),
        in_specs=[top_rows(shape)] * len(parts)
        + [row_block(shape, at), whole(bias), whole(gain), whole(shift)],
        out_specs=[top_rows(shape)] * 2,
        out_shape=[struct(shape, F32), struct(shape, BF16)],
        compiler_params=params(14),
        cost_estimate=cost(3),
        name="norm_two",
    )(*parts, x, bias, gain, shift)


def finish_kernel(count, *refs):
    parts, (after_ref, valid_ref, bias_ref, out_ref) = refs[:count], refs[count:]
    rows = after_ref.shape[0]
    branch = total(parts, rows) + bias_ref[...]
    out_ref[...] = (valid_ref[...] * (after_ref[...] + branch)).astype(BF16)


def finish(parts, after, valid, at, bias):
    return pl.pallas_call(
        partial(finish_kernel, len(parts)),
        grid=(1,),
        in_specs=[top_rows(after.shape)] * (len(parts) + 1)
        + [row_block((after.shape[0], 1), at), whole(bias)],
        out_specs=top_rows(after.shape),
        out_shape=struct(after.shape, BF16),
        compiler_params=params(14),
        cost_estimate=cost(2.5),
        name="finish",
    )(*parts, after, valid, bias)


def norm_back(upstream, xhat, rstd, gain):
    weighted = upstream * gain
    inner = jnp.mean(weighted * xhat, axis=-1, keepdims=True)
    level = jnp.mean(weighted, axis=-1, keepdims=True)
    return rstd * (weighted - level - xhat * inner)


def norm_two_back_kernel(count, *refs):
    parts = refs[:count]
    after_ref, top_ref, gain_ref, grad_ref, branch_ref, sums_ref = refs[count:]
    rows = after_ref.shape[0]
    upstream = total(parts, rows)
    xhat, rstd = norm_parts(after_ref[...])
    top = top_ref[...].astype(F32)
    grad = top + norm_back(upstream, xhat, rstd, gain_ref[...])
    branch = grad.astype(BF16)
    grad_ref[...] = grad
    branch_ref[...] = branch
    sums_ref[0:1] = jnp.sum(upstream * xhat, axis=0, keepdims=True)
    sums_ref[1:2] = jnp.sum(upstream, axis=0, keepdims=True)
    sums_ref[2:3] = jnp.sum(branch.astype(F32), axis=0, keepdims=True)
    sums_ref[3:4] = jnp.sum(top, axis=0, keepdims=True)


def norm_two_back(parts, after, top, at, gain):
    sums = struct((4, after.shape[1]), F32)
    return pl.pallas_call(
        partial(norm_two_back_kernel, len(parts)),
        grid=(1,),
        in_specs=[top_rows(after.shape)] * (len(parts) + 1)
        + [row_block(after.shape, at), whole(gain)],
        out_specs=[top_rows(after.shape)] * 2 + [whole(sums)],
        out_shape=[struct(after.shape, F32), struct(after.shape, BF16), sums],
        compiler_params=params(14),
        cost_estimate=cost(4),
        name="norm_two_back",
    )(*parts, after, top, gain)


def norm_one_back_kernel(counts, *refs):
    x_ref, valid_ref, gain_ref, out_ref = refs[-4:]
    at = 0
    for part, count in enumerate(counts):
        parts, grad_ref = refs[at : at + count], refs[at + count]
        at += count + 1
        rows = slice(part * ROWS, part * ROWS + ROWS)
        upstream = total(parts, ROWS) * valid_ref[rows]
        xhat, rstd = norm_parts(x_ref[rows].astype(F32))
        grad = grad_ref[...] + norm_back(upstream, xhat, rstd, gain_ref[...])
        out_ref[rows] = grad.astype(BF16)


def norm_one_back(windows, x, valid, gain):
    shape = (ROWS, x.shape[1])
    operands, specs = [], []
    for parts, grad in windows:
        operands += [part[0] for part in parts] + [grad]
        specs += [
            pl.BlockSpec(shape, lambda i, at=at: (at, 0)) for at in (part[1] for part in parts)
        ]
        specs.append(whole(grad))
    return pl.pallas_call(
        partial(norm_one_back_kernel, [len(parts) for parts, _ in windows]),
        grid=(1,),
        in_specs=specs + [whole(x), whole(valid), whole(gain)],
        out_specs=whole(x),
        out_shape=struct(x.shape, BF16),
        compiler_params=params(20),
        cost_estimate=cost(3.5 * len(windows)),
        name="norm_one_back",
    )(*operands, x, valid, gain)


def qkv_kernel(count, cols, offsets, *refs):
    pieces = refs[:count]
    x_ref, bias_ref, q_ref, k_ref, v_ref, w_ref, sems = refs[count:]
    wide = q_ref.shape[1]

    @pl.when(pl.program_id(0) == 0)
    def _():
        assemble(offsets, pieces, w_ref, sems)

    result = (dot(x_ref[...], w_ref[:, wide:]) + bias_ref[...]).astype(BF16)
    for slot, ref in enumerate((q_ref, k_ref, v_ref)):
        ref[:, :cols] = result[:, slot * cols : (slot + 1) * cols]
        if wide > cols:
            ref[:, cols:] = jnp.zeros((ref.shape[0], wide - cols), BF16)


def project(offsets, pieces, x, bias, cols, wide):
    rows, width = x.shape
    step = 2 * ROWS
    block = pl.BlockSpec((step, wide), lambda i, *_: (i, 0))
    total_cols = wide + 3 * cols
    return pl.pallas_call(
        partial(qkv_kernel, len(pieces), cols),
        grid_spec=pltpu.PrefetchScalarGridSpec(
            num_scalar_prefetch=1,
            grid=(rows // step,),
            in_specs=[ANY] * len(pieces)
            + [pl.BlockSpec((step, width), lambda i, *_: (i, 0)), whole(bias)],
            out_specs=[block, block, block, pl.BlockSpec((width, total_cols), lambda i, *_: (0, 0))],
            scratch_shapes=[pltpu.SemaphoreType.DMA((len(pieces),))],
        ),
        out_shape=[struct((rows, wide), BF16)] * 3 + [struct((width, total_cols), BF16)],
        compiler_params=params(28),
        cost_estimate=cost(14),
        name="qkv",
    )(offsets, *pieces, x, bias)


def head_spans(heads, wide):
    spans = []
    for head in range(heads):
        first, last = head * HD, head * HD + HD
        low = first // 128 * 128
        high = min((last + 127) // 128 * 128, wide)
        spans.append((low, high, first, last))
    return spans


def lane_mask(span):
    low, high, first, last = span
    lane = lax.broadcasted_iota(jnp.int32, (1, high - low), 1) + low
    return jnp.where((lane >= first) & (lane < last), 1.0, 0.0).astype(BF16)


def shift_counts():
    token = lax.broadcasted_iota(jnp.int32, (ROWS, 128), 0)
    row = (token * 9363) >> 17
    col = token - row * WIN
    return jnp.maximum(WIN - 1 - row, 0), WIN - 1 - col


def shift_lanes(values, counts, back):
    for step in (1, 2, 4, 8):
        moved = pltpu.roll(values, step if back else 128 - step, 1)
        values = jnp.where((counts & step) != 0, moved, values)
    return values


def lane_kind():
    lane = lax.broadcasted_iota(jnp.int32, (ROWS, 128), 1) & 31
    return lane < WIN, (lane >= 16) & (lane < 16 + WIN), lane == 31


def split_two(values):
    high = values.astype(BF16)
    return high, (values - high.astype(F32)).astype(BF16)


def bias_operand(q, rel_high, rel_low, counts):
    table = (dot(q, rel_high) + dot(q, rel_low)) * (1.0 / SCALE)
    by_row = shift_lanes(table[:, :128], counts[0], False)
    by_col = shift_lanes(table[:, 128:], counts[1], False)
    is_row, is_col, is_last = lane_kind()
    packed = jnp.where(
        is_row, by_row, jnp.where(is_col, by_col, jnp.where(is_last, 1.0, 0.0))
    )
    high, low = split_two(packed)
    return jnp.concatenate([high, low], axis=1)


def add_lanes(parts, values, span):
    low, high = span[0], span[1]
    for index in range(low // 128, high // 128):
        piece = values[:, index * 128 - low : index * 128 - low + 128]
        parts[index] = piece if parts[index] is None else parts[index] + piece


def attend_kernel(heads, split, q_ref, k_ref, v_ref, rh_ref, rl_ref, mark_ref, w_ref, *outs):
    mixed_ref, shares_ref = outs[:2]
    q, k, v = q_ref[...], k_ref[...], v_ref[...]
    wide = q.shape[1]
    bias = bias_operand(q, rh_ref[...], rl_ref[...], shift_counts())
    parts = [None] * (wide // 128)
    for head, span in enumerate(head_spans(heads, wide)):
        mask = lane_mask(span)
        cut = slice(span[0], span[1])
        scores = dot_nt(
            jnp.concatenate([q[:, cut], bias], axis=1),
            jnp.concatenate([k[:, cut] * mask, mark_ref[head]], axis=1),
        )
        top = jnp.max(scores, axis=-1, keepdims=True)
        shifted = jnp.exp(SCALE * (scores - top))
        norm = jnp.sum(shifted, axis=-1, keepdims=True)
        shares = (shifted * (1.0 / norm)).astype(BF16)
        shares_ref[:, head * 256 : head * 256 + ROWS] = shares
        add_lanes(parts, dot(shares, v[:, cut] * mask), span)
    mixed = jnp.concatenate(parts, axis=1).astype(BF16)
    cols = heads * HD
    mixed_ref[...] = mixed[:, :cols]
    branch = dot_nt(mixed, w_ref[...]).astype(BF16)
    if split:
        step = pl.program_id(0)
        for sent in range(split):

            @pl.when(step == sent)
            def _(sent=sent):
                outs[3 + sent][...] = branch

        @pl.when(step >= split)
        def _():
            outs[2][...] = branch
    else:
        outs[2][...] = branch


def split_specs(windows, split, width):
    rows = ROWS * (windows - split)
    if not split:
        return [pl.BlockSpec((ROWS, width), lambda i: (i, 0))], [struct((rows, width), BF16)]
    return (
        [
            pl.BlockSpec((ROWS, width), lambda i: (jnp.maximum(i - split, 0), 0)),
            pl.BlockSpec((ROWS, width), lambda i: (jnp.minimum(i, split - 1), 0)),
        ],
        [struct((rows, width), BF16), struct((ROWS * split, width), BF16)],
    )


def attend(heads, part, windows, split, q, k, v, rel_high, rel_low, marks, weights):
    wide = q.shape[1]
    width = weights.shape[0]

    def place(i):
        return (i + split) % windows if split else i

    block = pl.BlockSpec((ROWS, wide), lambda i: (part * windows + place(i), 0))
    specs, shapes = split_specs(windows, split, width)
    if split:
        one = struct((ROWS, width), BF16)
        specs, shapes = specs[:1] + [whole(one)] * split, shapes[:1] + [one] * split
    return pl.pallas_call(
        partial(attend_kernel, heads, split),
        grid=(windows,),
        in_specs=[
            block,
            block,
            block,
            whole(rel_high),
            whole(rel_low),
            whole(marks),
            pl.BlockSpec((width, wide), lambda i: (0, 0)),
        ],
        out_specs=[
            pl.BlockSpec((ROWS, heads * HD), lambda i: (place(i), 0)),
            pl.BlockSpec((ROWS, heads * 256), lambda i: (place(i), 0)),
        ]
        + specs,
        out_shape=[
            struct((windows * ROWS, heads * HD), BF16),
            struct((windows * ROWS, heads * 256), BF16),
        ]
        + shapes,
        compiler_params=params(16),
        cost_estimate=cost(13.5),
        name="attend",
    )(q, k, v, rel_high, rel_low, marks, weights)


def attend_back_kernel(heads, windows, split, count, *refs):
    pieces = refs[:count]
    q_ref, k_ref, v_ref, shares_ref, rh_ref, mark_ref, w_ref = refs[count : count + 7]
    normed_ref, valid_ref = refs[count + 7 : count + 9]
    grads_ref, branch_ref, rel_ref, sum_ref, norm_ref = refs[count + 9 : count + 14]
    outs = refs[count + 14 :]
    step = pl.program_id(0)

    @pl.when(step == 0)
    def _():
        start = 0
        for piece in pieces:
            branch_ref[start : start + piece.shape[0]] = piece[...]
            start += piece.shape[0]
        rel_ref[...] = jnp.zeros(rel_ref.shape, F32)
        sum_ref[...] = jnp.zeros(sum_ref.shape, F32)
        norm_ref[...] = jnp.zeros(norm_ref.shape, F32)

    place = lax.rem(step + split, windows) if split else step
    q, k, v = q_ref[...], k_ref[...], v_ref[...]
    wide = q.shape[1]
    top = branch_ref[pl.ds(pl.multiple_of(place * ROWS, 16), ROWS), :]
    grad_mixed = dot(top, w_ref[:, :wide]).astype(BF16)
    grad_q, grad_k, grad_v = ([None] * (wide // 128) for _ in range(3))
    grad_bias = None
    for head, span in enumerate(head_spans(heads, wide)):
        mask = lane_mask(span)
        cut = slice(span[0], span[1])
        size = span[1] - span[0]
        upper = grad_mixed[:, cut]
        rounded = shares_ref[:, head * 256 : head * 256 + ROWS]
        shares = rounded.astype(F32)
        weighted = shares * dot_nt(upper, v[:, cut] * mask)
        inner = jnp.sum(weighted, axis=-1, keepdims=True)
        grad_scores = (weighted - shares * inner).astype(BF16)
        add_lanes(grad_v, dot_tn(rounded, upper * mask), span)
        both = dot(
            grad_scores,
            jnp.concatenate([k[:, cut] * mask, mark_ref[head][:, :128]], axis=1),
        )
        add_lanes(grad_q, both[:, :size], span)
        part = both[:, size:]
        grad_bias = part if grad_bias is None else grad_bias + part
        add_lanes(grad_k, dot_tn(grad_scores, q[:, cut] * mask), span)
    counts = shift_counts()
    is_row, is_col, _ = lane_kind()
    by_row = shift_lanes(jnp.where(is_row, grad_bias, 0.0), counts[0], True)
    by_col = shift_lanes(jnp.where(is_col, grad_bias, 0.0), counts[1], True)
    packed = jnp.concatenate([by_row, by_col], axis=1).astype(BF16)
    extra = dot_nt(packed, rh_ref[...])
    rel_ref[...] += dot_tn(packed, q)
    grad_q = (SCALE * jnp.concatenate(grad_q, axis=1) + extra).astype(BF16)
    grad_k = (SCALE * jnp.concatenate(grad_k, axis=1)).astype(BF16)
    grad_v = jnp.concatenate(grad_v, axis=1).astype(BF16)
    cols = heads * HD
    for slot, grad in enumerate((grad_q, grad_k, grad_v)):
        grads_ref[:, slot * cols : (slot + 1) * cols] = grad[:, :cols]
    packed_grads = grads_ref[...]
    sum_ref[...] += jnp.sum(packed_grads.astype(F32), axis=0, keepdims=True)
    partial_sum = dot_nt(packed_grads, w_ref[:, wide:])
    norm_ref[0:1] += jnp.sum(partial_sum * normed_ref[...].astype(F32), axis=0, keepdims=True)
    norm_ref[1:2] += jnp.sum(partial_sum * valid_ref[...], axis=0, keepdims=True)
    result = partial_sum.astype(BF16)
    if split:
        keep_ref, send_ref = outs

        @pl.when(step < split)
        def _():
            send_ref[...] = result

        @pl.when(step >= split)
        def _():
            keep_ref[...] = result
    else:
        outs[0][...] = result


def attend_back(
    heads, part, windows, split, pieces, q, k, v, shares, rel_high, marks, weights, normed, valid
):
    wide = q.shape[1]
    width = weights.shape[0]

    def place(i):
        return (i + split) % windows if split else i

    block = pl.BlockSpec((ROWS, wide), lambda i: (part * windows + place(i), 0))
    specs, shapes = split_specs(windows, split, width)
    rows = windows * ROWS
    branch = struct((rows, width), BF16)
    rel = struct((256, wide), F32)
    sums = struct((1, 3 * heads * HD), F32)
    norms = struct((2, width), F32)
    return pl.pallas_call(
        partial(attend_back_kernel, heads, windows, split, len(pieces)),
        grid=(windows,),
        in_specs=[whole(piece) for piece in pieces]
        + [
            block,
            block,
            block,
            pl.BlockSpec((ROWS, heads * 256), lambda i: (place(i), 0)),
            whole(rel_high),
            whole(marks),
            whole(weights),
            pl.BlockSpec((ROWS, width), lambda i: (part * windows + place(i), 0)),
            pl.BlockSpec((ROWS, 1), lambda i: (part * windows + place(i), 0)),
        ],
        out_specs=[
            pl.BlockSpec((ROWS, 3 * heads * HD), lambda i: (place(i), 0)),
            whole(branch),
            whole(rel),
            whole(sums),
            whole(norms),
        ]
        + specs,
        out_shape=[struct((rows, 3 * heads * HD), BF16), branch, rel, sums, norms] + shapes,
        compiler_params=params(28),
        cost_estimate=cost(18.5),
        name="attend_back",
    )(*pieces, q, k, v, shares, rel_high, marks, weights, normed, valid)


def mlp_kernel(count, weights, split, offsets, *refs):
    pieces = refs[:count]
    weight_pieces = refs[count : count + weights]
    refs = refs[count + weights :]
    after_any, top_ref, bias_ref, down_bias_ref = refs[:4]
    active_ref, hidden_ref, normed_any, sum_ref = refs[4:8]
    outs = refs[8 : 12 if split else 10]
    up, down, normed_ref, after_ref, send_ref, out_send_ref, sems, row_sems = refs[len(outs) + 8 :]
    step = pl.program_id(0)
    steps = pl.num_programs(0)
    block = top_ref.shape[0]
    units = up.shape[1]
    copies = []
    for half, target in enumerate((down, up)):
        copies.append([])
        for index, piece in enumerate(weight_pieces):
            rows = piece.shape[0]
            start = pl.multiple_of(offsets[index], 16)
            copies[half].append(
                pltpu.make_async_copy(
                    piece.at[:, half * units : (half + 1) * units],
                    target.at[pl.ds(start, rows)],
                    sems.at[half, index],
                )
            )
    row_copies, start = [], 0
    for index, piece in enumerate(pieces):
        rows = piece.shape[0]
        row_copies.append(
            pltpu.make_async_copy(
                piece, normed_ref.at[pl.ds(start, rows)], row_sems.at[index]
            )
        )
        start += rows
    normed_out = pltpu.make_async_copy(normed_ref, normed_any, row_sems.at[count])
    after_in = pltpu.make_async_copy(after_any, after_ref, row_sems.at[count + 1])
    if split:
        send_out = pltpu.make_async_copy(send_ref, outs[1], row_sems.at[count + 2])
        out_send_out = pltpu.make_async_copy(out_send_ref, outs[3], row_sems.at[count + 3])

    @pl.when(step == 0)
    def _():
        for copy in row_copies + copies[1] + copies[0]:
            copy.start()
        after_in.start()
        sum_ref[...] = jnp.zeros(sum_ref.shape, F32)
        for copy in row_copies + copies[1]:
            copy.wait()
        normed_out.start()

    place = 1 - step if split else step
    normed = normed_ref[pl.ds(pl.multiple_of(place * block, 16), block), :]
    hidden = dot(normed, up[...]) + bias_ref[...]

    @pl.when(step == 0)
    def _():
        for copy in copies[0]:
            copy.wait()

    half = 0.5 * (1.0 + lax.erf(hidden * (0.5**0.5)))
    slope = half + hidden * jnp.exp(-0.5 * hidden * hidden) * float((2.0 * np.pi) ** -0.5)
    active = (hidden * half).astype(BF16)
    active_ref[...] = active
    grad = (dot(top_ref[...], down[...]) * slope).astype(BF16)
    hidden_ref[...] = grad
    sum_ref[...] += jnp.sum(grad.astype(F32), axis=0, keepdims=True)
    back = dot_nt(grad, up[...]).astype(BF16)
    result = dot_nt(active, down[...])
    if split:

        @pl.when(step == 0)
        def _():
            send_ref[...] = back
            out_send_ref[...] = result.astype(BF16)
            send_out.start()
            out_send_out.start()
            after_in.wait()

        @pl.when(step == 1)
        def _():
            outs[0][...] = back
            own = result[:ROWS] + after_ref[...] + down_bias_ref[...]
            outs[2][:ROWS] = own.astype(BF16)
            outs[2][ROWS:] = result[ROWS:].astype(BF16)
            send_out.wait()
            out_send_out.wait()
    else:
        outs[0][...] = back
        outs[1][...] = result.astype(BF16)

        @pl.when(step == 0)
        def _():
            after_in.wait()

    @pl.when(step == steps - 1)
    def _():
        normed_out.wait()


def mlp(offsets, pieces, weight_pieces, top, part, bias, after, down_bias, split):
    rows = sum(piece.shape[0] for piece in pieces)
    width = pieces[0].shape[1]
    units = weight_pieces[0].shape[1] // 2
    block = 2 * ROWS
    blocks = rows // block
    normed = struct((rows, width), BF16)
    sums = struct((1, units), F32)

    def place(i):
        return 1 - i if split else i

    wide = pl.BlockSpec((block, units), lambda i, *_: (place(i), 0))
    back = struct((block, width), BF16)
    if split:
        back_specs, back_shapes = [whole(back), ANY] * 2, [back] * 4
    else:
        back_specs = [pl.BlockSpec((block, width), lambda i, *_: (i, 0))] * 2
        back_shapes = [normed] * 2
    return pl.pallas_call(
        partial(mlp_kernel, len(pieces), len(weight_pieces), split),
        grid_spec=pltpu.PrefetchScalarGridSpec(
            num_scalar_prefetch=1,
            grid=(blocks,),
            in_specs=[ANY] * (len(pieces) + len(weight_pieces) + 1)
            + [
                pl.BlockSpec((block, width), lambda i, *_: (part * blocks + place(i), 0)),
                whole(bias),
                whole(down_bias),
            ],
            out_specs=[wide, wide, ANY, whole(sums)] + back_specs,
            scratch_shapes=[
                pltpu.VMEM((width, units), BF16),
                pltpu.VMEM((width, units), BF16),
                pltpu.VMEM((rows, width), BF16),
                pltpu.VMEM(after.shape, F32),
                pltpu.VMEM((block, width), BF16),
                pltpu.VMEM((block, width), BF16),
                pltpu.SemaphoreType.DMA((2, len(weight_pieces))),
                pltpu.SemaphoreType.DMA((len(pieces) + 4,)),
            ],
        ),
        out_shape=[struct((rows, units), BF16)] * 2 + [normed, sums] + back_shapes,
        compiler_params=params(48),
        cost_estimate=cost(21),
        name="mlp",
    )(offsets, *pieces, *weight_pieces, after, top, bias, down_bias)


SEND_PARTS = {2: ((2, 3), (0, 1)), 3: ((3,), (1, 2), (0,))}


def weight_grad_kernel(sizes, share, sends, targets, *refs):
    count = 2 * sum(sizes)
    operands = refs[:count]
    outs, (result, sems) = refs[count:-2], refs[-2:]
    keep_ref = outs[sends] if sends else None
    pair_ref = None if sends else outs[0]
    lead = keep_ref.shape[2] if sends else 0
    step = pl.program_id(0)
    steps = pl.num_programs(0)
    chunk = operands[0].shape[1]
    pieces = chunk // share
    base = pl.multiple_of(step * chunk, 16)
    at, first = 0, 0
    for size in sizes:
        value = None
        for _ in range(size):
            left, right = operands[at], operands[at + 1]
            at += 2
            term = dot_tn(left[...], right[...])
            value = term if value is None else value + term
        span = value.shape[1]
        result[pl.ds(base, chunk), first : first + span] = value.astype(BF16)
        first += span

    def copy(index, out, slot):
        return pltpu.make_async_copy(
            result.at[pl.ds(pl.multiple_of(index * share, 16), share), pl.ds(0, lead)],
            out.at[slot],
            sems.at[0, index],
        )

    def pair_copy(index, slot):
        return pltpu.make_async_copy(
            result.at[
                pl.ds(pl.multiple_of(index * share, 16), share),
                pl.ds(lead, result.shape[1] - lead),
            ],
            pair_ref.at[lax.rem(slot, 4), 1 - slot // 4],
            sems.at[1, index],
        )

    for piece in range(pieces):
        index = step * pieces + piece
        slot = targets[index]

        if lead:

            for out, slots in zip(outs, SEND_PARTS[sends]):

                @pl.when((slot >= slots[0]) & (slot <= slots[-1]))
                def _(out=out, slots=slots):
                    copy(index, out, slot - slots[0]).start()

            @pl.when(slot >= 4)
            def _():
                copy(index, keep_ref, slot - 4).start()

        if pair_ref is not None:
            pair_copy(index, slot).start()

    @pl.when(step == steps - 1)
    def _():
        for index in range(8):
            if lead:
                copy(index, keep_ref, 0).wait()
            if pair_ref is not None:
                pair_copy(index, 0).wait()


def plain_grad_kernel(sizes, *refs):
    count = 2 * sum(sizes)
    operands, out_ref = refs[:count], refs[count]
    at, first = 0, 0
    for size in sizes:
        value = None
        for _ in range(size):
            left, right = operands[at], operands[at + 1]
            at += 2
            term = dot_tn(left[...], right[...])
            value = term if value is None else value + term
        span = value.shape[1]
        out_ref[:, first : first + span] = value.astype(BF16)
        first += span


def weight_grad(targets, groups, share, sends=0):
    operands, specs = [], []
    chunk = 640 if targets is not None else 256
    total_cols = 0
    for group in groups:
        for left, at, rows, right in group:
            operands += [left, right]
            specs.append(pl.BlockSpec((rows, chunk), lambda i, *_, at=at: (at, i)))
            specs.append(whole(right))
        total_cols += group[0][3].shape[1]
    width = operands[0].shape[1]
    sizes = [len(group) for group in groups]
    if targets is None:
        return [
            pl.pallas_call(
                partial(plain_grad_kernel, sizes),
                grid=(width // chunk,),
                in_specs=specs,
                out_specs=pl.BlockSpec((chunk, total_cols), lambda i: (i, 0)),
                out_shape=struct((width, total_cols), BF16),
                compiler_params=params(36),
                cost_estimate=cost(13),
        name="weight_grad",
            )(*operands)
        ]
    if sends:
        counts = [len(slots) for slots in SEND_PARTS[sends]] + [4]
        shapes = [struct((count, share, total_cols), BF16) for count in counts]
    else:
        shapes = [struct((4, 2, share, total_cols), BF16)]
    return pl.pallas_call(
        partial(weight_grad_kernel, sizes, share, sends),
        grid_spec=pltpu.PrefetchScalarGridSpec(
            num_scalar_prefetch=1,
            grid=(width // chunk,),
            in_specs=specs,
            out_specs=[ANY] * len(shapes),
            scratch_shapes=[
                pltpu.VMEM((width, total_cols), BF16),
                pltpu.SemaphoreType.DMA((2, 8)),
            ],
        ),
        out_shape=shapes,
        compiler_params=params(36),
        cost_estimate=cost(13),
        name="weight_grad",
    )(targets, *operands)


def combine_kernel(layout, *refs):
    outs = refs[len(refs) - len(layout) :]
    at = 0
    for cells, out in zip(layout, outs):
        for row, lane, rows, lanes, terms in cells:
            value = None
            for lead, first in terms:
                term = refs[at][(0,) * lead + (slice(None), slice(first, first + lanes))]
                at += 1
                value = term.astype(F32) if value is None else value + term.astype(F32)
            out[row : row + rows, lane : lane + lanes] = value.astype(BF16)


def combine(*outs):
    operands, specs, layout = [], [], []
    for _, cells in outs:
        layout.append([])
        for row, lane, rows, lanes, terms in cells:
            places = []
            for array, index, first in terms:
                lead = array.ndim - 2
                block = (1,) * lead + (rows, array.shape[-1])
                place = tuple(index) + (0,) * (array.ndim - len(index))
                operands.append(array)
                specs.append(pl.BlockSpec(block, lambda i, place=place: place))
                places.append((lead, first))
            layout[-1].append((row, lane, rows, lanes, places))
    shapes = [struct(shape, BF16) for shape, _ in outs]
    return pl.pallas_call(
        partial(combine_kernel, layout),
        grid=(1,),
        in_specs=specs,
        out_specs=[whole(shape) for shape in shapes],
        out_shape=shapes,
        compiler_params=params(16),
        cost_estimate=cost(2),
        name="combine",
    )(*operands)


def place_kernel(order, *refs):
    pieces, out_ref = refs[:4], refs[4]
    for me in range(4):

        @pl.when(order[0] == me)
        def _(me=me):
            for part in range(pieces[0].shape[0] // ROWS):
                for index, step in enumerate((0, 2, 1, 3)):
                    start = (4 * part + (me ^ step)) * WTOK
                    value = pieces[index][part * ROWS : part * ROWS + WTOK]
                    out_ref[start : start + WTOK] = value.astype(F32)


def place_windows(order, pieces):
    height, width = pieces[0].shape
    rows = height // ROWS * 4 * WTOK
    lanes = width // 2
    return pl.pallas_call(
        place_kernel,
        grid_spec=pltpu.PrefetchScalarGridSpec(
            num_scalar_prefetch=1,
            grid=(2,),
            in_specs=[pl.BlockSpec((height, lanes), lambda i, *_: (0, i))] * 4,
            out_specs=pl.BlockSpec((rows, lanes), lambda i, *_: (0, i)),
        ),
        out_shape=struct((rows, width), F32),
        compiler_params=params(32),
        cost_estimate=cost(7),
        name="place_windows",
    )(order, *pieces)


def output_kernel(order, places, lives, *refs):
    pieces, out_ref, buffer = refs[:4], refs[4], refs[5]
    for me in range(4):

        @pl.when(order[0] == me)
        def _(me=me):
            for part in range(pieces[0].shape[0] // ROWS):
                for index, step in enumerate((0, 2, 1, 3)):
                    slot = 4 * part + (me ^ step)
                    value = pieces[index][part * ROWS : part * ROWS + WTOK].astype(F32)
                    value = value * token_valid(places[slot], lives[slot])
                    buffer[slot * WTOK : (slot + 1) * WTOK] = value

    out_ref[...] = buffer[...].astype(BF16)


def write_output(order, places, lives, pieces):
    height, width = pieces[0].shape
    rows = height // ROWS * 4 * WTOK
    lanes = width // 2
    return pl.pallas_call(
        output_kernel,
        grid_spec=pltpu.PrefetchScalarGridSpec(
            num_scalar_prefetch=3,
            grid=(2,),
            in_specs=[pl.BlockSpec((height, lanes), lambda i, *_: (0, i))] * 4,
            out_specs=pl.BlockSpec((rows, lanes), lambda i, *_: (0, i)),
            scratch_shapes=[pltpu.VMEM((rows, lanes), F32)],
        ),
        out_shape=struct((rows, width), BF16),
        compiler_params=params(32),
        cost_estimate=cost(7),
        name="write_output",
    )(order, places, lives, *pieces)


def key_marks(heads):
    marks = np.zeros((heads, ROWS, 256), np.float32)
    for head in range(heads):
        for token in range(WTOK):
            for half in (0, 128):
                marks[head, token, half + head * 32 + token // WIN] = 1.0
                marks[head, token, half + head * 32 + 16 + token % WIN] = 1.0
        marks[head, WTOK:, head * 32 + 31] = -1e30
    return marks.astype(BF16)


def rel_operand(rel_height, rel_width, heads, wide):
    high = rel_height[::-1].T
    flat = rel_width[::-1].T
    lanes = jnp.zeros((wide, 256), F32)

    def spread(block, row, lane):
        below = wide - row - HD
        return jnp.pad(block, ((row, below), (lane, 256 - lane - block.shape[1])))

    for head in range(heads):
        first = head * 32 + 16
        fit = min(RELN, 128 - first)
        lanes = lanes + spread(high, head * HD, head * 32)
        lanes = lanes + spread(flat[:, :fit], head * HD, 128 + first)
        if fit < RELN:
            lanes = lanes + spread(flat[:, fit:], head * HD, 128)
    return split_two(lanes)


def rel_result(sums, heads):
    high = jnp.zeros((RELN, HD), F32)
    flat = jnp.zeros((RELN, HD), F32)
    for head in range(heads):
        cols = sums[:, head * HD : head * HD + HD]
        high = high + cols[head * 32 : head * 32 + RELN]
        rolled = jnp.concatenate([cols[128:], cols[128:]], axis=0)
        flat = flat + rolled[head * 32 + 16 : head * 32 + 16 + RELN]
    return high[::-1], flat[::-1]


def add_all(values):
    out = values[0]
    for value in values[1:]:
        out = out + value
    return out


def tie(value, *others):
    return lax.optimization_barrier((value,) + others)[0]


def sync(*values):
    return lax.optimization_barrier(values)


def body(
    block_input,
    window_place,
    slot_live,
    norm_one_gain,
    norm_one_shift,
    qkv_weight,
    qv_bias,
    proj_weight,
    proj_bias,
    norm_two_gain,
    norm_two_shift,
    up_weight,
    up_bias,
    down_weight,
    down_bias,
    rel_height,
    rel_width,
    cotangent,
):
    data_parts = lax.axis_size("dp")
    model_parts = lax.axis_size("mp")
    data_index = lax.axis_index("dp")
    model_index = lax.axis_index("mp")
    width = block_input.shape[1]
    share = qkv_weight.shape[1]
    cols = qkv_weight.shape[2]
    heads = cols // HD
    wide = (cols + 127) // 128 * 128
    units = up_weight.shape[1]
    slots = window_place.shape[0]
    rings = data_parts == 8 and model_parts == 4 and slots == 8
    padded = (slots + model_parts - 1) // model_parts * model_parts
    halves = padded // 4 if rings else 1
    windows = padded // halves
    split = 2 if rings else 0
    part_rows = windows * ROWS
    own_rows = part_rows // model_parts

    if rings:
        depth, side = data_index // 2, data_index % 2
        y_bit, core_bit = model_index // 2, model_index % 2
        over_x = partial(lax.ppermute, axis_name="dp", perm=[(d, d ^ 1) for d in range(8)])
        over_z = partial(lax.ppermute, axis_name="dp", perm=[(d, (d + 2) % 8) for d in range(8)])
        over_y = partial(lax.ppermute, axis_name="mp", perm=[(m, m ^ 2) for m in range(4)])
        over_core = partial(lax.ppermute, axis_name="mp", perm=[(m, m ^ 1) for m in range(4)])

    def gather(piece):
        return [lax.all_gather(piece, "dp", axis=0, tiled=True)]

    if rings:
        offsets = []
        for back in range(4):
            behind = (depth - back) % 4
            offsets += [share * (2 * behind + side), share * (2 * behind + 1 - side)]
        offsets = jnp.stack(offsets).astype(jnp.int32)
    else:
        offsets = jnp.zeros((1,), jnp.int32)

    def scatter(parts):
        return lax.psum_scatter(parts[0], "dp", scatter_dimension=0, tiled=True).astype(F32)

    def rows_scatter(parts):
        return [lax.psum_scatter(parts[0], "mp", scatter_dimension=0, tiled=True)]

    def rows_gather(own):
        return [lax.all_gather(own, "mp", axis=0, tiled=True)]

    def own_slice(array):
        rows = array.shape[0] // model_parts
        return lax.dynamic_slice_in_dim(array, model_index * rows, rows, 0)

    first_piece = jnp.concatenate(
        [
            jnp.pad(proj_weight.T, ((0, 0), (0, wide - cols))),
            qkv_weight[0],
            qkv_weight[1],
            qkv_weight[2],
        ],
        axis=1,
    )
    other_piece = jnp.concatenate([down_weight.T, up_weight], 1)

    row = lambda v: v.reshape(1, -1)
    gain_one, shift_one = row(norm_one_gain), row(norm_one_shift)
    gain_two, shift_two = row(norm_two_gain), row(norm_two_shift)
    bias_local = lax.dynamic_slice_in_dim(qv_bias, model_index * cols, cols, 1)
    bias_qkv = row(jnp.stack([bias_local[0], jnp.zeros_like(bias_local[0]), bias_local[1]]))
    up_local = row(lax.dynamic_slice_in_dim(up_bias, model_index * units, units, 0))
    rel_high, rel_low = rel_operand(rel_height, rel_width, heads, wide)
    marks = jnp.asarray(key_marks(heads))

    steps = (0, 2, 1, 3)
    if rings:
        local = [model_index ^ step for step in steps]
        places = [4 * part + spot for part in range(halves) for spot in local]
    else:
        local = [jnp.int32(spot) for spot in range(windows)]
        places = local
    local = jnp.stack(local).astype(jnp.int32)
    places = jnp.stack(places).astype(jnp.int32)
    if rings:
        targets = []
        for d in range(8):
            ahead = (d // 2 - depth) % 4
            targets.append(ahead + jnp.where(d % 2 == side, 4, 0))
        targets = jnp.stack(targets).astype(jnp.int32)
    else:
        targets = None

    def by_window(array):
        array = array.reshape((slots, WTOK) + array.shape[1:])
        return jnp.pad(array, [(0, padded - slots)] + [(0, 0)] * (array.ndim - 1))

    places_all = jnp.pad(window_place, (0, padded - slots))
    lives_all = jnp.pad(slot_live, (0, padded - slots))
    blocks = [(part, part_rows) for part in range(halves)]

    def start(x):
        every = 4 if rings else 1
        return prepare(places, places_all, lives_all, x, gain_one, shift_one, every)

    def masked(top):
        return mask_rows(places, places_all, lives_all, top)

    def attention(part, q, k, v, weights):
        return attend(heads, part, windows, split, q, k, v, rel_high, rel_low, marks, weights)

    def attention_back(part, pieces, q, k, v, shares, weights):
        return attend_back(
            heads,
            part,
            windows,
            split,
            pieces,
            q,
            k,
            v,
            shares,
            rel_high,
            marks,
            weights,
            normed,
            valid,
        )

    def down_groups(mlps):
        return [[(grad_top, *blocks[i], mlps[i][0]) for i in range(halves)]]

    def up_groups(mlps):
        return [[(mlps[i][2], 0, part_rows, mlps[i][1]) for i in range(halves)]]

    def first_groups(backs, attended):
        return [
            [(normed, *blocks[i], backs[i][0]) for i in range(halves)],
            [(backs[i][1], 0, part_rows, attended[i][0]) for i in range(halves)],
        ]

    def bundle(sums_two, backs, mlps):
        qv_sums = add_all([item[3] for item in backs]).reshape(3, cols)[0::2]
        rel_sums = rel_result(add_all([item[2] for item in backs]), heads)
        up_sums = add_all([item[3] for item in mlps]).reshape(units)
        qv_full = lax.dynamic_update_slice_in_dim(
            jnp.zeros((2, width), F32), qv_sums, model_index * cols, 1
        )
        up_full = lax.dynamic_update_slice_in_dim(
            jnp.zeros(up_bias.shape, F32), up_sums, model_index * units, 0
        )
        norms = add_all([item[4] for item in backs])
        arrays = [norms, add_all(sums_two), up_full, qv_full, *rel_sums]
        flat = jnp.concatenate([array.reshape(-1) for array in arrays])
        count = (flat.size + 1023) // 1024 * 1024
        return jnp.pad(flat, (0, count - flat.size)).reshape(-1, 128)

    x_windows = by_window(block_input)
    if not rings:
        first_weights, other_weights = gather(first_piece), gather(other_piece)
        rows_in, own_valid, normed, valid = start(x_windows)
        grad_top = masked(by_window(cotangent))
        own_in, own_top, own_valid = own_slice(rows_in), own_slice(grad_top), own_slice(own_valid)
        q, k, v, weights = project(offsets, first_weights, normed, bias_qkv, cols, wide)
        attended = [attention(0, q, k, v, weights)]
        after, normed_two = norm_two(
            rows_scatter(attended[0][2:]), own_in, 0, row(proj_bias), gain_two, shift_two
        )
        none = jnp.zeros((8, 128), F32)
        mlps = [
            mlp(
                offsets,
                rows_gather(normed_two),
                other_weights,
                grad_top,
                0,
                up_local,
                none,
                row(down_bias),
                False,
            )
        ]
        grad_after, branch, sums = norm_two_back(
            rows_scatter(mlps[0][4:5]), after, own_top, 0, gain_two
        )
        sums_two = [sums]
        result = mlps[0][5]
        own = finish(rows_scatter([result]), after, own_valid, 0, row(down_bias))

        def unpad(array):
            array = array.reshape(padded, ROWS, width)[:slots, :WTOK]
            return array.reshape(slots * WTOK, width)

        block_output = unpad(rows_gather(own)[0])
        down_grad = scatter(weight_grad(None, down_groups(mlps), share))
        up_grad = scatter(weight_grad(None, up_groups(mlps), share))
        backs = [attention_back(0, rows_gather(branch), q, k, v, attended[0][1], weights)]
        parts = [(part, 0) for part in rows_scatter(backs[0][5:])]
        own = norm_one_back([(parts, grad_after)], own_in, own_valid, gain_one)
        input_grad = unpad(rows_gather(own)[0]).astype(F32)
        first_grad = scatter(weight_grad(None, first_groups(backs, attended), share))
        vector = lax.psum(bundle(sums_two, backs, mlps), ("dp", "mp"))
    else:
        def second_norm(part, keep, came, crossed):
            return norm_two(
                [keep, came, crossed], rows_in, part, bias_proj, gain_two, shift_two
            )

        def second_back(part, after, keep, came, crossed):
            return norm_two_back([keep, came, crossed], after, grad_top, 4 * part, gain_two)

        def spread(own, across):
            return [own, across, over_core(own), over_core(across)]

        rows = (ROWS, width)

        def second(keep, came, at=0):
            return (at, 0, *rows, [(keep, (1,), 0), (came, (1,), 0)])

        z1, x0 = over_z(first_piece), over_x(first_piece)
        z1, x0, x_windows, other_piece, rel_high, rel_low, cotangent = sync(
            z1, x0, x_windows, other_piece, rel_high, rel_low, cotangent
        )
        z2, x1 = over_z(z1), over_x(z1)
        rows_in, own_valid, normed, valid = start(x_windows)
        z2, x1, normed, cotangent, gain_two, shift_two, bias_proj, bias_down = sync(
            z2, x1, normed, cotangent, gain_two, shift_two, row(proj_bias), row(down_bias)
        )
        z3, x2 = over_z(z2), over_x(z2)
        z3, x2, normed, top_windows, other_piece = sync(
            z3, x2, normed, by_window(cotangent), other_piece
        )
        x3 = over_x(z3)
        oz1 = over_z(other_piece)
        grad_top = masked(top_windows)
        x3, normed, grad_top, other_late, gain_two, shift_two, bias_proj, bias_down = sync(
            x3, normed, grad_top, other_piece, gain_two, shift_two, bias_proj, bias_down
        )
        ox0 = over_x(other_late)
        first_weights = [first_piece, x0, z1, x1, z2, x2, z3, x3]
        q, k, v, weights = project(offsets, first_weights, normed, bias_qkv, cols, wide)
        oz1, ox0, q = sync(oz1, ox0, q)

        oz2, ox1 = over_z(oz1), over_x(oz1)
        a0 = attention(0, q, k, v, weights)
        oz2, ox1, a0 = sync(oz2, ox1, a0)
        oz3, ox2 = over_z(oz2), over_x(oz2)
        came0, came_y = over_core(a0[3]), over_core(a0[4])
        (passed0,) = combine((rows, [(0, 0, *rows, [(a0[2], (1,), 0), (came_y, (0,), 0)])]))
        crossed0 = over_y(passed0)
        a1 = attention(1, tie(q, passed0), k, v, weights)
        crossed0, a1 = sync(crossed0, a1)
        came_y, came1 = over_core(a1[4]), over_core(a1[3])
        (passed1,) = combine((rows, [(0, 0, *rows, [(a1[2], (1,), 0), (came_y, (0,), 0)])]))
        crossed1 = over_y(passed1)
        after0, own0 = second_norm(0, tie(a0[2], passed1, came1), came0, crossed0)
        across0 = over_y(own0)
        oz3, ox2 = sync(oz3, ox2, own0)[:2]
        ox3, ox4 = over_x(oz3[: share // 2]), over_x(oz3[share // 2 :])
        attended = [a0, a1]
        after1, own1 = second_norm(1, tie(a1[2], own0), came1, crossed1)
        ox3, ox4, across0, own1 = sync(ox3, ox4, across0, own1)
        other_weights = [other_piece, ox0, oz1, ox1, oz2, ox2, oz3, ox3, ox4]
        other_offsets = jnp.concatenate([offsets, offsets[7:] + share // 2])
        across1 = over_y(own1)
        pieces0 = spread(tie(own0, own1), across0)

        m0 = mlp(other_offsets, pieces0, other_weights, grad_top, 0, up_local, after0, bias_down, True)
        across1, m0 = sync(across1, m0)
        pieces1 = spread(own1, across1)
        came0, out_came0 = over_core(m0[5]), over_core(m0[7])
        (passed0,) = combine((rows, [second(m0[4], came0)]))
        crossed0 = over_y(passed0)
        pieces1[0] = tie(pieces1[0], passed0)
        m1 = mlp(other_offsets, pieces1, other_weights, grad_top, 1, up_local, after1, bias_down, True)
        crossed0, out_came0, m1 = sync(crossed0, out_came0, m1)
        mlps = [m0, m1]
        came1, out_came1 = over_core(m1[5]), over_core(m1[7])
        grad_after0, branch0, sums0 = second_back(0, after0, m0[4], came0, crossed0)
        across0 = over_y(branch0)
        passed1, out_passed0, out_passed1 = combine(
            (rows, [second(tie(m1[4], branch0), came1)]),
            (rows, [second(m0[6], out_came0)]),
            (rows, [second(m1[6], out_came1)]),
        )
        left = tie(m0, passed1)
        (down_pairs,) = weight_grad(targets, down_groups([left, m1]), share)
        across0, passed1, down_pairs = sync(across0, passed1, down_pairs)
        crossed1 = over_y(passed1)
        branches0 = spread(branch0, across0)
        left = tie(m0, down_pairs)
        up_high, up_low, up_keep = weight_grad(targets, up_groups([left, m1]), share, 2)
        down_held = over_z(down_pairs[3])
        crossed1, branches0, up_high, up_low, up_keep = sync(
            crossed1, branches0, up_high, up_low, up_keep
        )

        up_came_high = over_x(up_high)

        def down_cells(k, held, lane):
            return [
                (0, half * units, share, units, [(down_pairs, (k, half), 0), (held, at, first)])
                for half, (at, first) in enumerate(lane)
            ]

        grad_after1, branch1, sums1 = second_back(1, after1, m1[4], came1, crossed1)
        sums_two = [sums0, sums1]
        across1 = over_y(branch1)
        (down_held,) = combine(
            (
                (share, 2 * units),
                down_cells(2, tie(down_held, branch1), [((0,), 0), ((1,), 0)]),
            )
        )
        branches0[0] = tie(branches0[0], down_held)
        down_held = over_z(down_held)
        b0 = attention_back(0, branches0, q, k, v, a0[1], weights)
        across1, up_came_high, down_held, b0 = sync(across1, up_came_high, down_held, b0)
        branches1 = spread(branch1, across1)
        came0 = over_core(b0[6])
        up_came_low = over_x(up_low)

        passed0, held = combine(
            (rows, [second(b0[5], came0)]),
            ((share, 2 * units), down_cells(1, down_held, [((0,), 0), ((0,), units)])),
        )
        crossed0 = over_y(passed0)
        held = over_z(held)
        branches1[0] = tie(branches1[0], passed0)
        out_crossed0 = over_y(tie(out_passed0, passed0))
        b1 = attention_back(1, branches1, q, k, v, a1[1], weights)
        crossed0, held, up_came_low, out_crossed0, b1 = sync(
            crossed0, held, up_came_low, out_crossed0, b1
        )
        backs = [b0, b1]
        came1 = over_core(b1[6])
        vector = bundle(sums_two, backs, mlps)
        vector_came = lax.ppermute(vector, "mp", [(m, m ^ 1) for m in range(4)])
        came1, vector_came, vector = sync(came1, vector_came, vector)
        vector = vector + vector_came
        vector_came = lax.ppermute(vector, "mp", [(m, m ^ 2) for m in range(4)])
        down_held = held
        passed1, down_other, up_held = combine(
            (rows, [second(b1[5], came1)]),
            (
                (share, units),
                [(0, 0, share, units, [(down_pairs, (0, 1), 0), (down_held, (0,), units)])],
            ),
            (
                (share, units),
                [(0, 0, share, units, [(up_keep, (3,), 0), (up_came_high, (1,), 0)])],
            ),
        )
        crossed1 = over_y(passed1)
        up_held, down_other = over_z(up_held), over_x(down_other)
        left = tie(b0, passed1)
        out_crossed1 = over_y(tie(out_passed1, passed1))
        firsts = weight_grad(targets, first_groups([left, b1], attended), share, 3)
        crossed1, down_other, up_held, firsts = sync(crossed1, down_other, up_held, firsts)
        first_three, first_two, first_last, first_keep = firsts

        came_three = over_x(first_three)
        (up_sum,) = combine(
            (
                (share, units),
                [
                    (
                        0,
                        0,
                        share,
                        units,
                        [(up_keep, (2,), 0), (up_came_high, (0,), 0), (up_held, (0,), 0)],
                    )
                ],
            )
        )
        held = over_z(up_sum)
        own = norm_one_back(
            [
                ([(b0[5], 0), (came0, 0), (tie(crossed0, up_sum), 0)], grad_after0),
                ([(b1[5], 0), (came1, 0), (crossed1, 0)], grad_after1),
            ],
            rows_in,
            own_valid,
            gain_one,
        )
        in_across = over_y(tie(own, vector_came))
        (out_own,) = combine(
            (
                (2 * ROWS, width),
                [
                    (
                        part * ROWS,
                        0,
                        *rows,
                        [(keep, (0,), 0), (came, (0,), 0), (crossed, (0,), 0)],
                    )
                    for part, (keep, came, crossed) in enumerate(
                        (
                            (m0[6], out_came0, tie(out_crossed0, own)),
                            (m1[6], out_came1, out_crossed1),
                        )
                    )
                ],
            ),
        )
        came_three, held, own, out_own, vector, vector_came = sync(
            came_three, held, own, out_own, vector, vector_came
        )
        vector = vector + vector_came
        came_two = over_x(first_two)
        (held,) = combine(
            (
                (share, 2 * units),
                [
                    (0, 0, share, units, [(first_keep, (3,), 0), (came_three, (0,), 0)]),
                    (
                        0,
                        units,
                        share,
                        units,
                        [(up_keep, (1,), 0), (up_came_low, (1,), 0), (held, (0,), 0)],
                    ),
                ],
            ),
        )
        held = over_z(held)
        vector_came = lax.ppermute(vector, "dp", [(d, d ^ 2) for d in range(8)])
        out_across = over_y(tie(out_own, own))
        came_two, held, vector_came, in_across = sync(came_two, held, vector_came, in_across)
        vector = vector + vector_came
        up_last = held[:, units:]

        def first_cell(k, held):
            return (
                0,
                0,
                share,
                4 * cols,
                [(first_keep, (k,), 0), (came_two, (k - 1,), 0), (held, (0,), 0)],
            )

        (held,) = combine(((share, 4 * cols), [first_cell(2, held)]))
        held = over_z(held)
        vector_came = lax.ppermute(vector, "dp", [(d, d ^ 4) for d in range(8)])
        in_pieces = spread(own, in_across)
        input_grad = place_windows(local, in_pieces)
        held, vector_came, input_grad = sync(held, vector_came, input_grad)
        vector = vector + vector_came
        vector_came = lax.ppermute(vector, "dp", [(d, d ^ 1) for d in range(8)])
        came_last = over_x(tie(first_last, held))
        (held,) = combine(((share, 4 * cols), [first_cell(1, held)]))
        held = over_z(held)
        vector = vector + vector_came
        came_last, out_own, out_across = sync(came_last, out_own, out_across)
        out_pieces = spread(out_own, out_across)
        block_output = write_output(local, places_all, lives_all, out_pieces)

        def last(*values):
            out = values[0].astype(F32)
            for value in values[1:]:
                out = out + value.astype(F32)
            return out

        down_grad = last(down_pairs[0, 0], down_held[:, :units], down_other)
        up_grad = last(up_keep[0], up_came_low[0], up_last)
        first_grad = last(first_keep[0], came_last[0], held)

    shapes = [(2, width), (4, width), (up_bias.size,), (2, width), (RELN, HD), (RELN, HD)]
    outs, at = [], 0
    flat = vector.reshape(-1)
    for shape in shapes:
        size = int(np.prod(shape))
        outs.append(flat[at : at + size].reshape(shape))
        at += size
    one_sums, two_sums, up_bias_grad, qv_bias_grad, height_grad, width_grad = outs
    shift_one_grad = one_sums[1]
    gain_one_grad = (one_sums[0] - norm_one_shift * shift_one_grad) / norm_one_gain
    qkv_grad = jnp.stack([first_grad[:, slot * cols : (slot + 1) * cols] for slot in range(3)])
    proj_grad = first_grad[:, 3 * cols :].T
    return (
        block_output,
        input_grad,
        gain_one_grad,
        shift_one_grad,
        qkv_grad,
        qv_bias_grad,
        proj_grad,
        two_sums[2],
        two_sums[0],
        two_sums[1],
        up_grad,
        up_bias_grad,
        down_grad.T,
        two_sums[3],
        height_grad,
        width_grad,
    )


def solution(mesh):
    in_specs = (
        P("dp", None),
        P("dp"),
        P("dp"),
        P(),
        P(),
        P(None, "dp", "mp"),
        P(),
        P("mp", "dp"),
        P(),
        P(),
        P(),
        P("dp", "mp"),
        P(),
        P("mp", "dp"),
        P(),
        P(),
        P(),
        P("dp", None),
    )
    out_specs = (
        P("dp", None),
        P("dp", None),
        P(),
        P(),
        P(None, "dp", "mp"),
        P(),
        P("mp", "dp"),
        P(),
        P(),
        P(),
        P("dp", "mp"),
        P(),
        P("mp", "dp"),
        P(),
        P(),
        P(),
    )
    return jax.shard_map(body, mesh=mesh, in_specs=in_specs, out_specs=out_specs, check_vma=False)
```

```python
from functools import partial

import jax
import jax.numpy as jnp
import numpy as np
from jax import lax
from jax.experimental import pallas as pl
from jax.experimental.pallas import tpu as pltpu
from jax.sharding import PartitionSpec as P

HD = 80
WIN = 14
SIDE = 64
GRID = 5
WTOK = 196
RELN = 27
ROWS = 208
SCALE = HD ** (-0.5)
EPS = 1e-06
F32 = jnp.float32
BF16 = jnp.bfloat16
ANY = pl.BlockSpec(memory_space=pl.ANY)
highest = lax.Precision.HIGHEST


def dot(left, right):
    return lax.dot_general(left, right, (((1,), (0,)), ((), ())), preferred_element_type=F32)


def dot_nt(left, right):
    return lax.dot_general(left, right, (((1,), (1,)), ((), ())), preferred_element_type=F32)


def dot_tn(left, right):
    return lax.dot_general(left, right, (((0,), (0,)), ((), ())), preferred_element_type=F32)


def whole(array):
    zeros = (0,) * len(array.shape)
    return pl.BlockSpec(array.shape, lambda *_: zeros)


def params(megabytes):
    return pltpu.CompilerParams(vmem_limit_bytes=megabytes * 2**20)


def cost(micros):
    return pl.CostEstimate(
        flops=int(micros * 0.05e9), bytes_accessed=int(micros * 1.0e4), transcendentals=0
    )


def struct(shape, dtype):
    return jax.ShapeDtypeStruct(shape, dtype)


def assemble(offsets, pieces, target, sems):
    copies = []
    for index, piece in enumerate(pieces):
        count = piece.shape[0]
        start = pl.multiple_of(offsets[index], 16)
        copies.append(
            pltpu.make_async_copy(piece, target.at[pl.ds(start, count)], sems.at[index])
        )
    for copy in copies:
        copy.start()
    for copy in copies:
        copy.wait()


def norm_parts(values):
    center = jnp.mean(values, axis=-1, keepdims=True)
    centred = values - center
    spread = jnp.mean(centred * centred, axis=-1, keepdims=True)
    rstd = lax.rsqrt(spread + EPS)
    return centred * rstd, rstd


def token_valid(spot, live):
    token = lax.broadcasted_iota(jnp.int32, (WTOK, 1), 0)
    row = (token * 9363) >> 17
    col = token - row * WIN
    high = spot // GRID * WIN
    wide = spot % GRID * WIN
    inside = (high + row < SIDE) & (wide + col < SIDE) & (live == 1)
    return jnp.where(inside, 1.0, 0.0).astype(F32)


def pad_rows(values):
    empty = jnp.zeros((ROWS - WTOK, values.shape[1]), F32)
    return jnp.concatenate([values, empty], axis=0)


def prepare_kernel(every, order, places, lives, x_ref, gain_ref, shift_ref, *outs):
    rows_ref, own_ref, normed_ref, valid_ref = outs
    step = pl.program_id(0)
    slot = order[step]
    valid = token_valid(places[slot], lives[slot])
    x = x_ref[0].astype(F32)
    xhat, _ = norm_parts(x)
    normed_ref[...] = pad_rows((xhat * gain_ref[...] + shift_ref[...]) * valid).astype(BF16)
    valid_ref[...] = pad_rows(valid)

    @pl.when(lax.rem(step, every) == 0)
    def _():
        rows_ref[...] = pad_rows(x).astype(BF16)
        own_ref[...] = pad_rows(valid)


def prepare(order, places, lives, x, gain, shift, every):
    count = order.shape[0]
    width = x.shape[2]
    window = pl.BlockSpec((1, WTOK, width), lambda i, order, *_: (order[i], 0, 0))
    block = pl.BlockSpec((ROWS, width), lambda i, *_: (i, 0))
    return pl.pallas_call(
        partial(prepare_kernel, every),
        grid_spec=pltpu.PrefetchScalarGridSpec(
            num_scalar_prefetch=3,
            grid=(count,),
            in_specs=[window, whole(gain), whole(shift)],
            out_specs=[
                pl.BlockSpec((ROWS, width), lambda i, *_: (i // every, 0)),
                pl.BlockSpec((ROWS, 1), lambda i, *_: (i // every, 0)),
                block,
                pl.BlockSpec((ROWS, 1), lambda i, *_: (i, 0)),
            ],
        ),
        out_shape=[
            struct((count // every * ROWS, width), BF16),
            struct((count // every * ROWS, 1), F32),
            struct((count * ROWS, width), BF16),
            struct((count * ROWS, 1), F32),
        ],
        compiler_params=params(63),
        cost_estimate=cost(9),
        name="prepare",
    )(order, places, lives, x, gain, shift)


def mask_kernel(order, places, lives, top_ref, grad_ref):
    slot = order[pl.program_id(0)]
    valid = token_valid(places[slot], lives[slot])
    grad_ref[...] = pad_rows(top_ref[0].astype(F32) * valid).astype(BF16)


def mask_rows(order, places, lives, top):
    count = order.shape[0]
    width = top.shape[2]
    return pl.pallas_call(
        mask_kernel,
        grid_spec=pltpu.PrefetchScalarGridSpec(
            num_scalar_prefetch=3,
            grid=(count,),
            in_specs=[pl.BlockSpec((1, WTOK, width), lambda i, order, *_: (order[i], 0, 0))],
            out_specs=pl.BlockSpec((ROWS, width), lambda i, *_: (i, 0)),
        ),
        out_shape=struct((count * ROWS, width), BF16),
        compiler_params=params(63),
        cost_estimate=cost(6),
        name="mask_rows",
    )(order, places, lives, top)


def top_rows(shape):
    return pl.BlockSpec(shape, lambda i: (0, 0))


def row_block(shape, at):
    return pl.BlockSpec(shape, lambda i: (at, 0))


def total(refs, rows):
    value = refs[0][:rows].astype(F32)
    for ref in refs[1:]:
        value = value + ref[:rows].astype(F32)
    return value


def norm_two_kernel(count, *refs):
    parts, (x_ref, bias_ref, gain_ref, shift_ref, after_ref, normed_ref) = (
        refs[:count],
        refs[count:],
    )
    rows = x_ref.shape[0]
    after = x_ref[...].astype(F32) + total(parts, rows) + bias_ref[...]
    xhat, _ = norm_parts(after)
    after_ref[...] = after
    normed_ref[...] = (xhat * gain_ref[...] + shift_ref[...]).astype(BF16)


def norm_two(parts, x, at, bias, gain, shift):
    shape = (parts[-1].shape[0], x.shape[1])
    return pl.pallas_call(
        partial(norm_two_kernel, len(parts)),
        grid=(1,),
        in_specs=[top_rows(shape)] * len(parts)
        + [row_block(shape, at), whole(bias), whole(gain), whole(shift)],
        out_specs=[top_rows(shape)] * 2,
        out_shape=[struct(shape, F32), struct(shape, BF16)],
        compiler_params=params(14),
        cost_estimate=cost(3),
        name="norm_two",
    )(*parts, x, bias, gain, shift)


def finish_kernel(count, *refs):
    parts, (after_ref, valid_ref, bias_ref, out_ref) = refs[:count], refs[count:]
    rows = after_ref.shape[0]
    branch = total(parts, rows) + bias_ref[...]
    out_ref[...] = (valid_ref[...] * (after_ref[...] + branch)).astype(BF16)


def finish(parts, after, valid, at, bias):
    return pl.pallas_call(
        partial(finish_kernel, len(parts)),
        grid=(1,),
        in_specs=[top_rows(after.shape)] * (len(parts) + 1)
        + [row_block((after.shape[0], 1), at), whole(bias)],
        out_specs=top_rows(after.shape),
        out_shape=struct(after.shape, BF16),
        compiler_params=params(14),
        cost_estimate=cost(2.5),
        name="finish",
    )(*parts, after, valid, bias)


def norm_back(upstream, xhat, rstd, gain):
    weighted = upstream * gain
    inner = jnp.mean(weighted * xhat, axis=-1, keepdims=True)
    level = jnp.mean(weighted, axis=-1, keepdims=True)
    return rstd * (weighted - level - xhat * inner)


def norm_two_back_kernel(count, *refs):
    parts = refs[:count]
    after_ref, top_ref, gain_ref, grad_ref, branch_ref, sums_ref = refs[count:]
    rows = after_ref.shape[0]
    upstream = total(parts, rows)
    xhat, rstd = norm_parts(after_ref[...])
    top = top_ref[...].astype(F32)
    grad = top + norm_back(upstream, xhat, rstd, gain_ref[...])
    branch = grad.astype(BF16)
    grad_ref[...] = grad
    branch_ref[...] = branch
    sums_ref[0:1] = jnp.sum(upstream * xhat, axis=0, keepdims=True)
    sums_ref[1:2] = jnp.sum(upstream, axis=0, keepdims=True)
    sums_ref[2:3] = jnp.sum(branch.astype(F32), axis=0, keepdims=True)
    sums_ref[3:4] = jnp.sum(top, axis=0, keepdims=True)


def norm_two_back(parts, after, top, at, gain):
    sums = struct((4, after.shape[1]), F32)
    return pl.pallas_call(
        partial(norm_two_back_kernel, len(parts)),
        grid=(1,),
        in_specs=[top_rows(after.shape)] * (len(parts) + 1)
        + [row_block(after.shape, at), whole(gain)],
        out_specs=[top_rows(after.shape)] * 2 + [whole(sums)],
        out_shape=[struct(after.shape, F32), struct(after.shape, BF16), sums],
        compiler_params=params(14),
        cost_estimate=cost(4),
        name="norm_two_back",
    )(*parts, after, top, gain)


def norm_one_back_kernel(counts, *refs):
    x_ref, valid_ref, gain_ref, out_ref = refs[-4:]
    at = 0
    for part, count in enumerate(counts):
        parts, grad_ref = refs[at : at + count], refs[at + count]
        at += count + 1
        rows = slice(part * ROWS, part * ROWS + ROWS)
        upstream = total(parts, ROWS) * valid_ref[rows]
        xhat, rstd = norm_parts(x_ref[rows].astype(F32))
        grad = grad_ref[...] + norm_back(upstream, xhat, rstd, gain_ref[...])
        out_ref[rows] = grad.astype(BF16)


def norm_one_back(windows, x, valid, gain):
    shape = (ROWS, x.shape[1])
    operands, specs = [], []
    for parts, grad in windows:
        operands += [part[0] for part in parts] + [grad]
        specs += [
            pl.BlockSpec(shape, lambda i, at=at: (at, 0)) for at in (part[1] for part in parts)
        ]
        specs.append(whole(grad))
    return pl.pallas_call(
        partial(norm_one_back_kernel, [len(parts) for parts, _ in windows]),
        grid=(1,),
        in_specs=specs + [whole(x), whole(valid), whole(gain)],
        out_specs=whole(x),
        out_shape=struct(x.shape, BF16),
        compiler_params=params(20),
        cost_estimate=cost(3.5 * len(windows)),
        name="norm_one_back",
    )(*operands, x, valid, gain)


def qkv_kernel(count, cols, offsets, *refs):
    pieces = refs[:count]
    x_ref, bias_ref, q_ref, k_ref, v_ref, w_ref, sems = refs[count:]
    wide = q_ref.shape[1]

    @pl.when(pl.program_id(0) == 0)
    def _():
        assemble(offsets, pieces, w_ref, sems)

    result = (dot(x_ref[...], w_ref[:, wide:]) + bias_ref[...]).astype(BF16)
    for slot, ref in enumerate((q_ref, k_ref, v_ref)):
        ref[:, :cols] = result[:, slot * cols : (slot + 1) * cols]
        if wide > cols:
            ref[:, cols:] = jnp.zeros((ref.shape[0], wide - cols), BF16)


def project(offsets, pieces, x, bias, cols, wide):
    rows, width = x.shape
    step = 2 * ROWS
    block = pl.BlockSpec((step, wide), lambda i, *_: (i, 0))
    total_cols = wide + 3 * cols
    return pl.pallas_call(
        partial(qkv_kernel, len(pieces), cols),
        grid_spec=pltpu.PrefetchScalarGridSpec(
            num_scalar_prefetch=1,
            grid=(rows // step,),
            in_specs=[ANY] * len(pieces)
            + [pl.BlockSpec((step, width), lambda i, *_: (i, 0)), whole(bias)],
            out_specs=[block, block, block, pl.BlockSpec((width, total_cols), lambda i, *_: (0, 0))],
            scratch_shapes=[pltpu.SemaphoreType.DMA((len(pieces),))],
        ),
        out_shape=[struct((rows, wide), BF16)] * 3 + [struct((width, total_cols), BF16)],
        compiler_params=params(28),
        cost_estimate=cost(14),
        name="qkv",
    )(offsets, *pieces, x, bias)


def head_spans(heads, wide):
    spans = []
    for head in range(heads):
        first, last = head * HD, head * HD + HD
        low = first // 128 * 128
        high = min((last + 127) // 128 * 128, wide)
        spans.append((low, high, first, last))
    return spans


def lane_mask(span):
    low, high, first, last = span
    lane = lax.broadcasted_iota(jnp.int32, (1, high - low), 1) + low
    return jnp.where((lane >= first) & (lane < last), 1.0, 0.0).astype(BF16)


def shift_counts():
    token = lax.broadcasted_iota(jnp.int32, (ROWS, 128), 0)
    row = (token * 9363) >> 17
    col = token - row * WIN
    return jnp.maximum(WIN - 1 - row, 0), WIN - 1 - col


def shift_lanes(values, counts, back):
    for step in (1, 2, 4, 8):
        moved = pltpu.roll(values, step if back else 128 - step, 1)
        values = jnp.where((counts & step) != 0, moved, values)
    return values


def lane_kind():
    lane = lax.broadcasted_iota(jnp.int32, (ROWS, 128), 1) & 31
    return lane < WIN, (lane >= 16) & (lane < 16 + WIN), lane == 31


def split_two(values):
    high = values.astype(BF16)
    return high, (values - high.astype(F32)).astype(BF16)


def bias_operand(q, rel_high, rel_low, counts):
    table = (dot(q, rel_high) + dot(q, rel_low)) * (1.0 / SCALE)
    by_row = shift_lanes(table[:, :128], counts[0], False)
    by_col = shift_lanes(table[:, 128:], counts[1], False)
    is_row, is_col, is_last = lane_kind()
    packed = jnp.where(
        is_row, by_row, jnp.where(is_col, by_col, jnp.where(is_last, 1.0, 0.0))
    )
    high, low = split_two(packed)
    return jnp.concatenate([high, low], axis=1)


def add_lanes(parts, values, span):
    low, high = span[0], span[1]
    for index in range(low // 128, high // 128):
        piece = values[:, index * 128 - low : index * 128 - low + 128]
        parts[index] = piece if parts[index] is None else parts[index] + piece


def attend_kernel(heads, split, q_ref, k_ref, v_ref, rh_ref, rl_ref, mark_ref, w_ref, *outs):
    mixed_ref, shares_ref = outs[:2]
    q, k, v = q_ref[...], k_ref[...], v_ref[...]
    wide = q.shape[1]
    bias = bias_operand(q, rh_ref[...], rl_ref[...], shift_counts())
    parts = [None] * (wide // 128)
    for head, span in enumerate(head_spans(heads, wide)):
        mask = lane_mask(span)
        cut = slice(span[0], span[1])
        scores = dot_nt(
            jnp.concatenate([q[:, cut], bias], axis=1),
            jnp.concatenate([k[:, cut] * mask, mark_ref[head]], axis=1),
        )
        top = jnp.max(scores, axis=-1, keepdims=True)
        shifted = jnp.exp(SCALE * (scores - top))
        norm = jnp.sum(shifted, axis=-1, keepdims=True)
        shares = (shifted * (1.0 / norm)).astype(BF16)
        shares_ref[:, head * 256 : head * 256 + ROWS] = shares
        add_lanes(parts, dot(shares, v[:, cut] * mask), span)
    mixed = jnp.concatenate(parts, axis=1).astype(BF16)
    cols = heads * HD
    mixed_ref[...] = mixed[:, :cols]
    branch = dot_nt(mixed, w_ref[...]).astype(BF16)
    if split:
        step = pl.program_id(0)
        for sent in range(split):

            @pl.when(step == sent)
            def _(sent=sent):
                outs[3 + sent][...] = branch

        @pl.when(step >= split)
        def _():
            outs[2][...] = branch
    else:
        outs[2][...] = branch


def split_specs(windows, split, width):
    rows = ROWS * (windows - split)
    if not split:
        return [pl.BlockSpec((ROWS, width), lambda i: (i, 0))], [struct((rows, width), BF16)]
    return (
        [
            pl.BlockSpec((ROWS, width), lambda i: (jnp.maximum(i - split, 0), 0)),
            pl.BlockSpec((ROWS, width), lambda i: (jnp.minimum(i, split - 1), 0)),
        ],
        [struct((rows, width), BF16), struct((ROWS * split, width), BF16)],
    )


def attend(heads, part, windows, split, q, k, v, rel_high, rel_low, marks, weights):
    wide = q.shape[1]
    width = weights.shape[0]

    def place(i):
        return (i + split) % windows if split else i

    block = pl.BlockSpec((ROWS, wide), lambda i: (part * windows + place(i), 0))
    specs, shapes = split_specs(windows, split, width)
    if split:
        one = struct((ROWS, width), BF16)
        specs, shapes = specs[:1] + [whole(one)] * split, shapes[:1] + [one] * split
    return pl.pallas_call(
        partial(attend_kernel, heads, split),
        grid=(windows,),
        in_specs=[
            block,
            block,
            block,
            whole(rel_high),
            whole(rel_low),
            whole(marks),
            pl.BlockSpec((width, wide), lambda i: (0, 0)),
        ],
        out_specs=[
            pl.BlockSpec((ROWS, heads * HD), lambda i: (place(i), 0)),
            pl.BlockSpec((ROWS, heads * 256), lambda i: (place(i), 0)),
        ]
        + specs,
        out_shape=[
            struct((windows * ROWS, heads * HD), BF16),
            struct((windows * ROWS, heads * 256), BF16),
        ]
        + shapes,
        compiler_params=params(16),
        cost_estimate=cost(13.5),
        name="attend",
    )(q, k, v, rel_high, rel_low, marks, weights)


def attend_back_kernel(heads, windows, split, count, *refs):
    pieces = refs[:count]
    q_ref, k_ref, v_ref, shares_ref, rh_ref, mark_ref, w_ref = refs[count : count + 7]
    normed_ref, valid_ref = refs[count + 7 : count + 9]
    grads_ref, branch_ref, rel_ref, sum_ref, norm_ref = refs[count + 9 : count + 14]
    outs = refs[count + 14 :]
    step = pl.program_id(0)

    @pl.when(step == 0)
    def _():
        start = 0
        for piece in pieces:
            branch_ref[start : start + piece.shape[0]] = piece[...]
            start += piece.shape[0]
        rel_ref[...] = jnp.zeros(rel_ref.shape, F32)
        sum_ref[...] = jnp.zeros(sum_ref.shape, F32)
        norm_ref[...] = jnp.zeros(norm_ref.shape, F32)

    place = lax.rem(step + split, windows) if split else step
    q, k, v = q_ref[...], k_ref[...], v_ref[...]
    wide = q.shape[1]
    top = branch_ref[pl.ds(pl.multiple_of(place * ROWS, 16), ROWS), :]
    grad_mixed = dot(top, w_ref[:, :wide]).astype(BF16)
    grad_q, grad_k, grad_v = ([None] * (wide // 128) for _ in range(3))
    grad_bias = None
    for head, span in enumerate(head_spans(heads, wide)):
        mask = lane_mask(span)
        cut = slice(span[0], span[1])
        size = span[1] - span[0]
        upper = grad_mixed[:, cut]
        rounded = shares_ref[:, head * 256 : head * 256 + ROWS]
        shares = rounded.astype(F32)
        weighted = shares * dot_nt(upper, v[:, cut] * mask)
        inner = jnp.sum(weighted, axis=-1, keepdims=True)
        grad_scores = (weighted - shares * inner).astype(BF16)
        add_lanes(grad_v, dot_tn(rounded, upper * mask), span)
        both = dot(
            grad_scores,
            jnp.concatenate([k[:, cut] * mask, mark_ref[head][:, :128]], axis=1),
        )
        add_lanes(grad_q, both[:, :size], span)
        part = both[:, size:]
        grad_bias = part if grad_bias is None else grad_bias + part
        add_lanes(grad_k, dot_tn(grad_scores, q[:, cut] * mask), span)
    counts = shift_counts()
    is_row, is_col, _ = lane_kind()
    by_row = shift_lanes(jnp.where(is_row, grad_bias, 0.0), counts[0], True)
    by_col = shift_lanes(jnp.where(is_col, grad_bias, 0.0), counts[1], True)
    packed = jnp.concatenate([by_row, by_col], axis=1).astype(BF16)
    extra = dot_nt(packed, rh_ref[...])
    rel_ref[...] += dot_tn(packed, q)
    grad_q = (SCALE * jnp.concatenate(grad_q, axis=1) + extra).astype(BF16)
    grad_k = (SCALE * jnp.concatenate(grad_k, axis=1)).astype(BF16)
    grad_v = jnp.concatenate(grad_v, axis=1).astype(BF16)
    cols = heads * HD
    for slot, grad in enumerate((grad_q, grad_k, grad_v)):
        grads_ref[:, slot * cols : (slot + 1) * cols] = grad[:, :cols]
    packed_grads = grads_ref[...]
    sum_ref[...] += jnp.sum(packed_grads.astype(F32), axis=0, keepdims=True)
    partial_sum = dot_nt(packed_grads, w_ref[:, wide:])
    norm_ref[0:1] += jnp.sum(partial_sum * normed_ref[...].astype(F32), axis=0, keepdims=True)
    norm_ref[1:2] += jnp.sum(partial_sum * valid_ref[...], axis=0, keepdims=True)
    result = partial_sum.astype(BF16)
    if split:
        keep_ref, send_ref = outs

        @pl.when(step < split)
        def _():
            send_ref[...] = result

        @pl.when(step >= split)
        def _():
            keep_ref[...] = result
    else:
        outs[0][...] = result


def attend_back(
    heads, part, windows, split, pieces, q, k, v, shares, rel_high, marks, weights, normed, valid
):
    wide = q.shape[1]
    width = weights.shape[0]

    def place(i):
        return (i + split) % windows if split else i

    block = pl.BlockSpec((ROWS, wide), lambda i: (part * windows + place(i), 0))
    specs, shapes = split_specs(windows, split, width)
    rows = windows * ROWS
    branch = struct((rows, width), BF16)
    rel = struct((256, wide), F32)
    sums = struct((1, 3 * heads * HD), F32)
    norms = struct((2, width), F32)
    return pl.pallas_call(
        partial(attend_back_kernel, heads, windows, split, len(pieces)),
        grid=(windows,),
        in_specs=[whole(piece) for piece in pieces]
        + [
            block,
            block,
            block,
            pl.BlockSpec((ROWS, heads * 256), lambda i: (place(i), 0)),
            whole(rel_high),
            whole(marks),
            whole(weights),
            pl.BlockSpec((ROWS, width), lambda i: (part * windows + place(i), 0)),
            pl.BlockSpec((ROWS, 1), lambda i: (part * windows + place(i), 0)),
        ],
        out_specs=[
            pl.BlockSpec((ROWS, 3 * heads * HD), lambda i: (place(i), 0)),
            whole(branch),
            whole(rel),
            whole(sums),
            whole(norms),
        ]
        + specs,
        out_shape=[struct((rows, 3 * heads * HD), BF16), branch, rel, sums, norms] + shapes,
        compiler_params=params(28),
        cost_estimate=cost(18.5),
        name="attend_back",
    )(*pieces, q, k, v, shares, rel_high, marks, weights, normed, valid)


def mlp_kernel(count, weights, split, offsets, *refs):
    pieces = refs[:count]
    weight_pieces = refs[count : count + weights]
    refs = refs[count + weights :]
    after_any, top_ref, bias_ref, down_bias_ref = refs[:4]
    active_ref, hidden_ref, normed_any, sum_ref = refs[4:8]
    outs = refs[8 : 12 if split else 10]
    up, down, normed_ref, after_ref, send_ref, out_send_ref, sems, row_sems = refs[len(outs) + 8 :]
    step = pl.program_id(0)
    steps = pl.num_programs(0)
    block = top_ref.shape[0]
    units = up.shape[1]
    copies = []
    for half, target in enumerate((down, up)):
        copies.append([])
        for index, piece in enumerate(weight_pieces):
            rows = piece.shape[0]
            start = pl.multiple_of(offsets[index], 16)
            copies[half].append(
                pltpu.make_async_copy(
                    piece.at[:, half * units : (half + 1) * units],
                    target.at[pl.ds(start, rows)],
                    sems.at[half, index],
                )
            )
    row_copies, start = [], 0
    for index, piece in enumerate(pieces):
        rows = piece.shape[0]
        row_copies.append(
            pltpu.make_async_copy(
                piece, normed_ref.at[pl.ds(start, rows)], row_sems.at[index]
            )
        )
        start += rows
    normed_out = pltpu.make_async_copy(normed_ref, normed_any, row_sems.at[count])
    after_in = pltpu.make_async_copy(after_any, after_ref, row_sems.at[count + 1])
    if split:
        send_out = pltpu.make_async_copy(send_ref, outs[1], row_sems.at[count + 2])
        out_send_out = pltpu.make_async_copy(out_send_ref, outs[3], row_sems.at[count + 3])

    @pl.when(step == 0)
    def _():
        for copy in row_copies + copies[1] + copies[0]:
            copy.start()
        after_in.start()
        sum_ref[...] = jnp.zeros(sum_ref.shape, F32)
        for copy in row_copies + copies[1]:
            copy.wait()
        normed_out.start()

    place = 1 - step if split else step
    normed = normed_ref[pl.ds(pl.multiple_of(place * block, 16), block), :]
    hidden = dot(normed, up[...]) + bias_ref[...]

    @pl.when(step == 0)
    def _():
        for copy in copies[0]:
            copy.wait()

    half = 0.5 * (1.0 + lax.erf(hidden * (0.5**0.5)))
    slope = half + hidden * jnp.exp(-0.5 * hidden * hidden) * float((2.0 * np.pi) ** -0.5)
    active = (hidden * half).astype(BF16)
    active_ref[...] = active
    grad = (dot(top_ref[...], down[...]) * slope).astype(BF16)
    hidden_ref[...] = grad
    sum_ref[...] += jnp.sum(grad.astype(F32), axis=0, keepdims=True)
    back = dot_nt(grad, up[...]).astype(BF16)
    result = dot_nt(active, down[...])
    if split:

        @pl.when(step == 0)
        def _():
            send_ref[...] = back
            out_send_ref[...] = result.astype(BF16)
            send_out.start()
            out_send_out.start()
            after_in.wait()

        @pl.when(step == 1)
        def _():
            outs[0][...] = back
            own = result[:ROWS] + after_ref[...] + down_bias_ref[...]
            outs[2][:ROWS] = own.astype(BF16)
            outs[2][ROWS:] = result[ROWS:].astype(BF16)
            send_out.wait()
            out_send_out.wait()
    else:
        outs[0][...] = back
        outs[1][...] = result.astype(BF16)

        @pl.when(step == 0)
        def _():
            after_in.wait()

    @pl.when(step == steps - 1)
    def _():
        normed_out.wait()


def mlp(offsets, pieces, weight_pieces, top, part, bias, after, down_bias, split):
    rows = sum(piece.shape[0] for piece in pieces)
    width = pieces[0].shape[1]
    units = weight_pieces[0].shape[1] // 2
    block = 2 * ROWS
    blocks = rows // block
    normed = struct((rows, width), BF16)
    sums = struct((1, units), F32)

    def place(i):
        return 1 - i if split else i

    wide = pl.BlockSpec((block, units), lambda i, *_: (place(i), 0))
    back = struct((block, width), BF16)
    if split:
        back_specs, back_shapes = [whole(back), ANY] * 2, [back] * 4
    else:
        back_specs = [pl.BlockSpec((block, width), lambda i, *_: (i, 0))] * 2
        back_shapes = [normed] * 2
    return pl.pallas_call(
        partial(mlp_kernel, len(pieces), len(weight_pieces), split),
        grid_spec=pltpu.PrefetchScalarGridSpec(
            num_scalar_prefetch=1,
            grid=(blocks,),
            in_specs=[ANY] * (len(pieces) + len(weight_pieces) + 1)
            + [
                pl.BlockSpec((block, width), lambda i, *_: (part * blocks + place(i), 0)),
                whole(bias),
                whole(down_bias),
            ],
            out_specs=[wide, wide, ANY, whole(sums)] + back_specs,
            scratch_shapes=[
                pltpu.VMEM((width, units), BF16),
                pltpu.VMEM((width, units), BF16),
                pltpu.VMEM((rows, width), BF16),
                pltpu.VMEM(after.shape, F32),
                pltpu.VMEM((block, width), BF16),
                pltpu.VMEM((block, width), BF16),
                pltpu.SemaphoreType.DMA((2, len(weight_pieces))),
                pltpu.SemaphoreType.DMA((len(pieces) + 4,)),
            ],
        ),
        out_shape=[struct((rows, units), BF16)] * 2 + [normed, sums] + back_shapes,
        compiler_params=params(48),
        cost_estimate=cost(21),
        name="mlp",
    )(offsets, *pieces, *weight_pieces, after, top, bias, down_bias)


SEND_PARTS = {2: ((2, 3), (0, 1)), 3: ((3,), (1, 2), (0,))}


def weight_grad_kernel(sizes, share, sends, targets, *refs):
    count = 2 * sum(sizes)
    operands = refs[:count]
    outs, (result, sems) = refs[count:-2], refs[-2:]
    keep_ref = outs[sends] if sends else None
    pair_ref = None if sends else outs[0]
    lead = keep_ref.shape[2] if sends else 0
    step = pl.program_id(0)
    steps = pl.num_programs(0)
    chunk = operands[0].shape[1]
    pieces = chunk // share
    base = pl.multiple_of(step * chunk, 16)
    at, first = 0, 0
    for size in sizes:
        value = None
        for _ in range(size):
            left, right = operands[at], operands[at + 1]
            at += 2
            term = dot_tn(left[...], right[...])
            value = term if value is None else value + term
        span = value.shape[1]
        result[pl.ds(base, chunk), first : first + span] = value.astype(BF16)
        first += span

    def copy(index, out, slot):
        return pltpu.make_async_copy(
            result.at[pl.ds(pl.multiple_of(index * share, 16), share), pl.ds(0, lead)],
            out.at[slot],
            sems.at[0, index],
        )

    def pair_copy(index, slot):
        return pltpu.make_async_copy(
            result.at[
                pl.ds(pl.multiple_of(index * share, 16), share),
                pl.ds(lead, result.shape[1] - lead),
            ],
            pair_ref.at[lax.rem(slot, 4), 1 - slot // 4],
            sems.at[1, index],
        )

    for piece in range(pieces):
        index = step * pieces + piece
        slot = targets[index]

        if lead:

            for out, slots in zip(outs, SEND_PARTS[sends]):

                @pl.when((slot >= slots[0]) & (slot <= slots[-1]))
                def _(out=out, slots=slots):
                    copy(index, out, slot - slots[0]).start()

            @pl.when(slot >= 4)
            def _():
                copy(index, keep_ref, slot - 4).start()

        if pair_ref is not None:
            pair_copy(index, slot).start()

    @pl.when(step == steps - 1)
    def _():
        for index in range(8):
            if lead:
                copy(index, keep_ref, 0).wait()
            if pair_ref is not None:
                pair_copy(index, 0).wait()


def plain_grad_kernel(sizes, *refs):
    count = 2 * sum(sizes)
    operands, out_ref = refs[:count], refs[count]
    at, first = 0, 0
    for size in sizes:
        value = None
        for _ in range(size):
            left, right = operands[at], operands[at + 1]
            at += 2
            term = dot_tn(left[...], right[...])
            value = term if value is None else value + term
        span = value.shape[1]
        out_ref[:, first : first + span] = value.astype(BF16)
        first += span


def weight_grad(targets, groups, share, sends=0):
    operands, specs = [], []
    chunk = 640 if targets is not None else 256
    total_cols = 0
    for group in groups:
        for left, at, rows, right in group:
            operands += [left, right]
            specs.append(pl.BlockSpec((rows, chunk), lambda i, *_, at=at: (at, i)))
            specs.append(whole(right))
        total_cols += group[0][3].shape[1]
    width = operands[0].shape[1]
    sizes = [len(group) for group in groups]
    if targets is None:
        return [
            pl.pallas_call(
                partial(plain_grad_kernel, sizes),
                grid=(width // chunk,),
                in_specs=specs,
                out_specs=pl.BlockSpec((chunk, total_cols), lambda i: (i, 0)),
                out_shape=struct((width, total_cols), BF16),
                compiler_params=params(32),
                cost_estimate=cost(13),
        name="weight_grad",
            )(*operands)
        ]
    if sends:
        counts = [len(slots) for slots in SEND_PARTS[sends]] + [4]
        shapes = [struct((count, share, total_cols), BF16) for count in counts]
    else:
        shapes = [struct((4, 2, share, total_cols), BF16)]
    return pl.pallas_call(
        partial(weight_grad_kernel, sizes, share, sends),
        grid_spec=pltpu.PrefetchScalarGridSpec(
            num_scalar_prefetch=1,
            grid=(width // chunk,),
            in_specs=specs,
            out_specs=[ANY] * len(shapes),
            scratch_shapes=[
                pltpu.VMEM((width, total_cols), BF16),
                pltpu.SemaphoreType.DMA((2, 8)),
            ],
        ),
        out_shape=shapes,
        compiler_params=params(32),
        cost_estimate=cost(13),
        name="weight_grad",
    )(targets, *operands)


def combine_kernel(layout, *refs):
    outs = refs[len(refs) - len(layout) :]
    at = 0
    for cells, out in zip(layout, outs):
        for row, lane, rows, lanes, terms in cells:
            value = None
            for lead, first in terms:
                term = refs[at][(0,) * lead + (slice(None), slice(first, first + lanes))]
                at += 1
                value = term.astype(F32) if value is None else value + term.astype(F32)
            out[row : row + rows, lane : lane + lanes] = value.astype(BF16)


def combine(*outs):
    operands, specs, layout = [], [], []
    for _, cells in outs:
        layout.append([])
        for row, lane, rows, lanes, terms in cells:
            places = []
            for array, index, first in terms:
                lead = array.ndim - 2
                block = (1,) * lead + (rows, array.shape[-1])
                place = tuple(index) + (0,) * (array.ndim - len(index))
                operands.append(array)
                specs.append(pl.BlockSpec(block, lambda i, place=place: place))
                places.append((lead, first))
            layout[-1].append((row, lane, rows, lanes, places))
    shapes = [struct(shape, BF16) for shape, _ in outs]
    return pl.pallas_call(
        partial(combine_kernel, layout),
        grid=(1,),
        in_specs=specs,
        out_specs=[whole(shape) for shape in shapes],
        out_shape=shapes,
        compiler_params=params(16),
        cost_estimate=cost(2),
        name="combine",
    )(*operands)


def place_kernel(order, *refs):
    pieces, out_ref = refs[:4], refs[4]
    for me in range(4):

        @pl.when(order[0] == me)
        def _(me=me):
            for part in range(pieces[0].shape[0] // ROWS):
                for index, step in enumerate((0, 2, 1, 3)):
                    start = (4 * part + (me ^ step)) * WTOK
                    value = pieces[index][part * ROWS : part * ROWS + WTOK]
                    out_ref[start : start + WTOK] = value.astype(F32)


def place_windows(order, pieces):
    height, width = pieces[0].shape
    rows = height // ROWS * 4 * WTOK
    lanes = width // 2
    return pl.pallas_call(
        place_kernel,
        grid_spec=pltpu.PrefetchScalarGridSpec(
            num_scalar_prefetch=1,
            grid=(2,),
            in_specs=[pl.BlockSpec((height, lanes), lambda i, *_: (0, i))] * 4,
            out_specs=pl.BlockSpec((rows, lanes), lambda i, *_: (0, i)),
        ),
        out_shape=struct((rows, width), F32),
        compiler_params=params(32),
        cost_estimate=cost(7),
        name="place_windows",
    )(order, *pieces)


def output_kernel(order, places, lives, *refs):
    pieces, out_ref, buffer = refs[:4], refs[4], refs[5]
    for me in range(4):

        @pl.when(order[0] == me)
        def _(me=me):
            for part in range(pieces[0].shape[0] // ROWS):
                for index, step in enumerate((0, 2, 1, 3)):
                    slot = 4 * part + (me ^ step)
                    value = pieces[index][part * ROWS : part * ROWS + WTOK].astype(F32)
                    value = value * token_valid(places[slot], lives[slot])
                    buffer[slot * WTOK : (slot + 1) * WTOK] = value

    out_ref[...] = buffer[...].astype(BF16)


def write_output(order, places, lives, pieces):
    height, width = pieces[0].shape
    rows = height // ROWS * 4 * WTOK
    lanes = width // 2
    return pl.pallas_call(
        output_kernel,
        grid_spec=pltpu.PrefetchScalarGridSpec(
            num_scalar_prefetch=3,
            grid=(2,),
            in_specs=[pl.BlockSpec((height, lanes), lambda i, *_: (0, i))] * 4,
            out_specs=pl.BlockSpec((rows, lanes), lambda i, *_: (0, i)),
            scratch_shapes=[pltpu.VMEM((rows, lanes), F32)],
        ),
        out_shape=struct((rows, width), BF16),
        compiler_params=params(32),
        cost_estimate=cost(7),
        name="write_output",
    )(order, places, lives, *pieces)


def key_marks(heads):
    marks = np.zeros((heads, ROWS, 256), np.float32)
    for head in range(heads):
        for token in range(WTOK):
            for half in (0, 128):
                marks[head, token, half + head * 32 + token // WIN] = 1.0
                marks[head, token, half + head * 32 + 16 + token % WIN] = 1.0
        marks[head, WTOK:, head * 32 + 31] = -1e30
    return marks.astype(BF16)


def rel_operand(rel_height, rel_width, heads, wide):
    high = rel_height[::-1].T
    flat = rel_width[::-1].T
    lanes = jnp.zeros((wide, 256), F32)

    def spread(block, row, lane):
        below = wide - row - HD
        return jnp.pad(block, ((row, below), (lane, 256 - lane - block.shape[1])))

    for head in range(heads):
        first = head * 32 + 16
        fit = min(RELN, 128 - first)
        lanes = lanes + spread(high, head * HD, head * 32)
        lanes = lanes + spread(flat[:, :fit], head * HD, 128 + first)
        if fit < RELN:
            lanes = lanes + spread(flat[:, fit:], head * HD, 128)
    return split_two(lanes)


def rel_result(sums, heads):
    high = jnp.zeros((RELN, HD), F32)
    flat = jnp.zeros((RELN, HD), F32)
    for head in range(heads):
        cols = sums[:, head * HD : head * HD + HD]
        high = high + cols[head * 32 : head * 32 + RELN]
        rolled = jnp.concatenate([cols[128:], cols[128:]], axis=0)
        flat = flat + rolled[head * 32 + 16 : head * 32 + 16 + RELN]
    return high[::-1], flat[::-1]


def add_all(values):
    out = values[0]
    for value in values[1:]:
        out = out + value
    return out


def tie(value, *others):
    return lax.optimization_barrier((value,) + others)[0]


def sync(*values):
    return lax.optimization_barrier(values)


def body(
    block_input,
    window_place,
    slot_live,
    norm_one_gain,
    norm_one_shift,
    qkv_weight,
    qv_bias,
    proj_weight,
    proj_bias,
    norm_two_gain,
    norm_two_shift,
    up_weight,
    up_bias,
    down_weight,
    down_bias,
    rel_height,
    rel_width,
    cotangent,
):
    data_parts = lax.axis_size("dp")
    model_parts = lax.axis_size("mp")
    data_index = lax.axis_index("dp")
    model_index = lax.axis_index("mp")
    width = block_input.shape[1]
    share = qkv_weight.shape[1]
    cols = qkv_weight.shape[2]
    heads = cols // HD
    wide = (cols + 127) // 128 * 128
    units = up_weight.shape[1]
    slots = window_place.shape[0]
    rings = data_parts == 8 and model_parts == 4 and slots == 8
    padded = (slots + model_parts - 1) // model_parts * model_parts
    halves = padded // 4 if rings else 1
    windows = padded // halves
    split = 2 if rings else 0
    part_rows = windows * ROWS
    own_rows = part_rows // model_parts

    if rings:
        depth, side = data_index // 2, data_index % 2
        y_bit, core_bit = model_index // 2, model_index % 2
        over_x = partial(lax.ppermute, axis_name="dp", perm=[(d, d ^ 1) for d in range(8)])
        over_z = partial(lax.ppermute, axis_name="dp", perm=[(d, (d + 2) % 8) for d in range(8)])
        over_y = partial(lax.ppermute, axis_name="mp", perm=[(m, m ^ 2) for m in range(4)])
        over_core = partial(lax.ppermute, axis_name="mp", perm=[(m, m ^ 1) for m in range(4)])

    def gather(piece):
        return [lax.all_gather(piece, "dp", axis=0, tiled=True)]

    if rings:
        offsets = []
        for back in range(4):
            behind = (depth - back) % 4
            offsets += [share * (2 * behind + side), share * (2 * behind + 1 - side)]
        offsets = jnp.stack(offsets).astype(jnp.int32)
    else:
        offsets = jnp.zeros((1,), jnp.int32)

    def scatter(parts):
        return lax.psum_scatter(parts[0], "dp", scatter_dimension=0, tiled=True).astype(F32)

    def rows_scatter(parts):
        return [lax.psum_scatter(parts[0], "mp", scatter_dimension=0, tiled=True)]

    def rows_gather(own):
        return [lax.all_gather(own, "mp", axis=0, tiled=True)]

    def own_slice(array):
        rows = array.shape[0] // model_parts
        return lax.dynamic_slice_in_dim(array, model_index * rows, rows, 0)

    first_piece = jnp.concatenate(
        [
            jnp.pad(proj_weight.T, ((0, 0), (0, wide - cols))),
            qkv_weight[0],
            qkv_weight[1],
            qkv_weight[2],
        ],
        axis=1,
    )
    other_piece = jnp.concatenate([down_weight.T, up_weight], 1)

    row = lambda v: v.reshape(1, -1)
    gain_one, shift_one = row(norm_one_gain), row(norm_one_shift)
    gain_two, shift_two = row(norm_two_gain), row(norm_two_shift)
    bias_local = lax.dynamic_slice_in_dim(qv_bias, model_index * cols, cols, 1)
    bias_qkv = row(jnp.stack([bias_local[0], jnp.zeros_like(bias_local[0]), bias_local[1]]))
    up_local = row(lax.dynamic_slice_in_dim(up_bias, model_index * units, units, 0))
    rel_high, rel_low = rel_operand(rel_height, rel_width, heads, wide)
    marks = jnp.asarray(key_marks(heads))

    steps = (0, 2, 1, 3)
    if rings:
        local = [model_index ^ step for step in steps]
        places = [4 * part + spot for part in range(halves) for spot in local]
    else:
        local = [jnp.int32(spot) for spot in range(windows)]
        places = local
    local = jnp.stack(local).astype(jnp.int32)
    places = jnp.stack(places).astype(jnp.int32)
    if rings:
        targets = []
        for d in range(8):
            ahead = (d // 2 - depth) % 4
            targets.append(ahead + jnp.where(d % 2 == side, 4, 0))
        targets = jnp.stack(targets).astype(jnp.int32)
    else:
        targets = None

    def by_window(array):
        array = array.reshape((slots, WTOK) + array.shape[1:])
        return jnp.pad(array, [(0, padded - slots)] + [(0, 0)] * (array.ndim - 1))

    places_all = jnp.pad(window_place, (0, padded - slots))
    lives_all = jnp.pad(slot_live, (0, padded - slots))
    blocks = [(part, part_rows) for part in range(halves)]

    def start(x):
        every = 4 if rings else 1
        return prepare(places, places_all, lives_all, x, gain_one, shift_one, every)

    def masked(top):
        return mask_rows(places, places_all, lives_all, top)

    def attention(part, q, k, v, weights):
        return attend(heads, part, windows, split, q, k, v, rel_high, rel_low, marks, weights)

    def attention_back(part, pieces, q, k, v, shares, weights):
        return attend_back(
            heads,
            part,
            windows,
            split,
            pieces,
            q,
            k,
            v,
            shares,
            rel_high,
            marks,
            weights,
            normed,
            valid,
        )

    def down_groups(mlps):
        return [[(grad_top, *blocks[i], mlps[i][0]) for i in range(halves)]]

    def up_groups(mlps):
        return [[(mlps[i][2], 0, part_rows, mlps[i][1]) for i in range(halves)]]

    def first_groups(backs, attended):
        return [
            [(normed, *blocks[i], backs[i][0]) for i in range(halves)],
            [(backs[i][1], 0, part_rows, attended[i][0]) for i in range(halves)],
        ]

    def bundle(sums_two, backs, mlps):
        qv_sums = add_all([item[3] for item in backs]).reshape(3, cols)[0::2]
        rel_sums = rel_result(add_all([item[2] for item in backs]), heads)
        up_sums = add_all([item[3] for item in mlps]).reshape(units)
        qv_full = lax.dynamic_update_slice_in_dim(
            jnp.zeros((2, width), F32), qv_sums, model_index * cols, 1
        )
        up_full = lax.dynamic_update_slice_in_dim(
            jnp.zeros(up_bias.shape, F32), up_sums, model_index * units, 0
        )
        norms = add_all([item[4] for item in backs])
        arrays = [norms, add_all(sums_two), up_full, qv_full, *rel_sums]
        flat = jnp.concatenate([array.reshape(-1) for array in arrays])
        count = (flat.size + 1023) // 1024 * 1024
        return jnp.pad(flat, (0, count - flat.size)).reshape(-1, 128)

    x_windows = by_window(block_input)
    if not rings:
        first_weights, other_weights = gather(first_piece), gather(other_piece)
        rows_in, own_valid, normed, valid = start(x_windows)
        grad_top = masked(by_window(cotangent))
        own_in, own_top, own_valid = own_slice(rows_in), own_slice(grad_top), own_slice(own_valid)
        q, k, v, weights = project(offsets, first_weights, normed, bias_qkv, cols, wide)
        attended = [attention(0, q, k, v, weights)]
        after, normed_two = norm_two(
            rows_scatter(attended[0][2:]), own_in, 0, row(proj_bias), gain_two, shift_two
        )
        none = jnp.zeros((8, 128), F32)
        mlps = [
            mlp(
                offsets,
                rows_gather(normed_two),
                other_weights,
                grad_top,
                0,
                up_local,
                none,
                row(down_bias),
                False,
            )
        ]
        grad_after, branch, sums = norm_two_back(
            rows_scatter(mlps[0][4:5]), after, own_top, 0, gain_two
        )
        sums_two = [sums]
        result = mlps[0][5]
        own = finish(rows_scatter([result]), after, own_valid, 0, row(down_bias))

        def unpad(array):
            array = array.reshape(padded, ROWS, width)[:slots, :WTOK]
            return array.reshape(slots * WTOK, width)

        block_output = unpad(rows_gather(own)[0])
        down_grad = scatter(weight_grad(None, down_groups(mlps), share))
        up_grad = scatter(weight_grad(None, up_groups(mlps), share))
        backs = [attention_back(0, rows_gather(branch), q, k, v, attended[0][1], weights)]
        parts = [(part, 0) for part in rows_scatter(backs[0][5:])]
        own = norm_one_back([(parts, grad_after)], own_in, own_valid, gain_one)
        input_grad = unpad(rows_gather(own)[0]).astype(F32)
        first_grad = scatter(weight_grad(None, first_groups(backs, attended), share))
        vector = lax.psum(bundle(sums_two, backs, mlps), ("dp", "mp"))
    else:
        def second_norm(part, keep, came, crossed):
            return norm_two(
                [keep, came, crossed], rows_in, part, bias_proj, gain_two, shift_two
            )

        def second_back(part, after, keep, came, crossed):
            return norm_two_back([keep, came, crossed], after, grad_top, 4 * part, gain_two)

        def spread(own, across):
            return [own, across, over_core(own), over_core(across)]

        rows = (ROWS, width)

        def second(keep, came, at=0):
            return (at, 0, *rows, [(keep, (1,), 0), (came, (1,), 0)])

        z1, x0 = over_z(first_piece), over_x(first_piece)
        z1, x0, x_windows, other_piece, rel_high, rel_low, cotangent = sync(
            z1, x0, x_windows, other_piece, rel_high, rel_low, cotangent
        )
        z2, x1 = over_z(z1), over_x(z1)
        rows_in, own_valid, normed, valid = start(x_windows)
        z2, x1, normed, cotangent, gain_two, shift_two, bias_proj, bias_down = sync(
            z2, x1, normed, cotangent, gain_two, shift_two, row(proj_bias), row(down_bias)
        )
        z3, x2 = over_z(z2), over_x(z2)
        z3, x2, normed, top_windows, other_piece = sync(
            z3, x2, normed, by_window(cotangent), other_piece
        )
        x3 = over_x(z3)
        oz1 = over_z(other_piece)
        grad_top = masked(top_windows)
        x3, normed, grad_top, other_late, gain_two, shift_two, bias_proj, bias_down = sync(
            x3, normed, grad_top, other_piece, gain_two, shift_two, bias_proj, bias_down
        )
        ox0 = over_x(other_late)
        first_weights = [first_piece, x0, z1, x1, z2, x2, z3, x3]
        q, k, v, weights = project(offsets, first_weights, normed, bias_qkv, cols, wide)
        oz1, ox0, q = sync(oz1, ox0, q)

        oz2, ox1 = over_z(oz1), over_x(oz1)
        a0 = attention(0, q, k, v, weights)
        oz2, ox1, a0 = sync(oz2, ox1, a0)
        oz3, ox2 = over_z(oz2), over_x(oz2)
        came0, came_y = over_core(a0[3]), over_core(a0[4])
        (passed0,) = combine((rows, [(0, 0, *rows, [(a0[2], (1,), 0), (came_y, (0,), 0)])]))
        crossed0 = over_y(passed0)
        a1 = attention(1, tie(q, passed0), k, v, weights)
        crossed0, a1 = sync(crossed0, a1)
        came_y, came1 = over_core(a1[4]), over_core(a1[3])
        (passed1,) = combine((rows, [(0, 0, *rows, [(a1[2], (1,), 0), (came_y, (0,), 0)])]))
        crossed1 = over_y(passed1)
        after0, own0 = second_norm(0, tie(a0[2], passed1, came1), came0, crossed0)
        across0 = over_y(own0)
        oz3, ox2 = sync(oz3, ox2, own0)[:2]
        ox3, ox4 = over_x(oz3[: share // 2]), over_x(oz3[share // 2 :])
        attended = [a0, a1]
        after1, own1 = second_norm(1, tie(a1[2], own0), came1, crossed1)
        ox3, ox4, across0, own1 = sync(ox3, ox4, across0, own1)
        other_weights = [other_piece, ox0, oz1, ox1, oz2, ox2, oz3, ox3, ox4]
        other_offsets = jnp.concatenate([offsets, offsets[7:] + share // 2])
        across1 = over_y(own1)
        pieces0 = spread(tie(own0, own1), across0)

        m0 = mlp(other_offsets, pieces0, other_weights, grad_top, 0, up_local, after0, bias_down, True)
        across1, m0 = sync(across1, m0)
        pieces1 = spread(own1, across1)
        came0, out_came0 = over_core(m0[5]), over_core(m0[7])
        (passed0,) = combine((rows, [second(m0[4], came0)]))
        crossed0 = over_y(passed0)
        pieces1[0] = tie(pieces1[0], passed0)
        m1 = mlp(other_offsets, pieces1, other_weights, grad_top, 1, up_local, after1, bias_down, True)
        crossed0, out_came0, m1 = sync(crossed0, out_came0, m1)
        mlps = [m0, m1]
        came1, out_came1 = over_core(m1[5]), over_core(m1[7])
        grad_after0, branch0, sums0 = second_back(0, after0, m0[4], came0, crossed0)
        across0 = over_y(branch0)
        passed1, out_passed0, out_passed1 = combine(
            (rows, [second(tie(m1[4], branch0), came1)]),
            (rows, [second(m0[6], out_came0)]),
            (rows, [second(m1[6], out_came1)]),
        )
        left = tie(m0, passed1)
        (down_pairs,) = weight_grad(targets, down_groups([left, m1]), share)
        across0, passed1, down_pairs = sync(across0, passed1, down_pairs)
        crossed1 = over_y(passed1)
        branches0 = spread(branch0, across0)
        left = tie(m0, down_pairs)
        up_high, up_low, up_keep = weight_grad(targets, up_groups([left, m1]), share, 2)
        down_held = over_z(down_pairs[3])
        crossed1, branches0, up_high, up_low, up_keep = sync(
            crossed1, branches0, up_high, up_low, up_keep
        )

        up_came_high = over_x(up_high)

        def down_cells(k, held, lane):
            return [
                (0, half * units, share, units, [(down_pairs, (k, half), 0), (held, at, first)])
                for half, (at, first) in enumerate(lane)
            ]

        grad_after1, branch1, sums1 = second_back(1, after1, m1[4], came1, crossed1)
        sums_two = [sums0, sums1]
        across1 = over_y(branch1)
        (down_held,) = combine(
            (
                (share, 2 * units),
                down_cells(2, tie(down_held, branch1), [((0,), 0), ((1,), 0)]),
            )
        )
        branches0[0] = tie(branches0[0], down_held)
        down_held = over_z(down_held)
        b0 = attention_back(0, branches0, q, k, v, a0[1], weights)
        across1, up_came_high, down_held, b0 = sync(across1, up_came_high, down_held, b0)
        branches1 = spread(branch1, across1)
        came0 = over_core(b0[6])
        up_came_low = over_x(up_low)

        passed0, held = combine(
            (rows, [second(b0[5], came0)]),
            ((share, 2 * units), down_cells(1, down_held, [((0,), 0), ((0,), units)])),
        )
        crossed0 = over_y(passed0)
        held = over_z(held)
        branches1[0] = tie(branches1[0], passed0)
        out_crossed0 = over_y(tie(out_passed0, passed0))
        b1 = attention_back(1, branches1, q, k, v, a1[1], weights)
        crossed0, held, up_came_low, out_crossed0, b1 = sync(
            crossed0, held, up_came_low, out_crossed0, b1
        )
        backs = [b0, b1]
        came1 = over_core(b1[6])
        vector = bundle(sums_two, backs, mlps)
        vector_came = lax.ppermute(vector, "mp", [(m, m ^ 1) for m in range(4)])
        came1, vector_came, vector = sync(came1, vector_came, vector)
        vector = vector + vector_came
        vector_came = lax.ppermute(vector, "mp", [(m, m ^ 2) for m in range(4)])
        down_held = held
        passed1, down_other, up_held = combine(
            (rows, [second(b1[5], came1)]),
            (
                (share, units),
                [(0, 0, share, units, [(down_pairs, (0, 1), 0), (down_held, (0,), units)])],
            ),
            (
                (share, units),
                [(0, 0, share, units, [(up_keep, (3,), 0), (up_came_high, (1,), 0)])],
            ),
        )
        crossed1 = over_y(passed1)
        up_held, down_other = over_z(up_held), over_x(down_other)
        left = tie(b0, passed1)
        out_crossed1 = over_y(tie(out_passed1, passed1))
        firsts = weight_grad(targets, first_groups([left, b1], attended), share, 3)
        crossed1, down_other, up_held, firsts = sync(crossed1, down_other, up_held, firsts)
        first_three, first_two, first_last, first_keep = firsts

        came_three = over_x(first_three)
        (up_sum,) = combine(
            (
                (share, units),
                [
                    (
                        0,
                        0,
                        share,
                        units,
                        [(up_keep, (2,), 0), (up_came_high, (0,), 0), (up_held, (0,), 0)],
                    )
                ],
            )
        )
        held = over_z(up_sum)
        own = norm_one_back(
            [
                ([(b0[5], 0), (came0, 0), (tie(crossed0, up_sum), 0)], grad_after0),
                ([(b1[5], 0), (came1, 0), (crossed1, 0)], grad_after1),
            ],
            rows_in,
            own_valid,
            gain_one,
        )
        in_across = over_y(tie(own, vector_came))
        (out_own,) = combine(
            (
                (2 * ROWS, width),
                [
                    (
                        part * ROWS,
                        0,
                        *rows,
                        [(keep, (0,), 0), (came, (0,), 0), (crossed, (0,), 0)],
                    )
                    for part, (keep, came, crossed) in enumerate(
                        (
                            (m0[6], out_came0, tie(out_crossed0, own)),
                            (m1[6], out_came1, out_crossed1),
                        )
                    )
                ],
            ),
        )
        came_three, held, own, out_own, vector, vector_came = sync(
            came_three, held, own, out_own, vector, vector_came
        )
        vector = vector + vector_came
        came_two = over_x(first_two)
        (held,) = combine(
            (
                (share, 2 * units),
                [
                    (0, 0, share, units, [(first_keep, (3,), 0), (came_three, (0,), 0)]),
                    (
                        0,
                        units,
                        share,
                        units,
                        [(up_keep, (1,), 0), (up_came_low, (1,), 0), (held, (0,), 0)],
                    ),
                ],
            ),
        )
        held = over_z(held)
        vector_came = lax.ppermute(vector, "dp", [(d, d ^ 2) for d in range(8)])
        out_across = over_y(tie(out_own, own))
        came_two, held, vector_came, in_across = sync(came_two, held, vector_came, in_across)
        vector = vector + vector_came
        up_last = held[:, units:]

        def first_cell(k, held):
            return (
                0,
                0,
                share,
                4 * cols,
                [(first_keep, (k,), 0), (came_two, (k - 1,), 0), (held, (0,), 0)],
            )

        (held,) = combine(((share, 4 * cols), [first_cell(2, held)]))
        held = over_z(held)
        vector_came = lax.ppermute(vector, "dp", [(d, d ^ 4) for d in range(8)])
        in_pieces = spread(own, in_across)
        input_grad = place_windows(local, in_pieces)
        held, vector_came, input_grad = sync(held, vector_came, input_grad)
        vector = vector + vector_came
        vector_came = lax.ppermute(vector, "dp", [(d, d ^ 1) for d in range(8)])
        came_last = over_x(tie(first_last, held))
        (held,) = combine(((share, 4 * cols), [first_cell(1, held)]))
        held = over_z(held)
        vector = vector + vector_came
        came_last, out_own, out_across = sync(came_last, out_own, out_across)
        out_pieces = spread(out_own, out_across)
        block_output = write_output(local, places_all, lives_all, out_pieces)

        def last(*values):
            out = values[0].astype(F32)
            for value in values[1:]:
                out = out + value.astype(F32)
            return out

        down_grad = last(down_pairs[0, 0], down_held[:, :units], down_other)
        up_grad = last(up_keep[0], up_came_low[0], up_last)
        first_grad = last(first_keep[0], came_last[0], held)

    shapes = [(2, width), (4, width), (up_bias.size,), (2, width), (RELN, HD), (RELN, HD)]
    outs, at = [], 0
    flat = vector.reshape(-1)
    for shape in shapes:
        size = int(np.prod(shape))
        outs.append(flat[at : at + size].reshape(shape))
        at += size
    one_sums, two_sums, up_bias_grad, qv_bias_grad, height_grad, width_grad = outs
    shift_one_grad = one_sums[1]
    gain_one_grad = (one_sums[0] - norm_one_shift * shift_one_grad) / norm_one_gain
    qkv_grad = jnp.stack([first_grad[:, slot * cols : (slot + 1) * cols] for slot in range(3)])
    proj_grad = first_grad[:, 3 * cols :].T
    return (
        block_output,
        input_grad,
        gain_one_grad,
        shift_one_grad,
        qkv_grad,
        qv_bias_grad,
        proj_grad,
        two_sums[2],
        two_sums[0],
        two_sums[1],
        up_grad,
        up_bias_grad,
        down_grad.T,
        two_sums[3],
        height_grad,
        width_grad,
    )


def solution(mesh):
    in_specs = (
        P("dp", None),
        P("dp"),
        P("dp"),
        P(),
        P(),
        P(None, "dp", "mp"),
        P(),
        P("mp", "dp"),
        P(),
        P(),
        P(),
        P("dp", "mp"),
        P(),
        P("mp", "dp"),
        P(),
        P(),
        P(),
        P("dp", None),
    )
    out_specs = (
        P("dp", None),
        P("dp", None),
        P(),
        P(),
        P(None, "dp", "mp"),
        P(),
        P("mp", "dp"),
        P(),
        P(),
        P(),
        P("dp", "mp"),
        P(),
        P("mp", "dp"),
        P(),
        P(),
        P(),
    )
    return jax.shard_map(body, mesh=mesh, in_specs=in_specs, out_specs=out_specs, check_vma=False)
```

```python
from functools import partial

import jax
import jax.numpy as jnp
import numpy as np
from jax import lax
from jax.experimental import pallas as pl
from jax.experimental.pallas import tpu as pltpu
from jax.sharding import PartitionSpec as P

HD = 80
WIN = 14
SIDE = 64
GRID = 5
WTOK = 196
RELN = 27
ROWS = 208
SCALE = HD ** (-0.5)
EPS = 1e-06
F32 = jnp.float32
BF16 = jnp.bfloat16
ANY = pl.BlockSpec(memory_space=pl.ANY)
highest = lax.Precision.HIGHEST


def dot(left, right):
    return lax.dot_general(left, right, (((1,), (0,)), ((), ())), preferred_element_type=F32)


def dot_nt(left, right):
    return lax.dot_general(left, right, (((1,), (1,)), ((), ())), preferred_element_type=F32)


def dot_tn(left, right):
    return lax.dot_general(left, right, (((0,), (0,)), ((), ())), preferred_element_type=F32)


def whole(array):
    zeros = (0,) * len(array.shape)
    return pl.BlockSpec(array.shape, lambda *_: zeros)


def params(megabytes):
    return pltpu.CompilerParams(vmem_limit_bytes=megabytes * 2**20)


def cost(micros):
    return pl.CostEstimate(
        flops=int(micros * 0.05e9), bytes_accessed=int(micros * 1.0e4), transcendentals=0
    )


def struct(shape, dtype):
    return jax.ShapeDtypeStruct(shape, dtype)


def assemble(offsets, pieces, target, sems):
    copies = []
    for index, piece in enumerate(pieces):
        count = piece.shape[0]
        start = pl.multiple_of(offsets[index], 16)
        copies.append(
            pltpu.make_async_copy(piece, target.at[pl.ds(start, count)], sems.at[index])
        )
    for copy in copies:
        copy.start()
    for copy in copies:
        copy.wait()


def norm_parts(values):
    center = jnp.mean(values, axis=-1, keepdims=True)
    centred = values - center
    spread = jnp.mean(centred * centred, axis=-1, keepdims=True)
    rstd = lax.rsqrt(spread + EPS)
    return centred * rstd, rstd


def token_valid(spot, live):
    token = lax.broadcasted_iota(jnp.int32, (WTOK, 1), 0)
    row = (token * 9363) >> 17
    col = token - row * WIN
    high = spot // GRID * WIN
    wide = spot % GRID * WIN
    inside = (high + row < SIDE) & (wide + col < SIDE) & (live == 1)
    return jnp.where(inside, 1.0, 0.0).astype(F32)


def pad_rows(values):
    empty = jnp.zeros((ROWS - WTOK, values.shape[1]), F32)
    return jnp.concatenate([values, empty], axis=0)


def prepare_kernel(every, order, places, lives, x_ref, gain_ref, shift_ref, *outs):
    rows_ref, own_ref, normed_ref, valid_ref = outs
    step = pl.program_id(0)
    slot = order[step]
    valid = token_valid(places[slot], lives[slot])
    x = x_ref[0].astype(F32)
    xhat, _ = norm_parts(x)
    normed_ref[...] = pad_rows((xhat * gain_ref[...] + shift_ref[...]) * valid).astype(BF16)
    valid_ref[...] = pad_rows(valid)

    @pl.when(lax.rem(step, every) == 0)
    def _():
        rows_ref[...] = pad_rows(x).astype(BF16)
        own_ref[...] = pad_rows(valid)


def prepare(order, places, lives, x, gain, shift, every):
    count = order.shape[0]
    width = x.shape[2]
    window = pl.BlockSpec((1, WTOK, width), lambda i, order, *_: (order[i], 0, 0))
    block = pl.BlockSpec((ROWS, width), lambda i, *_: (i, 0))
    return pl.pallas_call(
        partial(prepare_kernel, every),
        grid_spec=pltpu.PrefetchScalarGridSpec(
            num_scalar_prefetch=3,
            grid=(count,),
            in_specs=[window, whole(gain), whole(shift)],
            out_specs=[
                pl.BlockSpec((ROWS, width), lambda i, *_: (i // every, 0)),
                pl.BlockSpec((ROWS, 1), lambda i, *_: (i // every, 0)),
                block,
                pl.BlockSpec((ROWS, 1), lambda i, *_: (i, 0)),
            ],
        ),
        out_shape=[
            struct((count // every * ROWS, width), BF16),
            struct((count // every * ROWS, 1), F32),
            struct((count * ROWS, width), BF16),
            struct((count * ROWS, 1), F32),
        ],
        compiler_params=params(63),
        cost_estimate=cost(9),
        name="prepare",
    )(order, places, lives, x, gain, shift)


def mask_kernel(order, places, lives, top_ref, grad_ref):
    slot = order[pl.program_id(0)]
    valid = token_valid(places[slot], lives[slot])
    grad_ref[...] = pad_rows(top_ref[0].astype(F32) * valid).astype(BF16)


def mask_rows(order, places, lives, top):
    count = order.shape[0]
    width = top.shape[2]
    return pl.pallas_call(
        mask_kernel,
        grid_spec=pltpu.PrefetchScalarGridSpec(
            num_scalar_prefetch=3,
            grid=(count,),
            in_specs=[pl.BlockSpec((1, WTOK, width), lambda i, order, *_: (order[i], 0, 0))],
            out_specs=pl.BlockSpec((ROWS, width), lambda i, *_: (i, 0)),
        ),
        out_shape=struct((count * ROWS, width), BF16),
        compiler_params=params(63),
        cost_estimate=cost(6),
        name="mask_rows",
    )(order, places, lives, top)


def top_rows(shape):
    return pl.BlockSpec(shape, lambda i: (0, 0))


def row_block(shape, at):
    return pl.BlockSpec(shape, lambda i: (at, 0))


def total(refs, rows):
    value = refs[0][:rows].astype(F32)
    for ref in refs[1:]:
        value = value + ref[:rows].astype(F32)
    return value


def norm_two_kernel(count, *refs):
    parts, (x_ref, bias_ref, gain_ref, shift_ref, after_ref, normed_ref) = (
        refs[:count],
        refs[count:],
    )
    rows = x_ref.shape[0]
    after = x_ref[...].astype(F32) + total(parts, rows) + bias_ref[...]
    xhat, _ = norm_parts(after)
    after_ref[...] = after
    normed_ref[...] = (xhat * gain_ref[...] + shift_ref[...]).astype(BF16)


def norm_two(parts, x, at, bias, gain, shift):
    shape = (parts[-1].shape[0], x.shape[1])
    return pl.pallas_call(
        partial(norm_two_kernel, len(parts)),
        grid=(1,),
        in_specs=[top_rows(shape)] * len(parts)
        + [row_block(shape, at), whole(bias), whole(gain), whole(shift)],
        out_specs=[top_rows(shape)] * 2,
        out_shape=[struct(shape, F32), struct(shape, BF16)],
        compiler_params=params(14),
        cost_estimate=cost(3),
        name="norm_two",
    )(*parts, x, bias, gain, shift)


def finish_kernel(count, *refs):
    parts, (after_ref, valid_ref, bias_ref, out_ref) = refs[:count], refs[count:]
    rows = after_ref.shape[0]
    branch = total(parts, rows) + bias_ref[...]
    out_ref[...] = (valid_ref[...] * (after_ref[...] + branch)).astype(BF16)


def finish(parts, after, valid, at, bias):
    return pl.pallas_call(
        partial(finish_kernel, len(parts)),
        grid=(1,),
        in_specs=[top_rows(after.shape)] * (len(parts) + 1)
        + [row_block((after.shape[0], 1), at), whole(bias)],
        out_specs=top_rows(after.shape),
        out_shape=struct(after.shape, BF16),
        compiler_params=params(14),
        cost_estimate=cost(2.5),
        name="finish",
    )(*parts, after, valid, bias)


def norm_back(upstream, xhat, rstd, gain):
    weighted = upstream * gain
    inner = jnp.mean(weighted * xhat, axis=-1, keepdims=True)
    level = jnp.mean(weighted, axis=-1, keepdims=True)
    return rstd * (weighted - level - xhat * inner)


def norm_two_back_kernel(count, *refs):
    parts = refs[:count]
    after_ref, top_ref, gain_ref, grad_ref, branch_ref, sums_ref = refs[count:]
    rows = after_ref.shape[0]
    upstream = total(parts, rows)
    xhat, rstd = norm_parts(after_ref[...])
    top = top_ref[...].astype(F32)
    grad = top + norm_back(upstream, xhat, rstd, gain_ref[...])
    branch = grad.astype(BF16)
    grad_ref[...] = grad
    branch_ref[...] = branch
    sums_ref[0:1] = jnp.sum(upstream * xhat, axis=0, keepdims=True)
    sums_ref[1:2] = jnp.sum(upstream, axis=0, keepdims=True)
    sums_ref[2:3] = jnp.sum(branch.astype(F32), axis=0, keepdims=True)
    sums_ref[3:4] = jnp.sum(top, axis=0, keepdims=True)


def norm_two_back(parts, after, top, at, gain):
    sums = struct((4, after.shape[1]), F32)
    return pl.pallas_call(
        partial(norm_two_back_kernel, len(parts)),
        grid=(1,),
        in_specs=[top_rows(after.shape)] * (len(parts) + 1)
        + [row_block(after.shape, at), whole(gain)],
        out_specs=[top_rows(after.shape)] * 2 + [whole(sums)],
        out_shape=[struct(after.shape, F32), struct(after.shape, BF16), sums],
        compiler_params=params(14),
        cost_estimate=cost(4),
        name="norm_two_back",
    )(*parts, after, top, gain)


def norm_one_back_kernel(counts, *refs):
    x_ref, valid_ref, gain_ref, out_ref = refs[-4:]
    at = 0
    for part, count in enumerate(counts):
        parts, grad_ref = refs[at : at + count], refs[at + count]
        at += count + 1
        rows = slice(part * ROWS, part * ROWS + ROWS)
        upstream = total(parts, ROWS) * valid_ref[rows]
        xhat, rstd = norm_parts(x_ref[rows].astype(F32))
        grad = grad_ref[...] + norm_back(upstream, xhat, rstd, gain_ref[...])
        out_ref[rows] = grad.astype(BF16)


def norm_one_back(windows, x, valid, gain):
    shape = (ROWS, x.shape[1])
    operands, specs = [], []
    for parts, grad in windows:
        operands += [part[0] for part in parts] + [grad]
        specs += [
            pl.BlockSpec(shape, lambda i, at=at: (at, 0)) for at in (part[1] for part in parts)
        ]
        specs.append(whole(grad))
    return pl.pallas_call(
        partial(norm_one_back_kernel, [len(parts) for parts, _ in windows]),
        grid=(1,),
        in_specs=specs + [whole(x), whole(valid), whole(gain)],
        out_specs=whole(x),
        out_shape=struct(x.shape, BF16),
        compiler_params=params(20),
        cost_estimate=cost(3.5 * len(windows)),
        name="norm_one_back",
    )(*operands, x, valid, gain)


def qkv_kernel(count, cols, offsets, *refs):
    pieces = refs[:count]
    x_ref, bias_ref, q_ref, k_ref, v_ref, w_ref, sems = refs[count:]
    wide = q_ref.shape[1]

    @pl.when(pl.program_id(0) == 0)
    def _():
        assemble(offsets, pieces, w_ref, sems)

    result = (dot(x_ref[...], w_ref[:, wide:]) + bias_ref[...]).astype(BF16)
    for slot, ref in enumerate((q_ref, k_ref, v_ref)):
        ref[:, :cols] = result[:, slot * cols : (slot + 1) * cols]
        if wide > cols:
            ref[:, cols:] = jnp.zeros((ref.shape[0], wide - cols), BF16)


def project(offsets, pieces, x, bias, cols, wide):
    rows, width = x.shape
    step = 2 * ROWS
    block = pl.BlockSpec((step, wide), lambda i, *_: (i, 0))
    total_cols = wide + 3 * cols
    return pl.pallas_call(
        partial(qkv_kernel, len(pieces), cols),
        grid_spec=pltpu.PrefetchScalarGridSpec(
            num_scalar_prefetch=1,
            grid=(rows // step,),
            in_specs=[ANY] * len(pieces)
            + [pl.BlockSpec((step, width), lambda i, *_: (i, 0)), whole(bias)],
            out_specs=[block, block, block, pl.BlockSpec((width, total_cols), lambda i, *_: (0, 0))],
            scratch_shapes=[pltpu.SemaphoreType.DMA((len(pieces),))],
        ),
        out_shape=[struct((rows, wide), BF16)] * 3 + [struct((width, total_cols), BF16)],
        compiler_params=params(28),
        cost_estimate=cost(14),
        name="qkv",
    )(offsets, *pieces, x, bias)


def head_spans(heads, wide):
    spans = []
    for head in range(heads):
        first, last = head * HD, head * HD + HD
        low = first // 128 * 128
        high = min((last + 127) // 128 * 128, wide)
        spans.append((low, high, first, last))
    return spans


def lane_mask(span):
    low, high, first, last = span
    lane = lax.broadcasted_iota(jnp.int32, (1, high - low), 1) + low
    return jnp.where((lane >= first) & (lane < last), 1.0, 0.0).astype(BF16)


def shift_counts():
    token = lax.broadcasted_iota(jnp.int32, (ROWS, 128), 0)
    row = (token * 9363) >> 17
    col = token - row * WIN
    return jnp.maximum(WIN - 1 - row, 0), WIN - 1 - col


def shift_lanes(values, counts, back):
    for step in (1, 2, 4, 8):
        moved = pltpu.roll(values, step if back else 128 - step, 1)
        values = jnp.where((counts & step) != 0, moved, values)
    return values


def lane_kind():
    lane = lax.broadcasted_iota(jnp.int32, (ROWS, 128), 1) & 31
    return lane < WIN, (lane >= 16) & (lane < 16 + WIN), lane == 31


def split_two(values):
    high = values.astype(BF16)
    return high, (values - high.astype(F32)).astype(BF16)


def bias_operand(q, rel_high, rel_low, counts):
    table = (dot(q, rel_high) + dot(q, rel_low)) * (1.0 / SCALE)
    by_row = shift_lanes(table[:, :128], counts[0], False)
    by_col = shift_lanes(table[:, 128:], counts[1], False)
    is_row, is_col, is_last = lane_kind()
    packed = jnp.where(
        is_row, by_row, jnp.where(is_col, by_col, jnp.where(is_last, 1.0, 0.0))
    )
    high, low = split_two(packed)
    return jnp.concatenate([high, low], axis=1)


def add_lanes(parts, values, span):
    low, high = span[0], span[1]
    for index in range(low // 128, high // 128):
        piece = values[:, index * 128 - low : index * 128 - low + 128]
        parts[index] = piece if parts[index] is None else parts[index] + piece


def attend_kernel(heads, split, q_ref, k_ref, v_ref, rh_ref, rl_ref, mark_ref, w_ref, *outs):
    mixed_ref, shares_ref = outs[:2]
    q, k, v = q_ref[...], k_ref[...], v_ref[...]
    wide = q.shape[1]
    bias = bias_operand(q, rh_ref[...], rl_ref[...], shift_counts())
    parts = [None] * (wide // 128)
    for head, span in enumerate(head_spans(heads, wide)):
        mask = lane_mask(span)
        cut = slice(span[0], span[1])
        scores = dot_nt(
            jnp.concatenate([q[:, cut], bias], axis=1),
            jnp.concatenate([k[:, cut] * mask, mark_ref[head]], axis=1),
        )
        top = jnp.max(scores, axis=-1, keepdims=True)
        shifted = jnp.exp(SCALE * (scores - top))
        norm = jnp.sum(shifted, axis=-1, keepdims=True)
        shares = (shifted * (1.0 / norm)).astype(BF16)
        shares_ref[:, head * 256 : head * 256 + ROWS] = shares
        add_lanes(parts, dot(shares, v[:, cut] * mask), span)
    mixed = jnp.concatenate(parts, axis=1).astype(BF16)
    cols = heads * HD
    mixed_ref[...] = mixed[:, :cols]
    branch = dot_nt(mixed, w_ref[...]).astype(BF16)
    if split:
        step = pl.program_id(0)
        for sent in range(split):

            @pl.when(step == sent)
            def _(sent=sent):
                outs[3 + sent][...] = branch

        @pl.when(step >= split)
        def _():
            outs[2][...] = branch
    else:
        outs[2][...] = branch


def split_specs(windows, split, width):
    rows = ROWS * (windows - split)
    if not split:
        return [pl.BlockSpec((ROWS, width), lambda i: (i, 0))], [struct((rows, width), BF16)]
    return (
        [
            pl.BlockSpec((ROWS, width), lambda i: (jnp.maximum(i - split, 0), 0)),
            pl.BlockSpec((ROWS, width), lambda i: (jnp.minimum(i, split - 1), 0)),
        ],
        [struct((rows, width), BF16), struct((ROWS * split, width), BF16)],
    )


def attend(heads, part, windows, split, q, k, v, rel_high, rel_low, marks, weights):
    wide = q.shape[1]
    width = weights.shape[0]

    def place(i):
        return (i + split) % windows if split else i

    block = pl.BlockSpec((ROWS, wide), lambda i: (part * windows + place(i), 0))
    specs, shapes = split_specs(windows, split, width)
    if split:
        one = struct((ROWS, width), BF16)
        specs, shapes = specs[:1] + [whole(one)] * split, shapes[:1] + [one] * split
    return pl.pallas_call(
        partial(attend_kernel, heads, split),
        grid=(windows,),
        in_specs=[
            block,
            block,
            block,
            whole(rel_high),
            whole(rel_low),
            whole(marks),
            pl.BlockSpec((width, wide), lambda i: (0, 0)),
        ],
        out_specs=[
            pl.BlockSpec((ROWS, heads * HD), lambda i: (place(i), 0)),
            pl.BlockSpec((ROWS, heads * 256), lambda i: (place(i), 0)),
        ]
        + specs,
        out_shape=[
            struct((windows * ROWS, heads * HD), BF16),
            struct((windows * ROWS, heads * 256), BF16),
        ]
        + shapes,
        compiler_params=params(16),
        cost_estimate=cost(13.5),
        name="attend",
    )(q, k, v, rel_high, rel_low, marks, weights)


def attend_back_kernel(heads, windows, split, count, *refs):
    pieces = refs[:count]
    q_ref, k_ref, v_ref, shares_ref, rh_ref, mark_ref, w_ref = refs[count : count + 7]
    normed_ref, valid_ref = refs[count + 7 : count + 9]
    grads_ref, branch_ref, rel_ref, sum_ref, norm_ref = refs[count + 9 : count + 14]
    outs = refs[count + 14 :]
    step = pl.program_id(0)

    @pl.when(step == 0)
    def _():
        start = 0
        for piece in pieces:
            branch_ref[start : start + piece.shape[0]] = piece[...]
            start += piece.shape[0]
        rel_ref[...] = jnp.zeros(rel_ref.shape, F32)
        sum_ref[...] = jnp.zeros(sum_ref.shape, F32)
        norm_ref[...] = jnp.zeros(norm_ref.shape, F32)

    place = lax.rem(step + split, windows) if split else step
    q, k, v = q_ref[...], k_ref[...], v_ref[...]
    wide = q.shape[1]
    top = branch_ref[pl.ds(pl.multiple_of(place * ROWS, 16), ROWS), :]
    grad_mixed = dot(top, w_ref[:, :wide]).astype(BF16)
    grad_q, grad_k, grad_v = ([None] * (wide // 128) for _ in range(3))
    grad_bias = None
    for head, span in enumerate(head_spans(heads, wide)):
        mask = lane_mask(span)
        cut = slice(span[0], span[1])
        size = span[1] - span[0]
        upper = grad_mixed[:, cut]
        rounded = shares_ref[:, head * 256 : head * 256 + ROWS]
        shares = rounded.astype(F32)
        weighted = shares * dot_nt(upper, v[:, cut] * mask)
        inner = jnp.sum(weighted, axis=-1, keepdims=True)
        grad_scores = (weighted - shares * inner).astype(BF16)
        add_lanes(grad_v, dot_tn(rounded, upper * mask), span)
        both = dot(
            grad_scores,
            jnp.concatenate([k[:, cut] * mask, mark_ref[head][:, :128]], axis=1),
        )
        add_lanes(grad_q, both[:, :size], span)
        part = both[:, size:]
        grad_bias = part if grad_bias is None else grad_bias + part
        add_lanes(grad_k, dot_tn(grad_scores, q[:, cut] * mask), span)
    counts = shift_counts()
    is_row, is_col, _ = lane_kind()
    by_row = shift_lanes(jnp.where(is_row, grad_bias, 0.0), counts[0], True)
    by_col = shift_lanes(jnp.where(is_col, grad_bias, 0.0), counts[1], True)
    packed = jnp.concatenate([by_row, by_col], axis=1).astype(BF16)
    extra = dot_nt(packed, rh_ref[...])
    rel_ref[...] += dot_tn(packed, q)
    grad_q = (SCALE * jnp.concatenate(grad_q, axis=1) + extra).astype(BF16)
    grad_k = (SCALE * jnp.concatenate(grad_k, axis=1)).astype(BF16)
    grad_v = jnp.concatenate(grad_v, axis=1).astype(BF16)
    cols = heads * HD
    for slot, grad in enumerate((grad_q, grad_k, grad_v)):
        grads_ref[:, slot * cols : (slot + 1) * cols] = grad[:, :cols]
    packed_grads = grads_ref[...]
    sum_ref[...] += jnp.sum(packed_grads.astype(F32), axis=0, keepdims=True)
    partial_sum = dot_nt(packed_grads, w_ref[:, wide:])
    norm_ref[0:1] += jnp.sum(partial_sum * normed_ref[...].astype(F32), axis=0, keepdims=True)
    norm_ref[1:2] += jnp.sum(partial_sum * valid_ref[...], axis=0, keepdims=True)
    result = partial_sum.astype(BF16)
    if split:
        keep_ref, send_ref = outs

        @pl.when(step < split)
        def _():
            send_ref[...] = result

        @pl.when(step >= split)
        def _():
            keep_ref[...] = result
    else:
        outs[0][...] = result


def attend_back(
    heads, part, windows, split, pieces, q, k, v, shares, rel_high, marks, weights, normed, valid
):
    wide = q.shape[1]
    width = weights.shape[0]

    def place(i):
        return (i + split) % windows if split else i

    block = pl.BlockSpec((ROWS, wide), lambda i: (part * windows + place(i), 0))
    specs, shapes = split_specs(windows, split, width)
    rows = windows * ROWS
    branch = struct((rows, width), BF16)
    rel = struct((256, wide), F32)
    sums = struct((1, 3 * heads * HD), F32)
    norms = struct((2, width), F32)
    return pl.pallas_call(
        partial(attend_back_kernel, heads, windows, split, len(pieces)),
        grid=(windows,),
        in_specs=[whole(piece) for piece in pieces]
        + [
            block,
            block,
            block,
            pl.BlockSpec((ROWS, heads * 256), lambda i: (place(i), 0)),
            whole(rel_high),
            whole(marks),
            whole(weights),
            pl.BlockSpec((ROWS, width), lambda i: (part * windows + place(i), 0)),
            pl.BlockSpec((ROWS, 1), lambda i: (part * windows + place(i), 0)),
        ],
        out_specs=[
            pl.BlockSpec((ROWS, 3 * heads * HD), lambda i: (place(i), 0)),
            whole(branch),
            whole(rel),
            whole(sums),
            whole(norms),
        ]
        + specs,
        out_shape=[struct((rows, 3 * heads * HD), BF16), branch, rel, sums, norms] + shapes,
        compiler_params=params(30),
        cost_estimate=cost(18.5),
        name="attend_back",
    )(*pieces, q, k, v, shares, rel_high, marks, weights, normed, valid)


def mlp_kernel(count, weights, split, offsets, *refs):
    pieces = refs[:count]
    weight_pieces = refs[count : count + weights]
    refs = refs[count + weights :]
    after_any, top_ref, bias_ref, down_bias_ref = refs[:4]
    active_ref, hidden_ref, normed_any, sum_ref = refs[4:8]
    outs = refs[8 : 12 if split else 10]
    up, down, normed_ref, after_ref, send_ref, out_send_ref, sems, row_sems = refs[len(outs) + 8 :]
    step = pl.program_id(0)
    steps = pl.num_programs(0)
    block = top_ref.shape[0]
    units = up.shape[1]
    copies = []
    for half, target in enumerate((down, up)):
        copies.append([])
        for index, piece in enumerate(weight_pieces):
            rows = piece.shape[0]
            start = pl.multiple_of(offsets[index], 16)
            copies[half].append(
                pltpu.make_async_copy(
                    piece.at[:, half * units : (half + 1) * units],
                    target.at[pl.ds(start, rows)],
                    sems.at[half, index],
                )
            )
    row_copies, start = [], 0
    for index, piece in enumerate(pieces):
        rows = piece.shape[0]
        row_copies.append(
            pltpu.make_async_copy(
                piece, normed_ref.at[pl.ds(start, rows)], row_sems.at[index]
            )
        )
        start += rows
    normed_out = pltpu.make_async_copy(normed_ref, normed_any, row_sems.at[count])
    after_in = pltpu.make_async_copy(after_any, after_ref, row_sems.at[count + 1])
    if split:
        send_out = pltpu.make_async_copy(send_ref, outs[1], row_sems.at[count + 2])
        out_send_out = pltpu.make_async_copy(out_send_ref, outs[3], row_sems.at[count + 3])

    @pl.when(step == 0)
    def _():
        for copy in row_copies + copies[1] + copies[0]:
            copy.start()
        after_in.start()
        sum_ref[...] = jnp.zeros(sum_ref.shape, F32)
        for copy in row_copies + copies[1]:
            copy.wait()
        normed_out.start()

    place = 1 - step if split else step
    normed = normed_ref[pl.ds(pl.multiple_of(place * block, 16), block), :]
    hidden = dot(normed, up[...]) + bias_ref[...]

    @pl.when(step == 0)
    def _():
        for copy in copies[0]:
            copy.wait()

    half = 0.5 * (1.0 + lax.erf(hidden * (0.5**0.5)))
    slope = half + hidden * jnp.exp(-0.5 * hidden * hidden) * float((2.0 * np.pi) ** -0.5)
    active = (hidden * half).astype(BF16)
    active_ref[...] = active
    grad = (dot(top_ref[...], down[...]) * slope).astype(BF16)
    hidden_ref[...] = grad
    sum_ref[...] += jnp.sum(grad.astype(F32), axis=0, keepdims=True)
    back = dot_nt(grad, up[...]).astype(BF16)
    result = dot_nt(active, down[...])
    if split:

        @pl.when(step == 0)
        def _():
            send_ref[...] = back
            out_send_ref[...] = result.astype(BF16)
            send_out.start()
            out_send_out.start()
            after_in.wait()

        @pl.when(step == 1)
        def _():
            outs[0][...] = back
            own = result[:ROWS] + after_ref[...] + down_bias_ref[...]
            outs[2][:ROWS] = own.astype(BF16)
            outs[2][ROWS:] = result[ROWS:].astype(BF16)
            send_out.wait()
            out_send_out.wait()
    else:
        outs[0][...] = back
        outs[1][...] = result.astype(BF16)

        @pl.when(step == 0)
        def _():
            after_in.wait()

    @pl.when(step == steps - 1)
    def _():
        normed_out.wait()


def mlp(offsets, pieces, weight_pieces, top, part, bias, after, down_bias, split):
    rows = sum(piece.shape[0] for piece in pieces)
    width = pieces[0].shape[1]
    units = weight_pieces[0].shape[1] // 2
    block = 2 * ROWS
    blocks = rows // block
    normed = struct((rows, width), BF16)
    sums = struct((1, units), F32)

    def place(i):
        return 1 - i if split else i

    wide = pl.BlockSpec((block, units), lambda i, *_: (place(i), 0))
    back = struct((block, width), BF16)
    if split:
        back_specs, back_shapes = [whole(back), ANY] * 2, [back] * 4
    else:
        back_specs = [pl.BlockSpec((block, width), lambda i, *_: (i, 0))] * 2
        back_shapes = [normed] * 2
    return pl.pallas_call(
        partial(mlp_kernel, len(pieces), len(weight_pieces), split),
        grid_spec=pltpu.PrefetchScalarGridSpec(
            num_scalar_prefetch=1,
            grid=(blocks,),
            in_specs=[ANY] * (len(pieces) + len(weight_pieces) + 1)
            + [
                pl.BlockSpec((block, width), lambda i, *_: (part * blocks + place(i), 0)),
                whole(bias),
                whole(down_bias),
            ],
            out_specs=[wide, wide, ANY, whole(sums)] + back_specs,
            scratch_shapes=[
                pltpu.VMEM((width, units), BF16),
                pltpu.VMEM((width, units), BF16),
                pltpu.VMEM((rows, width), BF16),
                pltpu.VMEM(after.shape, F32),
                pltpu.VMEM((block, width), BF16),
                pltpu.VMEM((block, width), BF16),
                pltpu.SemaphoreType.DMA((2, len(weight_pieces))),
                pltpu.SemaphoreType.DMA((len(pieces) + 4,)),
            ],
        ),
        out_shape=[struct((rows, units), BF16)] * 2 + [normed, sums] + back_shapes,
        compiler_params=params(48),
        cost_estimate=cost(21),
        name="mlp",
    )(offsets, *pieces, *weight_pieces, after, top, bias, down_bias)


SEND_PARTS = {2: ((2, 3), (0, 1)), 3: ((3,), (1, 2), (0,))}


def weight_grad_kernel(sizes, share, sends, targets, *refs):
    count = 2 * sum(sizes)
    operands = refs[:count]
    outs, (result, sems) = refs[count:-2], refs[-2:]
    keep_ref = outs[sends] if sends else None
    pair_ref = None if sends else outs[0]
    lead = keep_ref.shape[2] if sends else 0
    step = pl.program_id(0)
    steps = pl.num_programs(0)
    chunk = operands[0].shape[1]
    pieces = chunk // share
    base = pl.multiple_of(step * chunk, 16)
    at, first = 0, 0
    for size in sizes:
        value = None
        for _ in range(size):
            left, right = operands[at], operands[at + 1]
            at += 2
            term = dot_tn(left[...], right[...])
            value = term if value is None else value + term
        span = value.shape[1]
        result[pl.ds(base, chunk), first : first + span] = value.astype(BF16)
        first += span

    def copy(index, out, slot):
        return pltpu.make_async_copy(
            result.at[pl.ds(pl.multiple_of(index * share, 16), share), pl.ds(0, lead)],
            out.at[slot],
            sems.at[0, index],
        )

    def pair_copy(index, slot):
        return pltpu.make_async_copy(
            result.at[
                pl.ds(pl.multiple_of(index * share, 16), share),
                pl.ds(lead, result.shape[1] - lead),
            ],
            pair_ref.at[lax.rem(slot, 4), 1 - slot // 4],
            sems.at[1, index],
        )

    for piece in range(pieces):
        index = step * pieces + piece
        slot = targets[index]

        if lead:

            for out, slots in zip(outs, SEND_PARTS[sends]):

                @pl.when((slot >= slots[0]) & (slot <= slots[-1]))
                def _(out=out, slots=slots):
                    copy(index, out, slot - slots[0]).start()

            @pl.when(slot >= 4)
            def _():
                copy(index, keep_ref, slot - 4).start()

        if pair_ref is not None:
            pair_copy(index, slot).start()

    @pl.when(step == steps - 1)
    def _():
        for index in range(8):
            if lead:
                copy(index, keep_ref, 0).wait()
            if pair_ref is not None:
                pair_copy(index, 0).wait()


def plain_grad_kernel(sizes, *refs):
    count = 2 * sum(sizes)
    operands, out_ref = refs[:count], refs[count]
    at, first = 0, 0
    for size in sizes:
        value = None
        for _ in range(size):
            left, right = operands[at], operands[at + 1]
            at += 2
            term = dot_tn(left[...], right[...])
            value = term if value is None else value + term
        span = value.shape[1]
        out_ref[:, first : first + span] = value.astype(BF16)
        first += span


def weight_grad(targets, groups, share, sends=0):
    operands, specs = [], []
    chunk = 640 if targets is not None else 256
    total_cols = 0
    for group in groups:
        for left, at, rows, right in group:
            operands += [left, right]
            specs.append(pl.BlockSpec((rows, chunk), lambda i, *_, at=at: (at, i)))
            specs.append(whole(right))
        total_cols += group[0][3].shape[1]
    width = operands[0].shape[1]
    sizes = [len(group) for group in groups]
    if targets is None:
        return [
            pl.pallas_call(
                partial(plain_grad_kernel, sizes),
                grid=(width // chunk,),
                in_specs=specs,
                out_specs=pl.BlockSpec((chunk, total_cols), lambda i: (i, 0)),
                out_shape=struct((width, total_cols), BF16),
                compiler_params=params(32),
                cost_estimate=cost(13),
        name="weight_grad",
            )(*operands)
        ]
    if sends:
        counts = [len(slots) for slots in SEND_PARTS[sends]] + [4]
        shapes = [struct((count, share, total_cols), BF16) for count in counts]
    else:
        shapes = [struct((4, 2, share, total_cols), BF16)]
    return pl.pallas_call(
        partial(weight_grad_kernel, sizes, share, sends),
        grid_spec=pltpu.PrefetchScalarGridSpec(
            num_scalar_prefetch=1,
            grid=(width // chunk,),
            in_specs=specs,
            out_specs=[ANY] * len(shapes),
            scratch_shapes=[
                pltpu.VMEM((width, total_cols), BF16),
                pltpu.SemaphoreType.DMA((2, 8)),
            ],
        ),
        out_shape=shapes,
        compiler_params=params(32),
        cost_estimate=cost(13),
        name="weight_grad",
    )(targets, *operands)


def combine_kernel(layout, *refs):
    outs = refs[len(refs) - len(layout) :]
    at = 0
    for cells, out in zip(layout, outs):
        for row, lane, rows, lanes, terms in cells:
            value = None
            for lead, first in terms:
                term = refs[at][(0,) * lead + (slice(None), slice(first, first + lanes))]
                at += 1
                value = term.astype(F32) if value is None else value + term.astype(F32)
            out[row : row + rows, lane : lane + lanes] = value.astype(BF16)


def combine(*outs):
    operands, specs, layout = [], [], []
    for _, cells in outs:
        layout.append([])
        for row, lane, rows, lanes, terms in cells:
            places = []
            for array, index, first in terms:
                lead = array.ndim - 2
                block = (1,) * lead + (rows, array.shape[-1])
                place = tuple(index) + (0,) * (array.ndim - len(index))
                operands.append(array)
                specs.append(pl.BlockSpec(block, lambda i, place=place: place))
                places.append((lead, first))
            layout[-1].append((row, lane, rows, lanes, places))
    shapes = [struct(shape, BF16) for shape, _ in outs]
    return pl.pallas_call(
        partial(combine_kernel, layout),
        grid=(1,),
        in_specs=specs,
        out_specs=[whole(shape) for shape in shapes],
        out_shape=shapes,
        compiler_params=params(16),
        cost_estimate=cost(2),
        name="combine",
    )(*operands)


def place_kernel(order, *refs):
    pieces, out_ref = refs[:4], refs[4]
    for me in range(4):

        @pl.when(order[0] == me)
        def _(me=me):
            for part in range(pieces[0].shape[0] // ROWS):
                for index, step in enumerate((0, 2, 1, 3)):
                    start = (4 * part + (me ^ step)) * WTOK
                    value = pieces[index][part * ROWS : part * ROWS + WTOK]
                    out_ref[start : start + WTOK] = value.astype(F32)


def place_windows(order, pieces):
    height, width = pieces[0].shape
    rows = height // ROWS * 4 * WTOK
    lanes = width // 2
    return pl.pallas_call(
        place_kernel,
        grid_spec=pltpu.PrefetchScalarGridSpec(
            num_scalar_prefetch=1,
            grid=(2,),
            in_specs=[pl.BlockSpec((height, lanes), lambda i, *_: (0, i))] * 4,
            out_specs=pl.BlockSpec((rows, lanes), lambda i, *_: (0, i)),
        ),
        out_shape=struct((rows, width), F32),
        compiler_params=params(32),
        cost_estimate=cost(7),
        name="place_windows",
    )(order, *pieces)


def output_kernel(order, places, lives, *refs):
    pieces, out_ref, buffer = refs[:4], refs[4], refs[5]
    for me in range(4):

        @pl.when(order[0] == me)
        def _(me=me):
            for part in range(pieces[0].shape[0] // ROWS):
                for index, step in enumerate((0, 2, 1, 3)):
                    slot = 4 * part + (me ^ step)
                    value = pieces[index][part * ROWS : part * ROWS + WTOK].astype(F32)
                    value = value * token_valid(places[slot], lives[slot])
                    buffer[slot * WTOK : (slot + 1) * WTOK] = value

    out_ref[...] = buffer[...].astype(BF16)


def write_output(order, places, lives, pieces):
    height, width = pieces[0].shape
    rows = height // ROWS * 4 * WTOK
    lanes = width // 2
    return pl.pallas_call(
        output_kernel,
        grid_spec=pltpu.PrefetchScalarGridSpec(
            num_scalar_prefetch=3,
            grid=(2,),
            in_specs=[pl.BlockSpec((height, lanes), lambda i, *_: (0, i))] * 4,
            out_specs=pl.BlockSpec((rows, lanes), lambda i, *_: (0, i)),
            scratch_shapes=[pltpu.VMEM((rows, lanes), F32)],
        ),
        out_shape=struct((rows, width), BF16),
        compiler_params=params(32),
        cost_estimate=cost(7),
        name="write_output",
    )(order, places, lives, *pieces)


def key_marks(heads):
    marks = np.zeros((heads, ROWS, 256), np.float32)
    for head in range(heads):
        for token in range(WTOK):
            for half in (0, 128):
                marks[head, token, half + head * 32 + token // WIN] = 1.0
                marks[head, token, half + head * 32 + 16 + token % WIN] = 1.0
        marks[head, WTOK:, head * 32 + 31] = -1e30
    return marks.astype(BF16)


def rel_operand(rel_height, rel_width, heads, wide):
    high = rel_height[::-1].T
    flat = rel_width[::-1].T
    lanes = jnp.zeros((wide, 256), F32)

    def spread(block, row, lane):
        below = wide - row - HD
        return jnp.pad(block, ((row, below), (lane, 256 - lane - block.shape[1])))

    for head in range(heads):
        first = head * 32 + 16
        fit = min(RELN, 128 - first)
        lanes = lanes + spread(high, head * HD, head * 32)
        lanes = lanes + spread(flat[:, :fit], head * HD, 128 + first)
        if fit < RELN:
            lanes = lanes + spread(flat[:, fit:], head * HD, 128)
    return split_two(lanes)


def rel_result(sums, heads):
    high = jnp.zeros((RELN, HD), F32)
    flat = jnp.zeros((RELN, HD), F32)
    for head in range(heads):
        cols = sums[:, head * HD : head * HD + HD]
        high = high + cols[head * 32 : head * 32 + RELN]
        rolled = jnp.concatenate([cols[128:], cols[128:]], axis=0)
        flat = flat + rolled[head * 32 + 16 : head * 32 + 16 + RELN]
    return high[::-1], flat[::-1]


def add_all(values):
    out = values[0]
    for value in values[1:]:
        out = out + value
    return out


def tie(value, *others):
    return lax.optimization_barrier((value,) + others)[0]


def sync(*values):
    return lax.optimization_barrier(values)


def body(
    block_input,
    window_place,
    slot_live,
    norm_one_gain,
    norm_one_shift,
    qkv_weight,
    qv_bias,
    proj_weight,
    proj_bias,
    norm_two_gain,
    norm_two_shift,
    up_weight,
    up_bias,
    down_weight,
    down_bias,
    rel_height,
    rel_width,
    cotangent,
):
    data_parts = lax.axis_size("dp")
    model_parts = lax.axis_size("mp")
    data_index = lax.axis_index("dp")
    model_index = lax.axis_index("mp")
    width = block_input.shape[1]
    share = qkv_weight.shape[1]
    cols = qkv_weight.shape[2]
    heads = cols // HD
    wide = (cols + 127) // 128 * 128
    units = up_weight.shape[1]
    slots = window_place.shape[0]
    rings = data_parts == 8 and model_parts == 4 and slots == 8
    padded = (slots + model_parts - 1) // model_parts * model_parts
    halves = padded // 4 if rings else 1
    windows = padded // halves
    split = 2 if rings else 0
    part_rows = windows * ROWS
    own_rows = part_rows // model_parts

    if rings:
        depth, side = data_index // 2, data_index % 2
        y_bit, core_bit = model_index // 2, model_index % 2
        over_x = partial(lax.ppermute, axis_name="dp", perm=[(d, d ^ 1) for d in range(8)])
        over_z = partial(lax.ppermute, axis_name="dp", perm=[(d, (d + 2) % 8) for d in range(8)])
        over_y = partial(lax.ppermute, axis_name="mp", perm=[(m, m ^ 2) for m in range(4)])
        over_core = partial(lax.ppermute, axis_name="mp", perm=[(m, m ^ 1) for m in range(4)])

    def gather(piece):
        return [lax.all_gather(piece, "dp", axis=0, tiled=True)]

    if rings:
        offsets = []
        for back in range(4):
            behind = (depth - back) % 4
            offsets += [share * (2 * behind + side), share * (2 * behind + 1 - side)]
        offsets = jnp.stack(offsets).astype(jnp.int32)
    else:
        offsets = jnp.zeros((1,), jnp.int32)

    def scatter(parts):
        return lax.psum_scatter(parts[0], "dp", scatter_dimension=0, tiled=True).astype(F32)

    def rows_scatter(parts):
        return [lax.psum_scatter(parts[0], "mp", scatter_dimension=0, tiled=True)]

    def rows_gather(own):
        return [lax.all_gather(own, "mp", axis=0, tiled=True)]

    def own_slice(array):
        rows = array.shape[0] // model_parts
        return lax.dynamic_slice_in_dim(array, model_index * rows, rows, 0)

    first_piece = jnp.concatenate(
        [
            jnp.pad(proj_weight.T, ((0, 0), (0, wide - cols))),
            qkv_weight[0],
            qkv_weight[1],
            qkv_weight[2],
        ],
        axis=1,
    )
    other_piece = jnp.concatenate([down_weight.T, up_weight], 1)

    row = lambda v: v.reshape(1, -1)
    gain_one, shift_one = row(norm_one_gain), row(norm_one_shift)
    gain_two, shift_two = row(norm_two_gain), row(norm_two_shift)
    bias_local = lax.dynamic_slice_in_dim(qv_bias, model_index * cols, cols, 1)
    bias_qkv = row(jnp.stack([bias_local[0], jnp.zeros_like(bias_local[0]), bias_local[1]]))
    up_local = row(lax.dynamic_slice_in_dim(up_bias, model_index * units, units, 0))
    rel_high, rel_low = rel_operand(rel_height, rel_width, heads, wide)
    marks = jnp.asarray(key_marks(heads))

    steps = (0, 2, 1, 3)
    if rings:
        local = [model_index ^ step for step in steps]
        places = [4 * part + spot for part in range(halves) for spot in local]
    else:
        local = [jnp.int32(spot) for spot in range(windows)]
        places = local
    local = jnp.stack(local).astype(jnp.int32)
    places = jnp.stack(places).astype(jnp.int32)
    if rings:
        targets = []
        for d in range(8):
            ahead = (d // 2 - depth) % 4
            targets.append(ahead + jnp.where(d % 2 == side, 4, 0))
        targets = jnp.stack(targets).astype(jnp.int32)
    else:
        targets = None

    def by_window(array):
        array = array.reshape((slots, WTOK) + array.shape[1:])
        return jnp.pad(array, [(0, padded - slots)] + [(0, 0)] * (array.ndim - 1))

    places_all = jnp.pad(window_place, (0, padded - slots))
    lives_all = jnp.pad(slot_live, (0, padded - slots))
    blocks = [(part, part_rows) for part in range(halves)]

    def start(x):
        every = 4 if rings else 1
        return prepare(places, places_all, lives_all, x, gain_one, shift_one, every)

    def masked(top):
        return mask_rows(places, places_all, lives_all, top)

    def attention(part, q, k, v, weights):
        return attend(heads, part, windows, split, q, k, v, rel_high, rel_low, marks, weights)

    def attention_back(part, pieces, q, k, v, shares, weights):
        return attend_back(
            heads,
            part,
            windows,
            split,
            pieces,
            q,
            k,
            v,
            shares,
            rel_high,
            marks,
            weights,
            normed,
            valid,
        )

    def down_groups(mlps):
        return [[(grad_top, *blocks[i], mlps[i][0]) for i in range(halves)]]

    def up_groups(mlps):
        return [[(mlps[i][2], 0, part_rows, mlps[i][1]) for i in range(halves)]]

    def first_groups(backs, attended):
        return [
            [(normed, *blocks[i], backs[i][0]) for i in range(halves)],
            [(backs[i][1], 0, part_rows, attended[i][0]) for i in range(halves)],
        ]

    def bundle(sums_two, backs, mlps):
        qv_sums = add_all([item[3] for item in backs]).reshape(3, cols)[0::2]
        rel_sums = rel_result(add_all([item[2] for item in backs]), heads)
        up_sums = add_all([item[3] for item in mlps]).reshape(units)
        qv_full = lax.dynamic_update_slice_in_dim(
            jnp.zeros((2, width), F32), qv_sums, model_index * cols, 1
        )
        up_full = lax.dynamic_update_slice_in_dim(
            jnp.zeros(up_bias.shape, F32), up_sums, model_index * units, 0
        )
        norms = add_all([item[4] for item in backs])
        arrays = [norms, add_all(sums_two), up_full, qv_full, *rel_sums]
        flat = jnp.concatenate([array.reshape(-1) for array in arrays])
        count = (flat.size + 1023) // 1024 * 1024
        return jnp.pad(flat, (0, count - flat.size)).reshape(-1, 128)

    x_windows = by_window(block_input)
    if not rings:
        first_weights, other_weights = gather(first_piece), gather(other_piece)
        rows_in, own_valid, normed, valid = start(x_windows)
        grad_top = masked(by_window(cotangent))
        own_in, own_top, own_valid = own_slice(rows_in), own_slice(grad_top), own_slice(own_valid)
        q, k, v, weights = project(offsets, first_weights, normed, bias_qkv, cols, wide)
        attended = [attention(0, q, k, v, weights)]
        after, normed_two = norm_two(
            rows_scatter(attended[0][2:]), own_in, 0, row(proj_bias), gain_two, shift_two
        )
        none = jnp.zeros((8, 128), F32)
        mlps = [
            mlp(
                offsets,
                rows_gather(normed_two),
                other_weights,
                grad_top,
                0,
                up_local,
                none,
                row(down_bias),
                False,
            )
        ]
        grad_after, branch, sums = norm_two_back(
            rows_scatter(mlps[0][4:5]), after, own_top, 0, gain_two
        )
        sums_two = [sums]
        result = mlps[0][5]
        own = finish(rows_scatter([result]), after, own_valid, 0, row(down_bias))

        def unpad(array):
            array = array.reshape(padded, ROWS, width)[:slots, :WTOK]
            return array.reshape(slots * WTOK, width)

        block_output = unpad(rows_gather(own)[0])
        down_grad = scatter(weight_grad(None, down_groups(mlps), share))
        up_grad = scatter(weight_grad(None, up_groups(mlps), share))
        backs = [attention_back(0, rows_gather(branch), q, k, v, attended[0][1], weights)]
        parts = [(part, 0) for part in rows_scatter(backs[0][5:])]
        own = norm_one_back([(parts, grad_after)], own_in, own_valid, gain_one)
        input_grad = unpad(rows_gather(own)[0]).astype(F32)
        first_grad = scatter(weight_grad(None, first_groups(backs, attended), share))
        vector = lax.psum(bundle(sums_two, backs, mlps), ("dp", "mp"))
    else:
        def second_norm(part, keep, came, crossed):
            return norm_two(
                [keep, came, crossed], rows_in, part, bias_proj, gain_two, shift_two
            )

        def second_back(part, after, keep, came, crossed):
            return norm_two_back([keep, came, crossed], after, grad_top, 4 * part, gain_two)

        def spread(own, across):
            return [own, across, over_core(own), over_core(across)]

        rows = (ROWS, width)

        def second(keep, came, at=0):
            return (at, 0, *rows, [(keep, (1,), 0), (came, (1,), 0)])

        z1, x0 = over_z(first_piece), over_x(first_piece)
        z1, x0, x_windows, other_piece, rel_high, rel_low, cotangent = sync(
            z1, x0, x_windows, other_piece, rel_high, rel_low, cotangent
        )
        z2, x1 = over_z(z1), over_x(z1)
        rows_in, own_valid, normed, valid = start(x_windows)
        z2, x1, normed, cotangent, gain_two, shift_two, bias_proj, bias_down = sync(
            z2, x1, normed, cotangent, gain_two, shift_two, row(proj_bias), row(down_bias)
        )
        z3, x2 = over_z(z2), over_x(z2)
        z3, x2, normed, top_windows, other_piece = sync(
            z3, x2, normed, by_window(cotangent), other_piece
        )
        x3 = over_x(z3)
        oz1 = over_z(other_piece)
        grad_top = masked(top_windows)
        x3, normed, grad_top, other_late, gain_two, shift_two, bias_proj, bias_down = sync(
            x3, normed, grad_top, other_piece, gain_two, shift_two, bias_proj, bias_down
        )
        ox0 = over_x(other_late)
        first_weights = [first_piece, x0, z1, x1, z2, x2, z3, x3]
        q, k, v, weights = project(offsets, first_weights, normed, bias_qkv, cols, wide)
        oz1, ox0, q = sync(oz1, ox0, q)

        oz2, ox1 = over_z(oz1), over_x(oz1)
        a0 = attention(0, q, k, v, weights)
        oz2, ox1, a0 = sync(oz2, ox1, a0)
        oz3, ox2 = over_z(oz2), over_x(oz2)
        came0, came_y = over_core(a0[3]), over_core(a0[4])
        (passed0,) = combine((rows, [(0, 0, *rows, [(a0[2], (1,), 0), (came_y, (0,), 0)])]))
        crossed0 = over_y(passed0)
        a1 = attention(1, tie(q, passed0), k, v, weights)
        crossed0, a1 = sync(crossed0, a1)
        came_y, came1 = over_core(a1[4]), over_core(a1[3])
        (passed1,) = combine((rows, [(0, 0, *rows, [(a1[2], (1,), 0), (came_y, (0,), 0)])]))
        crossed1 = over_y(passed1)
        after0, own0 = second_norm(0, tie(a0[2], passed1, came1), came0, crossed0)
        across0 = over_y(own0)
        oz3, ox2 = sync(oz3, ox2, own0)[:2]
        ox3, ox4 = over_x(oz3[: share // 2]), over_x(oz3[share // 2 :])
        attended = [a0, a1]
        after1, own1 = second_norm(1, tie(a1[2], own0), came1, crossed1)
        ox3, ox4, across0, own1 = sync(ox3, ox4, across0, own1)
        other_weights = [other_piece, ox0, oz1, ox1, oz2, ox2, oz3, ox3, ox4]
        other_offsets = jnp.concatenate([offsets, offsets[7:] + share // 2])
        across1 = over_y(own1)
        pieces0 = spread(tie(own0, own1), across0)

        m0 = mlp(other_offsets, pieces0, other_weights, grad_top, 0, up_local, after0, bias_down, True)
        across1, m0 = sync(across1, m0)
        pieces1 = spread(own1, across1)
        came0, out_came0 = over_core(m0[5]), over_core(m0[7])
        (passed0,) = combine((rows, [second(m0[4], came0)]))
        crossed0 = over_y(passed0)
        pieces1[0] = tie(pieces1[0], passed0)
        m1 = mlp(other_offsets, pieces1, other_weights, grad_top, 1, up_local, after1, bias_down, True)
        crossed0, out_came0, m1 = sync(crossed0, out_came0, m1)
        mlps = [m0, m1]
        came1, out_came1 = over_core(m1[5]), over_core(m1[7])
        grad_after0, branch0, sums0 = second_back(0, after0, m0[4], came0, crossed0)
        across0 = over_y(branch0)
        passed1, out_passed0, out_passed1 = combine(
            (rows, [second(tie(m1[4], branch0), came1)]),
            (rows, [second(m0[6], out_came0)]),
            (rows, [second(m1[6], out_came1)]),
        )
        left = tie(m0, passed1)
        (down_pairs,) = weight_grad(targets, down_groups([left, m1]), share)
        across0, passed1, down_pairs = sync(across0, passed1, down_pairs)
        crossed1 = over_y(passed1)
        branches0 = spread(branch0, across0)
        left = tie(m0, down_pairs)
        up_high, up_low, up_keep = weight_grad(targets, up_groups([left, m1]), share, 2)
        down_held = over_z(down_pairs[3])
        crossed1, branches0, up_high, up_low, up_keep = sync(
            crossed1, branches0, up_high, up_low, up_keep
        )

        up_came_high = over_x(up_high)

        def down_cells(k, held, lane):
            return [
                (0, half * units, share, units, [(down_pairs, (k, half), 0), (held, at, first)])
                for half, (at, first) in enumerate(lane)
            ]

        grad_after1, branch1, sums1 = second_back(1, after1, m1[4], came1, crossed1)
        sums_two = [sums0, sums1]
        across1 = over_y(branch1)
        (down_held,) = combine(
            (
                (share, 2 * units),
                down_cells(2, tie(down_held, branch1), [((0,), 0), ((1,), 0)]),
            )
        )
        branches0[0] = tie(branches0[0], down_held)
        down_held = over_z(down_held)
        b0 = attention_back(0, branches0, q, k, v, a0[1], weights)
        across1, up_came_high, down_held, b0 = sync(across1, up_came_high, down_held, b0)
        branches1 = spread(branch1, across1)
        came0 = over_core(b0[6])
        up_came_low = over_x(up_low)

        passed0, held = combine(
            (rows, [second(b0[5], came0)]),
            ((share, 2 * units), down_cells(1, down_held, [((0,), 0), ((0,), units)])),
        )
        crossed0 = over_y(passed0)
        held = over_z(held)
        branches1[0] = tie(branches1[0], passed0)
        out_crossed0 = over_y(tie(out_passed0, passed0))
        b1 = attention_back(1, branches1, q, k, v, a1[1], weights)
        crossed0, held, up_came_low, out_crossed0, b1 = sync(
            crossed0, held, up_came_low, out_crossed0, b1
        )
        backs = [b0, b1]
        came1 = over_core(b1[6])
        vector = bundle(sums_two, backs, mlps)
        vector_came = lax.ppermute(vector, "mp", [(m, m ^ 1) for m in range(4)])
        came1, vector_came, vector = sync(came1, vector_came, vector)
        vector = vector + vector_came
        vector_came = lax.ppermute(vector, "mp", [(m, m ^ 2) for m in range(4)])
        down_held = held
        passed1, down_other, up_held = combine(
            (rows, [second(b1[5], came1)]),
            (
                (share, units),
                [(0, 0, share, units, [(down_pairs, (0, 1), 0), (down_held, (0,), units)])],
            ),
            (
                (share, units),
                [(0, 0, share, units, [(up_keep, (3,), 0), (up_came_high, (1,), 0)])],
            ),
        )
        crossed1 = over_y(passed1)
        up_held, down_other = over_z(up_held), over_x(down_other)
        left = tie(b0, passed1)
        out_crossed1 = over_y(tie(out_passed1, passed1))
        firsts = weight_grad(targets, first_groups([left, b1], attended), share, 3)
        crossed1, down_other, up_held, firsts = sync(crossed1, down_other, up_held, firsts)
        first_three, first_two, first_last, first_keep = firsts

        came_three = over_x(first_three)
        (up_sum,) = combine(
            (
                (share, units),
                [
                    (
                        0,
                        0,
                        share,
                        units,
                        [(up_keep, (2,), 0), (up_came_high, (0,), 0), (up_held, (0,), 0)],
                    )
                ],
            )
        )
        held = over_z(up_sum)
        own = norm_one_back(
            [
                ([(b0[5], 0), (came0, 0), (tie(crossed0, up_sum), 0)], grad_after0),
                ([(b1[5], 0), (came1, 0), (crossed1, 0)], grad_after1),
            ],
            rows_in,
            own_valid,
            gain_one,
        )
        in_across = over_y(tie(own, vector_came))
        (out_own,) = combine(
            (
                (2 * ROWS, width),
                [
                    (
                        part * ROWS,
                        0,
                        *rows,
                        [(keep, (0,), 0), (came, (0,), 0), (crossed, (0,), 0)],
                    )
                    for part, (keep, came, crossed) in enumerate(
                        (
                            (m0[6], out_came0, tie(out_crossed0, own)),
                            (m1[6], out_came1, out_crossed1),
                        )
                    )
                ],
            ),
        )
        came_three, held, own, out_own, vector, vector_came = sync(
            came_three, held, own, out_own, vector, vector_came
        )
        vector = vector + vector_came
        came_two = over_x(first_two)
        (held,) = combine(
            (
                (share, 2 * units),
                [
                    (0, 0, share, units, [(first_keep, (3,), 0), (came_three, (0,), 0)]),
                    (
                        0,
                        units,
                        share,
                        units,
                        [(up_keep, (1,), 0), (up_came_low, (1,), 0), (held, (0,), 0)],
                    ),
                ],
            ),
        )
        held = over_z(held)
        vector_came = lax.ppermute(vector, "dp", [(d, d ^ 2) for d in range(8)])
        out_across = over_y(tie(out_own, own))
        came_two, held, vector_came, in_across = sync(came_two, held, vector_came, in_across)
        vector = vector + vector_came
        up_last = held[:, units:]

        def first_cell(k, held):
            return (
                0,
                0,
                share,
                4 * cols,
                [(first_keep, (k,), 0), (came_two, (k - 1,), 0), (held, (0,), 0)],
            )

        (held,) = combine(((share, 4 * cols), [first_cell(2, held)]))
        held = over_z(held)
        vector_came = lax.ppermute(vector, "dp", [(d, d ^ 4) for d in range(8)])
        in_pieces = spread(own, in_across)
        input_grad = place_windows(local, in_pieces)
        held, vector_came, input_grad = sync(held, vector_came, input_grad)
        vector = vector + vector_came
        vector_came = lax.ppermute(vector, "dp", [(d, d ^ 1) for d in range(8)])
        came_last = over_x(tie(first_last, held))
        (held,) = combine(((share, 4 * cols), [first_cell(1, held)]))
        held = over_z(held)
        vector = vector + vector_came
        came_last, out_own, out_across = sync(came_last, out_own, out_across)
        out_pieces = spread(out_own, out_across)
        block_output = write_output(local, places_all, lives_all, out_pieces)

        def last(*values):
            out = values[0].astype(F32)
            for value in values[1:]:
                out = out + value.astype(F32)
            return out

        down_grad = last(down_pairs[0, 0], down_held[:, :units], down_other)
        up_grad = last(up_keep[0], up_came_low[0], up_last)
        first_grad = last(first_keep[0], came_last[0], held)

    shapes = [(2, width), (4, width), (up_bias.size,), (2, width), (RELN, HD), (RELN, HD)]
    outs, at = [], 0
    flat = vector.reshape(-1)
    for shape in shapes:
        size = int(np.prod(shape))
        outs.append(flat[at : at + size].reshape(shape))
        at += size
    one_sums, two_sums, up_bias_grad, qv_bias_grad, height_grad, width_grad = outs
    shift_one_grad = one_sums[1]
    gain_one_grad = (one_sums[0] - norm_one_shift * shift_one_grad) / norm_one_gain
    qkv_grad = jnp.stack([first_grad[:, slot * cols : (slot + 1) * cols] for slot in range(3)])
    proj_grad = first_grad[:, 3 * cols :].T
    return (
        block_output,
        input_grad,
        gain_one_grad,
        shift_one_grad,
        qkv_grad,
        qv_bias_grad,
        proj_grad,
        two_sums[2],
        two_sums[0],
        two_sums[1],
        up_grad,
        up_bias_grad,
        down_grad.T,
        two_sums[3],
        height_grad,
        width_grad,
    )


def solution(mesh):
    in_specs = (
        P("dp", None),
        P("dp"),
        P("dp"),
        P(),
        P(),
        P(None, "dp", "mp"),
        P(),
        P("mp", "dp"),
        P(),
        P(),
        P(),
        P("dp", "mp"),
        P(),
        P("mp", "dp"),
        P(),
        P(),
        P(),
        P("dp", None),
    )
    out_specs = (
        P("dp", None),
        P("dp", None),
        P(),
        P(),
        P(None, "dp", "mp"),
        P(),
        P("mp", "dp"),
        P(),
        P(),
        P(),
        P("dp", "mp"),
        P(),
        P("mp", "dp"),
        P(),
        P(),
        P(),
    )
    return jax.shard_map(body, mesh=mesh, in_specs=in_specs, out_specs=out_specs, check_vma=False)
```
